32 devices in a mesh: fsdp: 4 (over y, core), ctx: 4 (over z), tp: 2 (over x).
Axes of the slice: x: 2, y: 2, z: 4, core: 2. Of those that a mesh axis runs over, the one named last changes fastest.
Arguments:
- tokens: bfloat16 [4, 2048, 768], P('fsdp', 'ctx'), may hold values from -6 to 6
- segments: int32 [4, 2048], P('fsdp'), may hold values from 0 to 6, as said below
- routes: int32 [4, 2048, 2], P('fsdp', 'ctx'), may hold values from 0 to 7, all different within a row; in each aligned block of 512 rows (0 to 511, 512 to 1023, ..., all dimensions but the last counted through in order) at most 192 rows name the same one
- query_weight: bfloat16 [768, 768], P('fsdp', 'tp'), may hold values from -0.21875 to 0.21875
- key_weight: bfloat16 [768, 768], P('fsdp', 'tp'), may hold values from -0.21875 to 0.21875
- value_weight: bfloat16 [768, 768], P('fsdp', 'tp'), may hold values from -0.21875 to 0.21875
- out_weight: bfloat16 [768, 768], P('tp', 'fsdp'), may hold values from -3.5 to 3.5
- attn_gain: bfloat16 [768], P('fsdp'), may hold values from 0.099609375 to 1.8984375
- ffn_gain: bfloat16 [768], P('fsdp'), may hold values from 0.099609375 to 1.8984375
- router_weight: bfloat16 [768, 8], P('fsdp'), may hold values from -0.21875 to 0.21875
- shared_gate: bfloat16 [768, 2048], P('fsdp', 'tp'), may hold values from -0.21875 to 0.21875
- shared_up: bfloat16 [768, 2048], P('fsdp', 'tp'), may hold values from -0.21875 to 0.21875
- shared_down: bfloat16 [2048, 768], P('tp', 'fsdp'), may hold values from -0.125 to 0.125
- expert_gate: bfloat16 [8, 768, 2048], P(None, 'fsdp', 'tp'), may hold values from -0.21875 to 0.21875
- expert_up: bfloat16 [8, 768, 2048], P(None, 'fsdp', 'tp'), may hold values from -0.21875 to 0.21875
- expert_down: bfloat16 [8, 2048, 768], P(None, 'tp', 'fsdp'), may hold values from -0.125 to 0.125
- cotangent: bfloat16 [4, 2048, 768], P('fsdp', 'ctx'), may hold values from -6 to 6
Outputs:
- output: bfloat16 [4, 2048, 768], P('fsdp', 'ctx')
- input_grad: bfloat16 [4, 2048, 768], P('fsdp', 'ctx')
- grad_query_weight: float32 [768, 768], P('fsdp', 'tp')
- grad_key_weight: float32 [768, 768], P('fsdp', 'tp')
- grad_value_weight: float32 [768, 768], P('fsdp', 'tp')
- grad_out_weight: float32 [768, 768], P('tp', 'fsdp')
- grad_attn_gain: float32 [768], P('fsdp')
- grad_ffn_gain: float32 [768], P('fsdp')
- grad_router_weight: float32 [768, 8], P('fsdp')
- grad_shared_gate: float32 [768, 2048], P('fsdp', 'tp')
- grad_shared_up: float32 [768, 2048], P('fsdp', 'tp')
- grad_shared_down: float32 [2048, 768], P('tp', 'fsdp')
- grad_expert_gate: float32 [8, 768, 2048], P(None, 'fsdp', 'tp')
- grad_expert_up: float32 [8, 768, 2048], P(None, 'fsdp', 'tp')
- grad_expert_down: float32 [8, 2048, 768], P(None, 'tp', 'fsdp')
The draws below stay inside these ranges and needn't reach their ends.
Inputs may be any that keep to these rules, and one draw needn't show every extreme that they name: `segments`: document numbers never fall along a sequence. `routes`: each token names 2 different experts; in each aligned block of 512 positions of a sequence no expert is named more than 192 times, and in some block one expert is named exactly 192 times.
All inputs are finite; a program needn't handle non-finite values.
Results may differ from the reference program's by a relative error of at most 0.02.
Values may be sent and summed in bfloat16 or wider, within the bound.
No kernel may reach another device: no remote copies, remote signals or barrier semaphores. Data moves between devices by JAX's collectives and lax.ppermute only.
A program may use at most 256 MiB of HBM per device.

```python
import math
import jax
import jax.numpy as jnp
import numpy as np
from jax import lax

D = 768
HEADS = 12
HD = 64
FF = 2048
SFF = 2048
EXPERTS = 8
TOPK = 2
SEQ_LEN = 2048
WINDOW = 1024
SEQS = 4
BLK = 512
CAP = 192
N_CTX = 4


def draw_segments(key, part):
    key = jax.random.fold_in(key, 7)
    head_key, tail_key = jax.random.split(key)
    margin = SEQ_LEN // 8
    head = jax.random.randint(head_key, (SEQS, 3), 1, margin, dtype=jnp.int32)
    tail = jax.random.randint(tail_key, (SEQS, 3), SEQ_LEN - margin, SEQ_LEN, dtype=jnp.int32)
    cuts = jnp.concatenate([head, tail], axis=1)
    positions = jnp.arange(SEQ_LEN, dtype=jnp.int32)
    return jnp.sum((cuts[:, None, :] <= positions[None, :, None]).astype(jnp.int32), axis=2).astype(jnp.int32)


def with_spikes(values, own_key, source, target, blocks, factor):
    owner, partner = [(jnp.arange(values.shape[axis_at]) // (values.shape[axis_at] // blocks)).reshape([-1 if axis == axis_at else 1 for axis in range(values.ndim)]) for axis_at in (source, target)]
    chosen = jax.random.permutation(own_key, blocks)[partner]
    strong = (owner == chosen) | (owner == (partner + blocks // 2) % blocks)
    return jnp.where(strong, factor * values, values)


def levels(key, dims, cuts, low, top_value):
    def one(axis_at, parts):
        steps = jax.random.uniform(jax.random.fold_in(jax.random.fold_in(key, 6), axis_at), (parts,), jnp.float32, low / len(cuts), top_value / len(cuts))
        return jnp.repeat(jnp.exp(steps), dims[axis_at] // parts).reshape((-1,) + (1,) * (len(dims) - axis_at - 1))

    loudness = one(*cuts[0])
    for cut in cuts[1:]:
        loudness = loudness * one(*cut)
    return loudness


def assign_block(key, own, number, rows, number_of, top, bound, skew):
    sequence = jax.random.permutation(key, number_of)
    packed, common = load_shares(number_of, rows * top, bound, skew, True), load_shares(number_of, rows * top, bound, skew, False)
    places = jnp.arange(number_of)

    def named(sizes, turn):
        used = int((sizes > 0).sum())
        fixed = max(1, used // 4)
        shifted = fixed + (places - fixed + turn * (used - fixed)) % max(1, number_of - fixed)
        return jnp.zeros((number_of,), jnp.int32).at[sequence[jnp.where(places < fixed, places, shifted)]].set(jnp.asarray(sizes, jnp.int32))

    sizes = jnp.where(number % 4 == 0, named(packed, number // 4), named(common, number - number // 4 - 1))
    mixed = jax.random.permutation(jax.random.fold_in(own, 3), number_of)
    giver, sink = mixed[0:number_of // 2 * 2:2], mixed[1:number_of // 2 * 2:2]
    room = jnp.minimum(sizes[giver] - 1, bound - sizes[sink]) // 2
    room = jnp.where((giver == sequence[0]) | (sink == sequence[0]) | (sizes[sink] == 0), 0, jnp.maximum(room, 0))
    shifted = jax.random.randint(jax.random.fold_in(own, 4), (number_of // 2,), 0, 1 << 20) % (room + 1)
    sizes = sizes.at[giver].add(-shifted).at[sink].add(shifted)
    members = jnp.searchsorted(jnp.cumsum(sizes), jnp.arange(rows * top), side="right").astype(jnp.int32)
    listing = members.reshape(top, rows).T
    listing = listing[jax.random.permutation(jax.random.fold_in(own, 1), rows)]
    turn = jax.random.randint(jax.random.fold_in(own, 2), (rows, 1), 0, top)
    return jnp.take_along_axis(listing, (jnp.arange(top)[None, :] + turn) % top, axis=1)


def load_shares(amount, total, limit, slope, full):
    portions = [(1 << 20) // math.isqrt(grade ** slope) + 1 for grade in range(1, amount + 1)]
    largest = limit if full else min(limit, max(-(-total // amount), total * portions[0] // sum(portions)))
    least = 1 if total - largest >= amount - 1 else 0
    given, rest = [largest] + [least] * (amount - 1), total - largest - least * (amount - 1)
    while rest > 0:
        candidates = [i for i in range(1, amount) if given[i] < largest] or [i for i in range(1, amount) if given[i] < limit]
        pool, budget = sum([portions[i] for i in candidates]), rest
        for i in candidates:
            more = min(limit - given[i], max(1, budget * portions[i] // pool), rest)
            given[i] = given[i] + more
            rest = rest - more
    return np.array(given)


def gaussian(key, extent, scale, most, cuts=(), kind=jnp.bfloat16):
    entries = jax.random.normal(key, extent, jnp.float32) * scale
    if len(cuts) > 0:
        entries = levels(key, extent, cuts, -0.22, 0.18) * entries
    return jnp.clip(entries, min=-most, max=most).astype(kind)


def noise_with(rng, shape, scale, reach, cuts, heavy, held_as=jnp.bfloat16):
    drawn = scale * jax.random.normal(rng, shape, jnp.float32)
    if cuts:
        drawn = drawn * levels(rng, shape, cuts, -0.22, 0.18)
    return jnp.clip(with_spikes(drawn, jax.random.fold_in(rng, 3), *heavy), -reach, reach).astype(held_as)


def setup_inputs(seed: int = 0) -> dict:
    streams_of = jax.random.split(jax.random.key(seed), 18)
    tokens = noise_with(streams_of[0], (SEQS, SEQ_LEN, D), 1.0, 6.0, ((0, 4), (1, 4)), (0, 2, 4, 2.0))
    segments = draw_segments(jax.random.fold_in(streams_of[17], 71), 0)
    routes_keys = jax.random.split(jax.random.fold_in(streams_of[2], 1), SEQS * SEQ_LEN // BLK)
    routes_turns = jax.random.permutation(jax.random.fold_in(streams_of[2], 3), SEQS * SEQ_LEN // BLK)
    routes = jax.vmap(lambda own, number: assign_block(jax.random.fold_in(streams_of[2], 2), own, number, BLK, EXPERTS, TOPK, CAP, 2))(routes_keys, routes_turns).reshape((SEQS, SEQ_LEN, TOPK))
    query_weight = gaussian(streams_of[3], (D, HEADS * HD), D ** -0.5, 0.21875, ((0, 4), (1, 2)))
    key_weight = gaussian(streams_of[4], (D, HEADS * HD), D ** -0.5, 0.21875, ((0, 4), (1, 2)))
    value_weight = gaussian(streams_of[5], (D, HEADS * HD), D ** -0.5, 0.21875, ((0, 4), (1, 2)))
    out_weight = gaussian(streams_of[6], (HEADS * HD, D), (max(D // 256, 1)) ** -0.5, 3.5, ((0, 2), (1, 4)))
    attn_gain = jnp.clip(1.0 + 0.18 * jax.random.normal(streams_of[7], (D,), jnp.float32), 0.099609375, 1.8984375).astype(jnp.bfloat16)
    ffn_gain = jnp.clip(1.0 + 0.18 * jax.random.normal(streams_of[8], (D,), jnp.float32), 0.099609375, 1.8984375).astype(jnp.bfloat16)
    router_weight = gaussian(streams_of[9], (D, EXPERTS), D ** -0.5, 0.21875, ((0, 4),))
    shared_gate = gaussian(streams_of[10], (D, SFF), D ** -0.5, 0.21875, ((0, 4), (1, 2)))
    shared_up = gaussian(streams_of[11], (D, SFF), D ** -0.5, 0.21875, ((0, 4), (1, 2)))
    shared_down = gaussian(streams_of[12], (SFF, D), SFF ** -0.5, 0.125, ((0, 2), (1, 4)))
    expert_gate = gaussian(streams_of[13], (EXPERTS, D, FF), D ** -0.5, 0.21875, ((1, 4), (2, 2)))
    expert_up = gaussian(streams_of[14], (EXPERTS, D, FF), D ** -0.5, 0.21875, ((1, 4), (2, 2)))
    expert_down = gaussian(streams_of[15], (EXPERTS, FF, D), FF ** -0.5, 0.125, ((1, 2), (2, 4)))
    cotangent = noise_with(streams_of[16], (SEQS, SEQ_LEN, D), 1.0, 6.0, ((0, 4), (1, 4)), (0, 2, 4, 2.0))
    return dict(tokens=tokens, segments=segments, routes=routes, query_weight=query_weight, key_weight=key_weight, value_weight=value_weight, out_weight=out_weight, attn_gain=attn_gain, ffn_gain=ffn_gain, router_weight=router_weight, shared_gate=shared_gate, shared_up=shared_up, shared_down=shared_down, expert_gate=expert_gate, expert_up=expert_up, expert_down=expert_down, cotangent=cotangent)


@jax.custom_vjp
def low(v):
    return lax.optimization_barrier(v.astype(jnp.bfloat16)).astype(jnp.float32)

@jax.custom_vjp
def low_back(v):
    return v

def low_keep(v):
    return (low(v), None)

def low_pass(kept, grad):
    return (grad,)

def back_keep(v):
    return (v, None)

def back_low(kept, grad):
    return (low(grad),)
low.defvjp(low_keep, low_pass)
low_back.defvjp(back_keep, back_low)
EPS = 1e-06

def matmul_high(left, right):
    return jnp.dot(left, right, precision=lax.Precision.HIGHEST, preferred_element_type=jnp.float32)

def rotate(values, positions):
    head_size = values.shape[-1]
    half = head_size // 2
    rates = 10000.0 ** (-2.0 * jnp.arange(half, dtype=jnp.float32) / head_size)
    angles = positions.astype(jnp.float32)[:, None] * rates[None, :]
    cosine = jnp.cos(angles)[:, None, :]
    sine = jnp.sin(angles)[:, None, :]
    first = values[..., :half]
    second = values[..., half:]
    return jnp.concatenate([first * cosine - second * sine, second * cosine + first * sine], axis=-1)

def normalize(values, gain):
    return values * lax.rsqrt(lax.optimization_barrier(jnp.mean(values * values, axis=-1, keepdims=True)) + EPS) * gain

def attention(query, keys, values, segment_row):
    length = query.shape[0]
    block = length // N_CTX
    lead = 2 * block
    key_pad = jnp.concatenate([jnp.zeros((lead,) + keys.shape[1:], keys.dtype), keys], axis=0)
    value_pad = jnp.concatenate([jnp.zeros((lead,) + values.shape[1:], values.dtype), values], axis=0)
    segment_pad = jnp.concatenate([jnp.full((lead,), -1, jnp.int32), segment_row.astype(jnp.int32)], axis=0)
    score_scale = query.shape[-1] ** (-0.5)

    def one_block(index):
        start = (index * block).astype(jnp.int32)
        query_block = lax.dynamic_slice_in_dim(query, start, block, 0)
        key_block = lax.dynamic_slice_in_dim(key_pad, start, 3 * block, 0)
        value_block = lax.dynamic_slice_in_dim(value_pad, start, 3 * block, 0)
        query_segment = lax.dynamic_slice_in_dim(segment_row.astype(jnp.int32), start, block, 0)
        key_segment = lax.dynamic_slice_in_dim(segment_pad, start, 3 * block, 0)
        query_place = start + jnp.arange(block, dtype=jnp.int32)
        key_place = start - lead + jnp.arange(3 * block, dtype=jnp.int32)
        allowed = (query_segment[:, None] == key_segment[None, :]) & (key_place[None, :] <= query_place[:, None]) & (query_place[:, None] - key_place[None, :] < WINDOW)
        scores = jnp.einsum('qhd,khd->hqk', query_block, key_block, precision=lax.Precision.HIGHEST) * score_scale
        scores = low_back(scores)
        scores = jnp.where(allowed[None], scores, -1e+30)
        weights = jax.nn.softmax(scores, axis=-1)
        return jnp.einsum('hqk,khd->qhd', low(weights), value_block, precision=lax.Precision.HIGHEST)
    blocks = lax.map(jax.checkpoint(one_block), jnp.arange(N_CTX, dtype=jnp.int32))
    return blocks.reshape(query.shape)

def slots(route_rows):
    flat = route_rows.reshape(-1).astype(jnp.int32)
    count = flat.shape[0]
    hits = (flat[:, None] == jnp.arange(EXPERTS, dtype=jnp.int32)[None, :]).astype(jnp.int32)
    rank = lax.optimization_barrier(jnp.sum((jnp.cumsum(hits, axis=0).astype(jnp.int32) - hits) * hits, axis=1)).astype(jnp.int32)
    capacity = N_CTX * CAP
    slot_pick = (flat * capacity + rank).astype(jnp.int32)
    owner = (jnp.arange(count, dtype=jnp.int32) // route_rows.shape[1]).astype(jnp.int32)
    slot_token = jnp.full((EXPERTS * capacity,), route_rows.shape[0], jnp.int32).at[slot_pick].set(owner)
    return (slot_token, slot_pick)

def layer(inputs, weights, segment_row, route_rows, slot_token, slot_pick):
    query_weight, key_weight, value_weight, out_weight, attn_gain, ffn_gain, router_weight, shared_gate, shared_up, shared_down, expert_gate, expert_up, expert_down = weights
    length, width = inputs.shape
    heads = query_weight.shape[1] // HD
    positions = jnp.arange(length, dtype=jnp.int32)
    hidden = low(normalize(inputs, attn_gain))
    query = low(rotate(low_back(matmul_high(hidden, query_weight)).reshape(length, heads, HD), positions))
    keys = low(rotate(low_back(matmul_high(hidden, key_weight)).reshape(length, heads, HD), positions))
    values = low(low_back(matmul_high(hidden, value_weight))).reshape(length, heads, HD)
    attended = low(low_back(attention(query, keys, values, segment_row).reshape(length, heads * HD)))
    mixed = inputs + low_back(matmul_high(attended, out_weight))
    normed = low(normalize(mixed, ffn_gain))
    logits = low_back(matmul_high(normed, router_weight))
    chosen = jnp.take_along_axis(logits, route_rows.astype(jnp.int32), axis=1)
    gates = jax.nn.softmax(chosen, axis=-1)
    padded = jnp.concatenate([normed, jnp.zeros((1, width), normed.dtype)], axis=0)
    routed = padded[slot_token].reshape(EXPERTS, -1, width)
    expert_gating = low_back(jnp.einsum('ecd,edf->ecf', routed, expert_gate, precision=lax.Precision.HIGHEST))
    expert_linear = low_back(jnp.einsum('ecd,edf->ecf', routed, expert_up, precision=lax.Precision.HIGHEST))
    expert_active = low(jax.nn.silu(expert_gating) * expert_linear)
    expert_result = low_back(jnp.einsum('ecf,efd->ecd', expert_active, expert_down, precision=lax.Precision.HIGHEST)).reshape(-1, width)
    picked = expert_result[slot_pick].reshape(length, route_rows.shape[1], width)
    routed_sum = lax.optimization_barrier(jnp.sum(gates[:, :, None] * picked, axis=1))
    shared_gating = low_back(matmul_high(normed, shared_gate))
    shared_linear = low_back(matmul_high(normed, shared_up))
    shared_active = low(jax.nn.silu(shared_gating) * shared_linear)
    shared_result = low_back(matmul_high(shared_active, shared_down))
    return mixed + routed_sum + shared_result

def reference(tokens, segments, routes, query_weight, key_weight, value_weight, out_weight, attn_gain, ffn_gain, router_weight, shared_gate, shared_up, shared_down, expert_gate, expert_up, expert_down, cotangent):
    weights = tuple((item.astype(jnp.float32) for item in (query_weight, key_weight, value_weight, out_weight, attn_gain, ffn_gain, router_weight, shared_gate, shared_up, shared_down, expert_gate, expert_up, expert_down)))

    def per_sequence(totals, items):
        inputs, segment_row, route_rows, grad_out = items
        slot_token, slot_pick = slots(route_rows)

        def forward(inputs_f, weights_f):
            return layer(inputs_f, weights_f, segment_row, route_rows, slot_token, slot_pick)
        result, pullback = jax.vjp(forward, inputs.astype(jnp.float32), weights)
        grad_in, grad_weights = pullback(grad_out.astype(jnp.float32))
        totals = tuple((left + right for left, right in zip(totals, grad_weights)))
        return (totals, (result.astype(jnp.bfloat16), grad_in.astype(jnp.bfloat16)))
    zeros = tuple((jnp.zeros(item.shape, jnp.float32) for item in weights))
    totals, (outputs, grads_in) = lax.scan(per_sequence, zeros, (tokens, segments, routes, cotangent))
    return (outputs, grads_in, totals[0], totals[1], totals[2], totals[3], totals[4], totals[5], totals[6], totals[7], totals[8], totals[9], totals[10], totals[11], totals[12])
```

```python
import functools

import jax
import jax.numpy as jnp
from jax import lax
from jax.experimental import pallas as pl
from jax.experimental.pallas import tpu as pltpu
from jax.sharding import PartitionSpec as P

HD = 64
WINDOW = 1024
EPS = 1e-06
F32 = jnp.float32
BF16 = jnp.bfloat16
VMEM_BYTES = 56 * 1024 * 1024


def dot(left, right):
    return lax.dot_general(left, right, (((1,), (0,)), ((), ())), preferred_element_type=F32)


def dot_nt(left, right):
    return lax.dot_general(left, right, (((1,), (1,)), ((), ())), preferred_element_type=F32)


def dot_tn(left, right):
    return lax.dot_general(left, right, (((0,), (0,)), ((), ())), preferred_element_type=F32)


def core_swap(block):
    size = lax.axis_size("fsdp")
    return lax.ppermute(block, "fsdp", [(i, i ^ 1) for i in range(size)])


def pair_shift(block, distance):
    size = lax.axis_size("fsdp")
    pairs = size // 2
    route = [(i, ((i // 2 + distance) % pairs) * 2 + i % 2) for i in range(size)]
    return lax.ppermute(block, "fsdp", route)


def tp_shift(block, distance):
    size = lax.axis_size("tp")
    return lax.ppermute(block, "tp", [(i, (i + distance) % size) for i in range(size)])


def ctx_shift(block, distance):
    size = lax.axis_size("ctx")
    return lax.ppermute(block, "ctx", [(i, (i + distance) % size) for i in range(size)])


def ctx_open(block, distance):
    size = lax.axis_size("ctx")
    route = [(i, i + distance) for i in range(size) if 0 <= i + distance < size]
    return lax.ppermute(block, "ctx", route)


def pick(stack, index):
    return lax.dynamic_index_in_dim(stack, index, 0, keepdims=False)


def place(pieces, me):
    count = len(pieces)
    if count == 1:
        return pieces[0][None]
    if count == 2:
        first, second = pieces
        return jnp.where(me == 0, jnp.stack([first, second]), jnp.stack([second, first]))
    result = jnp.zeros((count,) + pieces[0].shape, pieces[0].dtype)
    for d, piece in enumerate(pieces):
        result = lax.dynamic_update_index_in_dim(result, piece, (me - d) % count, 0)
    return result


def all_sum(block, axis):
    size = lax.axis_size(axis)
    reach = 1
    while reach < size:
        other = lax.ppermute(block, axis, [(i, i ^ reach) for i in range(size)])
        block = block + other
        reach *= 2
    return block


def whole(shape):
    return pl.BlockSpec(shape, lambda *_: (0,) * len(shape))


def params():
    return pltpu.CompilerParams(vmem_limit_bytes=VMEM_BYTES)


def swap_halves(values):
    width = values.shape[-1]
    lane = lax.broadcasted_iota(jnp.int32, values.shape, 1)
    up = pltpu.roll(values, width - HD // 2, 1)
    down = pltpu.roll(values, HD // 2, 1)
    return jnp.where(lane % HD < HD // 2, up, down)


def widen(table, width):
    copies = -(-width // table.shape[1])
    return jnp.concatenate([table] * copies, axis=1)[:, :width]


def project_kernel(with_query, tok_ref, gain_ref, w_ref, cos_ref, sin_ref, hid_ref, k_ref, v_ref, *q_ref):
    inputs = tok_ref[...].astype(F32)
    scale = lax.rsqrt(jnp.mean(inputs * inputs, axis=-1, keepdims=True) + EPS)
    hidden = (inputs * scale * gain_ref[...]).astype(BF16)
    hid_ref[...] = hidden
    width = k_ref.shape[1]
    cosine = widen(cos_ref[...], width)
    sine = widen(sin_ref[...], width)
    keys = dot(hidden, w_ref[:, :width])
    k_ref[...] = (keys * cosine + swap_halves(keys) * sine).astype(BF16)
    v_ref[...] = dot(hidden, w_ref[:, width : 2 * width]).astype(BF16)
    if with_query:
        query = dot(hidden, w_ref[:, 2 * width : 3 * width])
        turned = (query * cosine + swap_halves(query) * sine).astype(BF16)
        q_ref[0][...] = turned * jnp.asarray(HD**-0.5, BF16)


def project(tokens, gain, weights, cosine, sine, width, with_query):
    rows, features = tokens.shape
    row = jax.ShapeDtypeStruct((rows, width), BF16)
    outs = [jax.ShapeDtypeStruct((rows, features), BF16), row, row] + [row] * with_query
    return pl.pallas_call(
        functools.partial(project_kernel, with_query),
        out_shape=outs,
        compiler_params=params(),
    )(tokens, gain, weights, cosine, sine)


def mask_bias(kseg, qseg, keys, queries):
    key = lax.broadcasted_iota(jnp.int32, (keys, queries), 0)
    query = lax.broadcasted_iota(jnp.int32, (keys, queries), 1)
    allowed = (key > query) & (key <= query + WINDOW) & (kseg == qseg)
    return jnp.where(allowed, 0.0, -1e30).astype(F32)


def head_only(values, head):
    lane = lax.broadcasted_iota(jnp.int32, values.shape, 1)
    return jnp.where(lane // HD == head, values, jnp.zeros_like(values))


def attend_kernel(tile, q_ref, k_ref, v_ref, kseg_ref, qseg_ref, out_ref, lse_ref, bias_ref):
    rows = q_ref.shape[0]
    span = WINDOW + tile
    tiles = rows // tile

    @pl.when(pl.program_id(0) == 0)
    def _():
        for j in range(tiles):
            bias_ref[j] = mask_bias(
                kseg_ref[pl.ds(j * tile, span), :], qseg_ref[:, pl.ds(j * tile, tile)], span, tile
            )

    keys = k_ref[...]
    values_t = v_ref[...].T
    for j in range(tiles):
        start = j * tile
        query = q_ref[pl.ds(start, tile), :]
        parts = []
        for head in range(2):
            scores = dot_nt(keys[start : start + span], head_only(query, head)) + bias_ref[j]
            top = jnp.max(scores, axis=0, keepdims=True)
            expo = jnp.exp(scores - top)
            total = jnp.sum(expo, axis=0, keepdims=True)
            part = dot(
                values_t[head * HD : (head + 1) * HD, start : start + span], expo.astype(BF16)
            )
            parts.append(part / total)
            lse_ref[0, pl.ds(head, 1), pl.ds(start, tile)] = top + jnp.log(total)
        out_ref[pl.ds(start, tile), :] = jnp.concatenate(parts, axis=0).T.astype(BF16)


def attend(query, keys, values, kseg, qseg):
    rows, width = query.shape
    span = keys.shape[0]
    tile = min(256, rows)
    pairs = -(-width // (2 * HD))
    columns = lambda count: pl.BlockSpec((count, 2 * HD), lambda i: (0, i))
    return pl.pallas_call(
        functools.partial(attend_kernel, tile),
        grid=(pairs,),
        in_specs=[columns(rows), columns(span), columns(span), whole((span, 1)), whole((1, rows))],
        out_specs=[columns(rows), pl.BlockSpec((1, 2, rows), lambda i: (i, 0, 0))],
        out_shape=[
            jax.ShapeDtypeStruct((rows, width), BF16),
            jax.ShapeDtypeStruct((pairs, 2, rows), F32),
        ],
        scratch_shapes=[pltpu.VMEM((rows // tile, WINDOW + tile, tile), F32)],
        compiler_params=params(),
    )(query, keys, values, kseg, qseg)


def attend_back_kernel(
    tile, q_ref, k_ref, v_ref, g_ref, lse_ref, kseg_ref, qseg_ref, cos_ref, sin_ref,
    dq_ref, dk_ref, dv_ref, bias_ref, dk_acc, dv_acc,
):
    rows = q_ref.shape[0]
    span = WINDOW + tile
    tiles = rows // tile
    total_keys = k_ref.shape[0]

    @pl.when(pl.program_id(0) == 0)
    def _():
        for j in range(tiles):
            bias_ref[j] = mask_bias(
                kseg_ref[pl.ds(j * tile, span), :], qseg_ref[:, pl.ds(j * tile, tile)], span, tile
            )

    keys = k_ref[...]
    values = v_ref[...]
    keys_t = keys.T
    dk_acc[...] = jnp.zeros_like(dk_acc)
    dv_acc[...] = jnp.zeros_like(dv_acc)
    cosine = cos_ref[...]
    sine = sin_ref[...]
    lead = total_keys - rows
    for j in range(tiles):
        start = j * tile
        query = q_ref[pl.ds(start, tile), :]
        grad = g_ref[pl.ds(start, tile), :]
        parts = []
        for head in range(2):
            query_one = head_only(query, head)
            grad_one = head_only(grad, head)
            scores = dot_nt(keys[start : start + span], query_one) + bias_ref[j]
            probs = jnp.exp(scores - lse_ref[0, pl.ds(head, 1), pl.ds(start, tile)])
            grad_probs = dot_nt(values[start : start + span], grad_one)
            delta = jnp.sum(probs * grad_probs, axis=0, keepdims=True)
            grad_scores = (probs * (grad_probs - delta)).astype(BF16)
            dv_acc[pl.ds(start, span), :] += dot(probs.astype(BF16), grad_one)
            dk_acc[pl.ds(start, span), :] += dot(grad_scores, query_one)
            parts.append(
                dot(keys_t[head * HD : (head + 1) * HD, start : start + span], grad_scores)
            )
        dq = jnp.concatenate(parts, axis=0).T * HD**-0.5
        places = pl.ds(lead + start, tile)
        dq_ref[pl.ds(start, tile), :] = (
            dq * cos_ref[places, :] - swap_halves(dq) * sin_ref[places, :]
        ).astype(BF16)
    dk = dk_acc[...]
    dk_ref[...] = (dk * cosine - swap_halves(dk) * sine).astype(BF16)
    dv_ref[...] = dv_acc[...].astype(BF16)


def attend_back(query, keys, values, grad, lse, kseg, qseg, cosine, sine):
    rows, width = query.shape
    span = keys.shape[0]
    tile = min(256, rows)
    pairs = -(-width // (2 * HD))
    columns = lambda count: pl.BlockSpec((count, 2 * HD), lambda i: (0, i))
    return pl.pallas_call(
        functools.partial(attend_back_kernel, tile),
        grid=(pairs,),
        in_specs=[
            columns(rows), columns(span), columns(span), columns(rows),
            pl.BlockSpec((1, 2, rows), lambda i: (i, 0, 0)),
            whole((span, 1)), whole((1, rows)), whole((span, 2 * HD)), whole((span, 2 * HD)),
        ],
        out_specs=[columns(rows), columns(span), columns(span)],
        out_shape=[
            jax.ShapeDtypeStruct((rows, width), BF16),
            jax.ShapeDtypeStruct((span, width), BF16),
            jax.ShapeDtypeStruct((span, width), BF16),
        ],
        scratch_shapes=[
            pltpu.VMEM((rows // tile, WINDOW + tile, tile), F32),
            pltpu.VMEM((span, 2 * HD), F32),
            pltpu.VMEM((span, 2 * HD), F32),
        ],
        compiler_params=params(),
    )(query, keys, values, grad, lse, kseg, qseg, cosine, sine)


def expert_kernel(
    capacity, parts, n_saved, e_ref, xo_ref, xp_ref, co_ref, cp_ref, to_ref, tp_ref,
    wgu_ref, wd_ref, sw_ref, rt_ref, *refs,
):
    out_ref, dx_ref, sx_ref, sr_ref, sh_ref, sa_ref, sb_ref, ssx_ref, ssh_ref, ssa_ref, ssb_ref = refs[n_saved:]
    e = e_ref[0]
    block, width = xo_ref.shape
    hidden = wd_ref.shape[1]
    units = sw_ref.shape[1] // 3
    experts = to_ref.shape[0]
    tok = block // parts
    xs = (xo_ref[...], xp_ref[...])
    cs = (co_ref[...], cp_ref[...])
    tables = (to_ref[...], tp_ref[...])
    row = lax.broadcasted_iota(jnp.int32, (experts, block), 0)
    slot = lax.broadcasted_iota(jnp.int32, (capacity, block), 0).astype(F32)
    hits, routed, cots, gate_slots = [], [], [], []
    for one, cot, table in zip(xs, cs, tables):
        logits = dot_nt(rt_ref[...], one)[:experts]
        named = table >= 0.0
        top = jnp.max(jnp.where(named, logits, -1e30), axis=0, keepdims=True)
        expo = jnp.where(named, jnp.exp(logits - top), 0.0)
        gates = expo / jnp.sum(expo, axis=0, keepdims=True)
        mine = row == e
        gate = jnp.sum(jnp.where(mine, gates, 0.0), axis=0, keepdims=True)
        position = jnp.sum(jnp.where(mine, table, 0.0), axis=0, keepdims=True)
        hit = slot == position
        spread = jnp.where(hit, 1.0, 0.0).astype(BF16)
        hits.append((hit, spread))
        routed.append(dot(spread, one).astype(BF16))
        cots.append(dot(spread, cot))
        gate_slots.append(jnp.sum(jnp.where(hit, gate, 0.0), axis=1, keepdims=True))
    routed = jnp.concatenate(routed, axis=0)
    cots = jnp.concatenate(cots, axis=0)
    gate_slots = jnp.concatenate(gate_slots, axis=0)
    grads = (gate_slots * cots).astype(BF16)
    share = sx_ref.shape[3]
    for q in range(sx_ref.shape[1]):
        sx_ref[0, q] = routed[:, q * share : (q + 1) * share]
        sr_ref[0, q] = grads[:, q * share : (q + 1) * share]
    both = dot(routed, wgu_ref[...])
    gating, linear = both[:, :hidden], both[:, hidden:]
    sigma = jax.nn.sigmoid(gating)
    silu = gating * sigma
    active = (silu * linear).astype(BF16)
    sh_ref[0] = active
    result = dot_nt(active, wd_ref[...])
    grad_active = dot(grads, wd_ref[...])
    grad_gating = (grad_active * linear * (sigma * (1.0 + gating * (1.0 - sigma)))).astype(BF16)
    grad_linear = (grad_active * silu).astype(BF16)
    sa_ref[0] = grad_gating
    sb_ref[0] = grad_linear
    grad_rows = dot_nt(grad_gating, wgu_ref[:, :hidden]) + dot_nt(grad_linear, wgu_ref[:, hidden:])
    grad_gates = jnp.sum(result * cots, axis=1, keepdims=True)
    weighted = jnp.concatenate([(gate_slots * result).astype(BF16), grad_rows.astype(BF16)], axis=1)

    shared = dot(xs[0], sw_ref[:, : 2 * units])
    gating, linear = shared[:, :units], shared[:, units:]
    sigma = jax.nn.sigmoid(gating)
    silu = gating * sigma
    active = (silu * linear).astype(BF16)
    grad_active = dot(cs[0], sw_ref[:, 2 * units :])
    grad_gating = (grad_active * linear * (sigma * (1.0 + gating * (1.0 - sigma)))).astype(BF16)
    grad_linear = (grad_active * silu).astype(BF16)
    ssx_ref[0] = xs[0]
    ssh_ref[0] = active
    ssa_ref[0] = grad_gating
    ssb_ref[0] = grad_linear
    shared_out = dot_nt(active, sw_ref[:, 2 * units :])
    shared_dx = dot_nt(grad_gating, sw_ref[:, :units]) + dot_nt(grad_linear, sw_ref[:, units : 2 * units])

    line = lax.broadcasted_iota(jnp.int32, (16, width), 0)
    for s in range(2):
        hit, spread = hits[s]
        rows = slice(s * capacity, (s + 1) * capacity)
        back = dot_tn(spread, weighted[rows])
        out, dx = back[:, :width], back[:, width:]
        gate_row = jnp.sum(jnp.where(hit, grad_gates[rows], 0.0), axis=0, keepdims=True)
        if s == 0:
            out = out + shared_out
            dx = dx + shared_dx
        for j in range(parts):
            piece = slice(j * tok, (j + 1) * tok)
            out_ref[s, j] = out[piece].astype(BF16)
            dx_ref[s, j, :tok] = dx[piece].astype(BF16)
            spare = jnp.zeros((1, width - tok), F32)
            padded = jnp.concatenate([gate_row[:, piece], spare], axis=1)
            dx_ref[s, j, tok:] = jnp.where(line == e, padded, 0.0).astype(BF16)


def expert_step(step, steps, capacity, pairs, parts, e, xs, cs, tables, wgu, wd, sw, router_t, saved):
    block, width = xs[0].shape
    hidden = wd.shape[1]
    units = sw.shape[1] // 3
    slots = 2 * capacity
    tok = block // parts
    shapes = [
        (pairs, slots, width // pairs), (pairs, slots, width // pairs),
        (slots, hidden), (slots, hidden), (slots, hidden),
        (block, width), (block, units), (block, units), (block, units),
    ]
    saved_specs = [pl.BlockSpec((1,) + s, functools.partial(lambda n, *_: (step,) + (0,) * n, len(s))) for s in shapes]
    outs = [
        jax.ShapeDtypeStruct((2, parts, tok, width), BF16),
        jax.ShapeDtypeStruct((2, parts, tok + 16, width), BF16),
    ] + [jax.ShapeDtypeStruct((steps,) + s, BF16) for s in shapes]
    operands = [e, xs[0], xs[1], cs[0], cs[1], tables[0], tables[1], wgu, wd, sw, router_t]
    in_specs = [pl.BlockSpec(memory_space=pltpu.SMEM)] + [whole(o.shape) for o in operands[1:]]
    first = len(operands)
    flops = 2 * slots * width * hidden * 6 + 2 * block * width * (units * 6 + capacity * 8)
    return pl.pallas_call(
        functools.partial(expert_kernel, capacity, parts, len(saved)),
        grid=(1,),
        in_specs=in_specs + [pl.BlockSpec(memory_space=pl.ANY)] * len(saved),
        out_specs=[whole(outs[0].shape), whole(outs[1].shape)] + saved_specs,
        out_shape=outs,
        input_output_aliases={first + i: 2 + i for i in range(len(saved))},
        compiler_params=params(),
        cost_estimate=pl.CostEstimate(flops=flops, bytes_accessed=20_000_000, transcendentals=0),
    )(*operands, *saved)


def norm_back(grad, values, scale, gain):
    grad_gain = jnp.sum(grad * values * scale, axis=0)
    scaled = grad * gain
    grad_values = scale * scaled - values * scale * scale * scale * jnp.mean(
        scaled * values, axis=-1, keepdims=True
    )
    return grad_values, grad_gain


def local(
    tokens,
    segments,
    routes,
    query_weight,
    key_weight,
    value_weight,
    out_weight,
    attn_gain,
    ffn_gain,
    router_weight,
    shared_gate,
    shared_up,
    shared_down,
    expert_gate,
    expert_up,
    expert_down,
    cotangent,
):
    fsdp, ctx, tp = (lax.axis_size(a) for a in ("fsdp", "ctx", "tp"))
    pairs = fsdp // 2
    me = lax.axis_index("fsdp")
    pair, core = me // 2, me % 2
    plane = lax.axis_index("ctx")
    lane = lax.axis_index("tp")
    tokens, cotangent, routes = tokens[0], cotangent[0], routes[0]
    block, width = tokens.shape
    share, cols = query_weight.shape
    experts = expert_gate.shape[0]
    hidden_units = expert_gate.shape[2]
    units = shared_gate.shape[1] // ctx
    top_count = routes.shape[1]
    capacity = 3 * top_count * block // (2 * experts)
    tok = block // tp
    mine = core + 2 * plane
    theirs = 1 - core + 2 * plane

    def pair_gather(piece):
        return place([piece] + [pair_shift(piece, d) for d in range(1, pairs)], pair)

    def full_rows(piece):
        rows = pair_gather(piece)
        both = place([rows, core_swap(rows)], core)
        return jnp.moveaxis(both, 0, 1).reshape(fsdp * piece.shape[0], piece.shape[1])

    prev_one = ctx_open(tokens, 1)
    prev_two = ctx_open(prev_one, 1)

    small = jnp.concatenate(
        [router_weight, attn_gain[:, None], ffn_gain[:, None],
         jnp.zeros((share, 128 - experts - 2), BF16)], axis=1)
    attn_full = full_rows(
        jnp.concatenate([key_weight, value_weight, query_weight, out_weight.T, small], axis=1))
    qkv_full = attn_full[:, : 3 * cols]
    out_full = attn_full[:, 3 * cols : 4 * cols]
    router_full = attn_full[:, 4 * cols : 4 * cols + experts]
    small_t = attn_full[:, 4 * cols : 4 * cols + 16].T
    router_t = jnp.concatenate([small_t[:experts], jnp.zeros((16 - experts, width), BF16)], axis=0)
    attn_scale = small_t[experts : experts + 1].astype(F32)
    ffn_scale = small_t[experts + 1 : experts + 2].astype(F32)

    chosen = routes.T
    hits = jnp.zeros((experts, block), jnp.bool_)
    for j in range(top_count):
        hits = hits | (chosen[j : j + 1] == jnp.arange(experts, dtype=jnp.int32)[:, None])
    spot = jnp.arange(block, dtype=jnp.int32)
    before = (spot[:, None] < spot[None, :]).astype(BF16)
    rank = dot(hits.astype(BF16), before)
    table = jnp.where(hits, rank, -1.0)
    tables = [table]
    for d in range(1, ctx):
        tables.append(ctx_shift(tables[-1], 1))
    peer_tables = core_swap(jnp.stack(tables))

    def expert_rows(stack, offset=0):
        own = pick(stack, mine + offset)
        other = core_swap(pick(stack, theirs + offset))
        chip = place([own, other], core)
        rows = pair_gather(chip)
        return rows.reshape(fsdp * own.shape[0], own.shape[1])

    gate_full = expert_rows(expert_gate)
    up_full = expert_rows(expert_up)
    wgu = jnp.concatenate([gate_full, up_full], axis=1)
    wd = expert_rows(jnp.swapaxes(lax.dynamic_slice_in_dim(expert_down, 2 * plane, 2, 0), 1, 2), -2 * plane)
    at = plane * units
    shared_mine = jnp.concatenate(
        [
            lax.dynamic_slice_in_dim(shared_gate, at, units, 1),
            lax.dynamic_slice_in_dim(shared_up, at, units, 1),
            lax.dynamic_slice_in_dim(shared_down, at, units, 0).T,
        ],
        axis=1,
    )
    sw = full_rows(shared_mine)

    cot_piece = lax.dynamic_slice_in_dim(cotangent, lane * tok, tok, 0)

    def tp_gather(piece):
        return place([piece] + [tp_shift(piece, j) for j in range(1, tp)], lane).reshape(
            tp * piece.shape[0], piece.shape[1])

    cots = [cotangent] + [None] * (ctx - 1)
    moving = cot_piece
    for j in range(1, ctx):
        moving = ctx_shift(moving, -1)
        cots[ctx - j] = tp_gather(moving)
    peer_cots = [core_swap(c) for c in cots]

    positions = (plane - 2) * block + jnp.arange(3 * block, dtype=jnp.int32)
    index = jnp.arange(2 * HD, dtype=jnp.int32)
    rates = 10000.0 ** (-2.0 * (index % (HD // 2)).astype(F32) / HD)
    angles = positions.astype(F32)[:, None] * rates[None, :]
    cosine = jnp.cos(angles)
    sine = jnp.where(index % HD < HD // 2, -1.0, 1.0) * jnp.sin(angles)
    segment_pad = jnp.concatenate([jnp.full((2 * block,), -1, jnp.int32), segments[0]])
    kseg = lax.dynamic_slice_in_dim(segment_pad, plane * block, 3 * block, 0)
    qseg = kseg[2 * block :][None, :]
    kseg = kseg[:, None]

    hid, key_parts, value_parts = [], [], []
    for j, source in ((2, tokens), (1, prev_one), (0, prev_two)):
        rows = slice(j * block, (j + 1) * block)
        got = project(source, attn_scale, qkv_full, cosine[rows], sine[rows], cols, j == 2)
        hid.insert(0, got[0])
        key_parts.insert(0, got[1])
        value_parts.insert(0, got[2])
        if j == 2:
            query = got[3]
    keys = jnp.concatenate(key_parts, axis=0)
    values = jnp.concatenate(value_parts, axis=0)
    attended, lse = attend(query, keys, values, kseg, qseg)
    partial = dot_nt(attended, out_full).reshape(tp, tok, width)
    mixed = pick(partial, lane)
    for j in range(1, tp):
        mixed = mixed + tp_shift(pick(partial, (lane + j) % tp).astype(BF16), j).astype(F32)
    inputs_mine = lax.dynamic_slice_in_dim(tokens, lane * tok, tok, 0).astype(F32)
    mixed = inputs_mine + mixed
    scale_ffn = lax.rsqrt(jnp.mean(mixed * mixed, axis=-1, keepdims=True) + EPS)
    normed_low = (mixed * scale_ffn * ffn_scale).astype(BF16)

    e = mine.astype(jnp.int32)[None]
    saved = []
    moving = normed_low
    out_sum = None
    dx_sum = None
    for d in range(ctx):
        if d:
            moving = ctx_shift(moving, 1)
        own_x = tp_gather(moving)
        peer_x = core_swap(own_x)
        got = expert_step(
            d, ctx, capacity, pairs, tp, e, (own_x, peer_x), (cots[d], peer_cots[d]),
            (tables[d], peer_tables[d]), wgu, wd, sw, router_t, saved)
        out_part, dx_part, saved = got[0], got[1], got[2:]

        def home(part):
            total = part[0].astype(F32) + core_swap(part[1]).astype(F32)
            kept = pick(total, lane)
            for j in range(1, tp):
                sent = pick(total, (lane + j) % tp).astype(BF16)
                kept = kept + tp_shift(sent, j).astype(F32)
            if d == 0:
                return kept
            return ctx_shift(kept.astype(BF16), -d).astype(F32)

        dx_home, out_home = home(dx_part), home(out_part)
        dx_sum = dx_home if dx_sum is None else dx_sum + dx_home
        out_sum = out_home if out_sum is None else out_sum + out_home
    sx, sr, sh, sa, sb, ssx, ssh, ssa, ssb = saved

    def contract(left, right):
        rows = left.shape[0] * left.shape[1]
        return dot_tn(left.reshape(rows, left.shape[2]), right.reshape(rows, right.shape[2]))

    def expert_grad(left, right):
        def piece(index):
            return contract(lax.dynamic_index_in_dim(left, index, 1, keepdims=False), right)

        sent = [pair_shift(piece((pair + j) % pairs).astype(BF16), j) for j in range(1, pairs)]
        total = piece(pair)
        for one in sent:
            total = total + one.astype(F32)
        total = total.astype(BF16).reshape(2, share, right.shape[2])
        own = pick(total, core)
        other = core_swap(pick(total, 1 - core))
        moving = place([own, other], core)
        pieces = [moving]
        for _ in range(1, ctx):
            moving = ctx_shift(moving, 1)
            pieces.append(moving)
        result = jnp.zeros((ctx,) + moving.shape, F32)
        for d, one in enumerate(pieces):
            result = lax.dynamic_update_index_in_dim(result, one.astype(F32), (plane - d) % ctx, 0)
        return result.reshape(experts, share, right.shape[2])

    def row_scatter(total):
        columns = total.shape[1]
        total = total.reshape(pairs, 2, share, columns)
        kept = lax.dynamic_index_in_dim(total, core, 1, keepdims=False)
        sent = lax.dynamic_index_in_dim(total, 1 - core, 1, keepdims=False).astype(BF16)
        total = kept + core_swap(sent).astype(F32)
        kept = pick(total, pair)
        for j in range(1, pairs):
            kept = kept + pair_shift(pick(total, (pair + j) % pairs).astype(BF16), j).astype(F32)
        return kept

    cot_stack = jnp.stack(cots)
    shared_grads = jnp.concatenate(
        [contract(ssx, ssa), contract(ssx, ssb), contract(cot_stack, ssh)], axis=1)
    moving = row_scatter(shared_grads).astype(BF16)
    pieces = [moving]
    for _ in range(1, ctx):
        moving = ctx_shift(moving, 1)
        pieces.append(moving)
    result = jnp.zeros((ctx,) + moving.shape, F32)
    for d, one in enumerate(pieces):
        result = lax.dynamic_update_index_in_dim(result, one.astype(F32), (plane - d) % ctx, 0)
    result = result.reshape(ctx, share, 3, units).transpose(2, 1, 0, 3).reshape(3, share, ctx * units)
    grad_shared_gate, grad_shared_up, grad_shared_down = result[0], result[1], result[2].T

    grad_expert_down = jnp.swapaxes(expert_grad(sr, sh), 1, 2)
    grad_expert_gate = expert_grad(sx, sa)
    grad_expert_up = expert_grad(sx, sb)

    output = tp_gather((mixed + out_sum).astype(BF16))

    grad_out = lax.dynamic_slice_in_dim(cotangent, lane * tok, tok, 0).astype(F32)
    grad_normed = dx_sum[:tok]
    grad_gates = dx_sum[tok : tok + experts, :tok].T
    named = lax.dynamic_slice_in_dim(hits, lane * tok, tok, 1).T
    logits = dot(normed_low, router_full)
    logits = jnp.where(named, logits, -1e30)
    expo = jnp.where(named, jnp.exp(logits - jnp.max(logits, axis=-1, keepdims=True)), 0.0)
    gates = expo / jnp.sum(expo, axis=-1, keepdims=True)
    grad_logits = (
        gates * (grad_gates - jnp.sum(gates * grad_gates, axis=-1, keepdims=True))
    ).astype(BF16)
    grad_router = dot_tn(grad_logits, normed_low)
    grad_normed = grad_normed + dot_nt(grad_logits, router_full)
    grad_mixed_norm, grad_ffn_gain = norm_back(grad_normed, mixed, scale_ffn, ffn_scale)
    grad_mixed = grad_out + grad_mixed_norm
    grad_mixed_low = tp_gather(grad_mixed.astype(BF16))
    grad_out_weight = dot_tn(grad_mixed_low, attended)
    grad_attended = dot(grad_mixed_low, out_full).astype(BF16)

    dq, dk, dv = attend_back(
        query, keys, values, grad_attended, lse, kseg, qseg, cosine, sine)
    hid_all = jnp.concatenate(hid, axis=0)
    attn_grads = jnp.concatenate(
        [dot_tn(hid_all, dk), dot_tn(hid_all, dv), dot_tn(hid[2], dq), grad_out_weight], axis=1)
    rows = row_scatter(attn_grads)
    total = rows.reshape(ctx, share // ctx, 4 * cols)
    kept = pick(total, plane)
    for j in range(1, ctx):
        kept = kept + ctx_shift(pick(total, (plane + j) % ctx).astype(BF16), j).astype(F32)
    kept = kept.astype(BF16)
    attn_rows = place([kept] + [ctx_shift(kept, j) for j in range(1, ctx)], plane)
    attn_rows = attn_rows.reshape(share, 4 * cols).astype(F32)
    grad_key_weight = attn_rows[:, :cols]
    grad_value_weight = attn_rows[:, cols : 2 * cols]
    grad_query_weight = attn_rows[:, 2 * cols : 3 * cols]
    grad_out_rows = attn_rows[:, 3 * cols :].T

    def hidden_back(j):
        piece = slice(j * block, (j + 1) * block)
        total = dot_nt(dk[piece], qkv_full[:, :cols]) + dot_nt(dv[piece], qkv_full[:, cols : 2 * cols])
        if j == 2:
            total = total + dot_nt(dq, qkv_full[:, 2 * cols :])
        total = total.reshape(tp, tok, width)
        kept = pick(total, lane)
        for i in range(1, tp):
            kept = kept + tp_shift(pick(total, (lane + i) % tp).astype(BF16), i).astype(F32)
        return kept

    carried = ctx_open(hidden_back(0).astype(BF16), -1).astype(F32)
    carried = ctx_open((hidden_back(1) + carried).astype(BF16), -1).astype(F32)
    grad_hidden = hidden_back(2) + carried
    scale_attn = lax.rsqrt(jnp.mean(inputs_mine * inputs_mine, axis=-1, keepdims=True) + EPS)
    grad_inputs_norm, grad_attn_gain = norm_back(grad_hidden, inputs_mine, scale_attn, attn_scale)
    input_grad = tp_gather((grad_mixed + grad_inputs_norm).astype(BF16))

    def sum_all(rows):
        for axis in ("fsdp", "tp", "ctx"):
            rows = all_sum(rows, axis)
        return lax.dynamic_slice_in_dim(rows, me * share, share, 1)

    early = sum_all(jnp.concatenate(
        [grad_router, grad_ffn_gain[None], jnp.zeros((16 - experts - 1, width), F32)], axis=0))
    late = sum_all(jnp.broadcast_to(grad_attn_gain[None], (8, width)))
    return (
        output[None],
        input_grad[None],
        grad_query_weight,
        grad_key_weight,
        grad_value_weight,
        grad_out_rows,
        late[0],
        early[experts],
        early[:experts].T,
        grad_shared_gate,
        grad_shared_up,
        grad_shared_down,
        grad_expert_gate,
        grad_expert_up,
        grad_expert_down,
    )


def solution(mesh):
    in_specs = (
        P("fsdp", "ctx", None),
        P("fsdp", None),
        P("fsdp", "ctx", None),
        P("fsdp", "tp"),
        P("fsdp", "tp"),
        P("fsdp", "tp"),
        P("tp", "fsdp"),
        P("fsdp"),
        P("fsdp"),
        P("fsdp", None),
        P("fsdp", "tp"),
        P("fsdp", "tp"),
        P("tp", "fsdp"),
        P(None, "fsdp", "tp"),
        P(None, "fsdp", "tp"),
        P(None, "tp", "fsdp"),
        P("fsdp", "ctx", None),
    )
    out_specs = (
        P("fsdp", "ctx", None),
        P("fsdp", "ctx", None),
        P("fsdp", "tp"),
        P("fsdp", "tp"),
        P("fsdp", "tp"),
        P("tp", "fsdp"),
        P("fsdp"),
        P("fsdp"),
        P("fsdp", None),
        P("fsdp", "tp"),
        P("fsdp", "tp"),
        P("tp", "fsdp"),
        P(None, "fsdp", "tp"),
        P(None, "fsdp", "tp"),
        P(None, "tp", "fsdp"),
    )
    return jax.shard_map(local, mesh=mesh, in_specs=in_specs, out_specs=out_specs, check_vma=False)
```

```python
import functools

import jax
import jax.numpy as jnp
from jax import lax
from jax.experimental import pallas as pl
from jax.experimental.pallas import tpu as pltpu
from jax.sharding import PartitionSpec as P

HD = 64
WINDOW = 1024
EPS = 1e-06
F32 = jnp.float32
BF16 = jnp.bfloat16
VMEM_BYTES = 56 * 1024 * 1024
COST_SCALE = 0.25


def dot(left, right):
    return lax.dot_general(left, right, (((1,), (0,)), ((), ())), preferred_element_type=F32)


def dot_nt(left, right):
    return lax.dot_general(left, right, (((1,), (1,)), ((), ())), preferred_element_type=F32)


def dot_tn(left, right):
    return lax.dot_general(left, right, (((0,), (0,)), ((), ())), preferred_element_type=F32)


def core_swap(block):
    size = lax.axis_size("fsdp")
    return lax.ppermute(block, "fsdp", [(i, i ^ 1) for i in range(size)])


def pair_shift(block, distance):
    size = lax.axis_size("fsdp")
    pairs = size // 2
    route = [(i, ((i // 2 + distance) % pairs) * 2 + i % 2) for i in range(size)]
    return lax.ppermute(block, "fsdp", route)


def tp_shift(block, distance):
    size = lax.axis_size("tp")
    return lax.ppermute(block, "tp", [(i, (i + distance) % size) for i in range(size)])


def ctx_shift(block, distance):
    size = lax.axis_size("ctx")
    return lax.ppermute(block, "ctx", [(i, (i + distance) % size) for i in range(size)])


def ctx_swap(block):
    size = lax.axis_size("ctx")
    return lax.ppermute(block, "ctx", [(i, i ^ 1) for i in range(size)])


def ctx_open(block, distance):
    size = lax.axis_size("ctx")
    route = [(i, i + distance) for i in range(size) if 0 <= i + distance < size]
    return lax.ppermute(block, "ctx", route)


def pick(stack, index):
    return lax.dynamic_index_in_dim(stack, index, 0, keepdims=False)


def place_rows(pieces, me):
    first, second = pieces
    return jnp.where(
        me == 0, jnp.stack([first, second], axis=1), jnp.stack([second, first], axis=1))


def place(pieces, me):
    count = len(pieces)
    if count == 1:
        return pieces[0][None]
    if count == 2:
        first, second = pieces
        return jnp.where(me == 0, jnp.stack([first, second]), jnp.stack([second, first]))
    result = jnp.zeros((count,) + pieces[0].shape, pieces[0].dtype)
    for d, piece in enumerate(pieces):
        result = lax.dynamic_update_index_in_dim(result, piece, (me - d) % count, 0)
    return result


def tie(values, *others):
    return lax.optimization_barrier((values, others))[0]


class Phases:
    def __init__(self):
        self.last = []

    def run(self, function, *values):
        given = function(*(tie(values, self.last) if self.last else values))
        self.last = jax.tree.leaves(given)
        return given


def all_sum(block, axis):
    size = lax.axis_size(axis)
    reach = 1
    while reach < size:
        other = lax.ppermute(block, axis, [(i, i ^ reach) for i in range(size)])
        block = block + other
        reach *= 2
    return block


def whole(shape):
    return pl.BlockSpec(shape, lambda *_: (0,) * len(shape))


def params():
    return pltpu.CompilerParams(vmem_limit_bytes=VMEM_BYTES)


def cost(microseconds):
    return pl.CostEstimate(flops=0, bytes_accessed=int(microseconds * COST_SCALE * 3.4e6), transcendentals=0)


def swap_halves(values):
    width = values.shape[-1]
    lane = lax.broadcasted_iota(jnp.int32, values.shape, 1)
    up = pltpu.roll(values, width - HD // 2, 1)
    down = pltpu.roll(values, HD // 2, 1)
    return jnp.where(lane % HD < HD // 2, up, down)


def widen(table, width):
    copies = -(-width // table.shape[1])
    return jnp.concatenate([table] * copies, axis=1)[:, :width]


def project_kernel(with_query, count, *refs):
    sources = refs[:count]
    gain_ref, w_ref, cos_ref, sin_ref = refs[count : count + 4]
    hid_ref, k_ref, v_ref = refs[len(refs) - 3 - with_query :][:3]
    width = k_ref.shape[1]
    cosine = widen(cos_ref[...], width)
    sine = widen(sin_ref[...], width)
    for i, tok_ref in enumerate(sources):

        @pl.when(pl.program_id(0) == i)
        def _():
            inputs = tok_ref[...].astype(F32)
            scale = lax.rsqrt(jnp.mean(inputs * inputs, axis=-1, keepdims=True) + EPS)
            hidden = (inputs * scale * gain_ref[...]).astype(BF16)
            hid_ref[...] = hidden
            keys = dot(hidden, w_ref[:, :width])
            k_ref[...] = (keys * cosine + swap_halves(keys) * sine).astype(BF16)
            v_ref[...] = dot(hidden, w_ref[:, width : 2 * width]).astype(BF16)
            if with_query and i == count - 1:
                query = dot(hidden, w_ref[:, 2 * width : 3 * width])
                turned = (query * cosine + swap_halves(query) * sine).astype(BF16)
                refs[-1][...] = turned * jnp.asarray(HD**-0.5, BF16)


def project(sources, gain, weights, cosine, sine, width, blocks, first, saved):
    rows, features = sources[0].shape
    count = len(sources)
    with_query = first + count == blocks
    shapes = [(blocks * rows, features), (blocks * rows, width), (blocks * rows, width)]
    outs = [jax.ShapeDtypeStruct(shape, BF16) for shape in shapes]
    specs = [pl.BlockSpec((rows, shape[1]), lambda i: (i + first, 0)) for shape in shapes]
    if with_query:
        outs.append(jax.ShapeDtypeStruct((rows, width), BF16))
        specs.append(whole((rows, width)))
    table = pl.BlockSpec((rows, cosine.shape[1]), lambda i: (i + first, 0))
    return pl.pallas_call(
        functools.partial(project_kernel, with_query, count),
        grid=(count,),
        in_specs=[whole(source.shape) for source in sources]
        + [whole(gain.shape), whole(weights.shape), table, table]
        + [pl.BlockSpec(memory_space=pl.ANY)] * len(saved),
        out_specs=specs,
        out_shape=outs,
        input_output_aliases={count + 4 + i: i for i in range(len(saved))},
        compiler_params=params(),
        cost_estimate=cost(1 + 3 * count),
    )(*sources, gain, weights, cosine, sine, *saved)


def mask_bias(kseg, qseg, keys, queries):
    key = lax.broadcasted_iota(jnp.int32, (keys, queries), 0)
    query = lax.broadcasted_iota(jnp.int32, (keys, queries), 1)
    allowed = (key > query) & (key <= query + WINDOW) & (kseg == qseg)
    return jnp.where(allowed, 0.0, -1e30).astype(F32)


def head_only(values, head):
    lane = lax.broadcasted_iota(jnp.int32, values.shape, 1)
    return jnp.where(lane // HD == head, values, jnp.zeros_like(values))


def attend_kernel(tile, q_ref, k_ref, v_ref, kseg_ref, qseg_ref, out_ref, lse_ref, bias_ref):
    rows = q_ref.shape[0]
    span = WINDOW + tile
    tiles = rows // tile

    @pl.when(pl.program_id(0) == 0)
    def _():
        for j in range(tiles):
            bias_ref[j] = mask_bias(
                kseg_ref[pl.ds(j * tile, span), :], qseg_ref[:, pl.ds(j * tile, tile)], span, tile
            )

    keys = k_ref[...]
    values_t = v_ref[...].T
    for j in range(tiles):
        start = j * tile
        query = q_ref[pl.ds(start, tile), :]
        parts = []
        for head in range(2):
            scores = dot_nt(keys[start : start + span], head_only(query, head)) + bias_ref[j]
            top = jnp.max(scores, axis=0, keepdims=True)
            expo = jnp.exp(scores - top)
            total = jnp.sum(expo, axis=0, keepdims=True)
            part = dot(
                values_t[head * HD : (head + 1) * HD, start : start + span], expo.astype(BF16)
            )
            parts.append(part / total)
            lse_ref[0, pl.ds(head, 1), pl.ds(start, tile)] = top + jnp.log(total)
        out_ref[pl.ds(start, tile), :] = jnp.concatenate(parts, axis=0).T.astype(BF16)


def attend(query, keys, values, kseg, qseg):
    rows, width = query.shape
    span = keys.shape[0]
    tile = min(256, rows)
    pairs = -(-width // (2 * HD))
    columns = lambda count: pl.BlockSpec((count, 2 * HD), lambda i: (0, i))
    return pl.pallas_call(
        functools.partial(attend_kernel, tile),
        grid=(pairs,),
        in_specs=[columns(rows), columns(span), columns(span), whole((span, 1)), whole((1, rows))],
        out_specs=[columns(rows), pl.BlockSpec((1, 2, rows), lambda i: (i, 0, 0))],
        out_shape=[
            jax.ShapeDtypeStruct((rows, width), BF16),
            jax.ShapeDtypeStruct((pairs, 2, rows), F32),
        ],
        scratch_shapes=[pltpu.VMEM((rows // tile, WINDOW + tile, tile), F32)],
        compiler_params=params(),
        cost_estimate=cost(13),
    )(query, keys, values, kseg, qseg)


def attend_back_kernel(
    tile, q_ref, k_ref, v_ref, g_ref, lse_ref, kseg_ref, qseg_ref, cos_ref, sin_ref,
    dq_ref, dk_ref, dv_ref, bias_ref, dk_acc, dv_acc,
):
    rows = q_ref.shape[0]
    span = WINDOW + tile
    tiles = rows // tile
    total_keys = k_ref.shape[0]

    @pl.when(pl.program_id(0) == 0)
    def _():
        for j in range(tiles):
            bias_ref[j] = mask_bias(
                kseg_ref[pl.ds(j * tile, span), :], qseg_ref[:, pl.ds(j * tile, tile)], span, tile
            )

    keys = k_ref[...]
    values = v_ref[...]
    keys_t = keys.T
    dk_acc[...] = jnp.zeros_like(dk_acc)
    dv_acc[...] = jnp.zeros_like(dv_acc)
    cosine = cos_ref[...]
    sine = sin_ref[...]
    lead = total_keys - rows
    for j in range(tiles):
        start = j * tile
        query = q_ref[pl.ds(start, tile), :]
        grad = g_ref[pl.ds(start, tile), :]
        parts = []
        for head in range(2):
            query_one = head_only(query, head)
            grad_one = head_only(grad, head)
            scores = dot_nt(keys[start : start + span], query_one) + bias_ref[j]
            probs = jnp.exp(scores - lse_ref[0, pl.ds(head, 1), pl.ds(start, tile)])
            grad_probs = dot_nt(values[start : start + span], grad_one)
            delta = jnp.sum(probs * grad_probs, axis=0, keepdims=True)
            grad_scores = (probs * (grad_probs - delta)).astype(BF16)
            dv_acc[pl.ds(start, span), :] += dot(probs.astype(BF16), grad_one)
            dk_acc[pl.ds(start, span), :] += dot(grad_scores, query_one)
            parts.append(
                dot(keys_t[head * HD : (head + 1) * HD, start : start + span], grad_scores)
            )
        dq = jnp.concatenate(parts, axis=0).T * HD**-0.5
        places = pl.ds(lead + start, tile)
        dq_ref[pl.ds(start, tile), :] = (
            dq * cos_ref[places, :] - swap_halves(dq) * sin_ref[places, :]
        ).astype(BF16)
    dk = dk_acc[...]
    dk_ref[...] = (dk * cosine - swap_halves(dk) * sine).astype(BF16)
    dv_ref[...] = dv_acc[...].astype(BF16)


def attend_back(query, keys, values, grad, lse, kseg, qseg, cosine, sine):
    rows, width = query.shape
    span = keys.shape[0]
    tile = min(256, rows)
    pairs = -(-width // (2 * HD))
    columns = lambda count: pl.BlockSpec((count, 2 * HD), lambda i: (0, i))
    return pl.pallas_call(
        functools.partial(attend_back_kernel, tile),
        grid=(pairs,),
        in_specs=[
            columns(rows), columns(span), columns(span), columns(rows),
            pl.BlockSpec((1, 2, rows), lambda i: (i, 0, 0)),
            whole((span, 1)), whole((1, rows)), whole((span, 2 * HD)), whole((span, 2 * HD)),
        ],
        out_specs=[columns(rows), columns(span), columns(span)],
        out_shape=[
            jax.ShapeDtypeStruct((rows, width), BF16),
            jax.ShapeDtypeStruct((span, width), BF16),
            jax.ShapeDtypeStruct((span, width), BF16),
        ],
        scratch_shapes=[
            pltpu.VMEM((rows // tile, WINDOW + tile, tile), F32),
            pltpu.VMEM((span, 2 * HD), F32),
            pltpu.VMEM((span, 2 * HD), F32),
        ],
        compiler_params=params(),
        cost_estimate=cost(18),
    )(query, keys, values, grad, lse, kseg, qseg, cosine, sine)


def expert_kernel(capacity, parts, experts, full, steps, n_saved, meta_ref, *refs):
    if full:
        count = steps * parts
        x_refs, c_refs, refs = refs[:count], refs[count : 2 * count], refs[2 * count :]
        w_ref, rt_ref = refs[:2]
        refs = refs[2 + n_saved :]
        dx_ref, sx_ref, sr_ref, sh_ref, sa_ref, sb_ref = refs[:6]
        ssx_ref, ssc_ref, ssh_ref, ssa_ref, ssb_ref, out_ref, x_all, c_all, t_all = refs[6:]
        tok, width = x_all.shape[1:]
        lane = meta_ref[1 + steps]
        for j in range(parts):
            spot = lax.rem(lane + parts - j, parts)
            for i in range(steps):

                @pl.when(pl.program_id(0) == i)
                def _():
                    x_all[spot] = x_refs[i * parts + j][...]
                    c_all[spot] = c_refs[i * parts + j][:tok]
                    if j == 0:
                        t_all[...] = c_refs[i * parts][tok:]

        block = tok * parts
        inputs = x_all[...].reshape(block, width)
        cot = c_all[...].reshape(block, width)
        low_table = t_all[...]
        ssx_ref[0] = inputs
        ssc_ref[0, :block] = cot
        ssc_ref[0, block:] = low_table
    else:
        x_ref, c_ref, w_ref, rt_ref = refs[:4]
        sx_ref, sr_ref, sh_ref, sa_ref, sb_ref = refs[4 + n_saved :]
        block, width = x_ref.shape[1:]
        tok = block // parts
        inputs = x_ref[0]
        cot = c_ref[0, :block]
        low_table = c_ref[0, block:]
    hidden = w_ref.shape[3]
    owned = sx_ref.shape[1]
    table = low_table[:, :block].astype(F32)[:experts]

    def weights(which):
        return w_ref[:, which].reshape(width, hidden)

    logits = dot_nt(rt_ref[...], inputs)[:experts]
    named = table >= 0.0
    top = jnp.max(jnp.where(named, logits, -1e30), axis=0, keepdims=True)
    expo = jnp.where(named, jnp.exp(logits - top), 0.0)
    gates = expo / jnp.sum(expo, axis=0, keepdims=True)
    row = lax.broadcasted_iota(jnp.int32, (experts, block), 0)
    slot = lax.broadcasted_iota(jnp.int32, (capacity, block), 0).astype(F32)
    hits, spreads, gate_slots = [], [], []
    for j in range(owned):
        mine = row == meta_ref[0] + j
        gate = jnp.sum(jnp.where(mine, gates, 0.0), axis=0, keepdims=True)
        position = jnp.sum(jnp.where(mine, table, 0.0), axis=0, keepdims=True)
        hit = slot == position
        hits.append(hit)
        spreads.append(jnp.where(hit, 1.0, 0.0).astype(BF16))
        gate_slots.append(jnp.sum(jnp.where(hit, gate, 0.0), axis=1, keepdims=True))
    spread = jnp.concatenate(spreads, axis=0)
    routed = dot(spread, inputs).astype(BF16)
    cots = dot(spread, cot)
    gate_slots = jnp.concatenate(gate_slots, axis=0)
    grads = (gate_slots * cots).astype(BF16)

    def branch(left, right, gate_weights, up_weights, down_weights):
        gating = dot(left, gate_weights)
        linear = dot(left, up_weights)
        sigma = jax.nn.sigmoid(gating)
        silu = gating * sigma
        active = (silu * linear).astype(BF16)
        grad_active = dot(right, down_weights)
        slope = sigma * (1.0 + gating * (1.0 - sigma))
        grad_gating = (grad_active * linear * slope).astype(BF16)
        grad_linear = (grad_active * silu).astype(BF16)
        if not full:
            return active, grad_gating, grad_linear
        result = dot_nt(active, down_weights)
        grad_left = dot_nt(grad_gating, gate_weights) + dot_nt(grad_linear, up_weights)
        return active, grad_gating, grad_linear, result, grad_left

    weighted = []
    gate_lines = []
    for j in range(owned):
        rows = slice(j * capacity, (j + 1) * capacity)
        sx_ref[0, j] = routed[rows]
        sr_ref[0, j] = grads[rows]
        got = branch(
            routed[rows], grads[rows], weights(j), weights(owned + j), weights(2 * owned + j))
        sh_ref[0, j], sa_ref[0, j], sb_ref[0, j] = got[:3]
        if full:
            result, grad_left = got[3:]
            grad_gates = jnp.sum(result * cots[rows], axis=1, keepdims=True)
            gate_lines.append(jnp.sum(jnp.where(hits[j], grad_gates, 0.0), axis=0, keepdims=True))
            weighted.append(jnp.concatenate(
                [(gate_slots[rows] * result).astype(BF16), grad_left.astype(BF16)], axis=1))
    if not full:
        return
    back = dot_tn(spread, jnp.concatenate(weighted, axis=0))

    units = ssh_ref.shape[2]
    common = weights(3 * owned)
    active, grad_gating, grad_linear, result, grad_left = branch(
        inputs, cot, common[:, :units], common[:, units : 2 * units], common[:, 2 * units : 3 * units])
    ssh_ref[0] = active
    ssa_ref[0] = grad_gating
    ssb_ref[0] = grad_linear
    out = back[:, :width] + result
    dx = back[:, width:] + grad_left
    line = lax.broadcasted_iota(jnp.int32, (16, width), 0)
    for j in range(parts):
        piece = slice(j * tok, (j + 1) * tok)
        out_ref[0, j] = out[piece].astype(BF16)
        dx_ref[0, j, :tok] = dx[piece].astype(BF16)
        spare = jnp.zeros((1, width - tok), F32)
        extra = jnp.zeros((16, width), F32)
        for i in range(owned):
            padded = jnp.concatenate([gate_lines[i][:, piece], spare], axis=1)
            extra = jnp.where(line == meta_ref[0] + i, padded, extra)
        dx_ref[0, j, tok:] = extra.astype(BF16)


def expert_shapes(owned, capacity, width, hidden):
    return [(owned, capacity, width)] * 2 + [(owned, capacity, hidden)] * 3


def placed(shape, where):
    return pl.BlockSpec((1,) + shape, lambda i, meta: (where(i, meta),) + (0,) * len(shape))


def expert_blocks(first, blocks, capacity, experts, units, meta, x_pieces, c_pieces, weights, router_t, saved):
    steps, parts = len(x_pieces), len(x_pieces[0])
    tok, width = x_pieces[0][0].shape
    block = tok * parts
    hidden = weights.shape[3]
    owned = weights.shape[1] // 3
    shapes = expert_shapes(owned, capacity, width, hidden)
    shapes += [(block, width), (block + 16, width), (block, units), (block, units), (block, units), (parts, tok, width)]
    here = lambda i, meta: first + i
    at_place = lambda i, meta: meta[1 + i]
    dx_shape = (parts, tok + 16, width)
    outs = [jax.ShapeDtypeStruct((steps,) + dx_shape, BF16)]
    outs += [jax.ShapeDtypeStruct((blocks,) + shape, BF16) for shape in shapes]
    specs = [placed(dx_shape, lambda i, meta: i)] + [placed(shape, here) for shape in shapes[:-1]]
    specs.append(placed(shapes[-1], at_place))
    xs = [piece for pieces in x_pieces for piece in pieces]
    operands = xs + [piece for pieces in c_pieces for piece in pieces] + [weights, router_t]
    in_specs = [whole(one.shape) for one in operands]
    in_specs += [pl.BlockSpec(memory_space=pl.ANY)] * len(saved)
    return pl.pallas_call(
        functools.partial(expert_kernel, capacity, parts, experts, True, steps, len(saved)),
        grid_spec=pltpu.PrefetchScalarGridSpec(
            num_scalar_prefetch=1,
            grid=(steps,),
            in_specs=in_specs,
            out_specs=specs,
            scratch_shapes=[pltpu.VMEM((parts, tok, width), BF16)] * 2 + [pltpu.VMEM((16, width), BF16)],
        ),
        out_shape=outs,
        input_output_aliases={1 + len(operands) + i: 1 + i for i in range(len(saved))},
        compiler_params=params(),
        cost_estimate=cost(13 * steps),
    )(meta, *operands, *saved)


def expert_again(d, capacity, parts, experts, meta, inputs, cots, weights, router_t, saved):
    blocks, block, width = inputs.shape
    hidden = weights.shape[3]
    shapes = expert_shapes(weights.shape[1] // 3, capacity, width, hidden)
    here = lambda i, meta: d
    return pl.pallas_call(
        functools.partial(expert_kernel, capacity, parts, experts, False, 1, len(saved)),
        grid_spec=pltpu.PrefetchScalarGridSpec(
            num_scalar_prefetch=1,
            grid=(1,),
            in_specs=[placed(inputs.shape[1:], here), placed(cots.shape[1:], here)]
            + [whole(weights.shape), whole(router_t.shape)]
            + [pl.BlockSpec(memory_space=pl.ANY)] * len(saved),
            out_specs=[placed(shape, here) for shape in shapes],
        ),
        out_shape=[jax.ShapeDtypeStruct((blocks,) + shape, BF16) for shape in shapes],
        input_output_aliases={5 + i: i for i in range(len(saved))},
        compiler_params=params(),
        cost_estimate=cost(9),
    )(meta, inputs, cots, weights, router_t, *saved)


def split_rows(value, core, sent_ref, kept_ref, *at):
    pairs = sent_ref.shape[0]
    share = value.shape[0] // (2 * pairs)
    for q in range(pairs):
        first = value[2 * q * share : (2 * q + 1) * share].astype(BF16)
        second = value[(2 * q + 1) * share : (2 * q + 2) * share].astype(BF16)
        index = (q,) + at
        kept_ref[index] = jnp.where(core == 0, first, second)
        sent_ref[index] = jnp.where(core == 0, second, first)


def weight_kernel(core_ref, left_ref, right_ref, sent_ref, kept_ref):
    steps, _, slots, rows = left_ref.shape
    left = left_ref[...].reshape(steps * slots, rows)
    right = right_ref[...].reshape(steps * slots, right_ref.shape[3])
    split_rows(dot_tn(left, right), core_ref[0], sent_ref, kept_ref, 0)


def weight_grads(core, left, right, pairs):
    steps, owned, slots, width = left.shape
    columns = right.shape[3]
    share = width // (2 * pairs)
    parts = 2 if columns % 256 == 0 else 1
    wide = columns // parts
    shape = jax.ShapeDtypeStruct((pairs, owned, share, columns), BF16)
    spec = pl.BlockSpec((pairs, 1, share, wide), lambda j, i, core: (0, j, 0, i))
    return pl.pallas_call(
        weight_kernel,
        grid_spec=pltpu.PrefetchScalarGridSpec(
            num_scalar_prefetch=1,
            grid=(owned, parts),
            in_specs=[
                pl.BlockSpec((steps, 1, slots, width), lambda j, i, core: (0, j, 0, 0)),
                pl.BlockSpec((steps, 1, slots, wide), lambda j, i, core: (0, j, 0, i)),
            ],
            out_specs=[spec, spec],
        ),
        out_shape=[shape, shape],
        compiler_params=params(),
        cost_estimate=cost(6),
    )(core, left, right)


def shared_grad_kernel(core_ref, x_ref, c_ref, a_ref, b_ref, h_ref, sent_ref, kept_ref, total_ref):
    step = pl.program_id(0)
    block, units = a_ref.shape[1:]

    @pl.when(step == 0)
    def _():
        total_ref[...] = jnp.zeros_like(total_ref)

    total_ref[:, :units] += dot_tn(x_ref[0], a_ref[0])
    total_ref[:, units : 2 * units] += dot_tn(x_ref[0], b_ref[0])
    total_ref[:, 2 * units :] += dot_tn(c_ref[0, :block], h_ref[0])

    @pl.when(step == pl.num_programs(0) - 1)
    def _():
        split_rows(total_ref[...], core_ref[0], sent_ref, kept_ref)


def shared_grads(core, x, c, a, b, h, pairs):
    operands = (x, c, a, b, h)
    width, units = x.shape[2], a.shape[2]
    shape = jax.ShapeDtypeStruct((pairs, width // (2 * pairs), 3 * units), BF16)
    return pl.pallas_call(
        shared_grad_kernel,
        grid_spec=pltpu.PrefetchScalarGridSpec(
            num_scalar_prefetch=1,
            grid=(x.shape[0],),
            in_specs=[pl.BlockSpec((1,) + o.shape[1:], lambda i, core: (i, 0, 0)) for o in operands],
            out_specs=[whole(shape.shape), whole(shape.shape)],
            scratch_shapes=[pltpu.VMEM((width, 3 * units), F32)],
        ),
        out_shape=[shape, shape],
        compiler_params=params(),
        cost_estimate=cost(8),
    )(core, *operands)


def attn_grad_kernel(core_ref, hid_ref, dk_ref, dv_ref, dq_ref, gm_ref, at_ref, small_ref, sent_ref, kept_ref):
    lead = hid_ref.shape[0] - dq_ref.shape[0]
    value = jnp.concatenate(
        [
            dot_tn(hid_ref[...], dk_ref[...]),
            dot_tn(hid_ref[...], dv_ref[...]),
            dot_tn(hid_ref[lead:, :], dq_ref[...]),
            dot_tn(gm_ref[...], at_ref[...]),
            small_ref[...].T,
        ],
        axis=1,
    )
    split_rows(value, core_ref[0], sent_ref, kept_ref)


def attn_grads_of(core, hid, dk, dv, dq, grad_mixed_low, attended, small, pairs):
    width, cols = hid.shape[1], dk.shape[1]
    shape = jax.ShapeDtypeStruct((pairs, width // (2 * pairs), 4 * cols + small.shape[0]), BF16)
    operands = (hid, dk, dv, dq, grad_mixed_low, attended, small)
    return pl.pallas_call(
        attn_grad_kernel,
        grid_spec=pltpu.PrefetchScalarGridSpec(
            num_scalar_prefetch=1,
            grid=(1,),
            in_specs=[whole(o.shape) for o in operands],
            out_specs=[whole(shape.shape), whole(shape.shape)],
        ),
        out_shape=[shape, shape],
        compiler_params=params(),
        cost_estimate=cost(8),
    )(core, *operands)


def hidden_back_kernel(count, *refs):
    sources = refs[:count]
    dk_ref, dv_ref, dq_ref, w_ref, out_ref, gain_ref = refs[count:]
    cols = dk_ref.shape[1]
    step = pl.program_id(0)

    @pl.when(step == 0)
    def _():
        gain_ref[...] = jnp.zeros_like(gain_ref)

    for i, tok_ref in enumerate(sources):

        @pl.when(step == i)
        def _():
            grad = dot_nt(dk_ref[...], w_ref[:, :cols]) + dot_nt(dv_ref[...], w_ref[:, cols : 2 * cols])
            if i == count - 1:
                grad = grad + dot_nt(dq_ref[...], w_ref[:, 2 * cols : 3 * cols])
            out_ref[0] = grad.astype(BF16)
            inputs = tok_ref[...].astype(F32)
            scale = lax.rsqrt(jnp.mean(inputs * inputs, axis=-1, keepdims=True) + EPS)
            gain_ref[...] += jnp.sum(grad * (inputs * scale), axis=0, keepdims=True)


def hidden_back(sources, dk, dv, dq, weights):
    count = len(sources)
    rows, width = sources[0].shape
    cols = dk.shape[1]
    part = pl.BlockSpec((rows, cols), lambda i: (i, 0))
    return pl.pallas_call(
        functools.partial(hidden_back_kernel, count),
        grid=(count,),
        in_specs=[whole((rows, width))] * count
        + [part, part, whole((rows, cols)), whole(weights.shape)],
        out_specs=[pl.BlockSpec((1, rows, width), lambda i: (i, 0, 0)), whole((1, width))],
        out_shape=[
            jax.ShapeDtypeStruct((count, rows, width), BF16),
            jax.ShapeDtypeStruct((1, width), F32),
        ],
        compiler_params=params(),
        cost_estimate=cost(7),
    )(*sources, dk, dv, dq, weights)


def collect_kernel(turned, places_ref, first_ref, second_ref, out_ref):
    step = pl.program_id(0)
    for half, ref in enumerate((first_ref, second_ref)):

        @pl.when(step // (pl.num_programs(0) // 2) == half)
        def _():
            piece = ref[0, 0].astype(F32)
            out_ref[0] = piece.T if turned else piece


def collect(places, first, second, skip, owned, turned):
    rows, columns = first.shape[2:]
    count = 4 * owned
    half = 2 * owned
    block = (1, columns, rows) if turned else (1, rows, columns)

    def part(start, low):
        def index(i, places):
            local = jnp.clip(i - start, 0, half - 1)
            return (local // owned, low + local % owned, 0, 0)

        return pl.BlockSpec((1, 1, rows, columns), index)

    return pl.pallas_call(
        functools.partial(collect_kernel, turned),
        grid_spec=pltpu.PrefetchScalarGridSpec(
            num_scalar_prefetch=1,
            grid=(count,),
            in_specs=[part(0, skip[0]), part(half, skip[1])],
            out_specs=pl.BlockSpec(block, lambda i, places: (places[i // half] * half + i % half, 0, 0)),
        ),
        out_shape=jax.ShapeDtypeStruct((count,) + block[1:], F32),
        compiler_params=params(),
        cost_estimate=cost(5),
    )(places, first, second)


def norm_back(grad, values, scale, gain):
    grad_gain = jnp.sum(grad * values * scale, axis=0)
    scaled = grad * gain
    grad_values = scale * scaled - values * scale * scale * scale * jnp.mean(
        scaled * values, axis=-1, keepdims=True
    )
    return grad_values, grad_gain


def local(
    tokens,
    segments,
    routes,
    query_weight,
    key_weight,
    value_weight,
    out_weight,
    attn_gain,
    ffn_gain,
    router_weight,
    shared_gate,
    shared_up,
    shared_down,
    expert_gate,
    expert_up,
    expert_down,
    cotangent,
):
    fsdp, ctx, tp = (lax.axis_size(a) for a in ("fsdp", "ctx", "tp"))
    pairs = fsdp // 2
    me = lax.axis_index("fsdp")
    pair, core = me // 2, me % 2
    plane = lax.axis_index("ctx")
    lane = lax.axis_index("tp")
    tokens, cotangent, routes = tokens[0], cotangent[0], routes[0]
    block, width = tokens.shape
    share, cols = query_weight.shape
    experts = expert_gate.shape[0]
    hidden_units = expert_gate.shape[2]
    units = shared_gate.shape[1] // ctx
    owned = experts // ctx
    top_count = routes.shape[1]
    capacity = 3 * top_count * block // (2 * experts)
    tok = block // tp
    core_index = core.astype(jnp.int32)[None]

    phases = Phases()

    def to_pairs(piece):
        return [pair_shift(piece, d) for d in range(1, pairs)]

    def to_tp(piece):
        return [tp_shift(piece, j) for j in range(1, tp)]

    def joined(*pieces):
        return place(pieces, lane).reshape(block, width)

    def start(*_):
        small = jnp.concatenate(
            [router_weight, attn_gain[:, None], ffn_gain[:, None],
             jnp.zeros((share, 128 - experts - 2), BF16)], axis=1)
        attn_mine = jnp.concatenate(
            [key_weight, value_weight, query_weight, out_weight.T, small], axis=1)
        return attn_mine, lax.dynamic_slice_in_dim(tokens, lane * tok, tok, 0)

    attn_mine, tokens_mine = phases.run(start)

    def cot_rows(cotangent, plane):
        chosen = routes.T
        hits = jnp.zeros((experts, block), jnp.bool_)
        for j in range(top_count):
            hits = hits | (chosen[j : j + 1] == jnp.arange(experts, dtype=jnp.int32)[:, None])
        spot = jnp.arange(block, dtype=jnp.int32)
        before = (spot[:, None] < spot[None, :]).astype(BF16)
        rank = dot(hits.astype(BF16), before)
        table = jnp.pad(jnp.where(hits, rank, -1.0).astype(BF16), ((0, 16 - experts), (0, width - block)))
        pieces = [
            lax.dynamic_slice_in_dim(cotangent, (lane - j) % tp * tok, tok, 0) for j in range(tp)]
        return [jnp.concatenate([pieces[0], table], axis=0)] + pieces[1:], hits

    def of_plane(stack, index):
        return lax.dynamic_slice_in_dim(stack, owned * index, owned, 0)

    def experts_of(index, expert_gate, expert_up, expert_down):
        return [
            of_plane(expert_gate, index),
            of_plane(expert_up, index),
            jnp.swapaxes(of_plane(expert_down, index), 1, 2),
        ]

    at = plane * units
    other_plane = plane ^ 2

    def weight_rows(expert_gate, expert_up, expert_down):
        shared_mine = jnp.concatenate(
            [
                lax.dynamic_slice_in_dim(shared_gate, at, units, 1),
                lax.dynamic_slice_in_dim(shared_up, at, units, 1),
                lax.dynamic_slice_in_dim(shared_down, at, units, 0).T,
                jnp.zeros((share, hidden_units - 3 * units), BF16),
            ],
            axis=1,
        )
        return jnp.concatenate(experts_of(plane, expert_gate, expert_up, expert_down) + [shared_mine[None]], axis=0)

    def tables(plane):
        positions = (plane - 2) * block + jnp.arange(3 * block, dtype=jnp.int32)
        index = jnp.arange(2 * HD, dtype=jnp.int32)
        rates = 10000.0 ** (-2.0 * (index % (HD // 2)).astype(F32) / HD)
        angles = positions.astype(F32)[:, None] * rates[None, :]
        sign = jnp.where(index % HD < HD // 2, -1.0, 1.0)
        segment_pad = jnp.concatenate([jnp.full((2 * block,), -1, jnp.int32), segments[0]])
        kseg = lax.dynamic_slice_in_dim(segment_pad, plane * block, 3 * block, 0)
        return jnp.cos(angles), sign * jnp.sin(angles), kseg[:, None], kseg[2 * block :][None, :]

    def phase_first(attn_mine, tokens_mine, plane, cotangent, expert_gate, expert_up, expert_down):
        return (
            to_pairs(attn_mine), core_swap(attn_mine), ctx_open(tokens_mine, 1), tables(plane),
            cot_rows(cotangent, plane), weight_rows(expert_gate, expert_up, expert_down))

    attn_far, attn_core, prev_one_mine, attn_tables, (cot_own, hits), weights_mine = phases.run(
        phase_first, attn_mine, tokens_mine, plane, cotangent, expert_gate, expert_up, expert_down)
    cosine, sine, kseg, qseg = attn_tables
    weights = lax.all_gather(weights_mine, "fsdp", axis=0)
    cot_mine = [cot_own[0]]
    attn_far_core, prev_one_other, prev_two_mine, got = phases.run(
        lambda attn_far, prev_one_mine, cot: (
            [core_swap(one) for one in attn_far], to_tp(prev_one_mine), ctx_open(prev_one_mine, 1),
            ctx_shift(cot, -1)),
        attn_far, prev_one_mine, cot_mine[-1])
    cot_mine.append(got)

    def all_rows(mine, far, across, far_across, columns):
        same = place([mine[:, columns]] + [one[:, columns] for one in far], pair)
        other = place([across[:, columns]] + [one[:, columns] for one in far_across], pair)
        return place_rows([same, other], core).reshape(width, same.shape[2])

    def project_near(tokens, prev_one_mine, prev_one_other, prev_two_mine, cot, *attn):
        sent = to_tp(prev_two_mine), ctx_shift(cot, -1)
        qkv_full = all_rows(*attn, slice(0, 3 * cols))
        small_t = all_rows(*attn, slice(4 * cols, 4 * cols + 128))[:, :16].T
        attn_scale = small_t[experts : experts + 1].astype(F32)
        prev_one = joined(prev_one_mine, *prev_one_other)
        first = project([prev_one, tokens], attn_scale, qkv_full, cosine, sine, cols, 3, 1, [])
        return qkv_full, small_t, attn_scale, prev_one, first, sent

    qkv_full, small_t, attn_scale, prev_one, first, (prev_two_other, got) = phases.run(
        project_near, tokens, prev_one_mine, prev_one_other, prev_two_mine, cot_mine[-1],
        attn_mine, attn_far, attn_core, attn_far_core)
    cot_mine.append(got)
    query = first[3]
    half = ctx // 2
    here = [(plane + d) % ctx for d in range(ctx)]

    def attention(prev_two_mine, prev_two_other, cots, *attn):
        cot_sent = ctx_shift(cots[-1], -1), to_tp(cots[1]), to_tp(cots[2])
        prev_two = joined(prev_two_mine, *prev_two_other)
        hid, keys, values = project(
            [prev_two], attn_scale, qkv_full, cosine, sine, cols, 3, 0, first[:3])
        attended, lse = attend(query, keys, values, kseg, qseg)
        out_full = all_rows(*attn, slice(3 * cols, 4 * cols))
        router_full = all_rows(*attn, slice(4 * cols, 4 * cols + 128))[:, :experts]
        partial = dot_nt(attended, out_full).astype(BF16).reshape(tp, tok, width)
        return cot_sent, prev_two, hid, keys, values, attended, lse, out_full, router_full, partial

    cot_sent, prev_two, hid, keys, values, attended, lse, out_full, router_full, partial = phases.run(
        attention, prev_two_mine, prev_two_other, cot_mine, attn_mine, attn_far, attn_core, attn_far_core)
    cot_mine.append(cot_sent[0])
    cot_other = [cot_own[1:], cot_sent[1], cot_sent[2]]

    def sent_tp(total):
        return [tp_shift(pick(total, (lane + j) % tp), j) for j in range(1, tp)]

    def sum_tp(total, got):
        result = pick(total, lane).astype(F32)
        for one in got:
            result = result + one.astype(F32)
        return result

    partial_other = phases.run(sent_tp, partial)
    router_t = jnp.concatenate([small_t[:experts], jnp.zeros((16 - experts, width), BF16)], axis=0)
    ffn_scale = small_t[experts + 1 : experts + 2].astype(F32)
    inputs_mine = tokens_mine.astype(F32)

    def normalize(partial, got):
        mixed = inputs_mine + sum_tp(partial, got)
        scale_ffn = lax.rsqrt(jnp.mean(mixed * mixed, axis=-1, keepdims=True) + EPS)
        return (mixed * scale_ffn * ffn_scale).astype(BF16), mixed, scale_ffn

    normed_low, mixed, scale_ffn = phases.run(normalize, partial, partial_other)

    mine, other = [normed_low], []
    for d in range(1, ctx):
        got, moved = phases.run(lambda one: (to_tp(one), ctx_shift(one, -1)), mine[-1])
        other.append(got)
        mine.append(moved)

    near, far = list(range(0, ctx, 2)), list(range(1, ctx, 2))

    def meta_of(blocks):
        return jnp.stack([owned * plane] + [here[d] for d in blocks] + [lane]).astype(jnp.int32)

    def pieces_of(mine, other, blocks):
        return [[mine[d]] + list(other[d]) for d in blocks]

    def near_blocks(last, last_cot, weights, mine, cot_mine, expert_gate, expert_up, expert_down):
        later = to_tp(last), to_tp(last_cot)
        got = expert_blocks(
            0, ctx, capacity, experts, units, meta_of(near), pieces_of(mine, other, near),
            pieces_of(cot_mine, cot_other, near), weights, router_t, [])
        again_mine = jnp.concatenate(experts_of(other_plane, expert_gate, expert_up, expert_down), axis=0)
        return later, got, again_mine

    later, got, again_mine = phases.run(
        near_blocks, mine[-1], cot_mine[-1], weights, mine[:-1], cot_mine[:-1], expert_gate, expert_up, expert_down)
    other_weights = lax.all_gather(again_mine, "fsdp", axis=0)
    other.append(later[0])
    cot_other.append(later[1])
    near_dx = [got[0][i] for i in range(half)]

    def far_blocks(dx, mine, other, cot_mine, cot_other, saved):
        sent = [sent_tp(one) for one in dx]
        got = expert_blocks(
            half, ctx, capacity, experts, units, meta_of(far), pieces_of(mine, other, far),
            pieces_of(cot_mine, cot_other, far), weights, router_t, saved)
        return sent, got

    near_sent, got = phases.run(far_blocks, near_dx, mine, other, cot_mine, cot_other, got[1:])
    far_dx = [got[0][i] for i in range(half)]
    sx, sr, sh, sa, sb, ssx, ssc, ssh, ssa, ssb, out_parts = got[1:]

    def sent_pairs(kept, got):
        return [
            pair_shift(
                (pick(kept, (pair + j) % pairs).astype(F32) + pick(got, (pair + j) % pairs).astype(F32)
                 ).astype(BF16), j)
            for j in range(1, pairs)
        ]

    def add_pairs(kept, got, far):
        result = pick(kept, pair).astype(F32) + pick(got, pair).astype(F32)
        for one in far:
            result = result + one.astype(F32)
        return result.astype(BF16)

    def weight_step(left, right):
        return weight_grads(core_index, left, right, pairs)

    def again(d, ssx, saved):
        meta = jnp.stack([owned * other_plane, plane]).astype(jnp.int32)
        return expert_again(
            d, capacity, tp, experts, meta, ssx, ssc, other_weights, router_t, saved)

    def back_through_norm(dx_sum):
        grad_normed = dx_sum[:tok]
        grad_gates = dx_sum[tok : tok + experts, :tok].T
        named = lax.dynamic_slice_in_dim(hits, lane * tok, tok, 1).T
        logits = jnp.where(named, dot(normed_low, router_full), -1e30)
        expo = jnp.where(named, jnp.exp(logits - jnp.max(logits, axis=-1, keepdims=True)), 0.0)
        gates = expo / jnp.sum(expo, axis=-1, keepdims=True)
        grad_logits = (
            gates * (grad_gates - jnp.sum(gates * grad_gates, axis=-1, keepdims=True))
        ).astype(BF16)
        grad_normed = grad_normed + dot_nt(grad_logits, router_full)
        grad_mixed_norm, grad_ffn_gain = norm_back(grad_normed, mixed, scale_ffn, ffn_scale)
        grad_out = lax.dynamic_slice_in_dim(cotangent, lane * tok, tok, 0).astype(F32)
        grad_mixed = grad_out + grad_mixed_norm
        return grad_mixed.astype(BF16), grad_mixed, grad_ffn_gain, dot_tn(grad_logits, normed_low)

    def out_sent(out_parts, d):
        return [
            tp_shift(lax.dynamic_index_in_dim(out_parts[d], (lane + j) % tp, 0, keepdims=False), j)
            for j in range(1, tp)
        ]

    def phase_one(near_dx, near_sent, far_dx, sr, sx):
        sent = [sent_tp(one) for one in far_dx]
        sums = [sum_tp(one, got) for one, got in zip(near_dx, near_sent)]
        home = [sums[0]] + [ctx_shift(one.astype(BF16), d) for d, one in zip(near[1:], sums[1:])]
        return sent, home, weight_step(sr, sh), weight_step(sx, sa)

    far_sent, home, down, gate = phases.run(phase_one, near_dx, near_sent, far_dx, sr, sx)

    def phase_two(far_dx, far_sent, down_sent, gate_sent, sx, ssx, out_parts):
        sums = [sum_tp(one, got) for one, got in zip(far_dx, far_sent)]
        more = [ctx_shift(one.astype(BF16), d) for d, one in zip(far, sums)]
        return (
            more, core_swap(down_sent), core_swap(gate_sent), out_sent(out_parts, 0),
            weight_step(sx, sb), again(0, ssx, []))

    more, down_got, gate_got, out_zero, up, other_saved = phases.run(
        phase_two, far_dx, far_sent, down[0], gate[0], sx, ssx, out_parts)

    def phase_three(home, down_kept, down_got, up_sent, ssx, saved, out_parts):
        sent = sent_pairs(down_kept, down_got), core_swap(up_sent), out_sent(out_parts, 1), out_sent(out_parts, 2)
        back = back_through_norm(sum(one.astype(F32) for one in home))
        return sent, back, again(1, ssx, saved)

    (down_far, up_got, out_one, out_two), back, other_saved = phases.run(
        phase_three, home + more, down[1], down_got, up[0], ssx, other_saved, out_parts)
    grad_mixed_low, grad_mixed, grad_ffn_gain, grad_router = back

    def phase_four(gate_kept, gate_got, grad_mixed_low, ssx, saved, out_parts):
        sent = sent_pairs(gate_kept, gate_got), to_tp(grad_mixed_low), out_sent(out_parts, 3)
        return sent, again(3, ssx, again(2, ssx, saved))

    (gate_far, grad_mixed_other, out_three), other_saved = phases.run(
        phase_four, gate[1], gate_got, grad_mixed_low, ssx, other_saved, out_parts)
    ox, orr, oh, oa, ob = other_saved

    def phase_five(up_kept, up_got, down, grad_mixed_low, grad_mixed_other, out_parts, out_far):
        sent = sent_pairs(up_kept, up_got)
        rows = joined(grad_mixed_low, *grad_mixed_other)
        grad_attended = dot(rows, out_full).astype(BF16)
        grads = attend_back(query, keys, values, grad_attended, lse, kseg, qseg, cosine, sine)
        total = lax.dynamic_index_in_dim(out_parts, lane, 1, keepdims=False).astype(F32)
        for j in range(tp - 1):
            total = total + jnp.stack([one[j] for one in out_far]).astype(F32)
        return sent, rows, grads, add_pairs(*down), total.astype(BF16)

    up_far, grad_mixed_rows, (dq, dk, dv), own_down, out_total = phases.run(
        phase_five, up[1], up_got, (down[1], down_got, down_far), grad_mixed_low, grad_mixed_other, out_parts,
        [out_zero, out_one, out_two, out_three])
    out_sum = lax.psum_scatter(out_total, "ctx", scatter_dimension=0, tiled=False)

    def phase_six(gate, up, dq, dk, dv, orr, ssx):
        back, gain_row = hidden_back([prev_two, prev_one, tokens], dk, dv, dq, qkv_full)
        return back, gain_row, add_pairs(*gate), add_pairs(*up), weight_step(orr, oh), shared_grads(
            core_index, ssx, ssc, ssa, ssb, ssh, pairs)

    back, gain_row, own_gate, own_up, other_down, shared = phases.run(
        phase_six, (gate[1], gate_got, gate_far), (up[1], up_got, up_far), dq, dk, dv, orr, ssx)
    groups = [[2 * i, 2 * i + 1] for i in range(ctx // 2)]
    own_all = lax.all_gather(
        jnp.concatenate([own_down, own_gate, own_up], axis=0), "ctx", axis=0, axis_index_groups=groups)
    small_rows = jnp.concatenate(
        [grad_router, grad_ffn_gain[None], gain_row, jnp.zeros((16 - experts - 2, width), F32)], axis=0)
    hidden_parts = [back[j].reshape(tp, tok, width) for j in range(3)]

    def phase_seven(hidden_parts, small_rows, down_sent, shared_sent, ox):
        sent = [sent_tp(hidden_parts[0]), sent_tp(hidden_parts[1]), all_sum(small_rows, "tp")]
        return sent, core_swap(down_sent), core_swap(shared_sent), weight_step(ox, oa), weight_step(ox, ob)

    hidden_sent, down_got, shared_got, other_gate, other_up = phases.run(
        phase_seven, hidden_parts, small_rows, other_down[0], shared[0], ox)
    small_rows = jnp.pad(hidden_sent[2], ((0, 112), (0, 0)))

    def phase_eight(hidden_parts, got, hid, down, gate_sent, up_sent):
        far_two = sum_tp(hidden_parts[0], got[0]).astype(BF16)
        sent = [
            sent_pairs(*down), ctx_open(far_two, -1), sent_tp(hidden_parts[2]), core_swap(gate_sent), core_swap(up_sent)]
        attn = attn_grads_of(
            core_index, hid, dk, dv, dq, grad_mixed_rows, attended, small_rows, pairs)
        return sent, attn

    (down_far, carried, hidden_mine_sent, gate_got, up_got), attn = phases.run(
        phase_eight, hidden_parts, hidden_sent, hid, (other_down[1], down_got), other_gate[0], other_up[0])

    def phase_nine(hidden_parts, got, carried, attn_sent, gate, down, shared):
        sent = sent_pairs(*gate)
        far_one = (sum_tp(hidden_parts[1], got[1]) + carried.astype(F32)).astype(BF16)
        return sent, ctx_open(far_one, -1), core_swap(attn_sent), add_pairs(*down), sent_pairs(*shared)

    gate_far, carried, attn_got, other_down, shared_far = phases.run(
        phase_nine, hidden_parts, hidden_sent, carried, attn[0], (other_gate[1], gate_got),
        (other_down[1], down_got, down_far), (shared[1], shared_got))

    def input_back(total, got, carried):
        grad_hidden = sum_tp(total, got) + carried.astype(F32)
        scale_attn = lax.rsqrt(jnp.mean(inputs_mine * inputs_mine, axis=-1, keepdims=True) + EPS)
        scaled = grad_hidden * attn_scale
        grad_norm = scale_attn * scaled - inputs_mine * scale_attn * scale_attn * scale_attn * jnp.mean(
            scaled * inputs_mine, axis=-1, keepdims=True)
        return (grad_mixed + grad_norm).astype(BF16)

    def phase_ten(hidden_parts, got, carried, attn, up, gate, shared, other_down):
        return (
            input_back(hidden_parts[2], got, carried), sent_pairs(*attn), sent_pairs(*up), add_pairs(*gate),
            add_pairs(*shared), ctx_swap(other_down))

    input_mine, attn_far, up_far, other_gate, own_shared, far_other_down = phases.run(
        phase_ten, hidden_parts, hidden_mine_sent, carried, (attn[1], attn_got), (other_up[1], up_got),
        (other_gate[1], gate_got, gate_far), (shared[1], shared_got, shared_far), other_down)
    all_shared = lax.all_gather(own_shared, "ctx", axis=0)
    odd = plane % 2

    def paired(one, got):
        return jnp.where(odd == 0, jnp.stack([one, got]), jnp.stack([got, one]))

    places = jnp.stack([plane // 2, 1 - plane // 2]).astype(jnp.int32)

    def phase_eleven(input_mine, attn, up, other_gate, other_down, far_other_down, own_all, out_sum):
        output_mine = (mixed + out_sum.astype(F32)).astype(BF16)
        return (
            to_tp(input_mine), add_pairs(*attn), add_pairs(*up), ctx_swap(other_gate),
            collect(places, own_all, paired(other_down, far_other_down), (0, 0), owned, True), output_mine)

    input_other, attn_rows, other_up, far_other_gate, grad_expert_down, output_mine = phases.run(
        phase_eleven, input_mine, (attn[1], attn_got, attn_far), (other_up[1], up_got, up_far), other_gate,
        other_down, far_other_down, own_all, out_sum)
    attn_rows = lax.psum(attn_rows, "ctx")

    def phase_twelve(other_up, other_gate, far_other_gate, input_mine, input_other, output_mine):
        return (
            ctx_swap(other_up), to_tp(output_mine), joined(input_mine, *input_other),
            collect(places, own_all, paired(other_gate, far_other_gate), (owned, 0), owned, False))

    far_other_up, output_other, input_grad, grad_expert_gate = phases.run(
        phase_twelve, other_up, other_gate, far_other_gate, input_mine, input_other, output_mine)
    grad_expert_up = collect(places, own_all, paired(other_up, far_other_up), (2 * owned, 0), owned, False)
    output = joined(output_mine, *output_other)
    attn_rows = attn_rows.astype(F32)
    grad_key_weight = attn_rows[:, :cols]
    grad_value_weight = attn_rows[:, cols : 2 * cols]
    grad_query_weight = attn_rows[:, 2 * cols : 3 * cols]
    grad_out_rows = attn_rows[:, 3 * cols : 4 * cols].T
    small_out = attn_rows[:, 4 * cols :]
    result = all_shared.astype(F32)
    result = result.reshape(ctx, share, 3, units).transpose(2, 1, 0, 3).reshape(3, share, ctx * units)
    grad_shared_gate, grad_shared_up, grad_shared_down = result[0], result[1], result[2].T
    return (
        output[None],
        input_grad[None],
        grad_query_weight,
        grad_key_weight,
        grad_value_weight,
        grad_out_rows,
        small_out[:, experts + 1],
        small_out[:, experts],
        small_out[:, :experts],
        grad_shared_gate,
        grad_shared_up,
        grad_shared_down,
        grad_expert_gate,
        grad_expert_up,
        grad_expert_down,
    )


def solution(mesh):
    in_specs = (
        P("fsdp", "ctx", None),
        P("fsdp", None),
        P("fsdp", "ctx", None),
        P("fsdp", "tp"),
        P("fsdp", "tp"),
        P("fsdp", "tp"),
        P("tp", "fsdp"),
        P("fsdp"),
        P("fsdp"),
        P("fsdp", None),
        P("fsdp", "tp"),
        P("fsdp", "tp"),
        P("tp", "fsdp"),
        P(None, "fsdp", "tp"),
        P(None, "fsdp", "tp"),
        P(None, "tp", "fsdp"),
        P("fsdp", "ctx", None),
    )
    out_specs = (
        P("fsdp", "ctx", None),
        P("fsdp", "ctx", None),
        P("fsdp", "tp"),
        P("fsdp", "tp"),
        P("fsdp", "tp"),
        P("tp", "fsdp"),
        P("fsdp"),
        P("fsdp"),
        P("fsdp", None),
        P("fsdp", "tp"),
        P("fsdp", "tp"),
        P("tp", "fsdp"),
        P(None, "fsdp", "tp"),
        P(None, "fsdp", "tp"),
        P(None, "tp", "fsdp"),
    )
    return jax.shard_map(local, mesh=mesh, in_specs=in_specs, out_specs=out_specs, check_vma=False)
```

```python
import functools

import jax
import jax.numpy as jnp
from jax import lax
from jax.experimental import pallas as pl
from jax.experimental.pallas import tpu as pltpu
from jax.sharding import PartitionSpec as P

HD = 64
WINDOW = 1024
EPS = 1e-06
F32 = jnp.float32
BF16 = jnp.bfloat16
VMEM_BYTES = 56 * 1024 * 1024
COST_SCALE = 0.1


def dot(left, right):
    return lax.dot_general(left, right, (((1,), (0,)), ((), ())), preferred_element_type=F32)


def dot_nt(left, right):
    return lax.dot_general(left, right, (((1,), (1,)), ((), ())), preferred_element_type=F32)


def dot_tn(left, right):
    return lax.dot_general(left, right, (((0,), (0,)), ((), ())), preferred_element_type=F32)


def core_swap(block):
    size = lax.axis_size("fsdp")
    return lax.ppermute(block, "fsdp", [(i, i ^ 1) for i in range(size)])


def pair_shift(block, distance):
    size = lax.axis_size("fsdp")
    pairs = size // 2
    route = [(i, ((i // 2 + distance) % pairs) * 2 + i % 2) for i in range(size)]
    return lax.ppermute(block, "fsdp", route)


def pair_swap(block, reach):
    size = lax.axis_size("fsdp")
    return lax.ppermute(block, "fsdp", [(i, i ^ (2 * reach)) for i in range(size)])


def tp_shift(block, distance):
    size = lax.axis_size("tp")
    return lax.ppermute(block, "tp", [(i, (i + distance) % size) for i in range(size)])


def ctx_shift(block, distance):
    size = lax.axis_size("ctx")
    return lax.ppermute(block, "ctx", [(i, (i + distance) % size) for i in range(size)])


def ctx_swap(block):
    size = lax.axis_size("ctx")
    return lax.ppermute(block, "ctx", [(i, i ^ 1) for i in range(size)])


def ctx_open(block, distance):
    size = lax.axis_size("ctx")
    route = [(i, i + distance) for i in range(size) if 0 <= i + distance < size]
    return lax.ppermute(block, "ctx", route)


def pick(stack, index):
    return lax.dynamic_index_in_dim(stack, index, 0, keepdims=False)


def place_rows(pieces, me):
    first, second = pieces
    return jnp.where(
        me == 0, jnp.stack([first, second], axis=1), jnp.stack([second, first], axis=1))


def place(pieces, me):
    count = len(pieces)
    if count == 1:
        return pieces[0][None]
    if count == 2:
        first, second = pieces
        return jnp.where(me == 0, jnp.stack([first, second]), jnp.stack([second, first]))
    result = jnp.zeros((count,) + pieces[0].shape, pieces[0].dtype)
    for d, piece in enumerate(pieces):
        result = lax.dynamic_update_index_in_dim(result, piece, (me - d) % count, 0)
    return result


def tie(values, *others):
    return lax.optimization_barrier((values, others))[0]


class Phases:
    def __init__(self):
        self.last = []

    def run(self, function, *values):
        given = function(*(tie(values, self.last) if self.last else values))
        self.last = jax.tree.leaves(given)
        return given


def all_sum(block, axis):
    size = lax.axis_size(axis)
    reach = 1
    while reach < size:
        other = lax.ppermute(block, axis, [(i, i ^ reach) for i in range(size)])
        block = block + other
        reach *= 2
    return block


def whole(shape):
    return pl.BlockSpec(shape, lambda *_: (0,) * len(shape))


def params():
    return pltpu.CompilerParams(vmem_limit_bytes=VMEM_BYTES)


def cost(microseconds):
    return pl.CostEstimate(flops=0, bytes_accessed=int(microseconds * COST_SCALE * 3.4e6), transcendentals=0)


def swap_halves(values):
    width = values.shape[-1]
    lane = lax.broadcasted_iota(jnp.int32, values.shape, 1)
    up = pltpu.roll(values, width - HD // 2, 1)
    down = pltpu.roll(values, HD // 2, 1)
    return jnp.where(lane % HD < HD // 2, up, down)


def widen(table, width):
    copies = -(-width // table.shape[1])
    return jnp.concatenate([table] * copies, axis=1)[:, :width]


def rotated(values, cosine, sine):
    return (values * cosine + swap_halves(values) * sine).astype(BF16)


def project_rows(inputs, gain, weights, cos_ref, sin_ref, hid_ref, k_ref, v_ref):
    scale = lax.rsqrt(jnp.mean(inputs * inputs, axis=-1, keepdims=True) + EPS)
    hidden = (inputs * scale * gain).astype(BF16)
    hid_ref[...] = hidden
    width = k_ref.shape[1]
    k_ref[...] = rotated(
        dot(hidden, weights[:, :width]), widen(cos_ref[...], width), widen(sin_ref[...], width))
    v_ref[...] = dot(hidden, weights[:, width : 2 * width]).astype(BF16)
    return hidden


def project_near_kernel(parts, pairs, meta_ref, tok_ref, *refs):
    prev_refs, refs = refs[:parts], refs[parts:]
    same_refs, cross_refs, refs = refs[:pairs], refs[pairs : 2 * pairs], refs[2 * pairs :]
    gain_ref, cos_ref, sin_ref, hid_ref, k_ref, v_ref, q_ref, w_ref, prev_ref, w_all, x_all = refs
    tok, features = x_all.shape[1:]
    share, columns = w_all.shape[1:]

    @pl.when(pl.program_id(0) == 0)
    def _():
        for d in range(pairs):
            row = 2 * lax.rem(meta_ref[1] + pairs - d, pairs)
            w_all[row + meta_ref[2]] = same_refs[d][...]
            w_all[row + 1 - meta_ref[2]] = cross_refs[d][...]
        for j in range(parts):
            x_all[lax.rem(meta_ref[0] + parts - j, parts)] = prev_refs[j][...]
        weights = w_all[...].reshape(2 * pairs * share, columns)
        w_ref[...] = weights
        inputs = x_all[...].reshape(parts * tok, features)
        prev_ref[...] = inputs
        project_rows(inputs.astype(F32), gain_ref[...], weights, cos_ref, sin_ref, hid_ref, k_ref, v_ref)

    @pl.when(pl.program_id(0) == 1)
    def _():
        weights = w_all[...].reshape(2 * pairs * share, columns)
        hidden = project_rows(
            tok_ref[...].astype(F32), gain_ref[...], weights, cos_ref, sin_ref, hid_ref, k_ref, v_ref)
        width = k_ref.shape[1]
        query = dot(hidden, weights[:, 2 * width :])
        q_ref[...] = rotated(
            query, widen(cos_ref[...], width), widen(sin_ref[...], width)) * jnp.asarray(HD**-0.5, BF16)


def project_near(meta, tokens, prev_pieces, same, cross, gain, cosine, sine):
    rows, features = tokens.shape
    share, columns = same[0].shape
    width = columns // 3
    tok = prev_pieces[0].shape[0]
    count = 2 * len(same) * share
    shapes = [(3 * rows, features), (3 * rows, width), (3 * rows, width)]
    block = lambda i, meta: (i + 1, 0)
    others = [(rows, width), (count, columns), (rows, features)]
    operands = [tokens, *prev_pieces, *same, *cross, gain]
    table = pl.BlockSpec((rows, cosine.shape[1]), block)
    return pl.pallas_call(
        functools.partial(project_near_kernel, len(prev_pieces), len(same)),
        grid_spec=pltpu.PrefetchScalarGridSpec(
            num_scalar_prefetch=1,
            grid=(2,),
            in_specs=[whole(o.shape) for o in operands] + [table, table],
            out_specs=[pl.BlockSpec((rows, shape[1]), block) for shape in shapes]
            + [whole(shape) for shape in others],
            scratch_shapes=[
                pltpu.VMEM((2 * len(same), share, columns), BF16),
                pltpu.VMEM((len(prev_pieces), tok, features), BF16),
            ],
        ),
        out_shape=[jax.ShapeDtypeStruct(shape, BF16) for shape in shapes + others],
        compiler_params=params(),
        cost_estimate=cost(7),
    )(meta, *operands, cosine, sine)


def project_far_kernel(parts, meta_ref, *refs):
    prev_refs, refs = refs[:parts], refs[parts:]
    w_ref, gain_ref, cos_ref, sin_ref, _, _, _, hid_ref, k_ref, v_ref, prev_ref, x_all = refs
    tok, features = x_all.shape[1:]
    for j in range(parts):
        x_all[lax.rem(meta_ref[0] + parts - j, parts)] = prev_refs[j][...]
    inputs = x_all[...].reshape(parts * tok, features)
    prev_ref[...] = inputs
    project_rows(inputs.astype(F32), gain_ref[...], w_ref[...], cos_ref, sin_ref, hid_ref, k_ref, v_ref)


def project_far(meta, prev_pieces, weights, gain, cosine, sine, saved):
    tok, features = prev_pieces[0].shape
    rows = tok * len(prev_pieces)
    width = weights.shape[1] // 3
    first = lambda i, meta: (0, 0)
    operands = [*prev_pieces, weights, gain]
    table = pl.BlockSpec((rows, cosine.shape[1]), first)
    return pl.pallas_call(
        functools.partial(project_far_kernel, len(prev_pieces)),
        grid_spec=pltpu.PrefetchScalarGridSpec(
            num_scalar_prefetch=1,
            grid=(1,),
            in_specs=[whole(o.shape) for o in operands] + [table, table]
            + [pl.BlockSpec(memory_space=pl.ANY)] * 3,
            out_specs=[pl.BlockSpec((rows, one.shape[1]), first) for one in saved]
            + [whole((rows, features))],
            scratch_shapes=[pltpu.VMEM((len(prev_pieces), tok, features), BF16)],
        ),
        out_shape=[jax.ShapeDtypeStruct(one.shape, BF16) for one in saved]
        + [jax.ShapeDtypeStruct((rows, features), BF16)],
        input_output_aliases={1 + len(operands) + 2 + i: i for i in range(3)},
        compiler_params=params(),
        cost_estimate=cost(4),
    )(meta, *operands, cosine, sine, *saved)


def prepare_kernel(parts, meta_ref, routes_ref, cot_ref, rates_ref, seg_ref, *refs):
    cos_ref, sin_ref, kseg_ref, qseg_ref, hits_ref = refs[:5]
    mine_ref, other_refs, seg_all = refs[5], refs[6:-1], refs[-1]
    block, width = cot_ref.shape
    tok = block // parts
    experts = hits_ref.shape[0]
    rows, lanes = cos_ref.shape
    short = 64
    origin = (meta_ref[1] - 2) * block
    far = (lax.broadcasted_iota(jnp.int32, (rows // short, lanes), 0) * short + origin).astype(F32) * rates_ref[...]
    near = lax.broadcasted_iota(jnp.int32, (short, lanes), 0).astype(F32) * rates_ref[...]
    far_cos, far_sin, near_cos, near_sin = jnp.cos(far), jnp.sin(far), jnp.cos(near), jnp.sin(near)
    sign = jnp.where(lax.broadcasted_iota(jnp.int32, (short, lanes), 1) % HD < HD // 2, -1.0, 1.0)
    signed_sin, signed_cos = sign * near_sin, sign * near_cos
    for h in range(rows // short):
        part = slice(h * short, (h + 1) * short)
        one_cos, one_sin = far_cos[h : h + 1], far_sin[h : h + 1]
        cos_ref[part] = one_cos * near_cos - one_sin * near_sin
        sin_ref[part] = one_sin * signed_cos + one_cos * signed_sin
    seg_all[:, : 2 * block] = jnp.full((1, 2 * block), -1, jnp.int32)
    seg_all[:, 2 * block :] = seg_ref[...]
    kseg = seg_all[:, pl.ds(pl.multiple_of(meta_ref[1] * block, block), rows)]
    qseg_ref[...] = kseg[:, rows - block :]
    kseg_ref[...] = jnp.broadcast_to(kseg, (8, rows)).T[:, :1]
    row = lax.broadcasted_iota(jnp.int32, (experts, block), 0)
    named = row == routes_ref[0:1, :]
    for j in range(1, routes_ref.shape[0]):
        named = named | (row == routes_ref[j : j + 1, :])
    hits = jnp.where(named, 1.0, 0.0).astype(F32)
    before = lax.broadcasted_iota(jnp.int32, (block, block), 0) < lax.broadcasted_iota(jnp.int32, (block, block), 1)
    rank = dot(hits.astype(BF16), jnp.where(before, 1.0, 0.0).astype(BF16))
    hits_ref[...] = hits
    table = jnp.concatenate([jnp.where(named, rank, -1.0), jnp.zeros((16 - experts, block), F32)], axis=0)
    mine_ref[tok:, :] = jnp.concatenate([table, jnp.zeros((16, width - block), F32)], axis=1).astype(BF16)
    for j, ref in enumerate((mine_ref,) + other_refs):
        start = lax.rem(meta_ref[0] + parts - j, parts) * tok
        ref[:tok, :] = cot_ref[pl.ds(pl.multiple_of(start, tok), tok), :]


def prepare(meta, parts, experts, routes_t, cotangent, segments):
    block, width = cotangent.shape
    tok = block // parts
    index = jnp.arange(2 * HD, dtype=jnp.int32)
    rates = (10000.0 ** (-2.0 * (index % (HD // 2)).astype(F32) / HD))[None, :]
    shapes = [
        ((3 * block, 2 * HD), F32), ((3 * block, 2 * HD), F32), ((3 * block, 1), jnp.int32), ((1, block), jnp.int32),
        ((experts, block), F32), ((tok + 16, width), BF16),
    ] + [((tok, width), BF16)] * (parts - 1)
    operands = (routes_t, cotangent, rates, segments)
    return pl.pallas_call(
        functools.partial(prepare_kernel, parts),
        grid_spec=pltpu.PrefetchScalarGridSpec(
            num_scalar_prefetch=1,
            grid=(1,),
            in_specs=[whole(o.shape) for o in operands],
            out_specs=[whole(shape) for shape, _ in shapes],
            scratch_shapes=[pltpu.VMEM((1, segments.shape[1] + 2 * block), jnp.int32)],
        ),
        out_shape=[jax.ShapeDtypeStruct(shape, kind) for shape, kind in shapes],
        compiler_params=params(),
        cost_estimate=cost(3),
    )(meta, *operands)


def bundle_kernel(plane_ref, *refs):
    stacks, shared, out_ref = refs[:3], refs[3:-1], refs[-1]
    owned = stacks[0].shape[0]
    for i, ref in enumerate(stacks):
        out_ref[i * owned : (i + 1) * owned] = ref[...]
    if shared:
        units = shared[0].shape[1]
        out_ref[3 * owned] = jnp.zeros(out_ref.shape[1:], BF16)
        for i, ref in enumerate(shared):
            out_ref[3 * owned, :, i * units : (i + 1) * units] = ref[...]


def bundle(plane, owned, units, stacks, shared):
    _, share, hidden = stacks[0].shape
    count = 3 * owned + bool(shared)
    return pl.pallas_call(
        bundle_kernel,
        grid_spec=pltpu.PrefetchScalarGridSpec(
            num_scalar_prefetch=1,
            grid=(1,),
            in_specs=[pl.BlockSpec((owned, share, hidden), lambda i, plane: (plane[0], 0, 0))] * 3
            + [pl.BlockSpec((share, units), lambda i, plane: (0, plane[0]))] * len(shared),
            out_specs=whole((count, share, hidden)),
        ),
        out_shape=jax.ShapeDtypeStruct((count, share, hidden), BF16),
        compiler_params=params(),
        cost_estimate=cost(3),
    )(plane.astype(jnp.int32)[None], *stacks, *shared)


def finish_kernel(meta_ref, mine_ref, *refs):
    count = len(refs) - 6
    pieces = (mine_ref,) + refs[:count]
    k_ref, v_ref, q_ref, o_ref, small_ref, all_ref = refs[count:]
    total = len(pieces)
    rows = mine_ref.shape[0]
    for d, ref in enumerate(pieces):
        all_ref[lax.rem(meta_ref[0] + total - d, total)] = ref[...].astype(F32)
    whole_rows = all_ref[...].reshape(total * rows, mine_ref.shape[1])
    share, cols = k_ref.shape
    for i, ref in enumerate((k_ref, v_ref, q_ref, o_ref)):
        ref[...] = whole_rows[:share, i * cols : (i + 1) * cols]
    small_ref[...] = whole_rows[share : share + 16, : small_ref.shape[1]]


def finish(meta, pieces, share, cols):
    rows, columns = pieces[0].shape
    shapes = [(share, cols)] * 4 + [(16, columns)]
    return pl.pallas_call(
        finish_kernel,
        grid_spec=pltpu.PrefetchScalarGridSpec(
            num_scalar_prefetch=1,
            grid=(1,),
            in_specs=[whole(piece.shape) for piece in pieces],
            out_specs=[whole(shape) for shape in shapes],
            scratch_shapes=[pltpu.VMEM((len(pieces), rows, columns), F32)],
        ),
        out_shape=[jax.ShapeDtypeStruct(shape, F32) for shape in shapes],
        compiler_params=params(),
        cost_estimate=cost(2),
    )(meta, *pieces)


def pack_kernel(lane_ref, k_ref, v_ref, q_ref, router_ref, gains_ref, tok_ref, qkv_ref, small_ref, mine_ref):
    width = k_ref.shape[1]
    for i, ref in enumerate((k_ref, v_ref, q_ref)):
        qkv_ref[:, i * width : (i + 1) * width] = ref[...]
    experts, share = router_ref.shape
    small_ref[...] = jnp.concatenate(
        [router_ref[...].astype(F32), gains_ref[...].astype(F32),
         jnp.zeros((small_ref.shape[0] - experts - 2, share), F32)], axis=0).astype(BF16)
    mine_ref[...] = tok_ref[...]


def pack(lane, parts, key_weight, value_weight, query_weight, router_t, gains, tokens):
    rows, width = tokens.shape
    share, cols = key_weight.shape
    part = (rows // parts, width)
    shapes = [(share, 3 * cols), (16, share), part]
    operands = (key_weight, value_weight, query_weight, router_t, gains)
    return pl.pallas_call(
        pack_kernel,
        grid_spec=pltpu.PrefetchScalarGridSpec(
            num_scalar_prefetch=1,
            grid=(1,),
            in_specs=[whole(o.shape) for o in operands]
            + [pl.BlockSpec(part, lambda i, lane: (lane[0], 0))],
            out_specs=[whole(shape) for shape in shapes],
        ),
        out_shape=[jax.ShapeDtypeStruct(shape, BF16) for shape in shapes],
        compiler_params=params(),
        cost_estimate=cost(2),
    )(lane.astype(jnp.int32)[None], *operands, tokens)


def mask_bias(kseg, qseg, keys, queries):
    key = lax.broadcasted_iota(jnp.int32, (keys, queries), 0)
    query = lax.broadcasted_iota(jnp.int32, (keys, queries), 1)
    allowed = (key > query) & (key <= query + WINDOW) & (kseg == qseg)
    return jnp.where(allowed, 0.0, -1e30).astype(F32)


def head_only(values, head):
    lane = lax.broadcasted_iota(jnp.int32, values.shape, 1)
    return jnp.where(lane // HD == head, values, jnp.zeros_like(values))


def attend_kernel(tile, q_ref, k_ref, v_ref, kseg_ref, qseg_ref, out_ref, lse_ref, bias_ref):
    rows = q_ref.shape[0]
    span = WINDOW + tile
    tiles = rows // tile

    @pl.when(pl.program_id(0) == 0)
    def _():
        for j in range(tiles):
            bias_ref[j] = mask_bias(
                kseg_ref[pl.ds(j * tile, span), :], qseg_ref[:, pl.ds(j * tile, tile)], span, tile
            )

    keys = k_ref[...]
    values_t = v_ref[...].T
    for j in range(tiles):
        start = j * tile
        query = q_ref[pl.ds(start, tile), :]
        parts = []
        for head in range(2):
            scores = dot_nt(keys[start : start + span], head_only(query, head)) + bias_ref[j]
            top = jnp.max(scores, axis=0, keepdims=True)
            expo = jnp.exp(scores - top)
            total = jnp.sum(expo, axis=0, keepdims=True)
            part = dot(
                values_t[head * HD : (head + 1) * HD, start : start + span], expo.astype(BF16)
            )
            parts.append(part / total)
            lse_ref[0, pl.ds(head, 1), pl.ds(start, tile)] = top + jnp.log(total)
        out_ref[pl.ds(start, tile), :] = jnp.concatenate(parts, axis=0).T.astype(BF16)


def attend(query, keys, values, kseg, qseg):
    rows, width = query.shape
    span = keys.shape[0]
    tile = min(256, rows)
    pairs = -(-width // (2 * HD))
    columns = lambda count: pl.BlockSpec((count, 2 * HD), lambda i: (0, i))
    return pl.pallas_call(
        functools.partial(attend_kernel, tile),
        grid=(pairs,),
        in_specs=[columns(rows), columns(span), columns(span), whole((span, 1)), whole((1, rows))],
        out_specs=[columns(rows), pl.BlockSpec((1, 2, rows), lambda i: (i, 0, 0))],
        out_shape=[
            jax.ShapeDtypeStruct((rows, width), BF16),
            jax.ShapeDtypeStruct((pairs, 2, rows), F32),
        ],
        scratch_shapes=[pltpu.VMEM((rows // tile, WINDOW + tile, tile), F32)],
        compiler_params=params(),
        cost_estimate=cost(13),
    )(query, keys, values, kseg, qseg)


def attend_back_kernel(
    tile, q_ref, k_ref, v_ref, g_ref, lse_ref, kseg_ref, qseg_ref, cos_ref, sin_ref,
    dq_ref, dk_ref, dv_ref, bias_ref, dk_acc, dv_acc,
):
    rows = q_ref.shape[0]
    span = WINDOW + tile
    tiles = rows // tile
    total_keys = k_ref.shape[0]

    @pl.when(pl.program_id(0) == 0)
    def _():
        for j in range(tiles):
            bias_ref[j] = mask_bias(
                kseg_ref[pl.ds(j * tile, span), :], qseg_ref[:, pl.ds(j * tile, tile)], span, tile
            )

    keys = k_ref[...]
    values = v_ref[...]
    keys_t = keys.T
    dk_acc[...] = jnp.zeros_like(dk_acc)
    dv_acc[...] = jnp.zeros_like(dv_acc)
    cosine = cos_ref[...]
    sine = sin_ref[...]
    lead = total_keys - rows
    for j in range(tiles):
        start = j * tile
        query = q_ref[pl.ds(start, tile), :]
        grad = g_ref[pl.ds(start, tile), :]
        parts = []
        for head in range(2):
            query_one = head_only(query, head)
            grad_one = head_only(grad, head)
            scores = dot_nt(keys[start : start + span], query_one) + bias_ref[j]
            probs = jnp.exp(scores - lse_ref[0, pl.ds(head, 1), pl.ds(start, tile)])
            grad_probs = dot_nt(values[start : start + span], grad_one)
            delta = jnp.sum(probs * grad_probs, axis=0, keepdims=True)
            grad_scores = (probs * (grad_probs - delta)).astype(BF16)
            dv_acc[pl.ds(start, span), :] += dot(probs.astype(BF16), grad_one)
            dk_acc[pl.ds(start, span), :] += dot(grad_scores, query_one)
            parts.append(
                dot(keys_t[head * HD : (head + 1) * HD, start : start + span], grad_scores)
            )
        dq = jnp.concatenate(parts, axis=0).T * HD**-0.5
        places = pl.ds(lead + start, tile)
        dq_ref[pl.ds(start, tile), :] = (
            dq * cos_ref[places, :] - swap_halves(dq) * sin_ref[places, :]
        ).astype(BF16)
    dk = dk_acc[...]
    dk_ref[...] = (dk * cosine - swap_halves(dk) * sine).astype(BF16)
    dv_ref[...] = dv_acc[...].astype(BF16)


def attend_back(query, keys, values, grad, lse, kseg, qseg, cosine, sine):
    rows, width = query.shape
    span = keys.shape[0]
    tile = min(256, rows)
    pairs = -(-width // (2 * HD))
    columns = lambda count: pl.BlockSpec((count, 2 * HD), lambda i: (0, i))
    return pl.pallas_call(
        functools.partial(attend_back_kernel, tile),
        grid=(pairs,),
        in_specs=[
            columns(rows), columns(span), columns(span), columns(rows),
            pl.BlockSpec((1, 2, rows), lambda i: (i, 0, 0)),
            whole((span, 1)), whole((1, rows)), whole((span, 2 * HD)), whole((span, 2 * HD)),
        ],
        out_specs=[columns(rows), columns(span), columns(span)],
        out_shape=[
            jax.ShapeDtypeStruct((rows, width), BF16),
            jax.ShapeDtypeStruct((span, width), BF16),
            jax.ShapeDtypeStruct((span, width), BF16),
        ],
        scratch_shapes=[
            pltpu.VMEM((rows // tile, WINDOW + tile, tile), F32),
            pltpu.VMEM((span, 2 * HD), F32),
            pltpu.VMEM((span, 2 * HD), F32),
        ],
        compiler_params=params(),
        cost_estimate=cost(18),
    )(query, keys, values, grad, lse, kseg, qseg, cosine, sine)


def expert_kernel(capacity, parts, experts, full, steps, n_saved, meta_ref, *refs):
    if full:
        count = steps * parts
        x_refs, c_refs, refs = refs[:count], refs[count : 2 * count], refs[2 * count :]
        w_ref, rt_ref = refs[:2]
        refs = refs[2 + n_saved :]
        dx_ref, sx_ref, sr_ref, sh_ref, sa_ref, sb_ref = refs[:6]
        ssx_ref, ssc_ref, ssh_ref, ssa_ref, ssb_ref, out_ref, x_all, c_all, t_all = refs[6:]
        tok, width = x_all.shape[1:]
        lane = meta_ref[1 + steps]
        for j in range(parts):
            spot = lax.rem(lane + parts - j, parts)
            for i in range(steps):

                @pl.when(pl.program_id(0) == i)
                def _():
                    x_all[spot] = x_refs[i * parts + j][...]
                    c_all[spot] = c_refs[i * parts + j][:tok]
                    if j == 0:
                        t_all[...] = c_refs[i * parts][tok:]

        block = tok * parts
        inputs = x_all[...].reshape(block, width)
        cot = c_all[...].reshape(block, width)
        low_table = t_all[...]
        ssx_ref[0] = inputs
        ssc_ref[0, :block] = cot
        ssc_ref[0, block:] = low_table
    else:
        x_ref, c_ref, w_ref, rt_ref = refs[:4]
        sx_ref, sr_ref, sh_ref, sa_ref, sb_ref = refs[4 + n_saved :]
        block, width = x_ref.shape[1:]
        tok = block // parts
        inputs = x_ref[0]
        cot = c_ref[0, :block]
        low_table = c_ref[0, block:]
    hidden = w_ref.shape[3]
    owned = sx_ref.shape[1]
    table = low_table[:, :block].astype(F32)[:experts]

    def weights(which):
        return w_ref[:, which].reshape(width, hidden)

    logits = dot_nt(rt_ref[...], inputs)[:experts]
    named = table >= 0.0
    top = jnp.max(jnp.where(named, logits, -1e30), axis=0, keepdims=True)
    expo = jnp.where(named, jnp.exp(logits - top), 0.0)
    gates = expo / jnp.sum(expo, axis=0, keepdims=True)
    row = lax.broadcasted_iota(jnp.int32, (experts, block), 0)
    slot = lax.broadcasted_iota(jnp.int32, (capacity, block), 0).astype(F32)
    hits, spreads, gate_slots = [], [], []
    for j in range(owned):
        mine = row == meta_ref[0] + j
        gate = jnp.sum(jnp.where(mine, gates, 0.0), axis=0, keepdims=True)
        position = jnp.sum(jnp.where(mine, table, 0.0), axis=0, keepdims=True)
        hit = slot == position
        hits.append(hit)
        spreads.append(jnp.where(hit, 1.0, 0.0).astype(BF16))
        gate_slots.append(jnp.sum(jnp.where(hit, gate, 0.0), axis=1, keepdims=True))
    spread = jnp.concatenate(spreads, axis=0)
    routed = dot(spread, inputs).astype(BF16)
    cots = dot(spread, cot)
    gate_slots = jnp.concatenate(gate_slots, axis=0)
    grads = (gate_slots * cots).astype(BF16)

    def branch(left, right, gate_weights, up_weights, down_weights):
        gating = dot(left, gate_weights)
        linear = dot(left, up_weights)
        sigma = jax.nn.sigmoid(gating)
        silu = gating * sigma
        active = (silu * linear).astype(BF16)
        grad_active = dot(right, down_weights)
        slope = sigma * (1.0 + gating * (1.0 - sigma))
        grad_gating = (grad_active * linear * slope).astype(BF16)
        grad_linear = (grad_active * silu).astype(BF16)
        if not full:
            return active, grad_gating, grad_linear
        result = dot_nt(active, down_weights)
        grad_left = dot_nt(grad_gating, gate_weights) + dot_nt(grad_linear, up_weights)
        return active, grad_gating, grad_linear, result, grad_left

    weighted = []
    gate_lines = []
    for j in range(owned):
        rows = slice(j * capacity, (j + 1) * capacity)
        sx_ref[0, j] = routed[rows]
        sr_ref[0, j] = grads[rows]
        got = branch(
            routed[rows], grads[rows], weights(j), weights(owned + j), weights(2 * owned + j))
        sh_ref[0, j], sa_ref[0, j], sb_ref[0, j] = got[:3]
        if full:
            result, grad_left = got[3:]
            grad_gates = jnp.sum(result * cots[rows], axis=1, keepdims=True)
            gate_lines.append(jnp.sum(jnp.where(hits[j], grad_gates, 0.0), axis=0, keepdims=True))
            weighted.append(jnp.concatenate(
                [(gate_slots[rows] * result).astype(BF16), grad_left.astype(BF16)], axis=1))
    if not full:
        return
    back = dot_tn(spread, jnp.concatenate(weighted, axis=0))

    units = ssh_ref.shape[2]
    common = weights(3 * owned)
    active, grad_gating, grad_linear, result, grad_left = branch(
        inputs, cot, common[:, :units], common[:, units : 2 * units], common[:, 2 * units : 3 * units])
    ssh_ref[0] = active
    ssa_ref[0] = grad_gating
    ssb_ref[0] = grad_linear
    out = back[:, :width] + result
    dx = back[:, width:] + grad_left
    line = lax.broadcasted_iota(jnp.int32, (16, width), 0)
    for j in range(parts):
        piece = slice(j * tok, (j + 1) * tok)
        out_ref[0, j] = out[piece].astype(BF16)
        dx_ref[0, j, :tok] = dx[piece].astype(BF16)
        spare = jnp.zeros((1, width - tok), F32)
        extra = jnp.zeros((16, width), F32)
        for i in range(owned):
            padded = jnp.concatenate([gate_lines[i][:, piece], spare], axis=1)
            extra = jnp.where(line == meta_ref[0] + i, padded, extra)
        dx_ref[0, j, tok:] = extra.astype(BF16)


def expert_shapes(owned, capacity, width, hidden):
    return [(owned, capacity, width)] * 2 + [(owned, capacity, hidden)] * 3


def placed(shape, where):
    return pl.BlockSpec((1,) + shape, lambda i, meta: (where(i, meta),) + (0,) * len(shape))


def expert_blocks(first, blocks, capacity, experts, units, meta, x_pieces, c_pieces, weights, router_t, saved):
    steps, parts = len(x_pieces), len(x_pieces[0])
    tok, width = x_pieces[0][0].shape
    block = tok * parts
    hidden = weights.shape[3]
    owned = weights.shape[1] // 3
    shapes = expert_shapes(owned, capacity, width, hidden)
    shapes += [(block, width), (block + 16, width), (block, units), (block, units), (block, units), (parts, tok, width)]
    here = lambda i, meta: first + i
    at_place = lambda i, meta: meta[1 + i]
    dx_shape = (parts, tok + 16, width)
    outs = [jax.ShapeDtypeStruct((steps,) + dx_shape, BF16)]
    outs += [jax.ShapeDtypeStruct((blocks,) + shape, BF16) for shape in shapes]
    specs = [placed(dx_shape, lambda i, meta: i)] + [placed(shape, here) for shape in shapes[:-1]]
    specs.append(placed(shapes[-1], at_place))
    xs = [piece for pieces in x_pieces for piece in pieces]
    operands = xs + [piece for pieces in c_pieces for piece in pieces] + [weights, router_t]
    in_specs = [whole(one.shape) for one in operands]
    in_specs += [pl.BlockSpec(memory_space=pl.ANY)] * len(saved)
    return pl.pallas_call(
        functools.partial(expert_kernel, capacity, parts, experts, True, steps, len(saved)),
        grid_spec=pltpu.PrefetchScalarGridSpec(
            num_scalar_prefetch=1,
            grid=(steps,),
            in_specs=in_specs,
            out_specs=specs,
            scratch_shapes=[pltpu.VMEM((parts, tok, width), BF16)] * 2 + [pltpu.VMEM((16, width), BF16)],
        ),
        out_shape=outs,
        input_output_aliases={1 + len(operands) + i: 1 + i for i in range(len(saved))},
        compiler_params=params(),
        cost_estimate=cost(13 * steps),
    )(meta, *operands, *saved)


def expert_again(first, steps, capacity, parts, experts, meta, inputs, cots, weights, router_t, saved):
    blocks, block, width = inputs.shape
    hidden = weights.shape[3]
    shapes = expert_shapes(weights.shape[1] // 3, capacity, width, hidden)
    here = lambda i, meta: first + i
    return pl.pallas_call(
        functools.partial(expert_kernel, capacity, parts, experts, False, steps, len(saved)),
        grid_spec=pltpu.PrefetchScalarGridSpec(
            num_scalar_prefetch=1,
            grid=(steps,),
            in_specs=[placed(inputs.shape[1:], here), placed(cots.shape[1:], here)]
            + [whole(weights.shape), whole(router_t.shape)]
            + [pl.BlockSpec(memory_space=pl.ANY)] * len(saved),
            out_specs=[placed(shape, here) for shape in shapes],
        ),
        out_shape=[jax.ShapeDtypeStruct((blocks,) + shape, BF16) for shape in shapes],
        input_output_aliases={5 + i: i for i in range(len(saved))},
        compiler_params=params(),
        cost_estimate=cost(6 * steps),
    )(meta, inputs, cots, weights, router_t, *saved)


def pair_sum_kernel(index_ref, kept_ref, got_ref, *refs):
    total = kept_ref[0].astype(F32) + got_ref[0].astype(F32)
    for ref in refs[:-1]:
        total = total + ref[...].astype(F32)
    refs[-1][...] = total.astype(BF16)


def pair_sum(index, kept, got, far):
    shape = kept.shape[1:]
    steps = shape[0] if len(shape) == 3 else 1
    part = (shape[0] // steps,) + shape[1:]
    rest = (0,) * (len(shape) - 1)
    picked = pl.BlockSpec((1,) + part, lambda i, index: (index[0], i) + rest)
    plain = pl.BlockSpec(part, lambda i, index: (i,) + rest)
    return pl.pallas_call(
        pair_sum_kernel,
        grid_spec=pltpu.PrefetchScalarGridSpec(
            num_scalar_prefetch=1,
            grid=(steps,),
            in_specs=[picked, picked] + [plain] * len(far),
            out_specs=plain,
        ),
        out_shape=jax.ShapeDtypeStruct(shape, BF16),
        compiler_params=params(),
        cost_estimate=cost(2),
    )(index.astype(jnp.int32)[None], kept, got, *far)


def split_rows(value, core, sent_ref, kept_ref, *at):
    pairs = sent_ref.shape[0]
    share = value.shape[0] // (2 * pairs)
    for q in range(pairs):
        first = value[2 * q * share : (2 * q + 1) * share].astype(BF16)
        second = value[(2 * q + 1) * share : (2 * q + 2) * share].astype(BF16)
        index = (q,) + at
        kept_ref[index] = jnp.where(core == 0, first, second)
        sent_ref[index] = jnp.where(core == 0, second, first)


def weight_kernel(core_ref, left_ref, right_ref, sent_ref, kept_ref):
    steps, _, slots, rows = left_ref.shape
    left = left_ref[...].reshape(steps * slots, rows)
    right = right_ref[...].reshape(steps * slots, right_ref.shape[3])
    split_rows(dot_tn(left, right), core_ref[0], sent_ref, kept_ref, 0)


def weight_grads(core, left, right, pairs):
    steps, owned, slots, width = left.shape
    columns = right.shape[3]
    share = width // (2 * pairs)
    parts, wide = 1, columns
    shape = jax.ShapeDtypeStruct((pairs, owned, share, columns), BF16)
    spec = pl.BlockSpec((pairs, 1, share, wide), lambda j, i, core: (0, j, 0, i))
    return pl.pallas_call(
        weight_kernel,
        grid_spec=pltpu.PrefetchScalarGridSpec(
            num_scalar_prefetch=1,
            grid=(owned, parts),
            in_specs=[
                pl.BlockSpec((steps, 1, slots, width), lambda j, i, core: (0, j, 0, 0)),
                pl.BlockSpec((steps, 1, slots, wide), lambda j, i, core: (0, j, 0, i)),
            ],
            out_specs=[spec, spec],
        ),
        out_shape=[shape, shape],
        compiler_params=params(),
        cost_estimate=cost(6),
    )(core, left, right)


def shared_grad_kernel(core_ref, x_ref, c_ref, a_ref, b_ref, h_ref, sent_ref, kept_ref, total_ref):
    step = pl.program_id(0)
    block, units = a_ref.shape[1:]

    @pl.when(step == 0)
    def _():
        total_ref[...] = jnp.zeros_like(total_ref)

    total_ref[:, :units] += dot_tn(x_ref[0], a_ref[0])
    total_ref[:, units : 2 * units] += dot_tn(x_ref[0], b_ref[0])
    total_ref[:, 2 * units :] += dot_tn(c_ref[0, :block], h_ref[0])

    @pl.when(step == pl.num_programs(0) - 1)
    def _():
        split_rows(total_ref[...], core_ref[0], sent_ref, kept_ref)


def shared_grads(core, x, c, a, b, h, pairs):
    operands = (x, c, a, b, h)
    width, units = x.shape[2], a.shape[2]
    shape = jax.ShapeDtypeStruct((pairs, width // (2 * pairs), 3 * units), BF16)
    return pl.pallas_call(
        shared_grad_kernel,
        grid_spec=pltpu.PrefetchScalarGridSpec(
            num_scalar_prefetch=1,
            grid=(x.shape[0],),
            in_specs=[pl.BlockSpec((1,) + o.shape[1:], lambda i, core: (i, 0, 0)) for o in operands],
            out_specs=[whole(shape.shape), whole(shape.shape)],
            scratch_shapes=[pltpu.VMEM((width, 3 * units), F32)],
        ),
        out_shape=[shape, shape],
        compiler_params=params(),
        cost_estimate=cost(8),
    )(core, *operands)


def attn_grad_kernel(core_ref, hid_ref, dk_ref, dv_ref, dq_ref, gm_ref, at_ref, sent_ref, kept_ref):
    lead = hid_ref.shape[0] - dq_ref.shape[0]
    value = jnp.concatenate(
        [
            dot_tn(hid_ref[...], dk_ref[...]),
            dot_tn(hid_ref[...], dv_ref[...]),
            dot_tn(hid_ref[lead:, :], dq_ref[...]),
            dot_tn(gm_ref[...], at_ref[...]),
        ],
        axis=1,
    )
    split_rows(value, core_ref[0], sent_ref, kept_ref)


def attn_grads_of(core, hid, dk, dv, dq, grad_mixed_low, attended, pairs):
    width, cols = hid.shape[1], dk.shape[1]
    shape = jax.ShapeDtypeStruct((pairs, width // (2 * pairs), 4 * cols), BF16)
    operands = (hid, dk, dv, dq, grad_mixed_low, attended)
    return pl.pallas_call(
        attn_grad_kernel,
        grid_spec=pltpu.PrefetchScalarGridSpec(
            num_scalar_prefetch=1,
            grid=(1,),
            in_specs=[whole(o.shape) for o in operands],
            out_specs=[whole(shape.shape), whole(shape.shape)],
        ),
        out_shape=[shape, shape],
        compiler_params=params(),
        cost_estimate=cost(8),
    )(core, *operands)


def hidden_back_kernel(count, *refs):
    sources = refs[:count]
    dk_ref, dv_ref, dq_ref, w_ref, out_ref, gain_ref = refs[count:]
    cols = dk_ref.shape[1]
    step = pl.program_id(0)

    @pl.when(step == 0)
    def _():
        gain_ref[...] = jnp.zeros_like(gain_ref)

    for i, tok_ref in enumerate(sources):

        @pl.when(step == i)
        def _():
            grad = dot_nt(dk_ref[...], w_ref[:, :cols]) + dot_nt(dv_ref[...], w_ref[:, cols : 2 * cols])
            if i == count - 1:
                grad = grad + dot_nt(dq_ref[...], w_ref[:, 2 * cols : 3 * cols])
            out_ref[0] = grad.astype(BF16)
            inputs = tok_ref[...].astype(F32)
            scale = lax.rsqrt(jnp.mean(inputs * inputs, axis=-1, keepdims=True) + EPS)
            gain_ref[...] += jnp.sum(grad * (inputs * scale), axis=0, keepdims=True)


def hidden_back(sources, dk, dv, dq, weights):
    count = len(sources)
    rows, width = sources[0].shape
    cols = dk.shape[1]
    part = pl.BlockSpec((rows, cols), lambda i: (i, 0))
    return pl.pallas_call(
        functools.partial(hidden_back_kernel, count),
        grid=(count,),
        in_specs=[whole((rows, width))] * count
        + [part, part, whole((rows, cols)), whole(weights.shape)],
        out_specs=[pl.BlockSpec((1, rows, width), lambda i: (i, 0, 0)), whole((1, width))],
        out_shape=[
            jax.ShapeDtypeStruct((count, rows, width), BF16),
            jax.ShapeDtypeStruct((1, width), F32),
        ],
        compiler_params=params(),
        cost_estimate=cost(7),
    )(*sources, dk, dv, dq, weights)


def collect_kernel(places_ref, *refs):
    group = pl.num_programs(0) // (len(refs) - 1)
    for i, piece_ref in enumerate(refs[:-1]):

        @pl.when(pl.program_id(0) // group == i)
        def _():
            refs[-1][...] = piece_ref[...].astype(F32)


def collect(places, pieces):
    group, rows, columns = pieces[0].shape
    block = (1, rows, columns)

    def part(i):
        return pl.BlockSpec(block, lambda step, places: (jnp.clip(step - i * group, 0, group - 1), 0, 0))

    return pl.pallas_call(
        collect_kernel,
        grid_spec=pltpu.PrefetchScalarGridSpec(
            num_scalar_prefetch=1,
            grid=(len(pieces) * group,),
            in_specs=[part(i) for i in range(len(pieces))],
            out_specs=pl.BlockSpec(
                block, lambda step, places: (places[step // group] * group + step % group, 0, 0)),
        ),
        out_shape=jax.ShapeDtypeStruct((len(pieces) * group, rows, columns), F32),
        compiler_params=params(),
        cost_estimate=cost(5),
    )(places, *pieces)


def norm_back(grad, values, scale, gain):
    grad_gain = jnp.sum(grad * values * scale, axis=0)
    scaled = grad * gain
    grad_values = scale * scaled - values * scale * scale * scale * jnp.mean(
        scaled * values, axis=-1, keepdims=True
    )
    return grad_values, grad_gain


def local(
    tokens,
    segments,
    routes,
    query_weight,
    key_weight,
    value_weight,
    out_weight,
    attn_gain,
    ffn_gain,
    router_weight,
    shared_gate,
    shared_up,
    shared_down,
    expert_gate,
    expert_up,
    expert_down,
    cotangent,
):
    fsdp, ctx, tp = (lax.axis_size(a) for a in ("fsdp", "ctx", "tp"))
    pairs = fsdp // 2
    me = lax.axis_index("fsdp")
    pair, core = me // 2, me % 2
    plane = lax.axis_index("ctx")
    lane = lax.axis_index("tp")
    tokens, cotangent, routes = tokens[0], cotangent[0], routes[0]
    block, width = tokens.shape
    share, cols = query_weight.shape
    experts = expert_gate.shape[0]
    hidden_units = expert_gate.shape[2]
    units = shared_gate.shape[1] // ctx
    owned = experts // ctx
    top_count = routes.shape[1]
    capacity = 3 * top_count * block // (2 * experts)
    tok = block // tp
    core_index = core.astype(jnp.int32)[None]

    phases = Phases()

    def to_pairs(piece):
        return [pair_shift(piece, d) for d in range(1, pairs)]

    def to_tp(piece):
        return [tp_shift(piece, j) for j in range(1, tp)]

    def joined(*pieces):
        return place(pieces, lane).reshape(block, width)

    other_plane = plane ^ 2

    gains = jnp.concatenate([attn_gain[None], ffn_gain[None]], axis=0)
    qkv_mine, small_mine, tokens_mine = pack(
        lane, tp, key_weight, value_weight, query_weight, router_weight.T, gains, tokens)
    small_core = core_swap(small_mine)
    qkv_mine, small_mine, tokens_mine, small_core = phases.run(
        lambda *given: given, qkv_mine, small_mine, tokens_mine, small_core)

    prepare_meta = jnp.stack([lane, plane]).astype(jnp.int32)

    def send_first(qkv, small, small_core, tokens_mine, cotangent):
        return (
            to_pairs(qkv), core_swap(qkv), to_pairs(jnp.concatenate([small, small_core], axis=0)),
            ctx_open(tokens_mine, 1),
            prepare(prepare_meta, tp, experts, routes.T, cotangent, segments))

    qkv_far, qkv_core, small_far, prev_one_mine, prepared = phases.run(
        send_first, qkv_mine, small_mine, small_core, tokens_mine, cotangent)
    cosine, sine, kseg, qseg, hits = prepared[:5]
    cot_own = prepared[5:]
    gathered = small_mine, small_core, small_far

    def all_small(small_mine, small_core, small_far):
        rows = place([jnp.concatenate([small_mine, small_core], axis=0)] + small_far, pair)
        rows = rows.reshape(pairs, 2, 16, share)
        rows = jnp.where(core == 0, rows, rows[:, ::-1])
        return rows.reshape(fsdp, 16, share).transpose(1, 0, 2).reshape(16, width)

    def send_second(qkv_far, prev_one_mine, out_weight, gathered, *stacks):
        return (
            [core_swap(one) for one in qkv_far], to_tp(prev_one_mine), ctx_open(prev_one_mine, 1),
            to_pairs(out_weight.T), all_small(*gathered), bundle(plane, owned, units, stacks[:3], stacks[3:]))

    qkv_far_core, prev_one_other, prev_two_mine, out_far, small_all, weights_mine = phases.run(
        send_second, qkv_far, prev_one_mine, out_weight, gathered, expert_gate, expert_up,
        jnp.swapaxes(expert_down, 1, 2), shared_gate, shared_up, shared_down.T)
    weights = lax.all_gather(weights_mine, "fsdp", axis=0)
    attn_scale = small_all[experts : experts + 1].astype(F32)
    ffn_scale = small_all[experts + 1 : experts + 2].astype(F32)
    router_t = jnp.concatenate([small_all[:experts], jnp.zeros((16 - experts, width), BF16)], axis=0)
    router_full = small_all[:experts].T
    here = [(plane + d) % ctx for d in range(ctx)]
    half = ctx // 2
    place_meta = jnp.stack([lane, pair, core]).astype(jnp.int32)

    def near_projection(prev_one_mine, prev_one_other, prev_two_mine, cot, out_weight, out_far, same, cross, scale):
        sent = (
            to_tp(prev_two_mine), ctx_shift(cot, -1), [core_swap(one) for one in [out_weight.T] + out_far])
        return sent, project_near(
            place_meta, tokens, [prev_one_mine] + prev_one_other, same, cross, scale, cosine, sine)

    (prev_two_other, cot_one, out_cross), first = phases.run(
        near_projection, prev_one_mine, prev_one_other, prev_two_mine, cot_own[0], out_weight, out_far,
        [qkv_mine] + qkv_far, [qkv_core] + qkv_far_core, attn_scale)
    query, qkv_full, prev_one = first[3:]

    def attention(prev_two_mine, prev_two_other, cot, cot_one, out_weight, out_far, out_cross):
        sent = ctx_shift(cot, -2), to_tp(cot_one)
        hid, keys, values, prev_two = project_far(
            place_meta, [prev_two_mine] + prev_two_other, qkv_full, attn_scale, cosine, sine, first[:3])
        attended, lse = attend(query, keys, values, kseg, qseg)
        same = place([out_weight.T] + out_far, pair)
        cross = place(out_cross, pair)
        out_full = place_rows([same, cross], core).reshape(width, cols)
        partial = dot_nt(attended, out_full).astype(BF16).reshape(tp, tok, width)
        return sent, hid, keys, values, prev_two, attended, lse, out_full, partial

    (cot_two, cot_one_other), hid, keys, values, prev_two, attended, lse, out_full, partial = phases.run(
        attention, prev_two_mine, prev_two_other, cot_own[0], cot_one, out_weight, out_far, out_cross)

    def sent_tp(total):
        return [tp_shift(pick(total, (lane + j) % tp), j) for j in range(1, tp)]

    def sum_tp(total, got):
        result = pick(total, lane).astype(F32)
        for one in got:
            result = result + one.astype(F32)
        return result

    def after_attention(partial, cot, gate, up, down):
        return (
            sent_tp(partial), ctx_shift(cot, -3),
            bundle(other_plane, owned, units, [gate, up, down], []))

    partial_other, cot_three, again_mine = phases.run(
        after_attention, partial, cot_own[0], expert_gate, expert_up, jnp.swapaxes(expert_down, 1, 2))
    inputs_mine = tokens_mine.astype(F32)

    def normalize(partial, got):
        mixed = inputs_mine + sum_tp(partial, got)
        scale_ffn = lax.rsqrt(jnp.mean(mixed * mixed, axis=-1, keepdims=True) + EPS)
        return (mixed * scale_ffn * ffn_scale).astype(BF16), mixed, scale_ffn

    normed_low, mixed, scale_ffn = phases.run(normalize, partial, partial_other)

    mine, other = [normed_low], []
    for d in range(1, ctx):
        got, moved = phases.run(lambda one: (to_tp(one), ctx_shift(one, -1)), mine[-1])
        other.append(got)
        mine.append(moved)

    near, far = list(range(half)), list(range(half, ctx))
    cot_mine = [cot_own[0], cot_one, cot_two, cot_three]

    def meta_of(blocks):
        return jnp.stack([owned * plane] + [here[d] for d in blocks] + [lane]).astype(jnp.int32)

    def pieces_of(mine, other):
        return [[one] + list(two) for one, two in zip(mine, other)]

    def near_blocks(last, cot_late, weights, x_mine, x_other, cot_mine, cot_other, again_mine):
        later = to_tp(last), [to_tp(one) for one in cot_late]
        got = expert_blocks(
            0, ctx, capacity, experts, units, meta_of(near), pieces_of(x_mine, x_other),
            pieces_of(cot_mine, cot_other), weights, router_t, [])
        return later, got, again_mine

    later, got, again_mine = phases.run(
        near_blocks, mine[-1], cot_mine[half:], weights, mine[:half], other[:half], cot_mine[:half],
        [cot_own[1:], cot_one_other], again_mine)
    other_weights = lax.all_gather(again_mine, "fsdp", axis=0)
    other.append(later[0])
    near_dx = [got[0][i] for i in range(half)]

    def far_blocks(dx, x_mine, x_other, cot_mine, cot_other, saved):
        sent = [sent_tp(one) for one in dx]
        got = expert_blocks(
            half, ctx, capacity, experts, units, meta_of(far), pieces_of(x_mine, x_other),
            pieces_of(cot_mine, cot_other), weights, router_t, saved)
        return sent, got

    near_sent, got = phases.run(
        far_blocks, near_dx, mine[half:], other[half:], cot_mine[half:], later[1], got[1:])
    far_dx = [got[0][i] for i in range(half)]
    sx, sr, sh, sa, sb, ssx, ssc, ssh, ssa, ssb, out_parts = got[1:]

    def for_pairs(kept, got):
        return [pair_sum((pair + j) % pairs, kept, got, []) for j in range(1, pairs)]

    def sent_pairs(rows):
        return [pair_shift(one, j + 1) for j, one in enumerate(rows)]

    def add_pairs(kept, got, far):
        return pair_sum(pair, kept, got, far)

    def weight_step(left, right):
        return weight_grads(core_index, left, right, pairs)

    def again(ssx):
        meta = jnp.stack([owned * other_plane, plane]).astype(jnp.int32)
        return expert_again(0, ctx, capacity, tp, experts, meta, ssx, ssc, other_weights, router_t, [])

    def back_through_norm(dx_sum):
        grad_normed = dx_sum[:tok]
        grad_gates = dx_sum[tok : tok + experts, :tok].T
        named = lax.dynamic_slice_in_dim(hits, lane * tok, tok, 1).T > 0.0
        logits = jnp.where(named, dot(normed_low, router_full), -1e30)
        expo = jnp.where(named, jnp.exp(logits - jnp.max(logits, axis=-1, keepdims=True)), 0.0)
        gates = expo / jnp.sum(expo, axis=-1, keepdims=True)
        grad_logits = (
            gates * (grad_gates - jnp.sum(gates * grad_gates, axis=-1, keepdims=True))
        ).astype(BF16)
        grad_normed = grad_normed + dot_nt(grad_logits, router_full)
        grad_mixed_norm, grad_ffn_gain = norm_back(grad_normed, mixed, scale_ffn, ffn_scale)
        grad_out = lax.dynamic_slice_in_dim(cotangent, lane * tok, tok, 0).astype(F32)
        grad_mixed = grad_out + grad_mixed_norm
        return grad_mixed.astype(BF16), grad_mixed, grad_ffn_gain, dot_tn(grad_logits, normed_low)

    def out_sent(out_parts, d):
        return [
            tp_shift(lax.dynamic_index_in_dim(out_parts[d], (lane + j) % tp, 0, keepdims=False), j)
            for j in range(1, tp)
        ]

    def phase_one(near_dx, near_sent, far_dx, sr, ssx):
        sent = sent_tp(far_dx[0])
        sums = [sum_tp(one, got) for one, got in zip(near_dx, near_sent)]
        home = [sums[0]] + [ctx_shift(one.astype(BF16), d) for d, one in zip(near[1:], sums[1:])]
        return sent, home, weight_step(sr, sh), shared_grads(core_index, ssx, ssc, ssa, ssb, ssh, pairs)

    first_sent, home, down, shared = phases.run(phase_one, near_dx, near_sent, far_dx, sr, ssx)

    def phase_one_more(far_dx, first_sent, down_sent, shared_sent, sx, out_parts):
        sent = core_swap(down_sent), core_swap(shared_sent), sent_tp(far_dx[1]), out_sent(out_parts, 0)
        more = ctx_shift(sum_tp(far_dx[0], first_sent).astype(BF16), far[0])
        return sent, more, weight_step(sx, sa), weight_step(sx, sb)

    (down_got, shared_got, second_sent, out_zero), more, gate, up = phases.run(
        phase_one_more, far_dx, first_sent, down[0], shared[0], sx, out_parts)
    home.append(more)

    def phase_two(far_dx, second_sent, down, shared, gate_sent, ssx, out_parts):
        sent = (
            sent_pairs(for_pairs(*down)), sent_pairs(for_pairs(*shared)), core_swap(gate_sent),
            [tp_shift(
                lax.dynamic_index_in_dim(out_parts, (lane + j) % tp, 1, keepdims=False)[1:], j)
             for j in range(1, tp)])
        more = ctx_shift(sum_tp(far_dx[1], second_sent).astype(BF16), far[1])
        return sent, more, again(ssx)

    (down_far, shared_far, gate_got, out_rest), more, other_saved = phases.run(
        phase_two, far_dx, second_sent, (down[1], down_got), (shared[1], shared_got), gate[0], ssx, out_parts)
    home.append(more)
    out_far = out_zero, out_rest
    ox, orr, oh, oa, ob = other_saved

    def out_sums(out_parts, out_far):
        total = lax.dynamic_index_in_dim(out_parts, lane, 1, keepdims=False).astype(F32)
        for one, rest in zip(*out_far):
            total = total + jnp.concatenate([one[None], rest], axis=0).astype(F32)
        return total.astype(BF16)

    out_total = phases.run(out_sums, out_parts, out_far)
    out_sum = lax.psum_scatter(out_total, "ctx", scatter_dimension=0, tiled=False)

    def phase_three(gate, up_sent, down, shared, home, orr, ox):
        sent = sent_pairs(for_pairs(*gate)), core_swap(up_sent)
        back = back_through_norm(sum(one.astype(F32) for one in home))
        return sent, back, add_pairs(*down), add_pairs(*shared), weight_step(orr, oh), weight_step(ox, oa)

    (gate_far, up_got), back, own_down, own_shared, other_down, other_gate = phases.run(
        phase_three, (gate[1], gate_got), up[0], (down[1], down_got, down_far), (shared[1], shared_got, shared_far),
        home, orr, ox)
    grad_mixed_low, grad_mixed, grad_ffn_gain, grad_router = back
    all_shared = lax.all_gather(own_shared, "ctx", axis=0)

    def phase_four(up, grad_mixed_low, own_down, down_sent, gate, ox, out_sum):
        sent = sent_pairs(for_pairs(*up)), to_tp(grad_mixed_low), ctx_swap(own_down), core_swap(down_sent)
        return sent, weight_step(ox, ob), add_pairs(*gate), out_sum

    (up_far, grad_mixed_other, far_down, down_got), other_up, own_gate, out_sum = phases.run(
        phase_four, (up[1], up_got), grad_mixed_low, own_down, other_down[0], (gate[1], gate_got, gate_far), ox,
        out_sum)

    def phase_five(down, gate_sent, up_sent, own_gate, up, grad_mixed_low, grad_mixed_other):
        sent = sent_pairs(for_pairs(*down)), core_swap(gate_sent), core_swap(up_sent), ctx_swap(own_gate)
        rows = joined(grad_mixed_low, *grad_mixed_other)
        grad_attended = dot(rows, out_full).astype(BF16)
        grads = attend_back(query, keys, values, grad_attended, lse, kseg, qseg, cosine, sine)
        return sent, rows, grads, add_pairs(*up)

    (down_far, gate_got, up_got, far_gate), grad_mixed_rows, (dq, dk, dv), own_up = phases.run(
        phase_five, (other_down[1], down_got), other_gate[0], other_up[0], own_gate,
        (up[1], up_got, up_far), grad_mixed_low, grad_mixed_other)

    def phase_six(gate, own_up, dq, dk, dv, hid, down, all_shared):
        sent = sent_pairs(for_pairs(*gate)), ctx_swap(own_up)
        back, gain_row = hidden_back([prev_two, prev_one, tokens], dk, dv, dq, qkv_full)
        attn = attn_grads_of(core_index, hid, dk, dv, dq, grad_mixed_rows, attended, pairs)
        return sent, back, gain_row, attn, add_pairs(*down), all_shared

    (gate_far, far_up), back, gain_row, attn, own_other_down, all_shared = phases.run(
        phase_six, (other_gate[1], gate_got), own_up, dq, dk, dv, hid, (other_down[1], down_got, down_far),
        all_shared)
    small_rows = jnp.concatenate(
        [grad_router, grad_ffn_gain[None], gain_row, jnp.zeros((16 - experts - 2, width), F32)], axis=0)
    hidden_parts = [back[j].reshape(tp, tok, width) for j in range(3)]

    def phase_seven(up, attn_sent, own_other_down, hidden_parts, small_rows, gate):
        sent = (
            sent_pairs(for_pairs(*up)), core_swap(attn_sent), ctx_swap(own_other_down), sent_tp(hidden_parts[0]),
            all_sum(small_rows, "tp"))
        return sent, add_pairs(*gate)

    (up_far, attn_got, far_other_down, far_two, small_rows), own_other_gate = phases.run(
        phase_seven, (other_up[1], up_got), attn[0], own_other_down, hidden_parts, small_rows,
        (other_gate[1], gate_got, gate_far))

    def shared_out(all_shared):
        result = all_shared.astype(F32)
        return result.reshape(ctx, share, 3, units).transpose(2, 1, 0, 3).reshape(3, share, ctx * units)

    def phase_eight(attn, own_other_gate, hidden_parts, far_two, small_rows, up, all_shared):
        carried = ctx_open(sum_tp(hidden_parts[0], far_two).astype(BF16), -1)
        sent = (
            carried, sent_pairs(for_pairs(*attn)), ctx_swap(own_other_gate), core_swap(small_rows),
            sent_tp(hidden_parts[1]))
        return sent, add_pairs(*up), shared_out(all_shared)

    (carried, attn_far, far_other_gate, small_got, far_one), own_other_up, result = phases.run(
        phase_eight, (attn[1], attn_got), own_other_gate, hidden_parts, far_two, small_rows,
        (other_up[1], up_got, up_far), all_shared)
    places = jnp.stack([plane, plane ^ 1, plane ^ 2, plane ^ 3]).astype(jnp.int32)

    def phase_nine(hidden_parts, far_one, carried, own_other_up, attn, small_rows, small_got, out_sum, own_down):
        carried = ctx_open(
            (sum_tp(hidden_parts[1], far_one) + carried.astype(F32)).astype(BF16), -1)
        output_mine = (mixed + out_sum.astype(F32)).astype(BF16)
        sent = carried, sent_tp(hidden_parts[2]), ctx_swap(own_other_up), to_tp(output_mine)
        small_rows = small_rows + small_got
        reach = 1
        while reach < pairs:
            small_rows = small_rows + pair_swap(small_rows, reach)
            reach *= 2
        return sent, small_rows, add_pairs(*attn), output_mine, collect(
            places, [own_down, far_down, own_other_down, far_other_down])

    (carried, hidden_other, far_other_up, output_other), small_rows, attn_rows, output_mine, grad_expert_down = phases.run(
        phase_nine, hidden_parts, far_one, carried, own_other_up, (attn[1], attn_got, attn_far), small_rows,
        small_got, out_sum, own_down)

    def input_back(total, got, carried):
        grad_hidden = sum_tp(total, got) + carried.astype(F32)
        scale_attn = lax.rsqrt(jnp.mean(inputs_mine * inputs_mine, axis=-1, keepdims=True) + EPS)
        scaled = grad_hidden * attn_scale
        grad_norm = scale_attn * scaled - inputs_mine * scale_attn * scale_attn * scale_attn * jnp.mean(
            scaled * inputs_mine, axis=-1, keepdims=True)
        return (grad_mixed + grad_norm).astype(BF16)

    def phase_ten(attn_rows, hidden_parts, hidden_other, carried, small_rows, own_gate, output_mine, output_other):
        input_mine = input_back(hidden_parts[2], hidden_other, carried)
        small = lax.dynamic_slice_in_dim(small_rows, me * share, share, 1).astype(BF16)
        small = jnp.pad(small, ((0, 16), (0, 4 * cols - share)))
        pieces = jnp.concatenate([attn_rows, small], axis=0).reshape(ctx, (share + 32) // ctx, 4 * cols)
        return (
            to_tp(input_mine), [ctx_shift(pick(pieces, (plane + d) % ctx), d) for d in range(1, ctx)],
            pick(pieces, plane), input_mine, joined(output_mine, *output_other),
            collect(places, [own_gate, far_gate, own_other_gate, far_other_gate]))

    input_other, attn_got, attn_piece, input_mine, output, grad_expert_gate = phases.run(
        phase_ten, attn_rows, hidden_parts, hidden_other, carried, small_rows, own_gate, output_mine, output_other)

    def phase_eleven(attn_piece, attn_got, own_up, input_mine, input_other):
        total = attn_piece.astype(F32)
        for one in attn_got:
            total = total + one.astype(F32)
        total = total.astype(BF16)
        return (
            total, [ctx_shift(total, d) for d in range(1, ctx)],
            collect(places, [own_up, far_up, own_other_up, far_other_up]), joined(input_mine, *input_other))

    attn_piece, attn_got, grad_expert_up, input_grad = phases.run(
        phase_eleven, attn_piece, attn_got, own_up, input_mine, input_other)
    grad_key_weight, grad_value_weight, grad_query_weight, grad_out_rows, small_out = finish(
        plane.astype(jnp.int32)[None], [attn_piece] + attn_got, share, cols)
    grad_out_rows = grad_out_rows.T
    grad_expert_down = jnp.swapaxes(grad_expert_down, 1, 2)
    small_out = small_out[:, :share]
    grad_shared_gate, grad_shared_up, grad_shared_down = result[0], result[1], result[2].T
    return (
        output[None],
        input_grad[None],
        grad_query_weight,
        grad_key_weight,
        grad_value_weight,
        grad_out_rows,
        small_out[experts + 1],
        small_out[experts],
        small_out[:experts].T,
        grad_shared_gate,
        grad_shared_up,
        grad_shared_down,
        grad_expert_gate,
        grad_expert_up,
        grad_expert_down,
    )


def solution(mesh):
    in_specs = (
        P("fsdp", "ctx", None),
        P("fsdp", None),
        P("fsdp", "ctx", None),
        P("fsdp", "tp"),
        P("fsdp", "tp"),
        P("fsdp", "tp"),
        P("tp", "fsdp"),
        P("fsdp"),
        P("fsdp"),
        P("fsdp", None),
        P("fsdp", "tp"),
        P("fsdp", "tp"),
        P("tp", "fsdp"),
        P(None, "fsdp", "tp"),
        P(None, "fsdp", "tp"),
        P(None, "tp", "fsdp"),
        P("fsdp", "ctx", None),
    )
    out_specs = (
        P("fsdp", "ctx", None),
        P("fsdp", "ctx", None),
        P("fsdp", "tp"),
        P("fsdp", "tp"),
        P("fsdp", "tp"),
        P("tp", "fsdp"),
        P("fsdp"),
        P("fsdp"),
        P("fsdp", None),
        P("fsdp", "tp"),
        P("fsdp", "tp"),
        P("tp", "fsdp"),
        P(None, "fsdp", "tp"),
        P(None, "fsdp", "tp"),
        P(None, "tp", "fsdp"),
    )
    return jax.shard_map(local, mesh=mesh, in_specs=in_specs, out_specs=out_specs, check_vma=False)
```

```python
import functools

import jax
import jax.numpy as jnp
from jax import lax
from jax.experimental import pallas as pl
from jax.experimental.pallas import tpu as pltpu
from jax.sharding import PartitionSpec as P

HD = 64
WINDOW = 1024
EPS = 1e-06
F32 = jnp.float32
BF16 = jnp.bfloat16
VMEM_BYTES = 56 * 1024 * 1024
COST_SCALE = 0.3


def dot(left, right):
    return lax.dot_general(left, right, (((1,), (0,)), ((), ())), preferred_element_type=F32)


def dot_nt(left, right):
    return lax.dot_general(left, right, (((1,), (1,)), ((), ())), preferred_element_type=F32)


def dot_tn(left, right):
    return lax.dot_general(left, right, (((0,), (0,)), ((), ())), preferred_element_type=F32)


def core_swap(block):
    size = lax.axis_size("fsdp")
    return lax.ppermute(block, "fsdp", [(i, i ^ 1) for i in range(size)])


def pair_shift(block, distance):
    size = lax.axis_size("fsdp")
    pairs = size // 2
    route = [(i, ((i // 2 + distance) % pairs) * 2 + i % 2) for i in range(size)]
    return lax.ppermute(block, "fsdp", route)


def pair_swap(block, reach):
    size = lax.axis_size("fsdp")
    return lax.ppermute(block, "fsdp", [(i, i ^ (2 * reach)) for i in range(size)])


def tp_shift(block, distance):
    size = lax.axis_size("tp")
    return lax.ppermute(block, "tp", [(i, (i + distance) % size) for i in range(size)])


def ctx_shift(block, distance):
    size = lax.axis_size("ctx")
    return lax.ppermute(block, "ctx", [(i, (i + distance) % size) for i in range(size)])


def ctx_swap(block, reach=1):
    size = lax.axis_size("ctx")
    return lax.ppermute(block, "ctx", [(i, i ^ reach) for i in range(size)])


def ctx_open(block, distance):
    size = lax.axis_size("ctx")
    route = [(i, i + distance) for i in range(size) if 0 <= i + distance < size]
    return lax.ppermute(block, "ctx", route)


def pick(stack, index):
    return lax.dynamic_index_in_dim(stack, index, 0, keepdims=False)


def place_rows(pieces, me):
    first, second = pieces
    return jnp.where(
        me == 0, jnp.stack([first, second], axis=1), jnp.stack([second, first], axis=1))


def place(pieces, me):
    count = len(pieces)
    if count == 1:
        return pieces[0][None]
    if count == 2:
        first, second = pieces
        return jnp.where(me == 0, jnp.stack([first, second]), jnp.stack([second, first]))
    result = jnp.zeros((count,) + pieces[0].shape, pieces[0].dtype)
    for d, piece in enumerate(pieces):
        result = lax.dynamic_update_index_in_dim(result, piece, (me - d) % count, 0)
    return result


def tie(values, *others):
    return lax.optimization_barrier((values, others))[0]


class Phases:
    def __init__(self):
        self.last = []

    def run(self, function, *values):
        given = function(*(tie(values, self.last) if self.last else values))
        self.last = jax.tree.leaves(given)
        return given


def all_sum(block, axis):
    size = lax.axis_size(axis)
    reach = 1
    while reach < size:
        other = lax.ppermute(block, axis, [(i, i ^ reach) for i in range(size)])
        block = block + other
        reach *= 2
    return block


def whole(shape):
    return pl.BlockSpec(shape, lambda *_: (0,) * len(shape))


def params():
    return pltpu.CompilerParams(vmem_limit_bytes=VMEM_BYTES)


def cost(microseconds):
    return pl.CostEstimate(flops=0, bytes_accessed=int(microseconds * COST_SCALE * 3.4e6), transcendentals=0)


def swap_halves(values):
    width = values.shape[-1]
    lane = lax.broadcasted_iota(jnp.int32, values.shape, 1)
    up = pltpu.roll(values, width - HD // 2, 1)
    down = pltpu.roll(values, HD // 2, 1)
    return jnp.where(lane % HD < HD // 2, up, down)


def widen(table, width):
    copies = -(-width // table.shape[1])
    return jnp.concatenate([table] * copies, axis=1)[:, :width]


def rotated(values, cosine, sine):
    return (values * cosine + swap_halves(values) * sine).astype(BF16)


def project_rows(inputs, gain, weights, cos_ref, sin_ref, hid_ref, k_ref, v_ref):
    scale = lax.rsqrt(jnp.mean(inputs * inputs, axis=-1, keepdims=True) + EPS)
    hidden = (inputs * scale * gain).astype(BF16)
    hid_ref[...] = hidden
    width = k_ref.shape[1]
    k_ref[...] = rotated(
        dot(hidden, weights[:, :width]), widen(cos_ref[...], width), widen(sin_ref[...], width))
    v_ref[...] = dot(hidden, weights[:, width : 2 * width]).astype(BF16)
    return hidden


def project_near_kernel(parts, pairs, meta_ref, tok_ref, *refs):
    prev_refs, refs = refs[:parts], refs[parts:]
    same_refs, cross_refs, refs = refs[:pairs], refs[pairs : 2 * pairs], refs[2 * pairs :]
    gain_ref, cos_ref, sin_ref, hid_ref, k_ref, v_ref, q_ref, w_ref, prev_ref, w_all, x_all = refs
    tok, features = x_all.shape[1:]
    share, columns = w_all.shape[1:]

    @pl.when(pl.program_id(0) == 0)
    def _():
        for d in range(pairs):
            row = 2 * lax.rem(meta_ref[1] + pairs - d, pairs)
            w_all[row + meta_ref[2]] = same_refs[d][...]
            w_all[row + 1 - meta_ref[2]] = cross_refs[d][...]
        for j in range(parts):
            x_all[lax.rem(meta_ref[0] + parts - j, parts)] = prev_refs[j][...]
        weights = w_all[...].reshape(2 * pairs * share, columns)
        w_ref[...] = weights
        inputs = x_all[...].reshape(parts * tok, features)
        prev_ref[...] = inputs
        project_rows(inputs.astype(F32), gain_ref[...], weights, cos_ref, sin_ref, hid_ref, k_ref, v_ref)

    @pl.when(pl.program_id(0) == 1)
    def _():
        weights = w_all[...].reshape(2 * pairs * share, columns)
        hidden = project_rows(
            tok_ref[...].astype(F32), gain_ref[...], weights, cos_ref, sin_ref, hid_ref, k_ref, v_ref)
        width = k_ref.shape[1]
        query = dot(hidden, weights[:, 2 * width :])
        q_ref[...] = rotated(
            query, widen(cos_ref[...], width), widen(sin_ref[...], width)) * jnp.asarray(HD**-0.5, BF16)


def project_near(meta, tokens, prev_pieces, same, cross, gain, cosine, sine):
    rows, features = tokens.shape
    share, columns = same[0].shape
    width = columns // 3
    tok = prev_pieces[0].shape[0]
    count = 2 * len(same) * share
    shapes = [(3 * rows, features), (3 * rows, width), (3 * rows, width)]
    block = lambda i, meta: (i + 1, 0)
    others = [(rows, width), (count, columns), (rows, features)]
    operands = [tokens, *prev_pieces, *same, *cross, gain]
    table = pl.BlockSpec((rows, cosine.shape[1]), block)
    return pl.pallas_call(
        functools.partial(project_near_kernel, len(prev_pieces), len(same)),
        grid_spec=pltpu.PrefetchScalarGridSpec(
            num_scalar_prefetch=1,
            grid=(2,),
            in_specs=[whole(o.shape) for o in operands] + [table, table],
            out_specs=[pl.BlockSpec((rows, shape[1]), block) for shape in shapes]
            + [whole(shape) for shape in others],
            scratch_shapes=[
                pltpu.VMEM((2 * len(same), share, columns), BF16),
                pltpu.VMEM((len(prev_pieces), tok, features), BF16),
            ],
        ),
        out_shape=[jax.ShapeDtypeStruct(shape, BF16) for shape in shapes + others],
        compiler_params=params(),
        cost_estimate=cost(7),
    )(meta, *operands, cosine, sine)


def project_far_kernel(parts, meta_ref, *refs):
    prev_refs, refs = refs[:parts], refs[parts:]
    w_ref, gain_ref, cos_ref, sin_ref, _, _, _, hid_ref, k_ref, v_ref, prev_ref, x_all = refs
    tok, features = x_all.shape[1:]
    for j in range(parts):
        x_all[lax.rem(meta_ref[0] + parts - j, parts)] = prev_refs[j][...]
    inputs = x_all[...].reshape(parts * tok, features)
    prev_ref[...] = inputs
    project_rows(inputs.astype(F32), gain_ref[...], w_ref[...], cos_ref, sin_ref, hid_ref, k_ref, v_ref)


def project_far(meta, prev_pieces, weights, gain, cosine, sine, saved):
    tok, features = prev_pieces[0].shape
    rows = tok * len(prev_pieces)
    width = weights.shape[1] // 3
    first = lambda i, meta: (0, 0)
    operands = [*prev_pieces, weights, gain]
    table = pl.BlockSpec((rows, cosine.shape[1]), first)
    return pl.pallas_call(
        functools.partial(project_far_kernel, len(prev_pieces)),
        grid_spec=pltpu.PrefetchScalarGridSpec(
            num_scalar_prefetch=1,
            grid=(1,),
            in_specs=[whole(o.shape) for o in operands] + [table, table]
            + [pl.BlockSpec(memory_space=pl.ANY)] * 3,
            out_specs=[pl.BlockSpec((rows, one.shape[1]), first) for one in saved]
            + [whole((rows, features))],
            scratch_shapes=[pltpu.VMEM((len(prev_pieces), tok, features), BF16)],
        ),
        out_shape=[jax.ShapeDtypeStruct(one.shape, BF16) for one in saved]
        + [jax.ShapeDtypeStruct((rows, features), BF16)],
        input_output_aliases={1 + len(operands) + 2 + i: i for i in range(3)},
        compiler_params=params(),
        cost_estimate=cost(4),
    )(meta, *operands, cosine, sine, *saved)


def prepare_kernel(parts, meta_ref, routes_ref, cot_ref, rates_ref, seg_ref, *refs):
    cos_ref, sin_ref, kseg_ref, qseg_ref, hits_ref = refs[:5]
    mine_ref, other_refs, seg_all = refs[5], refs[6:-1], refs[-1]
    block, width = cot_ref.shape
    tok = block // parts
    experts = hits_ref.shape[0]
    rows, lanes = cos_ref.shape
    short = 64
    origin = (meta_ref[1] - 2) * block
    far = (lax.broadcasted_iota(jnp.int32, (rows // short, lanes), 0) * short + origin).astype(F32) * rates_ref[...]
    near = lax.broadcasted_iota(jnp.int32, (short, lanes), 0).astype(F32) * rates_ref[...]
    far_cos, far_sin, near_cos, near_sin = jnp.cos(far), jnp.sin(far), jnp.cos(near), jnp.sin(near)
    sign = jnp.where(lax.broadcasted_iota(jnp.int32, (short, lanes), 1) % HD < HD // 2, -1.0, 1.0)
    signed_sin, signed_cos = sign * near_sin, sign * near_cos
    for h in range(rows // short):
        part = slice(h * short, (h + 1) * short)
        one_cos, one_sin = far_cos[h : h + 1], far_sin[h : h + 1]
        cos_ref[part] = one_cos * near_cos - one_sin * near_sin
        sin_ref[part] = one_sin * signed_cos + one_cos * signed_sin
    seg_all[:, : 2 * block] = jnp.full((1, 2 * block), -1, jnp.int32)
    seg_all[:, 2 * block :] = seg_ref[...]
    kseg = seg_all[:, pl.ds(pl.multiple_of(meta_ref[1] * block, block), rows)]
    qseg_ref[...] = kseg[:, rows - block :]
    kseg_ref[...] = jnp.broadcast_to(kseg, (8, rows)).T[:, :1]
    row = lax.broadcasted_iota(jnp.int32, (experts, block), 0)
    named = row == routes_ref[0:1, :]
    for j in range(1, routes_ref.shape[0]):
        named = named | (row == routes_ref[j : j + 1, :])
    hits = jnp.where(named, 1.0, 0.0).astype(F32)
    before = lax.broadcasted_iota(jnp.int32, (block, block), 0) < lax.broadcasted_iota(jnp.int32, (block, block), 1)
    rank = dot(hits.astype(BF16), jnp.where(before, 1.0, 0.0).astype(BF16))
    hits_ref[...] = hits
    table = jnp.concatenate([jnp.where(named, rank, -1.0), jnp.zeros((16 - experts, block), F32)], axis=0)
    mine_ref[tok:, :] = jnp.concatenate([table, jnp.zeros((16, width - block), F32)], axis=1).astype(BF16)
    for j, ref in enumerate((mine_ref,) + other_refs):
        start = lax.rem(meta_ref[0] + parts - j, parts) * tok
        ref[:tok, :] = cot_ref[pl.ds(pl.multiple_of(start, tok), tok), :]


def prepare(meta, parts, experts, routes_t, cotangent, segments):
    block, width = cotangent.shape
    tok = block // parts
    index = jnp.arange(2 * HD, dtype=jnp.int32)
    rates = (10000.0 ** (-2.0 * (index % (HD // 2)).astype(F32) / HD))[None, :]
    shapes = [
        ((3 * block, 2 * HD), F32), ((3 * block, 2 * HD), F32), ((3 * block, 1), jnp.int32), ((1, block), jnp.int32),
        ((experts, block), F32), ((tok + 16, width), BF16),
    ] + [((tok, width), BF16)] * (parts - 1)
    operands = (routes_t, cotangent, rates, segments)
    return pl.pallas_call(
        functools.partial(prepare_kernel, parts),
        grid_spec=pltpu.PrefetchScalarGridSpec(
            num_scalar_prefetch=1,
            grid=(1,),
            in_specs=[whole(o.shape) for o in operands],
            out_specs=[whole(shape) for shape, _ in shapes],
            scratch_shapes=[pltpu.VMEM((1, segments.shape[1] + 2 * block), jnp.int32)],
        ),
        out_shape=[jax.ShapeDtypeStruct(shape, kind) for shape, kind in shapes],
        compiler_params=params(),
        cost_estimate=cost(3),
    )(meta, *operands)


def bundle_kernel(index_ref, *refs):
    stacks, shared, out_ref = refs[:3], refs[3:-1], refs[-1]
    owned = stacks[0].shape[0]
    for i, ref in enumerate(stacks):
        out_ref[i * owned : (i + 1) * owned] = ref[...]
    if shared:
        units = shared[0].shape[1]
        gate_ref, up_ref, down_ref = shared
        out_ref[3 * owned, :, :units] = gate_ref[...]
        out_ref[3 * owned, :, units:] = up_ref[...]
        out_ref[3 * owned + 1, :, :units] = down_ref[...]
        out_ref[3 * owned + 1, :, units:] = jnp.zeros_like(down_ref)


def bundle(plane, owned, units, stacks, shared):
    _, share, hidden = stacks[0].shape
    count = 3 * owned + 2 * bool(shared)
    return pl.pallas_call(
        bundle_kernel,
        grid_spec=pltpu.PrefetchScalarGridSpec(
            num_scalar_prefetch=1,
            grid=(1,),
            in_specs=[pl.BlockSpec((owned, share, hidden), lambda i, index: (index[0], 0, 0))] * 3
            + [pl.BlockSpec((share, units), lambda i, index: (0, index[1]))] * len(shared),
            out_specs=whole((count, share, hidden)),
        ),
        out_shape=jax.ShapeDtypeStruct((count, share, hidden), BF16),
        compiler_params=params(),
        cost_estimate=cost(3),
    )(jnp.stack([plane, plane % 2]).astype(jnp.int32), *stacks, *shared)


def finish_kernel(meta_ref, mine_ref, *refs):
    count = len(refs) - 6
    pieces = (mine_ref,) + refs[:count]
    k_ref, v_ref, q_ref, o_ref, small_ref, all_ref = refs[count:]
    total = len(pieces)
    rows = mine_ref.shape[0]
    for d, ref in enumerate(pieces):
        all_ref[lax.rem(meta_ref[0] + total - d, total)] = ref[...].astype(F32)
    whole_rows = all_ref[...].reshape(total * rows, mine_ref.shape[1])
    share, cols = k_ref.shape
    for i, ref in enumerate((k_ref, v_ref, q_ref, o_ref)):
        ref[...] = whole_rows[:share, i * cols : (i + 1) * cols]
    small_ref[...] = whole_rows[share : share + 16, : small_ref.shape[1]]


def finish(meta, pieces, share, cols):
    rows, columns = pieces[0].shape
    shapes = [(share, cols)] * 4 + [(16, columns)]
    return pl.pallas_call(
        finish_kernel,
        grid_spec=pltpu.PrefetchScalarGridSpec(
            num_scalar_prefetch=1,
            grid=(1,),
            in_specs=[whole(piece.shape) for piece in pieces],
            out_specs=[whole(shape) for shape in shapes],
            scratch_shapes=[pltpu.VMEM((len(pieces), rows, columns), F32)],
        ),
        out_shape=[jax.ShapeDtypeStruct(shape, F32) for shape in shapes],
        compiler_params=params(),
        cost_estimate=cost(2),
    )(meta, *pieces)


def pack_kernel(lane_ref, k_ref, v_ref, q_ref, router_ref, gains_ref, tok_ref, qkv_ref, small_ref, mine_ref):
    width = k_ref.shape[1]
    for i, ref in enumerate((k_ref, v_ref, q_ref)):
        qkv_ref[:, i * width : (i + 1) * width] = ref[...]
    experts, share = router_ref.shape
    small_ref[...] = jnp.concatenate(
        [router_ref[...].astype(F32), gains_ref[...].astype(F32),
         jnp.zeros((small_ref.shape[0] - experts - 2, share), F32)], axis=0).astype(BF16)
    mine_ref[...] = tok_ref[...]


def pack(lane, parts, key_weight, value_weight, query_weight, router_t, gains, tokens):
    rows, width = tokens.shape
    share, cols = key_weight.shape
    part = (rows // parts, width)
    shapes = [(share, 3 * cols), (16, share), part]
    operands = (key_weight, value_weight, query_weight, router_t, gains)
    return pl.pallas_call(
        pack_kernel,
        grid_spec=pltpu.PrefetchScalarGridSpec(
            num_scalar_prefetch=1,
            grid=(1,),
            in_specs=[whole(o.shape) for o in operands]
            + [pl.BlockSpec(part, lambda i, lane: (lane[0], 0))],
            out_specs=[whole(shape) for shape in shapes],
        ),
        out_shape=[jax.ShapeDtypeStruct(shape, BF16) for shape in shapes],
        compiler_params=params(),
        cost_estimate=cost(2),
    )(lane.astype(jnp.int32)[None], *operands, tokens)


def mask_bias(kseg, qseg, keys, queries):
    key = lax.broadcasted_iota(jnp.int32, (keys, queries), 0)
    query = lax.broadcasted_iota(jnp.int32, (keys, queries), 1)
    allowed = (key > query) & (key <= query + WINDOW) & (kseg == qseg)
    return jnp.where(allowed, 0.0, -1e30).astype(F32)


def head_only(values, head):
    lane = lax.broadcasted_iota(jnp.int32, values.shape, 1)
    return jnp.where(lane // HD == head, values, jnp.zeros_like(values))


def attend_kernel(tile, q_ref, k_ref, v_ref, kseg_ref, qseg_ref, out_ref, lse_ref, bias_ref):
    rows = q_ref.shape[0]
    span = WINDOW + tile
    tiles = rows // tile

    @pl.when(pl.program_id(0) == 0)
    def _():
        for j in range(tiles):
            bias_ref[j] = mask_bias(
                kseg_ref[pl.ds(j * tile, span), :], qseg_ref[:, pl.ds(j * tile, tile)], span, tile
            )

    keys = k_ref[...]
    values_t = v_ref[...].T
    for j in range(tiles):
        start = j * tile
        query = q_ref[pl.ds(start, tile), :]
        parts = []
        for head in range(2):
            scores = dot_nt(keys[start : start + span], head_only(query, head)) + bias_ref[j]
            top = jnp.max(scores, axis=0, keepdims=True)
            expo = jnp.exp(scores - top)
            total = jnp.sum(expo, axis=0, keepdims=True)
            part = dot(
                values_t[head * HD : (head + 1) * HD, start : start + span], expo.astype(BF16)
            )
            parts.append(part / total)
            lse_ref[0, pl.ds(head, 1), pl.ds(start, tile)] = top + jnp.log(total)
        out_ref[pl.ds(start, tile), :] = jnp.concatenate(parts, axis=0).T.astype(BF16)


def attend(query, keys, values, kseg, qseg):
    rows, width = query.shape
    span = keys.shape[0]
    tile = min(256, rows)
    pairs = -(-width // (2 * HD))
    columns = lambda count: pl.BlockSpec((count, 2 * HD), lambda i: (0, i))
    return pl.pallas_call(
        functools.partial(attend_kernel, tile),
        grid=(pairs,),
        in_specs=[columns(rows), columns(span), columns(span), whole((span, 1)), whole((1, rows))],
        out_specs=[columns(rows), pl.BlockSpec((1, 2, rows), lambda i: (i, 0, 0))],
        out_shape=[
            jax.ShapeDtypeStruct((rows, width), BF16),
            jax.ShapeDtypeStruct((pairs, 2, rows), F32),
        ],
        scratch_shapes=[pltpu.VMEM((rows // tile, WINDOW + tile, tile), F32)],
        compiler_params=params(),
        cost_estimate=cost(13),
    )(query, keys, values, kseg, qseg)


def attend_back_kernel(
    tile, q_ref, k_ref, v_ref, g_ref, lse_ref, kseg_ref, qseg_ref, cos_ref, sin_ref,
    dq_ref, dk_ref, dv_ref, bias_ref, dk_acc, dv_acc,
):
    rows = q_ref.shape[0]
    span = WINDOW + tile
    tiles = rows // tile
    total_keys = k_ref.shape[0]

    @pl.when(pl.program_id(0) == 0)
    def _():
        for j in range(tiles):
            bias_ref[j] = mask_bias(
                kseg_ref[pl.ds(j * tile, span), :], qseg_ref[:, pl.ds(j * tile, tile)], span, tile
            )

    keys = k_ref[...]
    values = v_ref[...]
    keys_t = keys.T
    dk_acc[...] = jnp.zeros_like(dk_acc)
    dv_acc[...] = jnp.zeros_like(dv_acc)
    cosine = cos_ref[...]
    sine = sin_ref[...]
    lead = total_keys - rows
    for j in range(tiles):
        start = j * tile
        query = q_ref[pl.ds(start, tile), :]
        grad = g_ref[pl.ds(start, tile), :]
        parts = []
        for head in range(2):
            query_one = head_only(query, head)
            grad_one = head_only(grad, head)
            scores = dot_nt(keys[start : start + span], query_one) + bias_ref[j]
            probs = jnp.exp(scores - lse_ref[0, pl.ds(head, 1), pl.ds(start, tile)])
            grad_probs = dot_nt(values[start : start + span], grad_one)
            delta = jnp.sum(probs * grad_probs, axis=0, keepdims=True)
            grad_scores = (probs * (grad_probs - delta)).astype(BF16)
            dv_acc[pl.ds(start, span), :] += dot(probs.astype(BF16), grad_one)
            dk_acc[pl.ds(start, span), :] += dot(grad_scores, query_one)
            parts.append(
                dot(keys_t[head * HD : (head + 1) * HD, start : start + span], grad_scores)
            )
        dq = jnp.concatenate(parts, axis=0).T * HD**-0.5
        places = pl.ds(lead + start, tile)
        dq_ref[pl.ds(start, tile), :] = (
            dq * cos_ref[places, :] - swap_halves(dq) * sin_ref[places, :]
        ).astype(BF16)
    dk = dk_acc[...]
    dk_ref[...] = (dk * cosine - swap_halves(dk) * sine).astype(BF16)
    dv_ref[...] = dv_acc[...].astype(BF16)


def attend_back(query, keys, values, grad, lse, kseg, qseg, cosine, sine):
    rows, width = query.shape
    span = keys.shape[0]
    tile = min(256, rows)
    pairs = -(-width // (2 * HD))
    columns = lambda count: pl.BlockSpec((count, 2 * HD), lambda i: (0, i))
    return pl.pallas_call(
        functools.partial(attend_back_kernel, tile),
        grid=(pairs,),
        in_specs=[
            columns(rows), columns(span), columns(span), columns(rows),
            pl.BlockSpec((1, 2, rows), lambda i: (i, 0, 0)),
            whole((span, 1)), whole((1, rows)), whole((span, 2 * HD)), whole((span, 2 * HD)),
        ],
        out_specs=[columns(rows), columns(span), columns(span)],
        out_shape=[
            jax.ShapeDtypeStruct((rows, width), BF16),
            jax.ShapeDtypeStruct((span, width), BF16),
            jax.ShapeDtypeStruct((span, width), BF16),
        ],
        scratch_shapes=[
            pltpu.VMEM((rows // tile, WINDOW + tile, tile), F32),
            pltpu.VMEM((span, 2 * HD), F32),
            pltpu.VMEM((span, 2 * HD), F32),
        ],
        compiler_params=params(),
        cost_estimate=cost(18),
    )(query, keys, values, grad, lse, kseg, qseg, cosine, sine)


def expert_kernel(capacity, parts, experts, full, shared, pieces, added, steps, n_saved, meta_ref, *refs):
    w_all, w_sems = refs[-2:]
    owned = w_all.shape[1] // 3
    order = [kind * owned + j for j in range(owned) for kind in range(3)]
    order += list(range(3 * owned, w_all.shape[1]))
    if pieces:
        count = steps * parts
        x_refs, c_refs, refs = refs[:count], refs[count : 2 * count], refs[2 * count :]
        x_all, c_all, t_all = refs[-5:-2]
        tok, width = x_all.shape[1:]
        block = tok * parts
        for j in range(parts):
            spot = lax.rem(meta_ref[1] + parts - j, parts)
            for i in range(steps):

                @pl.when(pl.program_id(0) == i)
                def _():
                    x_all[spot] = x_refs[i * parts + j][...]
                    c_all[spot] = c_refs[i * parts + j][:tok]
                    if j == 0:
                        t_all[...] = c_refs[i * parts][tok:]

        inputs = x_all[...].reshape(block, width)
        cot = c_all[...].reshape(block, width)
        low_table = t_all[...]
    else:
        x_ref, c_ref = refs[:2]
        refs = refs[2:]
        block, width = x_ref.shape[1:]
        tok = block // parts
        inputs = x_ref[0]
        cot = c_ref[0, :block]
        low_table = c_ref[0, block:]
    w_ref, rt_ref = refs[:2]
    refs = refs[2:]

    def weight_copy(which):
        return pltpu.make_async_copy(w_ref.at[:, which], w_all.at[:, which], w_sems.at[which])

    @pl.when(pl.program_id(0) == 0)
    def _():
        for j in range(w_all.shape[1]):
            weight_copy(order[j]).start()

    if added:
        more_dx_ref, more_out_ref = refs[:2]
        refs = refs[2:]
    refs = refs[n_saved:]
    if full:
        dx_ref, out_ref = refs[:2]
        refs = refs[2:]
    sx_ref, sr_ref, sh_ref, sa_ref, sb_ref = refs[:5]
    refs = refs[: 10 if shared else 5]
    if shared:
        ssx_ref, ssc_ref, ssh_ref, ssa_ref, ssb_ref = refs[5:]
        ssx_ref[0] = inputs
        ssc_ref[0, :block] = cot
        ssc_ref[0, block:] = low_table
    hidden = w_ref.shape[3]
    table = low_table[:, :block].astype(F32)[:experts]

    def weights(which):
        @pl.when(pl.program_id(0) == 0)
        def _():
            weight_copy(which).wait()

        return w_all[:, which].reshape(width, hidden)

    logits = dot_nt(rt_ref[...], inputs)[:experts]
    named = table >= 0.0
    top = jnp.max(jnp.where(named, logits, -1e30), axis=0, keepdims=True)
    expo = jnp.where(named, jnp.exp(logits - top), 0.0)
    gates = expo / jnp.sum(expo, axis=0, keepdims=True)
    row = lax.broadcasted_iota(jnp.int32, (experts, block), 0)
    slot = lax.broadcasted_iota(jnp.int32, (capacity, block), 0).astype(F32)
    hits, spreads, gate_slots = [], [], []
    for j in range(owned):
        mine = row == meta_ref[0] + j
        gate = jnp.sum(jnp.where(mine, gates, 0.0), axis=0, keepdims=True)
        position = jnp.sum(jnp.where(mine, table, 0.0), axis=0, keepdims=True)
        hit = slot == position
        hits.append(hit)
        spreads.append(jnp.where(hit, 1.0, 0.0).astype(BF16))
        gate_slots.append(jnp.sum(jnp.where(hit, gate, 0.0), axis=1, keepdims=True))
    spread = jnp.concatenate(spreads, axis=0)
    routed = dot(spread, inputs).astype(BF16)
    cots = dot(spread, cot)
    gate_slots = jnp.concatenate(gate_slots, axis=0)
    grads = (gate_slots * cots).astype(BF16)

    def branch(left, right, gate_weights, up_weights, down_weights):
        gating = dot(left, gate_weights)
        linear = dot(left, up_weights)
        sigma = jax.nn.sigmoid(gating)
        silu = gating * sigma
        active = (silu * linear).astype(BF16)
        grad_active = dot(right, down_weights)
        slope = sigma * (1.0 + gating * (1.0 - sigma))
        grad_gating = (grad_active * linear * slope).astype(BF16)
        grad_linear = (grad_active * silu).astype(BF16)
        if not full:
            return active, grad_gating, grad_linear
        result = dot_nt(active, down_weights)
        grad_left = dot_nt(grad_gating, gate_weights) + dot_nt(grad_linear, up_weights)
        return active, grad_gating, grad_linear, result, grad_left

    weighted = []
    gate_lines = []
    for j in range(owned):
        rows = slice(j * capacity, (j + 1) * capacity)
        sx_ref[0, j] = routed[rows]
        sr_ref[0, j] = grads[rows]
        got = branch(
            routed[rows], grads[rows], weights(j), weights(owned + j), weights(2 * owned + j))
        sh_ref[0, j], sa_ref[0, j], sb_ref[0, j] = got[:3]
        if full:
            result, grad_left = got[3:]
            grad_gates = jnp.sum(result * cots[rows], axis=1, keepdims=True)
            gate_lines.append(jnp.sum(jnp.where(hits[j], grad_gates, 0.0), axis=0, keepdims=True))
            weighted.append(jnp.concatenate(
                [(gate_slots[rows] * result).astype(BF16), grad_left.astype(BF16)], axis=1))
    if shared:
        units = ssh_ref.shape[2]
        first, second = weights(3 * owned), weights(3 * owned + 1)
        got = branch(inputs, cot, first[:, :units], first[:, units : 2 * units], second[:, :units])
        ssh_ref[0], ssa_ref[0], ssb_ref[0] = got[:3]
    if not full:
        return
    back = dot_tn(spread, jnp.concatenate(weighted, axis=0))
    out, dx = back[:, :width], back[:, width:]
    if shared:
        out = out + got[3]
        dx = dx + got[4]
    line = lax.broadcasted_iota(jnp.int32, (16, width), 0)
    for j in range(parts):
        piece = slice(j * tok, (j + 1) * tok)
        spare = jnp.zeros((1, width - tok), F32)
        extra = jnp.zeros((16, width), F32)
        for i in range(owned):
            padded = jnp.concatenate([gate_lines[i][:, piece], spare], axis=1)
            extra = jnp.where(line == meta_ref[0] + i, padded, extra)
        out_piece, dx_piece = out[piece], dx[piece]
        if added:
            out_piece = out_piece + more_out_ref[0, j].astype(F32)
            dx_piece = dx_piece + more_dx_ref[0, j, :tok].astype(F32)
            extra = extra + more_dx_ref[0, j, tok:].astype(F32)
        out_ref[0, j] = out_piece.astype(BF16)
        dx_ref[0, j, :tok] = dx_piece.astype(BF16)
        dx_ref[0, j, tok:] = extra.astype(BF16)


def expert_shapes(owned, capacity, width, hidden):
    return [(owned, capacity, width)] * 2 + [(owned, capacity, hidden)] * 3


def placed(shape, where):
    return pl.BlockSpec((1,) + shape, lambda i, meta: (where(i, meta),) + (0,) * len(shape))


def expert_blocks(
    first, blocks, steps, capacity, parts, experts, units, full, meta, sources, weights, router_t, more, saved,
):
    pieces = isinstance(sources[0], list)
    shared = units > 0
    if pieces:
        tok, width = sources[0][0][0].shape
    else:
        block, width = sources[0].shape[1:]
        tok = block // parts
    block = tok * parts
    hidden = weights.shape[3]
    owned = weights.shape[1] // 3
    here = lambda i, meta: first + i
    step = lambda i, meta: i
    shapes = expert_shapes(owned, capacity, width, hidden)
    if shared:
        shapes += [(block, width), (block + 16, width), (block, units), (block, units), (block, units)]
    tops = [(parts, tok + 16, width), (parts, tok, width)] if full else []
    outs = [jax.ShapeDtypeStruct((steps,) + shape, BF16) for shape in tops]
    outs += [jax.ShapeDtypeStruct((blocks,) + shape, BF16) for shape in shapes]
    specs = [placed(shape, step) for shape in tops] + [placed(shape, here) for shape in shapes]
    if pieces:
        operands = [piece for source in sources for block_pieces in source for piece in block_pieces]
        in_specs = [whole(one.shape) for one in operands]
        scratch = [pltpu.VMEM((parts, tok, width), BF16)] * 2 + [pltpu.VMEM((16, width), BF16)]
    else:
        operands = list(sources)
        in_specs = [placed(one.shape[1:], here) for one in operands]
        scratch = []
    scratch += [pltpu.VMEM(weights.shape, BF16), pltpu.SemaphoreType.DMA((weights.shape[1],))]
    operands += [weights, router_t] + list(more)
    in_specs += [pl.BlockSpec(memory_space=pl.ANY), whole(router_t.shape)] + [placed(one.shape[1:], step) for one in more]
    in_specs += [pl.BlockSpec(memory_space=pl.ANY)] * len(saved)
    return pl.pallas_call(
        functools.partial(
            expert_kernel, capacity, parts, experts, full, shared, pieces, len(more) > 0, steps, len(saved)),
        grid_spec=pltpu.PrefetchScalarGridSpec(
            num_scalar_prefetch=1,
            grid=(steps,),
            in_specs=in_specs,
            out_specs=specs,
            scratch_shapes=scratch,
        ),
        out_shape=outs,
        input_output_aliases={1 + len(operands) + i: len(tops) + i for i in range(len(saved))},
        compiler_params=params(),
        cost_estimate=cost((12 if full else 6) * steps),
    )(meta, *operands, *saved)


def pair_sum_kernel(index_ref, kept_ref, got_ref, *refs):
    total = kept_ref[0].astype(F32) + got_ref[0].astype(F32)
    for ref in refs[:-1]:
        total = total + ref[...].astype(F32)
    refs[-1][...] = total.astype(BF16)


def pair_sum(index, kept, got, far):
    shape = kept.shape[1:]
    steps = shape[0] if len(shape) == 3 else 1
    part = (shape[0] // steps,) + shape[1:]
    rest = (0,) * (len(shape) - 1)
    picked = pl.BlockSpec((1,) + part, lambda i, index: (index[0], i) + rest)
    plain = pl.BlockSpec(part, lambda i, index: (i,) + rest)
    return pl.pallas_call(
        pair_sum_kernel,
        grid_spec=pltpu.PrefetchScalarGridSpec(
            num_scalar_prefetch=1,
            grid=(steps,),
            in_specs=[picked, picked] + [plain] * len(far),
            out_specs=plain,
        ),
        out_shape=jax.ShapeDtypeStruct(shape, BF16),
        compiler_params=params(),
        cost_estimate=cost(2),
    )(index.astype(jnp.int32)[None], kept, got, *far)


def attn_pieces_kernel(meta_ref, kept_ref, got_ref, small_ref, *refs):
    count = len(refs) - 1
    far_refs, out_refs, all_ref = refs[: count - 4], refs[count - 4 : count], refs[-1]
    total = kept_ref[0].astype(F32) + got_ref[0].astype(F32)
    for ref in far_refs:
        total = total + ref[...].astype(F32)
    share, columns = total.shape
    all_ref[:share] = total
    all_ref[share:] = jnp.zeros((all_ref.shape[0] - share, columns), F32)
    all_ref[share : share + small_ref.shape[0], : small_ref.shape[1]] = small_ref[...]
    rows = out_refs[0].shape[0]
    for d, ref in enumerate(out_refs):
        first = lax.rem(meta_ref[1] + d, 4) * rows
        ref[...] = all_ref[pl.ds(pl.multiple_of(first, 8), rows)].astype(BF16)


def attn_pieces(pair, plane, kept, got, far, small):
    share, columns = kept.shape[1:]
    rows = (share + 32) // 4
    picked = pl.BlockSpec((1, share, columns), lambda i, meta: (meta[0], 0, 0))
    return pl.pallas_call(
        attn_pieces_kernel,
        grid_spec=pltpu.PrefetchScalarGridSpec(
            num_scalar_prefetch=1,
            grid=(1,),
            in_specs=[picked, picked, whole(small.shape)] + [whole(one.shape) for one in far],
            out_specs=[whole((rows, columns))] * 4,
            scratch_shapes=[pltpu.VMEM((4 * rows, columns), F32)],
        ),
        out_shape=[jax.ShapeDtypeStruct((rows, columns), BF16)] * 4,
        compiler_params=params(),
        cost_estimate=cost(3),
    )(jnp.stack([pair, plane]).astype(jnp.int32), kept, got, small, *far)


def split_rows(value, core, sent_ref, kept_ref, *at):
    pairs = sent_ref.shape[0]
    share = value.shape[0] // (2 * pairs)
    for q in range(pairs):
        first = value[2 * q * share : (2 * q + 1) * share].astype(BF16)
        second = value[(2 * q + 1) * share : (2 * q + 2) * share].astype(BF16)
        index = (q,) + at
        kept_ref[index] = jnp.where(core == 0, first, second)
        sent_ref[index] = jnp.where(core == 0, second, first)


def weight_kernel(core_ref, left_ref, right_ref, sent_ref, kept_ref):
    steps, _, slots, rows = left_ref.shape
    left = left_ref[...].reshape(steps * slots, rows)
    right = right_ref[...].reshape(steps * slots, right_ref.shape[3])
    split_rows(dot_tn(left, right), core_ref[0], sent_ref, kept_ref, 0)


def weight_grads(core, left, right, pairs):
    steps, owned, slots, width = left.shape
    columns = right.shape[3]
    share = width // (2 * pairs)
    parts, wide = 1, columns
    shape = jax.ShapeDtypeStruct((pairs, owned, share, columns), BF16)
    spec = pl.BlockSpec((pairs, 1, share, wide), lambda j, i, core: (0, j, 0, i))
    return pl.pallas_call(
        weight_kernel,
        grid_spec=pltpu.PrefetchScalarGridSpec(
            num_scalar_prefetch=1,
            grid=(owned, parts),
            in_specs=[
                pl.BlockSpec((steps, 1, slots, width), lambda j, i, core: (0, j, 0, 0)),
                pl.BlockSpec((steps, 1, slots, wide), lambda j, i, core: (0, j, 0, i)),
            ],
            out_specs=[spec, spec],
        ),
        out_shape=[shape, shape],
        compiler_params=params(),
        cost_estimate=cost(6),
    )(core, left, right)


def shared_grad_kernel(core_ref, x_ref, c_ref, a_ref, b_ref, h_ref, sent_ref, kept_ref, total_ref):
    step = pl.program_id(0)
    block, units = a_ref.shape[1:]

    @pl.when(step == 0)
    def _():
        total_ref[...] = jnp.zeros_like(total_ref)

    total_ref[:, :units] += dot_tn(x_ref[0], a_ref[0])
    total_ref[:, units : 2 * units] += dot_tn(x_ref[0], b_ref[0])
    total_ref[:, 2 * units :] += dot_tn(c_ref[0, :block], h_ref[0])

    @pl.when(step == pl.num_programs(0) - 1)
    def _():
        split_rows(total_ref[...], core_ref[0], sent_ref, kept_ref)


def shared_grads(core, x, c, a, b, h, pairs):
    operands = (x, c, a, b, h)
    width, units = x.shape[2], a.shape[2]
    shape = jax.ShapeDtypeStruct((pairs, width // (2 * pairs), 3 * units), BF16)
    return pl.pallas_call(
        shared_grad_kernel,
        grid_spec=pltpu.PrefetchScalarGridSpec(
            num_scalar_prefetch=1,
            grid=(x.shape[0],),
            in_specs=[pl.BlockSpec((1,) + o.shape[1:], lambda i, core: (i, 0, 0)) for o in operands],
            out_specs=[whole(shape.shape), whole(shape.shape)],
            scratch_shapes=[pltpu.VMEM((width, 3 * units), F32)],
        ),
        out_shape=[shape, shape],
        compiler_params=params(),
        cost_estimate=cost(8),
    )(core, *operands)


def attn_grad_kernel(core_ref, hid_ref, dk_ref, dv_ref, dq_ref, gm_ref, at_ref, sent_ref, kept_ref):
    lead = hid_ref.shape[0] - dq_ref.shape[0]
    value = jnp.concatenate(
        [
            dot_tn(hid_ref[...], dk_ref[...]),
            dot_tn(hid_ref[...], dv_ref[...]),
            dot_tn(hid_ref[lead:, :], dq_ref[...]),
            dot_tn(gm_ref[...], at_ref[...]),
        ],
        axis=1,
    )
    split_rows(value, core_ref[0], sent_ref, kept_ref)


def attn_grads_of(core, hid, dk, dv, dq, grad_mixed_low, attended, pairs):
    width, cols = hid.shape[1], dk.shape[1]
    shape = jax.ShapeDtypeStruct((pairs, width // (2 * pairs), 4 * cols), BF16)
    operands = (hid, dk, dv, dq, grad_mixed_low, attended)
    return pl.pallas_call(
        attn_grad_kernel,
        grid_spec=pltpu.PrefetchScalarGridSpec(
            num_scalar_prefetch=1,
            grid=(1,),
            in_specs=[whole(o.shape) for o in operands],
            out_specs=[whole(shape.shape), whole(shape.shape)],
        ),
        out_shape=[shape, shape],
        compiler_params=params(),
        cost_estimate=cost(8),
    )(core, *operands)


def hidden_back_kernel(count, *refs):
    sources = refs[:count]
    dk_ref, dv_ref, dq_ref, w_ref = refs[count : count + 4]
    out_refs, gain_ref = refs[count + 4 : -1], refs[-1]
    cols = dk_ref.shape[1]
    step = pl.program_id(0)

    @pl.when(step == 0)
    def _():
        gain_ref[...] = jnp.zeros_like(gain_ref)

    for i, tok_ref in enumerate(sources):

        @pl.when(step == i)
        def _():
            grad = dot_nt(dk_ref[...], w_ref[:, :cols]) + dot_nt(dv_ref[...], w_ref[:, cols : 2 * cols])
            if i == count - 1:
                grad = grad + dot_nt(dq_ref[...], w_ref[:, 2 * cols : 3 * cols])
            out_refs[i][...] = grad.astype(BF16)
            inputs = tok_ref[...].astype(F32)
            scale = lax.rsqrt(jnp.mean(inputs * inputs, axis=-1, keepdims=True) + EPS)
            gain_ref[...] += jnp.sum(grad * (inputs * scale), axis=0, keepdims=True)


def hidden_back(sources, dk, dv, dq, weights):
    count = len(sources)
    rows, width = sources[0].shape
    cols = dk.shape[1]
    part = pl.BlockSpec((rows, cols), lambda i: (i, 0))
    return pl.pallas_call(
        functools.partial(hidden_back_kernel, count),
        grid=(count,),
        in_specs=[whole((rows, width))] * count
        + [part, part, whole((rows, cols)), whole(weights.shape)],
        out_specs=[whole((rows, width))] * count + [whole((1, width))],
        out_shape=[jax.ShapeDtypeStruct((rows, width), BF16)] * count + [jax.ShapeDtypeStruct((1, width), F32)],
        compiler_params=params(),
        cost_estimate=cost(7),
    )(*sources, dk, dv, dq, weights)


def collect_kernel(places_ref, first_ref, second_ref, out_ref):
    for half, ref in enumerate((first_ref, second_ref)):

        @pl.when(pl.program_id(0) // (pl.num_programs(0) // 2) == half)
        def _():
            out_ref[...] = ref[0].astype(F32)


def collect(places, first, second):
    _, owned, rows, columns = first.shape
    half = 2 * owned
    block = (1, rows, columns)

    def part(start):
        def index(step, places):
            local = jnp.clip(step - start, 0, half - 1)
            return (local // owned, local % owned, 0, 0)

        return pl.BlockSpec((1,) + block, index)

    return pl.pallas_call(
        collect_kernel,
        grid_spec=pltpu.PrefetchScalarGridSpec(
            num_scalar_prefetch=1,
            grid=(2 * half,),
            in_specs=[part(0), part(half)],
            out_specs=pl.BlockSpec(
                block, lambda step, places: (places[step // half] * half + step % half, 0, 0)),
        ),
        out_shape=jax.ShapeDtypeStruct((2 * half, rows, columns), F32),
        compiler_params=params(),
        cost_estimate=cost(5),
    )(places, first, second)


def norm_back(grad, values, scale, gain):
    grad_gain = jnp.sum(grad * values * scale, axis=0)
    scaled = grad * gain
    grad_values = scale * scaled - values * scale * scale * scale * jnp.mean(
        scaled * values, axis=-1, keepdims=True
    )
    return grad_values, grad_gain


def local(
    tokens,
    segments,
    routes,
    query_weight,
    key_weight,
    value_weight,
    out_weight,
    attn_gain,
    ffn_gain,
    router_weight,
    shared_gate,
    shared_up,
    shared_down,
    expert_gate,
    expert_up,
    expert_down,
    cotangent,
):
    fsdp, ctx, tp = (lax.axis_size(a) for a in ("fsdp", "ctx", "tp"))
    pairs = fsdp // 2
    me = lax.axis_index("fsdp")
    pair, core = me // 2, me % 2
    plane = lax.axis_index("ctx")
    lane = lax.axis_index("tp")
    tokens, cotangent, routes = tokens[0], cotangent[0], routes[0]
    block, width = tokens.shape
    share, cols = query_weight.shape
    experts = expert_gate.shape[0]
    hidden_units = expert_gate.shape[2]
    units = shared_gate.shape[1] // 2
    owned = experts // ctx
    top_count = routes.shape[1]
    capacity = 3 * top_count * block // (2 * experts)
    tok = block // tp
    core_index = core.astype(jnp.int32)[None]

    phases = Phases()

    def to_pairs(piece):
        return [pair_shift(piece, d) for d in range(1, pairs)]

    def to_tp(piece):
        return [tp_shift(piece, j) for j in range(1, tp)]

    def joined(*pieces):
        return place(pieces, lane).reshape(block, width)

    other_plane = plane ^ 2

    gains = jnp.concatenate([attn_gain[None], ffn_gain[None]], axis=0)
    qkv_mine, small_mine, tokens_mine = pack(
        lane, tp, key_weight, value_weight, query_weight, router_weight.T, gains, tokens)
    small_core = core_swap(small_mine)
    qkv_mine, small_mine, tokens_mine, small_core = phases.run(
        lambda *given: given, qkv_mine, small_mine, tokens_mine, small_core)

    prepare_meta = jnp.stack([lane, plane]).astype(jnp.int32)

    def send_first(qkv, small, small_core, tokens_mine, cotangent):
        prepared = prepare(prepare_meta, tp, experts, routes.T, cotangent, segments)
        return (
            to_pairs(qkv), core_swap(qkv), to_pairs(jnp.concatenate([small, small_core], axis=0)),
            ctx_open(tokens_mine, 1),
            prepared)

    qkv_far, qkv_core, small_far, prev_one_mine, prepared = phases.run(
        send_first, qkv_mine, small_mine, small_core, tokens_mine, cotangent)
    cosine, sine, kseg, qseg, hits = prepared[:5]
    cot_own = prepared[5:]
    gathered = small_mine, small_core, small_far

    def all_small(small_mine, small_core, small_far):
        rows = place([jnp.concatenate([small_mine, small_core], axis=0)] + small_far, pair)
        rows = rows.reshape(pairs, 2, 16, share)
        rows = jnp.where(core == 0, rows, rows[:, ::-1])
        return rows.reshape(fsdp, 16, share).transpose(1, 0, 2).reshape(16, width)

    def send_second(qkv_far, prev_one_mine, out_weight, gathered, *stacks):
        return (
            [core_swap(one) for one in qkv_far], to_tp(prev_one_mine), ctx_open(prev_one_mine, 1),
            to_pairs(out_weight.T), all_small(*gathered), bundle(plane, owned, units, stacks[:3], stacks[3:]))

    qkv_far_core, prev_one_other, prev_two_mine, out_far, small_all, weights_mine = phases.run(
        send_second, qkv_far, prev_one_mine, out_weight, gathered, expert_gate, expert_up,
        jnp.swapaxes(expert_down, 1, 2), shared_gate, shared_up, shared_down.T)
    weights = lax.all_gather(weights_mine, "fsdp", axis=0)
    attn_scale = small_all[experts : experts + 1].astype(F32)
    ffn_scale = small_all[experts + 1 : experts + 2].astype(F32)
    router_t = jnp.concatenate([small_all[:experts], jnp.zeros((16 - experts, width), BF16)], axis=0)
    router_full = small_all[:experts].T
    here = [(plane + d) % ctx for d in range(ctx)]
    half = ctx // 2
    place_meta = jnp.stack([lane, pair, core]).astype(jnp.int32)

    def near_projection(prev_one_mine, prev_one_other, prev_two_mine, cot, out_weight, out_far, same, cross, scale):
        sent = (
            to_tp(prev_two_mine), ctx_swap(cot), [core_swap(one) for one in [out_weight.T] + out_far])
        return sent, project_near(
            place_meta, tokens, [prev_one_mine] + prev_one_other, same, cross, scale, cosine, sine)

    (prev_two_other, cot_one, out_cross), first = phases.run(
        near_projection, prev_one_mine, prev_one_other, prev_two_mine, cot_own[0], out_weight, out_far,
        [qkv_mine] + qkv_far, [qkv_core] + qkv_far_core, attn_scale)
    query, qkv_full, prev_one = first[3:]

    def attention(prev_two_mine, prev_two_other, cot, cot_one, out_weight, out_far, out_cross):
        sent = ctx_swap(cot, 2), to_tp(cot_one)
        hid, keys, values, prev_two = project_far(
            place_meta, [prev_two_mine] + prev_two_other, qkv_full, attn_scale, cosine, sine, first[:3])
        attended, lse = attend(query, keys, values, kseg, qseg)
        same = place([out_weight.T] + out_far, pair)
        cross = place(out_cross, pair)
        out_full = place_rows([same, cross], core).reshape(width, cols)
        partial = dot_nt(attended, out_full).astype(BF16).reshape(tp, tok, width)
        return sent, hid, keys, values, prev_two, attended, lse, out_full, partial

    (cot_two, cot_one_other), hid, keys, values, prev_two, attended, lse, out_full, partial = phases.run(
        attention, prev_two_mine, prev_two_other, cot_own[0], cot_one, out_weight, out_far, out_cross)

    def sent_tp(total):
        return [tp_shift(pick(total, (lane + j) % tp), j) for j in range(1, tp)]

    def sum_tp(total, got):
        result = pick(total, lane).astype(F32)
        for one in got:
            result = result + one.astype(F32)
        return result

    def after_attention(partial, cot_two, gate, up, down):
        return sent_tp(partial), ctx_swap(cot_two), bundle(other_plane, owned, units, [gate, up, down], [])

    partial_other, cot_three, again_mine = phases.run(
        after_attention, partial, cot_two, expert_gate, expert_up, jnp.swapaxes(expert_down, 1, 2))
    inputs_mine = tokens_mine.astype(F32)

    def normalize(partial, got):
        mixed = inputs_mine + sum_tp(partial, got)
        scale_ffn = lax.rsqrt(jnp.mean(mixed * mixed, axis=-1, keepdims=True) + EPS)
        return (mixed * scale_ffn * ffn_scale).astype(BF16), mixed, scale_ffn

    normed_low, mixed, scale_ffn = phases.run(normalize, partial, partial_other)

    x_zero, x_one, x_two, cot_two_other = phases.run(
        lambda one, cot: (to_tp(one), ctx_swap(one), ctx_swap(one, 2), to_tp(cot)), normed_low, cot_two)
    other_zero = x_zero
    other_one, x_three = phases.run(lambda one, two: (to_tp(one), ctx_swap(two)), x_one, x_two)
    half = ctx // 2
    near_meta = jnp.stack([owned * plane, lane]).astype(jnp.int32)
    far_meta = jnp.stack([owned * other_plane, lane]).astype(jnp.int32)

    def joint(mine, other):
        return [[one] + list(two) for one, two in zip(mine, other)]

    def blocks_of(first, full, meta, with_units, sources, weights, more, saved):
        return expert_blocks(
            first, ctx, half, capacity, tp, experts, with_units, full, meta, sources, weights, router_t, more, saved)

    def own_full(x_two, x_three, cot_three, weights, x_mine, x_other, cot_mine, cot_other, again_mine):
        sent = to_tp(x_two), to_tp(x_three), to_tp(cot_three)
        sources = joint(x_mine, x_other), joint(cot_mine, cot_other)
        return sent, blocks_of(0, True, near_meta, units, sources, weights, [], []), again_mine

    (other_two, other_three, cot_three_other), got, again_mine = phases.run(
        own_full, x_two, x_three, cot_three, weights, [normed_low, x_one], [other_zero, other_one],
        [cot_own[0], cot_one], [cot_own[1:], cot_one_other], again_mine)
    other_weights = lax.all_gather(again_mine, "fsdp", axis=0)
    more = got[:2]

    def weight_step(left, right):
        return weight_grads(core_index, left, right, pairs)

    def own_rest(x_mine, x_other, cot_mine, cot_other, weights, saved):
        sources = joint(x_mine, x_other), joint(cot_mine, cot_other)
        saved = blocks_of(half, False, near_meta, units, sources, weights, [], saved)
        sx, sr, sh, sa, sb = saved[:5]
        down = weight_step(sr, sh)
        return saved, down, core_swap(down[0]), weight_step(sx, sa), weight_step(sx, sb)

    saved, down, down_got, gate, up = phases.run(
        own_rest, [x_two, x_three], [other_two, other_three], [cot_two, cot_three],
        [cot_two_other, cot_three_other], weights, got[2:])
    sx, sr, sh, sa, sb, ssx, ssc, ssh, ssa, ssb = saved


    def for_pairs(kept, got):
        return [pair_sum((pair + j) % pairs, kept, got, []) for j in range(1, pairs)]

    def sent_pairs(rows):
        return [pair_shift(one, j + 1) for j, one in enumerate(rows)]

    def add_pairs(kept, got, far):
        return pair_sum(pair, kept, got, far)

    def other_full(down, gate_sent, up_sent, ssx, other_weights, more):
        sent = sent_pairs(for_pairs(*down)), core_swap(gate_sent), core_swap(up_sent)
        return sent, blocks_of(0, True, far_meta, 0, (ssx, ssc), other_weights, more, [])

    (down_far, gate_got, up_got), got = phases.run(
        other_full, (down[1], down_got), gate[0], up[0], ssx, other_weights, more)
    dx, out = got[:2]

    def back_through_norm(dx_sum):
        grad_normed = dx_sum[:tok]
        grad_gates = dx_sum[tok : tok + experts, :tok].T
        named = lax.dynamic_slice_in_dim(hits, lane * tok, tok, 1).T > 0.0
        logits = jnp.where(named, dot(normed_low, router_full), -1e30)
        expo = jnp.where(named, jnp.exp(logits - jnp.max(logits, axis=-1, keepdims=True)), 0.0)
        gates = expo / jnp.sum(expo, axis=-1, keepdims=True)
        grad_logits = (
            gates * (grad_gates - jnp.sum(gates * grad_gates, axis=-1, keepdims=True))
        ).astype(BF16)
        grad_normed = grad_normed + dot_nt(grad_logits, router_full)
        grad_mixed_norm, grad_ffn_gain = norm_back(grad_normed, mixed, scale_ffn, ffn_scale)
        grad_out = lax.dynamic_slice_in_dim(cotangent, lane * tok, tok, 0).astype(F32)
        grad_mixed = grad_out + grad_mixed_norm
        return grad_mixed.astype(BF16), grad_mixed, grad_ffn_gain, dot_tn(grad_logits, normed_low)

    def phase_one(gate, dx, down, ssx, saved):
        sent = sent_pairs(for_pairs(*gate)), sent_tp(dx[1]), sent_tp(dx[0])
        saved = blocks_of(half, False, far_meta, 0, (ssx, ssc), other_weights, [], saved)
        return sent, saved, weight_step(saved[1], saved[2]), add_pairs(*down)

    (gate_far, dx_one, dx_zero), other_saved, other_down, own_down = phases.run(
        phase_one, (gate[1], gate_got), dx, (down[1], down_got, down_far), ssx, got[2:])
    ox, orr, oh, oa, ob = other_saved
    groups = [[2 * i, 2 * i + 1] for i in range(ctx // 2)]

    def neighbours(piece):
        return lax.all_gather(piece, "ctx", axis=0, axis_index_groups=groups)

    both_down = neighbours(own_down)

    def phase_two(up, down_sent, dx, dx_one, gate, ox, out):
        sent = (
            sent_pairs(for_pairs(*up)), core_swap(down_sent),
            ctx_swap(sum_tp(dx[1], dx_one).astype(BF16)), sent_tp(out[1]))
        return sent, add_pairs(*gate), weight_step(ox, oa), weight_step(ox, ob)

    (up_far, down_got, home, out_one), own_gate, other_gate, other_up = phases.run(
        phase_two, (up[1], up_got), other_down[0], dx, dx_one, (gate[1], gate_got, gate_far), ox, out)

    both_gate = neighbours(own_gate)

    def phase_three(down, gate_sent, both, dx, dx_zero, home, up, ssx):
        back = back_through_norm(sum_tp(dx[0], dx_zero) + home.astype(F32))
        sent = (
            sent_pairs(for_pairs(*down)), core_swap(gate_sent), to_tp(back[0]))
        shared = shared_grads(core_index, ssx, ssc, ssa, ssb, ssh, pairs)
        return sent, back, add_pairs(*up), shared, both

    sent, back, own_up, shared, both_down = phases.run(
        phase_three, (other_down[1], down_got), other_gate[0], both_down, dx, dx_zero, home, (up[1], up_got, up_far), ssx)
    down_far, gate_got, grad_mixed_other = sent
    both_up = neighbours(own_up)
    grad_mixed_low, grad_mixed, grad_ffn_gain, grad_router = back

    def phase_four(gate, up_sent, both, down, grad_mixed_low, grad_mixed_other, out):
        sent = (
            sent_pairs(for_pairs(*gate)), core_swap(up_sent), sent_tp(out[0]))
        rows = joined(grad_mixed_low, *grad_mixed_other)
        grad_attended = dot(rows, out_full).astype(BF16)
        grads = attend_back(query, keys, values, grad_attended, lse, kseg, qseg, cosine, sine)
        return sent, rows, grads, add_pairs(*down), both

    (gate_far, up_got, out_zero), grad_mixed_rows, (dq, dk, dv), own_other_down, both_gate = phases.run(
        phase_four, (other_gate[1], gate_got), other_up[0], both_gate,
        (other_down[1], down_got, down_far), grad_mixed_low, grad_mixed_other, out)

    both_other_down = neighbours(own_other_down)

    def phase_five(up, both, dq, dk, dv, hid, gate, shared_sent):
        back = hidden_back([prev_two, prev_one, tokens], dk, dv, dq, qkv_full)
        hidden_parts = [one.reshape(tp, tok, width) for one in back[:-1]]
        small_rows = jnp.concatenate(
            [grad_router, grad_ffn_gain[None], back[-1], jnp.zeros((16 - experts - 2, width), F32)], axis=0)
        sent = (
            sent_pairs(for_pairs(*up)), all_sum(small_rows, "tp"), sent_tp(hidden_parts[0]), core_swap(shared_sent))
        attn = attn_grads_of(core_index, hid, dk, dv, dq, grad_mixed_rows, attended, pairs)
        return sent, hidden_parts, attn, add_pairs(*gate), both

    (up_far, small_rows, far_two, shared_got), hidden_parts, attn, own_other_gate, both_up = phases.run(
        phase_five, (other_up[1], up_got), both_up, dq, dk, dv, hid, (other_gate[1], gate_got, gate_far),
        shared[0])

    both_other_gate = neighbours(own_other_gate)

    def phase_six(attn_sent, both, shared, hidden_parts, far_two, small_rows, up, out, out_one):
        sent = (
            core_swap(attn_sent), sent_pairs(for_pairs(*shared)),
            ctx_open(sum_tp(hidden_parts[0], far_two).astype(BF16), -1), sent_tp(hidden_parts[1]),
            ctx_swap(sum_tp(out[1], out_one).astype(BF16)), core_swap(small_rows))
        return sent, add_pairs(*up), both

    (attn_got, shared_far, carried, far_one, out_home, small_got), own_other_up, both_other_down = phases.run(
        phase_six, attn[0], both_other_down, (shared[1], shared_got), hidden_parts, far_two, small_rows, (other_up[1], up_got, up_far), out,
        out_one)
    both_other_up = neighbours(own_other_up)
    places = jnp.stack([plane // 2, 1 - plane // 2]).astype(jnp.int32)

    def phase_seven(
        attn, both, hidden_parts, far_one, carried, small_rows, small_got, both_down, both_other_down, shared, out, out_zero, out_home
    ):
        carried = ctx_open(
            (sum_tp(hidden_parts[1], far_one) + carried.astype(F32)).astype(BF16), -1)
        sent = sent_pairs(for_pairs(*attn)), carried, sent_tp(hidden_parts[2])
        small_rows = small_rows + small_got
        reach = 1
        while reach < pairs:
            small_rows = small_rows + pair_swap(small_rows, reach)
            reach *= 2
        small_rows = lax.dynamic_slice_in_dim(small_rows, me * share, share, 1)
        output_mine = (mixed + sum_tp(out[0], out_zero) + out_home.astype(F32)).astype(BF16)
        return sent, small_rows, add_pairs(*shared), collect(places, both_down, both_other_down), both, output_mine

    (attn_far, carried, hidden_other), small_rows, own_shared, grad_expert_down, both_other_gate, output_mine = phases.run(
        phase_seven, (attn[1], attn_got), both_other_gate, hidden_parts, far_one, carried, small_rows, small_got,
        both_down, both_other_down, (shared[1], shared_got, shared_far), out, out_zero, out_home)
    both_shared = neighbours(own_shared)

    def input_back(total, got, carried):
        grad_hidden = sum_tp(total, got) + carried.astype(F32)
        scale_attn = lax.rsqrt(jnp.mean(inputs_mine * inputs_mine, axis=-1, keepdims=True) + EPS)
        scaled = grad_hidden * attn_scale
        grad_norm = scale_attn * scaled - inputs_mine * scale_attn * scale_attn * scale_attn * jnp.mean(
            scaled * inputs_mine, axis=-1, keepdims=True)
        return (grad_mixed + grad_norm).astype(BF16)

    def phase_eight(
        attn, hidden_parts, hidden_other, carried, small_rows, both_gate, both_other_gate, both_up, both_other_up, output_mine
    ):
        pieces = attn_pieces(pair, plane, *attn, small_rows)
        input_mine = input_back(hidden_parts[2], hidden_other, carried)
        return (
            [ctx_shift(pieces[d], d) for d in range(1, ctx)], to_tp(input_mine), to_tp(output_mine), pieces[0],
            input_mine, collect(places, both_gate, both_other_gate), collect(places, both_up, both_other_up))

    attn_got, input_other, output_other, attn_piece, input_mine, grad_expert_gate, grad_expert_up = phases.run(
        phase_eight, (attn[1], attn_got, attn_far), hidden_parts, hidden_other, carried, small_rows, both_gate,
        both_other_gate, both_up, both_other_up, output_mine)

    def phase_nine(attn_piece, attn_got, input_mine, input_other, output_mine, output_other, both_shared):
        total = attn_piece.astype(F32)
        for one in attn_got:
            total = total + one.astype(F32)
        total = total.astype(BF16)
        halves = both_shared.astype(F32)
        result = [
            jnp.concatenate([one[:, i * units : (i + 1) * units] for one in halves], axis=1) for i in range(3)]
        return (
            total, [ctx_shift(total, d) for d in range(1, ctx)], joined(input_mine, *input_other),
            joined(output_mine, *output_other), result)

    attn_piece, attn_got, input_grad, output, result = phases.run(
        phase_nine, attn_piece, attn_got, input_mine, input_other, output_mine, output_other, both_shared)
    grad_key_weight, grad_value_weight, grad_query_weight, grad_out_rows, small_out = finish(
        plane.astype(jnp.int32)[None], [attn_piece] + attn_got, share, cols)
    grad_out_rows = grad_out_rows.T
    grad_expert_down = jnp.swapaxes(grad_expert_down, 1, 2)
    small_out = small_out[:, :share]
    grad_shared_gate, grad_shared_up, grad_shared_down = result[0], result[1], result[2].T
    return (
        output[None],
        input_grad[None],
        grad_query_weight,
        grad_key_weight,
        grad_value_weight,
        grad_out_rows,
        small_out[experts + 1],
        small_out[experts],
        small_out[:experts].T,
        grad_shared_gate,
        grad_shared_up,
        grad_shared_down,
        grad_expert_gate,
        grad_expert_up,
        grad_expert_down,
    )


def solution(mesh):
    in_specs = (
        P("fsdp", "ctx", None),
        P("fsdp", None),
        P("fsdp", "ctx", None),
        P("fsdp", "tp"),
        P("fsdp", "tp"),
        P("fsdp", "tp"),
        P("tp", "fsdp"),
        P("fsdp"),
        P("fsdp"),
        P("fsdp", None),
        P("fsdp", "tp"),
        P("fsdp", "tp"),
        P("tp", "fsdp"),
        P(None, "fsdp", "tp"),
        P(None, "fsdp", "tp"),
        P(None, "tp", "fsdp"),
        P("fsdp", "ctx", None),
    )
    out_specs = (
        P("fsdp", "ctx", None),
        P("fsdp", "ctx", None),
        P("fsdp", "tp"),
        P("fsdp", "tp"),
        P("fsdp", "tp"),
        P("tp", "fsdp"),
        P("fsdp"),
        P("fsdp"),
        P("fsdp", None),
        P("fsdp", "tp"),
        P("fsdp", "tp"),
        P("tp", "fsdp"),
        P(None, "fsdp", "tp"),
        P(None, "fsdp", "tp"),
        P(None, "tp", "fsdp"),
    )
    return jax.shard_map(local, mesh=mesh, in_specs=in_specs, out_specs=out_specs, check_vma=False)
```

```python
import functools

import jax
import jax.numpy as jnp
from jax import lax
from jax.experimental import pallas as pl
from jax.experimental.pallas import tpu as pltpu
from jax.sharding import PartitionSpec as P

HD = 64
WINDOW = 1024
EPS = 1e-06
F32 = jnp.float32
BF16 = jnp.bfloat16
VMEM_BYTES = 56 * 1024 * 1024
COST_SCALE = 0.3


def dot(left, right):
    return lax.dot_general(left, right, (((1,), (0,)), ((), ())), preferred_element_type=F32)


def dot_nt(left, right):
    return lax.dot_general(left, right, (((1,), (1,)), ((), ())), preferred_element_type=F32)


def dot_tn(left, right):
    return lax.dot_general(left, right, (((0,), (0,)), ((), ())), preferred_element_type=F32)


def core_swap(block):
    size = lax.axis_size("fsdp")
    return lax.ppermute(block, "fsdp", [(i, i ^ 1) for i in range(size)])


def pair_shift(block, distance):
    size = lax.axis_size("fsdp")
    pairs = size // 2
    route = [(i, ((i // 2 + distance) % pairs) * 2 + i % 2) for i in range(size)]
    return lax.ppermute(block, "fsdp", route)


def pair_swap(block, reach):
    size = lax.axis_size("fsdp")
    return lax.ppermute(block, "fsdp", [(i, i ^ (2 * reach)) for i in range(size)])


def tp_shift(block, distance):
    size = lax.axis_size("tp")
    return lax.ppermute(block, "tp", [(i, (i + distance) % size) for i in range(size)])


def ctx_shift(block, distance):
    size = lax.axis_size("ctx")
    return lax.ppermute(block, "ctx", [(i, (i + distance) % size) for i in range(size)])


def ctx_swap(block, reach=1):
    size = lax.axis_size("ctx")
    return lax.ppermute(block, "ctx", [(i, i ^ reach) for i in range(size)])


def ctx_open(block, distance):
    size = lax.axis_size("ctx")
    route = [(i, i + distance) for i in range(size) if 0 <= i + distance < size]
    return lax.ppermute(block, "ctx", route)


def pick(stack, index):
    return lax.dynamic_index_in_dim(stack, index, 0, keepdims=False)


def place_rows(pieces, me):
    first, second = pieces
    return jnp.where(
        me == 0, jnp.stack([first, second], axis=1), jnp.stack([second, first], axis=1))


def place(pieces, me):
    count = len(pieces)
    if count == 1:
        return pieces[0][None]
    if count == 2:
        first, second = pieces
        return jnp.where(me == 0, jnp.stack([first, second]), jnp.stack([second, first]))
    result = jnp.zeros((count,) + pieces[0].shape, pieces[0].dtype)
    for d, piece in enumerate(pieces):
        result = lax.dynamic_update_index_in_dim(result, piece, (me - d) % count, 0)
    return result


def tie(values, *others):
    return lax.optimization_barrier((values, others))[0]


class Phases:
    def __init__(self):
        self.last = []

    def run(self, function, *values):
        given = function(*(tie(values, self.last) if self.last else values))
        self.last = jax.tree.leaves(given)
        return given


def all_sum(block, axis):
    size = lax.axis_size(axis)
    reach = 1
    while reach < size:
        other = lax.ppermute(block, axis, [(i, i ^ reach) for i in range(size)])
        block = block + other
        reach *= 2
    return block


def whole(shape):
    return pl.BlockSpec(shape, lambda *_: (0,) * len(shape))


def params():
    return pltpu.CompilerParams(vmem_limit_bytes=VMEM_BYTES)


def cost(microseconds):
    return pl.CostEstimate(flops=0, bytes_accessed=int(microseconds * COST_SCALE * 3.4e6), transcendentals=0)


def swap_halves(values):
    width = values.shape[-1]
    lane = lax.broadcasted_iota(jnp.int32, values.shape, 1)
    up = pltpu.roll(values, width - HD // 2, 1)
    down = pltpu.roll(values, HD // 2, 1)
    return jnp.where(lane % HD < HD // 2, up, down)


def widen(table, width):
    copies = -(-width // table.shape[1])
    return jnp.concatenate([table] * copies, axis=1)[:, :width]


def rotated(values, cosine, sine):
    return (values * cosine + swap_halves(values) * sine).astype(BF16)


def project_rows(inputs, gain, weights, cos_ref, sin_ref, hid_ref, k_ref, v_ref):
    scale = lax.rsqrt(jnp.mean(inputs * inputs, axis=-1, keepdims=True) + EPS)
    hidden = (inputs * scale * gain).astype(BF16)
    hid_ref[...] = hidden
    width = k_ref.shape[1]
    k_ref[...] = rotated(
        dot(hidden, weights[:, :width]), widen(cos_ref[...], width), widen(sin_ref[...], width))
    v_ref[...] = dot(hidden, weights[:, width : 2 * width]).astype(BF16)
    return hidden


def project_near_kernel(parts, pairs, meta_ref, tok_ref, *refs):
    prev_refs, refs = refs[:parts], refs[parts:]
    same_refs, cross_refs, refs = refs[:pairs], refs[pairs : 2 * pairs], refs[2 * pairs :]
    gain_ref, cos_ref, sin_ref, hid_ref, k_ref, v_ref, q_ref, w_ref, prev_ref, w_all, x_all = refs
    tok, features = x_all.shape[1:]
    share, columns = w_all.shape[1:]

    @pl.when(pl.program_id(0) == 0)
    def _():
        for d in range(pairs):
            row = 2 * lax.rem(meta_ref[1] + pairs - d, pairs)
            w_all[row + meta_ref[2]] = same_refs[d][...]
            w_all[row + 1 - meta_ref[2]] = cross_refs[d][...]
        for j in range(parts):
            x_all[lax.rem(meta_ref[0] + parts - j, parts)] = prev_refs[j][...]
        weights = w_all[...].reshape(2 * pairs * share, columns)
        w_ref[...] = weights
        inputs = x_all[...].reshape(parts * tok, features)
        prev_ref[...] = inputs
        project_rows(inputs.astype(F32), gain_ref[...], weights, cos_ref, sin_ref, hid_ref, k_ref, v_ref)

    @pl.when(pl.program_id(0) == 1)
    def _():
        weights = w_all[...].reshape(2 * pairs * share, columns)
        hidden = project_rows(
            tok_ref[...].astype(F32), gain_ref[...], weights, cos_ref, sin_ref, hid_ref, k_ref, v_ref)
        width = k_ref.shape[1]
        query = dot(hidden, weights[:, 2 * width :])
        q_ref[...] = rotated(
            query, widen(cos_ref[...], width), widen(sin_ref[...], width)) * jnp.asarray(HD**-0.5, BF16)


def project_near(meta, tokens, prev_pieces, same, cross, gain, cosine, sine):
    rows, features = tokens.shape
    share, columns = same[0].shape
    width = columns // 3
    tok = prev_pieces[0].shape[0]
    count = 2 * len(same) * share
    shapes = [(3 * rows, features), (3 * rows, width), (3 * rows, width)]
    block = lambda i, meta: (i + 1, 0)
    others = [(rows, width), (count, columns), (rows, features)]
    operands = [tokens, *prev_pieces, *same, *cross, gain]
    table = pl.BlockSpec((rows, cosine.shape[1]), block)
    return pl.pallas_call(
        functools.partial(project_near_kernel, len(prev_pieces), len(same)),
        grid_spec=pltpu.PrefetchScalarGridSpec(
            num_scalar_prefetch=1,
            grid=(2,),
            in_specs=[whole(o.shape) for o in operands] + [table, table],
            out_specs=[pl.BlockSpec((rows, shape[1]), block) for shape in shapes]
            + [whole(shape) for shape in others],
            scratch_shapes=[
                pltpu.VMEM((2 * len(same), share, columns), BF16),
                pltpu.VMEM((len(prev_pieces), tok, features), BF16),
            ],
        ),
        out_shape=[jax.ShapeDtypeStruct(shape, BF16) for shape in shapes + others],
        compiler_params=params(),
        cost_estimate=cost(7),
    )(meta, *operands, cosine, sine)


def project_far_kernel(parts, meta_ref, *refs):
    prev_refs, refs = refs[:parts], refs[parts:]
    w_ref, gain_ref, cos_ref, sin_ref, _, _, _, hid_ref, k_ref, v_ref, prev_ref, x_all = refs
    tok, features = x_all.shape[1:]
    for j in range(parts):
        x_all[lax.rem(meta_ref[0] + parts - j, parts)] = prev_refs[j][...]
    inputs = x_all[...].reshape(parts * tok, features)
    prev_ref[...] = inputs
    project_rows(inputs.astype(F32), gain_ref[...], w_ref[...], cos_ref, sin_ref, hid_ref, k_ref, v_ref)


def project_far(meta, prev_pieces, weights, gain, cosine, sine, saved):
    tok, features = prev_pieces[0].shape
    rows = tok * len(prev_pieces)
    width = weights.shape[1] // 3
    first = lambda i, meta: (0, 0)
    operands = [*prev_pieces, weights, gain]
    table = pl.BlockSpec((rows, cosine.shape[1]), first)
    return pl.pallas_call(
        functools.partial(project_far_kernel, len(prev_pieces)),
        grid_spec=pltpu.PrefetchScalarGridSpec(
            num_scalar_prefetch=1,
            grid=(1,),
            in_specs=[whole(o.shape) for o in operands] + [table, table]
            + [pl.BlockSpec(memory_space=pl.ANY)] * 3,
            out_specs=[pl.BlockSpec((rows, one.shape[1]), first) for one in saved]
            + [whole((rows, features))],
            scratch_shapes=[pltpu.VMEM((len(prev_pieces), tok, features), BF16)],
        ),
        out_shape=[jax.ShapeDtypeStruct(one.shape, BF16) for one in saved]
        + [jax.ShapeDtypeStruct((rows, features), BF16)],
        input_output_aliases={1 + len(operands) + 2 + i: i for i in range(3)},
        compiler_params=params(),
        cost_estimate=cost(4),
    )(meta, *operands, cosine, sine, *saved)


def prepare_kernel(parts, meta_ref, routes_ref, cot_ref, rates_ref, seg_ref, *refs):
    cos_ref, sin_ref, kseg_ref, qseg_ref, hits_ref = refs[:5]
    mine_ref, other_refs, seg_all = refs[5], refs[6:-1], refs[-1]
    block, width = cot_ref.shape
    tok = block // parts
    experts = hits_ref.shape[0]
    rows, lanes = cos_ref.shape
    short = 64
    origin = (meta_ref[1] - 2) * block
    far = (lax.broadcasted_iota(jnp.int32, (rows // short, lanes), 0) * short + origin).astype(F32) * rates_ref[...]
    near = lax.broadcasted_iota(jnp.int32, (short, lanes), 0).astype(F32) * rates_ref[...]
    far_cos, far_sin, near_cos, near_sin = jnp.cos(far), jnp.sin(far), jnp.cos(near), jnp.sin(near)
    sign = jnp.where(lax.broadcasted_iota(jnp.int32, (short, lanes), 1) % HD < HD // 2, -1.0, 1.0)
    signed_sin, signed_cos = sign * near_sin, sign * near_cos
    for h in range(rows // short):
        part = slice(h * short, (h + 1) * short)
        one_cos, one_sin = far_cos[h : h + 1], far_sin[h : h + 1]
        cos_ref[part] = one_cos * near_cos - one_sin * near_sin
        sin_ref[part] = one_sin * signed_cos + one_cos * signed_sin
    seg_all[:, : 2 * block] = jnp.full((1, 2 * block), -1, jnp.int32)
    seg_all[:, 2 * block :] = seg_ref[...]
    kseg = seg_all[:, pl.ds(pl.multiple_of(meta_ref[1] * block, block), rows)]
    qseg_ref[...] = kseg[:, rows - block :]
    kseg_ref[...] = jnp.broadcast_to(kseg, (8, rows)).T[:, :1]
    row = lax.broadcasted_iota(jnp.int32, (experts, block), 0)
    named = row == routes_ref[0:1, :]
    for j in range(1, routes_ref.shape[0]):
        named = named | (row == routes_ref[j : j + 1, :])
    hits = jnp.where(named, 1.0, 0.0).astype(F32)
    before = lax.broadcasted_iota(jnp.int32, (block, block), 0) < lax.broadcasted_iota(jnp.int32, (block, block), 1)
    rank = dot(hits.astype(BF16), jnp.where(before, 1.0, 0.0).astype(BF16))
    hits_ref[...] = hits
    table = jnp.concatenate([jnp.where(named, rank, -1.0), jnp.zeros((16 - experts, block), F32)], axis=0)
    mine_ref[tok:, :] = jnp.concatenate([table, jnp.zeros((16, width - block), F32)], axis=1).astype(BF16)
    for j, ref in enumerate((mine_ref,) + other_refs):
        start = lax.rem(meta_ref[0] + parts - j, parts) * tok
        ref[:tok, :] = cot_ref[pl.ds(pl.multiple_of(start, tok), tok), :]


def prepare(meta, parts, experts, routes_t, cotangent, segments):
    block, width = cotangent.shape
    tok = block // parts
    index = jnp.arange(2 * HD, dtype=jnp.int32)
    rates = (10000.0 ** (-2.0 * (index % (HD // 2)).astype(F32) / HD))[None, :]
    shapes = [
        ((3 * block, 2 * HD), F32), ((3 * block, 2 * HD), F32), ((3 * block, 1), jnp.int32), ((1, block), jnp.int32),
        ((experts, block), F32), ((tok + 16, width), BF16),
    ] + [((tok, width), BF16)] * (parts - 1)
    operands = (routes_t, cotangent, rates, segments)
    return pl.pallas_call(
        functools.partial(prepare_kernel, parts),
        grid_spec=pltpu.PrefetchScalarGridSpec(
            num_scalar_prefetch=1,
            grid=(1,),
            in_specs=[whole(o.shape) for o in operands],
            out_specs=[whole(shape) for shape, _ in shapes],
            scratch_shapes=[pltpu.VMEM((1, segments.shape[1] + 2 * block), jnp.int32)],
        ),
        out_shape=[jax.ShapeDtypeStruct(shape, kind) for shape, kind in shapes],
        compiler_params=params(),
        cost_estimate=cost(3),
    )(meta, *operands)


def bundle_kernel(index_ref, *refs):
    stacks, shared, out_ref = refs[:3], refs[3:-1], refs[-1]
    owned = stacks[0].shape[0]
    for i, ref in enumerate(stacks):
        out_ref[i * owned : (i + 1) * owned] = ref[...]
    if shared:
        units = shared[0].shape[1]
        gate_ref, up_ref, down_ref = shared
        out_ref[3 * owned, :, :units] = gate_ref[...]
        out_ref[3 * owned, :, units:] = up_ref[...]
        out_ref[3 * owned + 1, :, :units] = down_ref[...]
        out_ref[3 * owned + 1, :, units:] = jnp.zeros_like(down_ref)


def bundle(plane, owned, units, stacks, shared):
    _, share, hidden = stacks[0].shape
    count = 3 * owned + 2 * bool(shared)
    return pl.pallas_call(
        bundle_kernel,
        grid_spec=pltpu.PrefetchScalarGridSpec(
            num_scalar_prefetch=1,
            grid=(1,),
            in_specs=[pl.BlockSpec((owned, share, hidden), lambda i, index: (index[0], 0, 0))] * 3
            + [pl.BlockSpec((share, units), lambda i, index: (0, index[1]))] * len(shared),
            out_specs=whole((count, share, hidden)),
        ),
        out_shape=jax.ShapeDtypeStruct((count, share, hidden), BF16),
        compiler_params=params(),
        cost_estimate=cost(3),
    )(jnp.stack([plane, plane % 2]).astype(jnp.int32), *stacks, *shared)


def finish_kernel(meta_ref, mine_ref, *refs):
    count = len(refs) - 6
    pieces = (mine_ref,) + refs[:count]
    k_ref, v_ref, q_ref, o_ref, small_ref, all_ref = refs[count:]
    total = len(pieces)
    rows = mine_ref.shape[0]
    for d, ref in enumerate(pieces):
        all_ref[lax.rem(meta_ref[0] + total - d, total)] = ref[...].astype(F32)
    whole_rows = all_ref[...].reshape(total * rows, mine_ref.shape[1])
    share, cols = k_ref.shape
    for i, ref in enumerate((k_ref, v_ref, q_ref, o_ref)):
        ref[...] = whole_rows[:share, i * cols : (i + 1) * cols]
    small_ref[...] = whole_rows[share : share + 16, : small_ref.shape[1]]


def finish(meta, pieces, share, cols):
    rows, columns = pieces[0].shape
    shapes = [(share, cols)] * 4 + [(16, columns)]
    return pl.pallas_call(
        finish_kernel,
        grid_spec=pltpu.PrefetchScalarGridSpec(
            num_scalar_prefetch=1,
            grid=(1,),
            in_specs=[whole(piece.shape) for piece in pieces],
            out_specs=[whole(shape) for shape in shapes],
            scratch_shapes=[pltpu.VMEM((len(pieces), rows, columns), F32)],
        ),
        out_shape=[jax.ShapeDtypeStruct(shape, F32) for shape in shapes],
        compiler_params=params(),
        cost_estimate=cost(2),
    )(meta, *pieces)


def pack_kernel(lane_ref, k_ref, v_ref, q_ref, router_ref, gains_ref, tok_ref, qkv_ref, small_ref, mine_ref):
    width = k_ref.shape[1]
    for i, ref in enumerate((k_ref, v_ref, q_ref)):
        qkv_ref[:, i * width : (i + 1) * width] = ref[...]
    experts, share = router_ref.shape
    small_ref[...] = jnp.concatenate(
        [router_ref[...].astype(F32), gains_ref[...].astype(F32),
         jnp.zeros((small_ref.shape[0] - experts - 2, share), F32)], axis=0).astype(BF16)
    mine_ref[...] = tok_ref[...]


def pack(lane, parts, key_weight, value_weight, query_weight, router_t, gains, tokens):
    rows, width = tokens.shape
    share, cols = key_weight.shape
    part = (rows // parts, width)
    shapes = [(share, 3 * cols), (16, share), part]
    operands = (key_weight, value_weight, query_weight, router_t, gains)
    return pl.pallas_call(
        pack_kernel,
        grid_spec=pltpu.PrefetchScalarGridSpec(
            num_scalar_prefetch=1,
            grid=(1,),
            in_specs=[whole(o.shape) for o in operands]
            + [pl.BlockSpec(part, lambda i, lane: (lane[0], 0))],
            out_specs=[whole(shape) for shape in shapes],
        ),
        out_shape=[jax.ShapeDtypeStruct(shape, BF16) for shape in shapes],
        compiler_params=params(),
        cost_estimate=cost(2),
    )(lane.astype(jnp.int32)[None], *operands, tokens)


def mask_bias(kseg, qseg, keys, queries):
    key = lax.broadcasted_iota(jnp.int32, (keys, queries), 0)
    query = lax.broadcasted_iota(jnp.int32, (keys, queries), 1)
    allowed = (key > query) & (key <= query + WINDOW) & (kseg == qseg)
    return jnp.where(allowed, 0.0, -1e30).astype(F32)


def head_only(values, head):
    lane = lax.broadcasted_iota(jnp.int32, values.shape, 1)
    return jnp.where(lane // HD == head, values, jnp.zeros_like(values))


def attend_kernel(tile, q_ref, k_ref, v_ref, kseg_ref, qseg_ref, out_ref, lse_ref, bias_ref):
    rows = q_ref.shape[0]
    span = WINDOW + tile
    tiles = rows // tile

    @pl.when(pl.program_id(0) == 0)
    def _():
        for j in range(tiles):
            bias_ref[j] = mask_bias(
                kseg_ref[pl.ds(j * tile, span), :], qseg_ref[:, pl.ds(j * tile, tile)], span, tile
            )

    keys = k_ref[...]
    values_t = v_ref[...].T
    for j in range(tiles):
        start = j * tile
        query = q_ref[pl.ds(start, tile), :]
        parts = []
        for head in range(2):
            scores = dot_nt(keys[start : start + span], head_only(query, head)) + bias_ref[j]
            top = jnp.max(scores, axis=0, keepdims=True)
            expo = jnp.exp(scores - top)
            total = jnp.sum(expo, axis=0, keepdims=True)
            part = dot(
                values_t[head * HD : (head + 1) * HD, start : start + span], expo.astype(BF16)
            )
            parts.append(part / total)
            lse_ref[0, pl.ds(head, 1), pl.ds(start, tile)] = top + jnp.log(total)
        out_ref[pl.ds(start, tile), :] = jnp.concatenate(parts, axis=0).T.astype(BF16)


def attend(query, keys, values, kseg, qseg):
    rows, width = query.shape
    span = keys.shape[0]
    tile = min(256, rows)
    pairs = -(-width // (2 * HD))
    columns = lambda count: pl.BlockSpec((count, 2 * HD), lambda i: (0, i))
    return pl.pallas_call(
        functools.partial(attend_kernel, tile),
        grid=(pairs,),
        in_specs=[columns(rows), columns(span), columns(span), whole((span, 1)), whole((1, rows))],
        out_specs=[columns(rows), pl.BlockSpec((1, 2, rows), lambda i: (i, 0, 0))],
        out_shape=[
            jax.ShapeDtypeStruct((rows, width), BF16),
            jax.ShapeDtypeStruct((pairs, 2, rows), F32),
        ],
        scratch_shapes=[pltpu.VMEM((rows // tile, WINDOW + tile, tile), F32)],
        compiler_params=params(),
        cost_estimate=cost(13),
    )(query, keys, values, kseg, qseg)


def attend_back_kernel(
    tile, q_ref, k_ref, v_ref, g_ref, lse_ref, kseg_ref, qseg_ref, cos_ref, sin_ref,
    dq_ref, dk_ref, dv_ref, bias_ref, dk_acc, dv_acc,
):
    rows = q_ref.shape[0]
    span = WINDOW + tile
    tiles = rows // tile
    total_keys = k_ref.shape[0]

    @pl.when(pl.program_id(0) == 0)
    def _():
        for j in range(tiles):
            bias_ref[j] = mask_bias(
                kseg_ref[pl.ds(j * tile, span), :], qseg_ref[:, pl.ds(j * tile, tile)], span, tile
            )

    keys = k_ref[...]
    values = v_ref[...]
    keys_t = keys.T
    dk_acc[...] = jnp.zeros_like(dk_acc)
    dv_acc[...] = jnp.zeros_like(dv_acc)
    cosine = cos_ref[...]
    sine = sin_ref[...]
    lead = total_keys - rows
    for j in range(tiles):
        start = j * tile
        query = q_ref[pl.ds(start, tile), :]
        grad = g_ref[pl.ds(start, tile), :]
        parts = []
        for head in range(2):
            query_one = head_only(query, head)
            grad_one = head_only(grad, head)
            scores = dot_nt(keys[start : start + span], query_one) + bias_ref[j]
            probs = jnp.exp(scores - lse_ref[0, pl.ds(head, 1), pl.ds(start, tile)])
            grad_probs = dot_nt(values[start : start + span], grad_one)
            delta = jnp.sum(probs * grad_probs, axis=0, keepdims=True)
            grad_scores = (probs * (grad_probs - delta)).astype(BF16)
            dv_acc[pl.ds(start, span), :] += dot(probs.astype(BF16), grad_one)
            dk_acc[pl.ds(start, span), :] += dot(grad_scores, query_one)
            parts.append(
                dot(keys_t[head * HD : (head + 1) * HD, start : start + span], grad_scores)
            )
        dq = jnp.concatenate(parts, axis=0).T * HD**-0.5
        places = pl.ds(lead + start, tile)
        dq_ref[pl.ds(start, tile), :] = (
            dq * cos_ref[places, :] - swap_halves(dq) * sin_ref[places, :]
        ).astype(BF16)
    dk = dk_acc[...]
    dk_ref[...] = (dk * cosine - swap_halves(dk) * sine).astype(BF16)
    dv_ref[...] = dv_acc[...].astype(BF16)


def attend_back(query, keys, values, grad, lse, kseg, qseg, cosine, sine):
    rows, width = query.shape
    span = keys.shape[0]
    tile = min(256, rows)
    pairs = -(-width // (2 * HD))
    columns = lambda count: pl.BlockSpec((count, 2 * HD), lambda i: (0, i))
    return pl.pallas_call(
        functools.partial(attend_back_kernel, tile),
        grid=(pairs,),
        in_specs=[
            columns(rows), columns(span), columns(span), columns(rows),
            pl.BlockSpec((1, 2, rows), lambda i: (i, 0, 0)),
            whole((span, 1)), whole((1, rows)), whole((span, 2 * HD)), whole((span, 2 * HD)),
        ],
        out_specs=[columns(rows), columns(span), columns(span)],
        out_shape=[
            jax.ShapeDtypeStruct((rows, width), BF16),
            jax.ShapeDtypeStruct((span, width), BF16),
            jax.ShapeDtypeStruct((span, width), BF16),
        ],
        scratch_shapes=[
            pltpu.VMEM((rows // tile, WINDOW + tile, tile), F32),
            pltpu.VMEM((span, 2 * HD), F32),
            pltpu.VMEM((span, 2 * HD), F32),
        ],
        compiler_params=params(),
        cost_estimate=cost(18),
    )(query, keys, values, grad, lse, kseg, qseg, cosine, sine)


def expert_kernel(capacity, parts, experts, full, shared, pieces, added, steps, n_saved, meta_ref, *refs):
    w_all, w_sems = refs[-2:]
    owned = w_all.shape[1] // 3
    order = [kind * owned + j for j in range(owned) for kind in range(3)]
    order += list(range(3 * owned, w_all.shape[1]))
    if pieces:
        count = steps * parts
        x_refs, c_refs, refs = refs[:count], refs[count : 2 * count], refs[2 * count :]
        x_all, c_all, t_all = refs[-5:-2]
        tok, width = x_all.shape[1:]
        block = tok * parts
        for j in range(parts):
            spot = lax.rem(meta_ref[1] + parts - j, parts)
            for i in range(steps):

                @pl.when(pl.program_id(0) == i)
                def _():
                    x_all[spot] = x_refs[i * parts + j][...]
                    c_all[spot] = c_refs[i * parts + j][:tok]
                    if j == 0:
                        t_all[...] = c_refs[i * parts][tok:]

        inputs = x_all[...].reshape(block, width)
        cot = c_all[...].reshape(block, width)
        low_table = t_all[...]
    else:
        x_ref, c_ref = refs[:2]
        refs = refs[2:]
        block, width = x_ref.shape[1:]
        tok = block // parts
        inputs = x_ref[0]
        cot = c_ref[0, :block]
        low_table = c_ref[0, block:]
    w_ref, rt_ref = refs[:2]
    refs = refs[2:]

    def weight_copy(which):
        return pltpu.make_async_copy(w_ref.at[:, which], w_all.at[:, which], w_sems.at[which])

    @pl.when(pl.program_id(0) == 0)
    def _():
        for j in range(w_all.shape[1]):
            weight_copy(order[j]).start()

    if added:
        more_dx_ref, more_out_ref = refs[:2]
        refs = refs[2:]
    refs = refs[n_saved:]
    if full:
        dx_ref, out_ref = refs[:2]
        refs = refs[2:]
    sx_ref, sr_ref, sh_ref, sa_ref, sb_ref = refs[:5]
    if shared:
        ssh_ref, ssa_ref, ssb_ref = refs[5:8]
    if pieces:
        ssx_ref, ssc_ref = refs[5:7]
        ssx_ref[0] = inputs
        ssc_ref[0, :block] = cot
        ssc_ref[0, block:] = low_table
    hidden = w_ref.shape[3]
    table = low_table[:, :block].astype(F32)[:experts]

    def weights(which):
        @pl.when(pl.program_id(0) == 0)
        def _():
            weight_copy(which).wait()

        return w_all[:, which].reshape(width, hidden)

    logits = dot_nt(rt_ref[...], inputs)[:experts]
    named = table >= 0.0
    top = jnp.max(jnp.where(named, logits, -1e30), axis=0, keepdims=True)
    expo = jnp.where(named, jnp.exp(logits - top), 0.0)
    gates = expo / jnp.sum(expo, axis=0, keepdims=True)
    row = lax.broadcasted_iota(jnp.int32, (experts, block), 0)
    slot = lax.broadcasted_iota(jnp.int32, (capacity, block), 0).astype(F32)
    hits, spreads, gate_slots = [], [], []
    for j in range(owned):
        mine = row == meta_ref[0] + j
        gate = jnp.sum(jnp.where(mine, gates, 0.0), axis=0, keepdims=True)
        position = jnp.sum(jnp.where(mine, table, 0.0), axis=0, keepdims=True)
        hit = slot == position
        hits.append(hit)
        spreads.append(jnp.where(hit, 1.0, 0.0).astype(BF16))
        gate_slots.append(jnp.sum(jnp.where(hit, gate, 0.0), axis=1, keepdims=True))
    spread = jnp.concatenate(spreads, axis=0)
    routed = dot(spread, inputs).astype(BF16)
    cots = dot(spread, cot)
    gate_slots = jnp.concatenate(gate_slots, axis=0)
    grads = (gate_slots * cots).astype(BF16)

    def branch(left, right, gate_weights, up_weights, down_weights):
        gating = dot(left, gate_weights)
        linear = dot(left, up_weights)
        sigma = jax.nn.sigmoid(gating)
        silu = gating * sigma
        active = (silu * linear).astype(BF16)
        grad_active = dot(right, down_weights)
        slope = sigma * (1.0 + gating * (1.0 - sigma))
        grad_gating = (grad_active * linear * slope).astype(BF16)
        grad_linear = (grad_active * silu).astype(BF16)
        if not full:
            return active, grad_gating, grad_linear
        result = dot_nt(active, down_weights)
        grad_left = dot_nt(grad_gating, gate_weights) + dot_nt(grad_linear, up_weights)
        return active, grad_gating, grad_linear, result, grad_left

    weighted = []
    gate_lines = []
    for j in range(owned):
        rows = slice(j * capacity, (j + 1) * capacity)
        sx_ref[0, j] = routed[rows]
        sr_ref[0, j] = grads[rows]
        got = branch(
            routed[rows], grads[rows], weights(j), weights(owned + j), weights(2 * owned + j))
        sh_ref[0, j], sa_ref[0, j], sb_ref[0, j] = got[:3]
        if full:
            result, grad_left = got[3:]
            grad_gates = jnp.sum(result * cots[rows], axis=1, keepdims=True)
            gate_lines.append(jnp.sum(jnp.where(hits[j], grad_gates, 0.0), axis=0, keepdims=True))
            weighted.append(jnp.concatenate(
                [(gate_slots[rows] * result).astype(BF16), grad_left.astype(BF16)], axis=1))
    if shared:
        units = ssh_ref.shape[2]
        first, second = weights(3 * owned), weights(3 * owned + 1)
        got = branch(inputs, cot, first[:, :units], first[:, units : 2 * units], second[:, :units])
        ssh_ref[0], ssa_ref[0], ssb_ref[0] = got[:3]
    if not full:
        return
    back = dot_tn(spread, jnp.concatenate(weighted, axis=0))
    out, dx = back[:, :width], back[:, width:]
    if shared:
        out = out + got[3]
        dx = dx + got[4]
    line = lax.broadcasted_iota(jnp.int32, (16, width), 0)
    for j in range(parts):
        piece = slice(j * tok, (j + 1) * tok)
        spare = jnp.zeros((1, width - tok), F32)
        extra = jnp.zeros((16, width), F32)
        for i in range(owned):
            padded = jnp.concatenate([gate_lines[i][:, piece], spare], axis=1)
            extra = jnp.where(line == meta_ref[0] + i, padded, extra)
        out_piece, dx_piece = out[piece], dx[piece]
        if added:
            out_piece = out_piece + more_out_ref[0, j].astype(F32)
            dx_piece = dx_piece + more_dx_ref[0, j, :tok].astype(F32)
            extra = extra + more_dx_ref[0, j, tok:].astype(F32)
        out_ref[0, j] = out_piece.astype(BF16)
        dx_ref[0, j, :tok] = dx_piece.astype(BF16)
        dx_ref[0, j, tok:] = extra.astype(BF16)


def expert_shapes(owned, capacity, width, hidden):
    return [(owned, capacity, width)] * 2 + [(owned, capacity, hidden)] * 3


def placed(shape, where):
    return pl.BlockSpec((1,) + shape, lambda i, meta: (where(i, meta),) + (0,) * len(shape))


def expert_blocks(
    first, blocks, steps, capacity, parts, experts, units, full, meta, sources, weights, router_t, more, saved,
):
    pieces = isinstance(sources[0], list)
    shared = units > 0
    if pieces:
        tok, width = sources[0][0][0].shape
    else:
        block, width = sources[0].shape[1:]
        tok = block // parts
    block = tok * parts
    hidden = weights.shape[3]
    owned = weights.shape[1] // 3
    here = lambda i, meta: first + i
    step = lambda i, meta: i
    shapes = expert_shapes(owned, capacity, width, hidden)
    if shared:
        shapes += [(block, units)] * 3
    if pieces:
        shapes += [(block, width), (block + 16, width)]
    tops = [(parts, tok + 16, width), (parts, tok, width)] if full else []
    outs = [jax.ShapeDtypeStruct((blocks // 2,) + shape, BF16) for shape in tops]
    outs += [jax.ShapeDtypeStruct((blocks,) + shape, BF16) for shape in shapes]
    specs = [placed(shape, here) for shape in tops + shapes]
    if pieces:
        operands = [piece for source in sources for block_pieces in source for piece in block_pieces]
        in_specs = [whole(one.shape) for one in operands]
        scratch = [pltpu.VMEM((parts, tok, width), BF16)] * 2 + [pltpu.VMEM((16, width), BF16)]
    else:
        operands = list(sources)
        in_specs = [placed(one.shape[1:], here) for one in operands]
        scratch = []
    scratch += [pltpu.VMEM(weights.shape, BF16), pltpu.SemaphoreType.DMA((weights.shape[1],))]
    operands += [weights, router_t] + list(more)
    in_specs += [pl.BlockSpec(memory_space=pl.ANY), whole(router_t.shape)] + [placed(one.shape[1:], step) for one in more]
    in_specs += [pl.BlockSpec(memory_space=pl.ANY)] * len(saved)
    return pl.pallas_call(
        functools.partial(
            expert_kernel, capacity, parts, experts, full, shared, pieces, len(more) > 0, steps, len(saved)),
        grid_spec=pltpu.PrefetchScalarGridSpec(
            num_scalar_prefetch=1,
            grid=(steps,),
            in_specs=in_specs,
            out_specs=specs,
            scratch_shapes=scratch,
        ),
        out_shape=outs,
        input_output_aliases={1 + len(operands) + i: i for i in range(len(saved))},
        compiler_params=params(),
        cost_estimate=cost((12 if full else 6) * steps),
    )(meta, *operands, *saved)


def pair_sums_kernel(counts, index_ref, *refs):
    outs = refs[len(refs) - len(counts) :]
    for count, out_ref in zip(counts, outs):
        job, refs = refs[:count], refs[count:]
        total = job[0][0].astype(F32) + job[1][0].astype(F32)
        for ref in job[2:]:
            total = total + ref[...].astype(F32)
        out_ref[...] = total.astype(BF16)


def pair_sums(jobs):
    cut = all(kept.ndim == 4 for _, kept, _, _ in jobs)
    operands, in_specs, out_specs, out_shape = [], [], [], []
    for n, (_, kept, got, far) in enumerate(jobs):
        shape = kept.shape[1:]
        part = ((1,) if cut else shape[:1]) + shape[1:]
        rest = (0,) * (len(shape) - 1)
        picked = pl.BlockSpec((1,) + part, lambda i, index, n=n, rest=rest: (index[n], i) + rest)
        plain = pl.BlockSpec(part, lambda i, index, rest=rest: (i,) + rest)
        operands += [kept, got, *far]
        in_specs += [picked, picked] + [plain] * len(far)
        out_specs.append(plain)
        out_shape.append(jax.ShapeDtypeStruct(shape, BF16))
    return pl.pallas_call(
        functools.partial(pair_sums_kernel, [2 + len(far) for _, _, _, far in jobs]),
        grid_spec=pltpu.PrefetchScalarGridSpec(
            num_scalar_prefetch=1,
            grid=(jobs[0][1].shape[1] if cut else 1,),
            in_specs=in_specs,
            out_specs=out_specs,
        ),
        out_shape=out_shape,
        compiler_params=params(),
        cost_estimate=cost(3),
    )(jnp.stack([index for index, _, _, _ in jobs]).astype(jnp.int32), *operands)


def attn_pieces_kernel(meta_ref, kept_ref, got_ref, small_ref, *refs):
    count = len(refs) - 1
    far_refs, out_refs, all_ref = refs[: count - 4], refs[count - 4 : count], refs[-1]
    total = kept_ref[0].astype(F32) + got_ref[0].astype(F32)
    for ref in far_refs:
        total = total + ref[...].astype(F32)
    share, columns = total.shape
    all_ref[:share] = total
    all_ref[share:] = jnp.zeros((all_ref.shape[0] - share, columns), F32)
    all_ref[share : share + small_ref.shape[0], : small_ref.shape[1]] = small_ref[...]
    rows = out_refs[0].shape[0]
    for d, ref in enumerate(out_refs):
        first = lax.rem(meta_ref[1] + d, 4) * rows
        ref[...] = all_ref[pl.ds(pl.multiple_of(first, 8), rows)].astype(BF16)


def attn_pieces(pair, plane, kept, got, far, small):
    share, columns = kept.shape[1:]
    rows = (share + 32) // 4
    picked = pl.BlockSpec((1, share, columns), lambda i, meta: (meta[0], 0, 0))
    return pl.pallas_call(
        attn_pieces_kernel,
        grid_spec=pltpu.PrefetchScalarGridSpec(
            num_scalar_prefetch=1,
            grid=(1,),
            in_specs=[picked, picked, whole(small.shape)] + [whole(one.shape) for one in far],
            out_specs=[whole((rows, columns))] * 4,
            scratch_shapes=[pltpu.VMEM((4 * rows, columns), F32)],
        ),
        out_shape=[jax.ShapeDtypeStruct((rows, columns), BF16)] * 4,
        compiler_params=params(),
        cost_estimate=cost(3),
    )(jnp.stack([pair, plane]).astype(jnp.int32), kept, got, small, *far)


def split_rows(value, core, sent_ref, kept_ref, *at):
    pairs = sent_ref.shape[0]
    share = value.shape[0] // (2 * pairs)
    for q in range(pairs):
        first = value[2 * q * share : (2 * q + 1) * share].astype(BF16)
        second = value[(2 * q + 1) * share : (2 * q + 2) * share].astype(BF16)
        index = (q,) + at
        kept_ref[index] = jnp.where(core == 0, first, second)
        sent_ref[index] = jnp.where(core == 0, second, first)


def weight_kernel(count, core_ref, left_ref, *refs):
    steps, _, slots, rows = left_ref.shape
    left = left_ref[...].reshape(steps * slots, rows)
    for n, right_ref in enumerate(refs[:count]):
        right = right_ref[...].reshape(steps * slots, right_ref.shape[3])
        split_rows(dot_tn(left, right), core_ref[0], *refs[count + 2 * n : count + 2 * n + 2], 0)


def weight_grads(core, left, rights, pairs):
    steps, owned, slots, width = left.shape
    columns = rights[0].shape[3]
    share = width // (2 * pairs)
    shape = jax.ShapeDtypeStruct((pairs, owned, share, columns), BF16)
    spec = pl.BlockSpec((pairs, 1, share, columns), lambda j, core: (0, j, 0, 0))
    given = pl.pallas_call(
        functools.partial(weight_kernel, len(rights)),
        grid_spec=pltpu.PrefetchScalarGridSpec(
            num_scalar_prefetch=1,
            grid=(owned,),
            in_specs=[
                pl.BlockSpec((steps, 1, slots, one.shape[3]), lambda j, core: (0, j, 0, 0))
                for one in [left, *rights]
            ],
            out_specs=[spec] * (2 * len(rights)),
        ),
        out_shape=[shape] * (2 * len(rights)),
        compiler_params=params(),
        cost_estimate=cost(5 * len(rights)),
    )(core, left, *rights)
    return [given[2 * n : 2 * n + 2] for n in range(len(rights))]


def shared_grad_kernel(core_ref, x_ref, c_ref, a_ref, b_ref, h_ref, sent_ref, kept_ref, total_ref):
    step = pl.program_id(0)
    block, units = a_ref.shape[1:]

    @pl.when(step == 0)
    def _():
        total_ref[...] = jnp.zeros_like(total_ref)

    total_ref[:, :units] += dot_tn(x_ref[0], a_ref[0])
    total_ref[:, units : 2 * units] += dot_tn(x_ref[0], b_ref[0])
    total_ref[:, 2 * units :] += dot_tn(c_ref[0, :block], h_ref[0])

    @pl.when(step == pl.num_programs(0) - 1)
    def _():
        split_rows(total_ref[...], core_ref[0], sent_ref, kept_ref)


def shared_grads(core, x, c, a, b, h, pairs):
    operands = (x, c, a, b, h)
    width, units = x.shape[2], a.shape[2]
    shape = jax.ShapeDtypeStruct((pairs, width // (2 * pairs), 3 * units), BF16)
    return pl.pallas_call(
        shared_grad_kernel,
        grid_spec=pltpu.PrefetchScalarGridSpec(
            num_scalar_prefetch=1,
            grid=(x.shape[0],),
            in_specs=[pl.BlockSpec((1,) + o.shape[1:], lambda i, core: (i, 0, 0)) for o in operands],
            out_specs=[whole(shape.shape), whole(shape.shape)],
            scratch_shapes=[pltpu.VMEM((width, 3 * units), F32)],
        ),
        out_shape=[shape, shape],
        compiler_params=params(),
        cost_estimate=cost(8),
    )(core, *operands)


def attn_grad_kernel(core_ref, hid_ref, dk_ref, dv_ref, dq_ref, gm_ref, at_ref, sent_ref, kept_ref):
    lead = hid_ref.shape[0] - dq_ref.shape[0]
    value = jnp.concatenate(
        [
            dot_tn(hid_ref[...], dk_ref[...]),
            dot_tn(hid_ref[...], dv_ref[...]),
            dot_tn(hid_ref[lead:, :], dq_ref[...]),
            dot_tn(gm_ref[...], at_ref[...]),
        ],
        axis=1,
    )
    split_rows(value, core_ref[0], sent_ref, kept_ref)


def attn_grads_of(core, hid, dk, dv, dq, grad_mixed_low, attended, pairs):
    width, cols = hid.shape[1], dk.shape[1]
    shape = jax.ShapeDtypeStruct((pairs, width // (2 * pairs), 4 * cols), BF16)
    operands = (hid, dk, dv, dq, grad_mixed_low, attended)
    return pl.pallas_call(
        attn_grad_kernel,
        grid_spec=pltpu.PrefetchScalarGridSpec(
            num_scalar_prefetch=1,
            grid=(1,),
            in_specs=[whole(o.shape) for o in operands],
            out_specs=[whole(shape.shape), whole(shape.shape)],
        ),
        out_shape=[shape, shape],
        compiler_params=params(),
        cost_estimate=cost(8),
    )(core, *operands)


def hidden_back_kernel(count, *refs):
    sources = refs[:count]
    dk_ref, dv_ref, dq_ref, w_ref = refs[count : count + 4]
    out_refs, gain_ref = refs[count + 4 : -1], refs[-1]
    cols = dk_ref.shape[1]
    step = pl.program_id(0)

    @pl.when(step == 0)
    def _():
        gain_ref[...] = jnp.zeros_like(gain_ref)

    for i, tok_ref in enumerate(sources):

        @pl.when(step == i)
        def _():
            grad = dot_nt(dk_ref[...], w_ref[:, :cols]) + dot_nt(dv_ref[...], w_ref[:, cols : 2 * cols])
            if i == count - 1:
                grad = grad + dot_nt(dq_ref[...], w_ref[:, 2 * cols : 3 * cols])
            out_refs[i][...] = grad.astype(BF16)
            inputs = tok_ref[...].astype(F32)
            scale = lax.rsqrt(jnp.mean(inputs * inputs, axis=-1, keepdims=True) + EPS)
            gain_ref[...] += jnp.sum(grad * (inputs * scale), axis=0, keepdims=True)


def hidden_back(sources, dk, dv, dq, weights):
    count = len(sources)
    rows, width = sources[0].shape
    cols = dk.shape[1]
    part = pl.BlockSpec((rows, cols), lambda i: (i, 0))
    return pl.pallas_call(
        functools.partial(hidden_back_kernel, count),
        grid=(count,),
        in_specs=[whole((rows, width))] * count
        + [part, part, whole((rows, cols)), whole(weights.shape)],
        out_specs=[whole((rows, width))] * count + [whole((1, width))],
        out_shape=[jax.ShapeDtypeStruct((rows, width), BF16)] * count + [jax.ShapeDtypeStruct((1, width), F32)],
        compiler_params=params(),
        cost_estimate=cost(7),
    )(*sources, dk, dv, dq, weights)


def collect_kernel(places_ref, first_ref, second_ref, out_ref):
    for half, ref in enumerate((first_ref, second_ref)):

        @pl.when(pl.program_id(0) // (pl.num_programs(0) // 2) == half)
        def _():
            out_ref[...] = ref[0].astype(F32)


def collect(places, first, second):
    _, owned, rows, columns = first.shape
    half = 2 * owned
    block = (1, rows, columns)

    def part(start):
        def index(step, places):
            local = jnp.clip(step - start, 0, half - 1)
            return (local // owned, local % owned, 0, 0)

        return pl.BlockSpec((1,) + block, index)

    return pl.pallas_call(
        collect_kernel,
        grid_spec=pltpu.PrefetchScalarGridSpec(
            num_scalar_prefetch=1,
            grid=(2 * half,),
            in_specs=[part(0), part(half)],
            out_specs=pl.BlockSpec(
                block, lambda step, places: (places[step // half] * half + step % half, 0, 0)),
        ),
        out_shape=jax.ShapeDtypeStruct((2 * half, rows, columns), F32),
        compiler_params=params(),
        cost_estimate=cost(5),
    )(places, first, second)


def norm_back(grad, values, scale, gain):
    grad_gain = jnp.sum(grad * values * scale, axis=0)
    scaled = grad * gain
    grad_values = scale * scaled - values * scale * scale * scale * jnp.mean(
        scaled * values, axis=-1, keepdims=True
    )
    return grad_values, grad_gain


def local(
    tokens,
    segments,
    routes,
    query_weight,
    key_weight,
    value_weight,
    out_weight,
    attn_gain,
    ffn_gain,
    router_weight,
    shared_gate,
    shared_up,
    shared_down,
    expert_gate,
    expert_up,
    expert_down,
    cotangent,
):
    fsdp, ctx, tp = (lax.axis_size(a) for a in ("fsdp", "ctx", "tp"))
    pairs = fsdp // 2
    me = lax.axis_index("fsdp")
    pair, core = me // 2, me % 2
    plane = lax.axis_index("ctx")
    lane = lax.axis_index("tp")
    tokens, cotangent, routes = tokens[0], cotangent[0], routes[0]
    block, width = tokens.shape
    share, cols = query_weight.shape
    experts = expert_gate.shape[0]
    hidden_units = expert_gate.shape[2]
    units = shared_gate.shape[1] // 2
    owned = experts // ctx
    top_count = routes.shape[1]
    capacity = 3 * top_count * block // (2 * experts)
    tok = block // tp
    core_index = core.astype(jnp.int32)[None]

    phases = Phases()

    def to_pairs(piece):
        return [pair_shift(piece, d) for d in range(1, pairs)]

    def to_tp(piece):
        return [tp_shift(piece, j) for j in range(1, tp)]

    def joined(*pieces):
        return place(pieces, lane).reshape(block, width)

    other_plane = plane ^ 2

    gains = jnp.concatenate([attn_gain[None], ffn_gain[None]], axis=0)
    qkv_mine, small_mine, tokens_mine = pack(
        lane, tp, key_weight, value_weight, query_weight, router_weight.T, gains, tokens)
    small_core = core_swap(small_mine)
    qkv_mine, small_mine, tokens_mine, small_core = phases.run(
        lambda *given: given, qkv_mine, small_mine, tokens_mine, small_core)

    prepare_meta = jnp.stack([lane, plane]).astype(jnp.int32)

    def send_first(qkv, small, small_core, tokens_mine, cotangent):
        prepared = prepare(prepare_meta, tp, experts, routes.T, cotangent, segments)
        return (
            to_pairs(qkv), core_swap(qkv), to_pairs(jnp.concatenate([small, small_core], axis=0)),
            ctx_open(tokens_mine, 1),
            prepared)

    qkv_far, qkv_core, small_far, prev_one_mine, prepared = phases.run(
        send_first, qkv_mine, small_mine, small_core, tokens_mine, cotangent)
    cosine, sine, kseg, qseg, hits = prepared[:5]
    cot_own = prepared[5:]
    gathered = small_mine, small_core, small_far

    def all_small(small_mine, small_core, small_far):
        rows = place([jnp.concatenate([small_mine, small_core], axis=0)] + small_far, pair)
        rows = rows.reshape(pairs, 2, 16, share)
        rows = jnp.where(core == 0, rows, rows[:, ::-1])
        return rows.reshape(fsdp, 16, share).transpose(1, 0, 2).reshape(16, width)

    def send_second(qkv_far, prev_one_mine, out_weight, gathered, *stacks):
        return (
            [core_swap(one) for one in qkv_far], to_tp(prev_one_mine), ctx_open(prev_one_mine, 1),
            to_pairs(out_weight.T), all_small(*gathered), bundle(plane, owned, units, stacks, []))

    qkv_far_core, prev_one_other, prev_two_mine, out_far, small_all, weights_mine = phases.run(
        send_second, qkv_far, prev_one_mine, out_weight, gathered, expert_gate, expert_up,
        jnp.swapaxes(expert_down, 1, 2))
    weights = lax.all_gather(weights_mine, "fsdp", axis=0)
    attn_scale = small_all[experts : experts + 1].astype(F32)
    ffn_scale = small_all[experts + 1 : experts + 2].astype(F32)
    router_t = jnp.concatenate([small_all[:experts], jnp.zeros((16 - experts, width), BF16)], axis=0)
    router_full = small_all[:experts].T
    here = [(plane + d) % ctx for d in range(ctx)]
    half = ctx // 2
    place_meta = jnp.stack([lane, pair, core]).astype(jnp.int32)

    def near_projection(prev_one_mine, prev_one_other, prev_two_mine, cot, out_weight, out_far, same, cross, scale):
        sent = (
            to_tp(prev_two_mine), ctx_swap(cot), [core_swap(one) for one in [out_weight.T] + out_far])
        return sent, project_near(
            place_meta, tokens, [prev_one_mine] + prev_one_other, same, cross, scale, cosine, sine)

    (prev_two_other, cot_one, out_cross), first = phases.run(
        near_projection, prev_one_mine, prev_one_other, prev_two_mine, cot_own[0], out_weight, out_far,
        [qkv_mine] + qkv_far, [qkv_core] + qkv_far_core, attn_scale)
    query, qkv_full, prev_one = first[3:]

    def attention(prev_two_mine, prev_two_other, cot, cot_one, out_weight, out_far, out_cross):
        sent = ctx_swap(cot, 2), to_tp(cot_one)
        hid, keys, values, prev_two = project_far(
            place_meta, [prev_two_mine] + prev_two_other, qkv_full, attn_scale, cosine, sine, first[:3])
        attended, lse = attend(query, keys, values, kseg, qseg)
        same = place([out_weight.T] + out_far, pair)
        cross = place(out_cross, pair)
        out_full = place_rows([same, cross], core).reshape(width, cols)
        partial = dot_nt(attended, out_full).astype(BF16).reshape(tp, tok, width)
        return sent, hid, keys, values, prev_two, attended, lse, out_full, partial

    (cot_two, cot_one_other), hid, keys, values, prev_two, attended, lse, out_full, partial = phases.run(
        attention, prev_two_mine, prev_two_other, cot_own[0], cot_one, out_weight, out_far, out_cross)

    def sent_tp(total):
        return [tp_shift(pick(total, (lane + j) % tp), j) for j in range(1, tp)]

    def sum_tp(total, got):
        result = pick(total, lane).astype(F32)
        for one in got:
            result = result + one.astype(F32)
        return result

    def after_attention(partial, cot_two, *stacks):
        return sent_tp(partial), ctx_swap(cot_two), bundle(other_plane, owned, units, stacks[:3], stacks[3:])

    partial_other, cot_three, again_mine = phases.run(
        after_attention, partial, cot_two, expert_gate, expert_up, jnp.swapaxes(expert_down, 1, 2), shared_gate,
        shared_up, shared_down.T)
    other_weights = lax.all_gather(again_mine, "fsdp", axis=0)
    inputs_mine = tokens_mine.astype(F32)

    def normalize(partial, got):
        mixed = inputs_mine + sum_tp(partial, got)
        scale_ffn = lax.rsqrt(jnp.mean(mixed * mixed, axis=-1, keepdims=True) + EPS)
        return (mixed * scale_ffn * ffn_scale).astype(BF16), mixed, scale_ffn

    normed_low, mixed, scale_ffn = phases.run(normalize, partial, partial_other)

    x_zero, x_one = phases.run(lambda one: (to_tp(one), ctx_swap(one)), normed_low)
    half = ctx // 2
    near_meta = jnp.stack([owned * plane, lane]).astype(jnp.int32)
    far_meta = jnp.stack([owned * other_plane, lane]).astype(jnp.int32)

    def joint(mine, other):
        return [[one] + list(two) for one, two in zip(mine, other)]

    def blocks_of(first, steps, full, meta, with_units, sources, weights, more, saved):
        return expert_blocks(
            first, ctx, steps, capacity, tp, experts, with_units, full, meta, sources, weights, router_t, more, saved)

    def own_step(first, full, weights, x_pieces, cot_pieces, saved):
        return blocks_of(first, 1, full, near_meta, 0, ([x_pieces], [cot_pieces]), weights, [], saved)

    def block_zero(normed_low, x_zero, cot_own, x_one, cot_two, weights):
        sent = to_tp(x_one), ctx_swap(normed_low, 2), to_tp(cot_two)
        return sent, own_step(0, True, weights, [normed_low] + x_zero, cot_own, [])

    (other_one, x_two, cot_two_other), saved = phases.run(
        block_zero, normed_low, x_zero, cot_own, x_one, cot_two, weights)

    def block_one(x_one, other_one, cot_one, cot_one_other, x_two, cot_three, weights, saved):
        sent = to_tp(x_two), ctx_swap(x_two), to_tp(cot_three)
        return sent, own_step(1, True, weights, [x_one] + other_one, [cot_one] + cot_one_other, saved)

    (other_two, x_three, cot_three_other), saved = phases.run(
        block_one, x_one, other_one, cot_one, cot_one_other, x_two, cot_three, weights, saved)
    more = saved[:2]

    def block_two(x_two, other_two, cot_two, cot_two_other, x_three, weights, saved):
        sent = to_tp(x_three)
        return sent, own_step(2, False, weights, [x_two] + other_two, [cot_two] + cot_two_other, saved)

    other_three, saved = phases.run(
        block_two, x_two, other_two, cot_two, cot_two_other, x_three, weights, saved[2:])

    def weight_step(left, right):
        return weight_grads(core_index, left, [right], pairs)[0]

    def weight_pair(left, one, two):
        return weight_grads(core_index, left, [one, two], pairs)

    def own_rest(x_three, other_three, cot_three, cot_three_other, weights, saved):
        saved = own_step(3, False, weights, [x_three] + other_three, [cot_three] + cot_three_other, saved)
        sx, sr, sh, sa, sb = saved[:5]
        down = weight_step(sr, sh)
        return saved, down, core_swap(down[0]), *weight_pair(sx, sa, sb)

    saved, down, down_got, gate, up = phases.run(
        own_rest, x_three, other_three, cot_three, cot_three_other, weights, saved)
    sx, sr, sh, sa, sb, ssx, ssc = saved


    def sums(sent, *own):
        jobs = [((pair + j) % pairs, *sent, []) for j in range(1, pairs)] if sent else []
        given = pair_sums(jobs + [(pair, *one) for one in own])
        return [given[: len(jobs)], *given[len(jobs) :]]

    def sent_pairs(rows):
        return [pair_shift(one, j + 1) for j, one in enumerate(rows)]

    def other_full(down, gate_sent, up_sent, ssx, other_weights, more):
        sent = sent_pairs(sums(down)[0]), core_swap(gate_sent), core_swap(up_sent)
        return sent, blocks_of(0, half, True, far_meta, units, (ssx, ssc), other_weights, more, [])

    (down_far, gate_got, up_got), got = phases.run(
        other_full, (down[1], down_got), gate[0], up[0], ssx, other_weights, more)
    dx, out = (one.reshape((half * tp,) + one.shape[2:]) for one in got[:2])

    def sent_tp_of(stack, block_index):
        return [tp_shift(pick(stack, block_index * tp + (lane + j) % tp), j) for j in range(1, tp)]

    def sum_tp_of(stack, block_index, far):
        result = pick(stack, block_index * tp + lane).astype(F32)
        for one in far:
            result = result + one.astype(F32)
        return result

    def back_through_norm(dx_sum):
        grad_normed = dx_sum[:tok]
        grad_gates = dx_sum[tok : tok + experts, :tok].T
        named = lax.dynamic_slice_in_dim(hits, lane * tok, tok, 1).T > 0.0
        logits = jnp.where(named, dot(normed_low, router_full), -1e30)
        expo = jnp.where(named, jnp.exp(logits - jnp.max(logits, axis=-1, keepdims=True)), 0.0)
        gates = expo / jnp.sum(expo, axis=-1, keepdims=True)
        grad_logits = (
            gates * (grad_gates - jnp.sum(gates * grad_gates, axis=-1, keepdims=True))
        ).astype(BF16)
        grad_normed = grad_normed + dot_nt(grad_logits, router_full)
        grad_mixed_norm, grad_ffn_gain = norm_back(grad_normed, mixed, scale_ffn, ffn_scale)
        grad_out = lax.dynamic_slice_in_dim(cotangent, lane * tok, tok, 0).astype(F32)
        grad_mixed = grad_out + grad_mixed_norm
        return grad_mixed.astype(BF16), grad_mixed, grad_ffn_gain, dot_tn(grad_logits, normed_low)

    def phase_one(gate, dx, down, ssx, saved):
        rows, own_down = sums(gate, down)
        sent = sent_pairs(rows), sent_tp_of(dx, 1), sent_tp_of(dx, 0)
        saved = blocks_of(half, half, False, far_meta, units, (ssx, ssc), other_weights, [], saved)
        return sent, saved, weight_step(saved[1], saved[2]), own_down

    (gate_far, dx_one, dx_zero), other_saved, other_down, own_down = phases.run(
        phase_one, (gate[1], gate_got), dx, (down[1], down_got, down_far), ssx, got[2:])
    ox, orr, oh, oa, ob, ssh, ssa, ssb = other_saved
    groups = [[2 * i, 2 * i + 1] for i in range(ctx // 2)]

    def neighbours(piece):
        return lax.all_gather(piece, "ctx", axis=0, axis_index_groups=groups)

    both_down = neighbours(own_down)

    def phase_two(up, down_sent, dx, dx_one, gate, ox, out):
        rows, own_gate = sums(up, gate)
        sent = (
            sent_pairs(rows), core_swap(down_sent),
            ctx_swap(sum_tp_of(dx, 1, dx_one).astype(BF16)), sent_tp_of(out, 1))
        other_gate, other_up = weight_pair(ox, oa, ob)
        return sent, own_gate, other_gate, other_up

    (up_far, down_got, home, out_one), own_gate, other_gate, other_up = phases.run(
        phase_two, (up[1], up_got), other_down[0], dx, dx_one, (gate[1], gate_got, gate_far), ox, out)

    both_gate = neighbours(own_gate)

    def phase_three(down, gate_sent, both, dx, dx_zero, home, up, ssx, out, out_one):
        back = back_through_norm(sum_tp_of(dx, 0, dx_zero) + home.astype(F32))
        rows, own_up = sums(down, up)
        sent = (
            sent_pairs(rows), core_swap(gate_sent), to_tp(back[0]), ctx_swap(sum_tp_of(out, 1, out_one).astype(BF16)))
        shared = shared_grads(core_index, ssx, ssc, ssa, ssb, ssh, pairs)
        return sent, back, own_up, shared, both

    sent, back, own_up, shared, both_down = phases.run(
        phase_three, (other_down[1], down_got), other_gate[0], both_down, dx, dx_zero, home, (up[1], up_got, up_far), ssx,
        out, out_one)
    down_far, gate_got, grad_mixed_other, out_home = sent
    both_up = neighbours(own_up)
    grad_mixed_low, grad_mixed, grad_ffn_gain, grad_router = back

    def phase_four(gate, up_sent, shared_sent, both, down, grad_mixed_low, grad_mixed_other, out):
        summed, own_other_down = sums(gate, down)
        sent = sent_pairs(summed), core_swap(up_sent), core_swap(shared_sent), sent_tp_of(out, 0)
        rows = joined(grad_mixed_low, *grad_mixed_other)
        grad_attended = dot(rows, out_full).astype(BF16)
        grads = attend_back(query, keys, values, grad_attended, lse, kseg, qseg, cosine, sine)
        return sent, rows, grads, own_other_down, both

    (gate_far, up_got, shared_got, out_zero), grad_mixed_rows, (dq, dk, dv), own_other_down, both_gate = phases.run(
        phase_four, (other_gate[1], gate_got), other_up[0], shared[0], both_gate,
        (other_down[1], down_got, down_far), grad_mixed_low, grad_mixed_other, out)

    both_other_down = neighbours(own_other_down)

    def phase_five(up, both, dq, dk, dv, hid, gate):
        back = hidden_back([prev_two, prev_one, tokens], dk, dv, dq, qkv_full)
        hidden_parts = [one.reshape(tp, tok, width) for one in back[:-1]]
        small_rows = jnp.concatenate(
            [grad_router, grad_ffn_gain[None], back[-1], jnp.zeros((16 - experts - 2, width), F32)], axis=0)
        rows, own_other_gate = sums(up, gate)
        sent = sent_pairs(rows), all_sum(small_rows, "tp"), sent_tp(hidden_parts[0])
        attn = attn_grads_of(core_index, hid, dk, dv, dq, grad_mixed_rows, attended, pairs)
        return sent, hidden_parts, attn, own_other_gate, both

    (up_far, small_rows, far_two), hidden_parts, attn, own_other_gate, both_up = phases.run(
        phase_five, (other_up[1], up_got), both_up, dq, dk, dv, hid,
        (other_gate[1], gate_got, gate_far))

    both_other_gate = neighbours(own_other_gate)
    places = jnp.stack([plane // 2, 1 - plane // 2]).astype(jnp.int32)

    def phase_six(attn_sent, both, shared, hidden_parts, far_two, small_rows, up):
        rows, own_other_up = sums(shared, up)
        sent = (
            core_swap(attn_sent), sent_pairs(rows),
            ctx_open(sum_tp(hidden_parts[0], far_two).astype(BF16), -1), sent_tp(hidden_parts[1]),
            core_swap(small_rows))
        return sent, own_other_up, both, collect(places, both_down, both)

    (attn_got, shared_far, carried, far_one, small_got), own_other_up, both_other_down, grad_expert_down = phases.run(
        phase_six, attn[0], both_other_down, (shared[1], shared_got), hidden_parts, far_two, small_rows,
        (other_up[1], up_got, up_far))
    both_other_up = neighbours(own_other_up)

    def phase_seven(
        attn, both, hidden_parts, far_one, carried, small_rows, small_got, both_gate, shared, out, out_zero, out_home
    ):
        carried = ctx_open(
            (sum_tp(hidden_parts[1], far_one) + carried.astype(F32)).astype(BF16), -1)
        rows, own_shared = sums(attn, shared)
        sent = sent_pairs(rows), carried, sent_tp(hidden_parts[2])
        small_rows = small_rows + small_got
        reach = 1
        while reach < pairs:
            small_rows = small_rows + pair_swap(small_rows, reach)
            reach *= 2
        small_rows = lax.dynamic_slice_in_dim(small_rows, me * share, share, 1)
        output_mine = (mixed + sum_tp_of(out, 0, out_zero) + out_home.astype(F32)).astype(BF16)
        return sent, small_rows, own_shared, collect(places, both_gate, both), output_mine

    (attn_far, carried, hidden_other), small_rows, own_shared, grad_expert_gate, output_mine = phases.run(
        phase_seven, (attn[1], attn_got), both_other_gate, hidden_parts, far_one, carried, small_rows, small_got,
        both_gate, (shared[1], shared_got, shared_far), out, out_zero, out_home)
    both_shared = neighbours(own_shared)

    def input_back(total, got, carried):
        grad_hidden = sum_tp(total, got) + carried.astype(F32)
        scale_attn = lax.rsqrt(jnp.mean(inputs_mine * inputs_mine, axis=-1, keepdims=True) + EPS)
        scaled = grad_hidden * attn_scale
        grad_norm = scale_attn * scaled - inputs_mine * scale_attn * scale_attn * scale_attn * jnp.mean(
            scaled * inputs_mine, axis=-1, keepdims=True)
        return (grad_mixed + grad_norm).astype(BF16)

    def phase_eight(
        attn, hidden_parts, hidden_other, carried, small_rows, both_up, both_other_up, output_mine
    ):
        pieces = attn_pieces(pair, plane, *attn, small_rows)
        input_mine = input_back(hidden_parts[2], hidden_other, carried)
        return (
            [ctx_shift(pieces[d], d) for d in range(1, ctx)], to_tp(input_mine), to_tp(output_mine), pieces[0],
            input_mine, collect(places, both_up, both_other_up))

    attn_got, input_other, output_other, attn_piece, input_mine, grad_expert_up = phases.run(
        phase_eight, (attn[1], attn_got, attn_far), hidden_parts, hidden_other, carried, small_rows, both_up,
        both_other_up, output_mine)

    def phase_nine(attn_piece, attn_got, input_mine, input_other, output_mine, output_other, both_shared):
        total = attn_piece.astype(F32)
        for one in attn_got:
            total = total + one.astype(F32)
        total = total.astype(BF16)
        halves = both_shared.astype(F32)
        result = [
            jnp.concatenate([one[:, i * units : (i + 1) * units] for one in halves], axis=1) for i in range(3)]
        return (
            total, [ctx_shift(total, d) for d in range(1, ctx)], joined(input_mine, *input_other),
            joined(output_mine, *output_other), result)

    attn_piece, attn_got, input_grad, output, result = phases.run(
        phase_nine, attn_piece, attn_got, input_mine, input_other, output_mine, output_other, both_shared)
    grad_key_weight, grad_value_weight, grad_query_weight, grad_out_rows, small_out = finish(
        plane.astype(jnp.int32)[None], [attn_piece] + attn_got, share, cols)
    grad_out_rows = grad_out_rows.T
    grad_expert_down = jnp.swapaxes(grad_expert_down, 1, 2)
    small_out = small_out[:, :share]
    grad_shared_gate, grad_shared_up, grad_shared_down = result[0], result[1], result[2].T
    return (
        output[None],
        input_grad[None],
        grad_query_weight,
        grad_key_weight,
        grad_value_weight,
        grad_out_rows,
        small_out[experts + 1],
        small_out[experts],
        small_out[:experts].T,
        grad_shared_gate,
        grad_shared_up,
        grad_shared_down,
        grad_expert_gate,
        grad_expert_up,
        grad_expert_down,
    )


def solution(mesh):
    in_specs = (
        P("fsdp", "ctx", None),
        P("fsdp", None),
        P("fsdp", "ctx", None),
        P("fsdp", "tp"),
        P("fsdp", "tp"),
        P("fsdp", "tp"),
        P("tp", "fsdp"),
        P("fsdp"),
        P("fsdp"),
        P("fsdp", None),
        P("fsdp", "tp"),
        P("fsdp", "tp"),
        P("tp", "fsdp"),
        P(None, "fsdp", "tp"),
        P(None, "fsdp", "tp"),
        P(None, "tp", "fsdp"),
        P("fsdp", "ctx", None),
    )
    out_specs = (
        P("fsdp", "ctx", None),
        P("fsdp", "ctx", None),
        P("fsdp", "tp"),
        P("fsdp", "tp"),
        P("fsdp", "tp"),
        P("tp", "fsdp"),
        P("fsdp"),
        P("fsdp"),
        P("fsdp", None),
        P("fsdp", "tp"),
        P("fsdp", "tp"),
        P("tp", "fsdp"),
        P(None, "fsdp", "tp"),
        P(None, "fsdp", "tp"),
        P(None, "tp", "fsdp"),
    )
    return jax.shard_map(local, mesh=mesh, in_specs=in_specs, out_specs=out_specs, check_vma=False)
```

```python
import functools

import jax
import jax.numpy as jnp
from jax import lax
from jax.experimental import pallas as pl
from jax.experimental.pallas import tpu as pltpu
from jax.sharding import PartitionSpec as P

HD = 64
WINDOW = 1024
EPS = 1e-06
F32 = jnp.float32
BF16 = jnp.bfloat16
VMEM_BYTES = 56 * 1024 * 1024
COST_SCALE = 0.3


def dot(left, right):
    return lax.dot_general(left, right, (((1,), (0,)), ((), ())), preferred_element_type=F32)


def dot_nt(left, right):
    return lax.dot_general(left, right, (((1,), (1,)), ((), ())), preferred_element_type=F32)


def dot_tn(left, right):
    return lax.dot_general(left, right, (((0,), (0,)), ((), ())), preferred_element_type=F32)


def core_swap(block):
    size = lax.axis_size("fsdp")
    return lax.ppermute(block, "fsdp", [(i, i ^ 1) for i in range(size)])


def pair_shift(block, distance):
    size = lax.axis_size("fsdp")
    pairs = size // 2
    route = [(i, ((i // 2 + distance) % pairs) * 2 + i % 2) for i in range(size)]
    return lax.ppermute(block, "fsdp", route)


def pair_swap(block, reach):
    size = lax.axis_size("fsdp")
    return lax.ppermute(block, "fsdp", [(i, i ^ (2 * reach)) for i in range(size)])


def tp_shift(block, distance):
    size = lax.axis_size("tp")
    return lax.ppermute(block, "tp", [(i, (i + distance) % size) for i in range(size)])


def ctx_shift(block, distance):
    size = lax.axis_size("ctx")
    return lax.ppermute(block, "ctx", [(i, (i + distance) % size) for i in range(size)])


def ctx_swap(block, reach=1):
    size = lax.axis_size("ctx")
    return lax.ppermute(block, "ctx", [(i, i ^ reach) for i in range(size)])


def ctx_open(block, distance):
    size = lax.axis_size("ctx")
    route = [(i, i + distance) for i in range(size) if 0 <= i + distance < size]
    return lax.ppermute(block, "ctx", route)


def pick(stack, index):
    return lax.dynamic_index_in_dim(stack, index, 0, keepdims=False)


def place_rows(pieces, me):
    first, second = pieces
    return jnp.where(
        me == 0, jnp.stack([first, second], axis=1), jnp.stack([second, first], axis=1))


def place(pieces, me):
    count = len(pieces)
    if count == 1:
        return pieces[0][None]
    if count == 2:
        first, second = pieces
        return jnp.where(me == 0, jnp.stack([first, second]), jnp.stack([second, first]))
    result = jnp.zeros((count,) + pieces[0].shape, pieces[0].dtype)
    for d, piece in enumerate(pieces):
        result = lax.dynamic_update_index_in_dim(result, piece, (me - d) % count, 0)
    return result


def tie(values, *others):
    return lax.optimization_barrier((values, others))[0]


class Phases:
    def __init__(self):
        self.last = []

    def run(self, function, *values):
        given = function(*(tie(values, self.last) if self.last else values))
        self.last = jax.tree.leaves(given)
        return given


def all_sum(block, axis):
    size = lax.axis_size(axis)
    reach = 1
    while reach < size:
        other = lax.ppermute(block, axis, [(i, i ^ reach) for i in range(size)])
        block = block + other
        reach *= 2
    return block


LANE, PAIR, CORE, PLANE, OWN_EXPERTS, FAR_EXPERTS, FAR_PLANE, OWN_HALF, OTHER_HALF, PARITY, NEXT_PAIR = range(11)


def whole(shape):
    return pl.BlockSpec(shape, lambda *_: (0,) * len(shape))


def params():
    return pltpu.CompilerParams(vmem_limit_bytes=VMEM_BYTES)


def cost(microseconds):
    return pl.CostEstimate(flops=0, bytes_accessed=int(microseconds * COST_SCALE * 3.4e6), transcendentals=0)


def swap_halves(values):
    width = values.shape[-1]
    lane = lax.broadcasted_iota(jnp.int32, values.shape, 1)
    up = pltpu.roll(values, width - HD // 2, 1)
    down = pltpu.roll(values, HD // 2, 1)
    return jnp.where(lane % HD < HD // 2, up, down)


def widen(table, width):
    copies = -(-width // table.shape[1])
    return jnp.concatenate([table] * copies, axis=1)[:, :width]


def rotated(values, cosine, sine):
    return (values * cosine + swap_halves(values) * sine).astype(BF16)


def project_rows(inputs, gain, weights, cos_ref, sin_ref, hid_ref, k_ref, v_ref):
    scale = lax.rsqrt(jnp.mean(inputs * inputs, axis=-1, keepdims=True) + EPS)
    hidden = (inputs * scale * gain).astype(BF16)
    hid_ref[...] = hidden
    width = k_ref.shape[1]
    k_ref[...] = rotated(
        dot(hidden, weights[:, :width]), widen(cos_ref[...], width), widen(sin_ref[...], width))
    v_ref[...] = dot(hidden, weights[:, width : 2 * width]).astype(BF16)
    return hidden


def project_near_kernel(parts, pairs, meta_ref, tok_ref, *refs):
    prev_refs, refs = refs[:parts], refs[parts:]
    same_refs, cross_refs, refs = refs[:pairs], refs[pairs : 2 * pairs], refs[2 * pairs :]
    gain_ref, cos_ref, sin_ref, hid_ref, k_ref, v_ref, q_ref, w_ref, prev_ref, w_all, x_all = refs
    tok, features = x_all.shape[1:]
    share, columns = w_all.shape[1:]

    @pl.when(pl.program_id(0) == 0)
    def _():
        for d in range(pairs):
            row = 2 * lax.rem(meta_ref[PAIR] + pairs - d, pairs)
            w_all[row + meta_ref[CORE]] = same_refs[d][...]
            w_all[row + 1 - meta_ref[CORE]] = cross_refs[d][...]
        for j in range(parts):
            x_all[lax.rem(meta_ref[LANE] + parts - j, parts)] = prev_refs[j][...]
        weights = w_all[...].reshape(2 * pairs * share, columns)
        w_ref[...] = weights
        inputs = x_all[...].reshape(parts * tok, features)
        prev_ref[...] = inputs
        project_rows(inputs.astype(F32), gain_ref[...], weights, cos_ref, sin_ref, hid_ref, k_ref, v_ref)

    @pl.when(pl.program_id(0) == 1)
    def _():
        weights = w_all[...].reshape(2 * pairs * share, columns)
        hidden = project_rows(
            tok_ref[...].astype(F32), gain_ref[...], weights, cos_ref, sin_ref, hid_ref, k_ref, v_ref)
        width = k_ref.shape[1]
        query = dot(hidden, weights[:, 2 * width :])
        q_ref[...] = rotated(
            query, widen(cos_ref[...], width), widen(sin_ref[...], width)) * jnp.asarray(HD**-0.5, BF16)


def project_near(meta, tokens, prev_pieces, same, cross, gain, cosine, sine):
    rows, features = tokens.shape
    share, columns = same[0].shape
    width = columns // 3
    tok = prev_pieces[0].shape[0]
    count = 2 * len(same) * share
    shapes = [(3 * rows, features), (3 * rows, width), (3 * rows, width)]
    block = lambda i, meta: (i + 1, 0)
    others = [(rows, width), (count, columns), (rows, features)]
    operands = [tokens, *prev_pieces, *same, *cross, gain]
    table = pl.BlockSpec((rows, cosine.shape[1]), block)
    return pl.pallas_call(
        functools.partial(project_near_kernel, len(prev_pieces), len(same)),
        grid_spec=pltpu.PrefetchScalarGridSpec(
            num_scalar_prefetch=1,
            grid=(2,),
            in_specs=[whole(o.shape) for o in operands] + [table, table],
            out_specs=[pl.BlockSpec((rows, shape[1]), block) for shape in shapes]
            + [whole(shape) for shape in others],
            scratch_shapes=[
                pltpu.VMEM((2 * len(same), share, columns), BF16),
                pltpu.VMEM((len(prev_pieces), tok, features), BF16),
            ],
        ),
        out_shape=[jax.ShapeDtypeStruct(shape, BF16) for shape in shapes + others],
        compiler_params=params(),
        cost_estimate=cost(7),
    )(meta, *operands, cosine, sine)


def project_far_kernel(parts, meta_ref, *refs):
    prev_refs, refs = refs[:parts], refs[parts:]
    w_ref, gain_ref, cos_ref, sin_ref, _, _, _, hid_ref, k_ref, v_ref, prev_ref, x_all = refs
    tok, features = x_all.shape[1:]
    for j in range(parts):
        x_all[lax.rem(meta_ref[LANE] + parts - j, parts)] = prev_refs[j][...]
    inputs = x_all[...].reshape(parts * tok, features)
    prev_ref[...] = inputs
    project_rows(inputs.astype(F32), gain_ref[...], w_ref[...], cos_ref, sin_ref, hid_ref, k_ref, v_ref)


def project_far(meta, prev_pieces, weights, gain, cosine, sine, saved):
    tok, features = prev_pieces[0].shape
    rows = tok * len(prev_pieces)
    width = weights.shape[1] // 3
    first = lambda i, meta: (0, 0)
    operands = [*prev_pieces, weights, gain]
    table = pl.BlockSpec((rows, cosine.shape[1]), first)
    return pl.pallas_call(
        functools.partial(project_far_kernel, len(prev_pieces)),
        grid_spec=pltpu.PrefetchScalarGridSpec(
            num_scalar_prefetch=1,
            grid=(1,),
            in_specs=[whole(o.shape) for o in operands] + [table, table]
            + [pl.BlockSpec(memory_space=pl.ANY)] * 3,
            out_specs=[pl.BlockSpec((rows, one.shape[1]), first) for one in saved]
            + [whole((rows, features))],
            scratch_shapes=[pltpu.VMEM((len(prev_pieces), tok, features), BF16)],
        ),
        out_shape=[jax.ShapeDtypeStruct(one.shape, BF16) for one in saved]
        + [jax.ShapeDtypeStruct((rows, features), BF16)],
        input_output_aliases={1 + len(operands) + 2 + i: i for i in range(3)},
        compiler_params=params(),
        cost_estimate=cost(4),
    )(meta, *operands, cosine, sine, *saved)


def prepare_kernel(parts, meta_ref, routes_ref, cot_ref, rates_ref, seg_ref, *refs):
    cos_ref, sin_ref, kseg_ref, qseg_ref, hits_ref = refs[:5]
    mine_ref, other_refs, seg_all = refs[5], refs[6:-1], refs[-1]
    block, width = cot_ref.shape
    tok = block // parts
    experts = hits_ref.shape[0]
    rows, lanes = cos_ref.shape
    short = 64
    origin = (meta_ref[PLANE] - 2) * block
    far = (lax.broadcasted_iota(jnp.int32, (rows // short, lanes), 0) * short + origin).astype(F32) * rates_ref[...]
    near = lax.broadcasted_iota(jnp.int32, (short, lanes), 0).astype(F32) * rates_ref[...]
    far_cos, far_sin, near_cos, near_sin = jnp.cos(far), jnp.sin(far), jnp.cos(near), jnp.sin(near)
    sign = jnp.where(lax.broadcasted_iota(jnp.int32, (short, lanes), 1) % HD < HD // 2, -1.0, 1.0)
    signed_sin, signed_cos = sign * near_sin, sign * near_cos
    for h in range(rows // short):
        part = slice(h * short, (h + 1) * short)
        one_cos, one_sin = far_cos[h : h + 1], far_sin[h : h + 1]
        cos_ref[part] = one_cos * near_cos - one_sin * near_sin
        sin_ref[part] = one_sin * signed_cos + one_cos * signed_sin
    seg_all[:, : 2 * block] = jnp.full((1, 2 * block), -1, jnp.int32)
    seg_all[:, 2 * block :] = seg_ref[...]
    kseg = seg_all[:, pl.ds(pl.multiple_of(meta_ref[PLANE] * block, block), rows)]
    qseg_ref[...] = kseg[:, rows - block :]
    kseg_ref[...] = jnp.broadcast_to(kseg, (8, rows)).T[:, :1]
    row = lax.broadcasted_iota(jnp.int32, (experts, block), 0)
    named = row == routes_ref[0:1, :]
    for j in range(1, routes_ref.shape[0]):
        named = named | (row == routes_ref[j : j + 1, :])
    hits = jnp.where(named, 1.0, 0.0).astype(F32)
    before = lax.broadcasted_iota(jnp.int32, (block, block), 0) < lax.broadcasted_iota(jnp.int32, (block, block), 1)
    rank = dot(hits.astype(BF16), jnp.where(before, 1.0, 0.0).astype(BF16))
    hits_ref[...] = hits
    table = jnp.concatenate([jnp.where(named, rank, -1.0), jnp.zeros((16 - experts, block), F32)], axis=0)
    mine_ref[tok:, :] = jnp.concatenate([table, jnp.zeros((16, width - block), F32)], axis=1).astype(BF16)
    for j, ref in enumerate((mine_ref,) + other_refs):
        start = lax.rem(meta_ref[LANE] + parts - j, parts) * tok
        ref[:tok, :] = cot_ref[pl.ds(pl.multiple_of(start, tok), tok), :]


def prepare(meta, parts, experts, routes_t, cotangent, segments):
    block, width = cotangent.shape
    tok = block // parts
    index = jnp.arange(2 * HD, dtype=jnp.int32)
    rates = (10000.0 ** (-2.0 * (index % (HD // 2)).astype(F32) / HD))[None, :]
    shapes = [
        ((3 * block, 2 * HD), F32), ((3 * block, 2 * HD), F32), ((3 * block, 1), jnp.int32), ((1, block), jnp.int32),
        ((experts, block), F32), ((tok + 16, width), BF16),
    ] + [((tok, width), BF16)] * (parts - 1)
    operands = (routes_t, cotangent, rates, segments)
    return pl.pallas_call(
        functools.partial(prepare_kernel, parts),
        grid_spec=pltpu.PrefetchScalarGridSpec(
            num_scalar_prefetch=1,
            grid=(1,),
            in_specs=[whole(o.shape) for o in operands],
            out_specs=[whole(shape) for shape, _ in shapes],
            scratch_shapes=[pltpu.VMEM((1, segments.shape[1] + 2 * block), jnp.int32)],
        ),
        out_shape=[jax.ShapeDtypeStruct(shape, kind) for shape, kind in shapes],
        compiler_params=params(),
        cost_estimate=cost(3),
    )(meta, *operands)


def bundle_kernel(at_ref, *refs):
    own, far, shared, (own_ref, far_ref) = refs[:3], refs[3:6], refs[6:9], refs[9:]
    owned = own[0].shape[0]
    for i in range(3):
        own_ref[i * owned : (i + 1) * owned] = own[i][...]
        far_ref[i * owned : (i + 1) * owned] = far[i][...]
    units = shared[0].shape[1]
    gate_ref, up_ref, down_ref = shared
    far_ref[3 * owned, :, :units] = gate_ref[...]
    far_ref[3 * owned, :, units:] = up_ref[...]
    far_ref[3 * owned + 1, :, :units] = down_ref[...]
    far_ref[3 * owned + 1, :, units:] = jnp.zeros_like(down_ref)


def bundles(at, owned, units, stacks, shared):
    _, share, hidden = stacks[0].shape

    def rows_of(which):
        return [pl.BlockSpec((owned, share, hidden), lambda i, at: (at[which], 0, 0))] * 3

    shapes = [(3 * owned, share, hidden), (3 * owned + 2, share, hidden)]
    return pl.pallas_call(
        bundle_kernel,
        grid_spec=pltpu.PrefetchScalarGridSpec(
            num_scalar_prefetch=1,
            grid=(1,),
            in_specs=rows_of(PLANE) + rows_of(FAR_PLANE)
            + [pl.BlockSpec((share, units), lambda i, at: (0, at[PARITY]))] * 3,
            out_specs=[whole(shape) for shape in shapes],
        ),
        out_shape=[jax.ShapeDtypeStruct(shape, BF16) for shape in shapes],
        compiler_params=params(),
        cost_estimate=cost(5),
    )(at, *stacks, *stacks, *shared)


def finish_kernel(meta_ref, mine_ref, *refs):
    count = len(refs) - 6
    pieces = (mine_ref,) + refs[:count]
    k_ref, v_ref, q_ref, o_ref, small_ref, all_ref = refs[count:]
    total = len(pieces)
    rows = mine_ref.shape[0]
    for d, ref in enumerate(pieces):
        all_ref[lax.rem(meta_ref[PLANE] + total - d, total)] = ref[...].astype(F32)
    whole_rows = all_ref[...].reshape(total * rows, mine_ref.shape[1])
    share, cols = k_ref.shape
    for i, ref in enumerate((k_ref, v_ref, q_ref, o_ref)):
        ref[...] = whole_rows[:share, i * cols : (i + 1) * cols]
    small_ref[...] = whole_rows[:share, 4 * cols :].T[:16]


def finish(meta, pieces, share, cols):
    rows, columns = pieces[0].shape
    shapes = [(share, cols)] * 4 + [(16, share)]
    return pl.pallas_call(
        finish_kernel,
        grid_spec=pltpu.PrefetchScalarGridSpec(
            num_scalar_prefetch=1,
            grid=(1,),
            in_specs=[whole(piece.shape) for piece in pieces],
            out_specs=[whole(shape) for shape in shapes],
            scratch_shapes=[pltpu.VMEM((len(pieces), rows, columns), F32)],
        ),
        out_shape=[jax.ShapeDtypeStruct(shape, F32) for shape in shapes],
        compiler_params=params(),
        cost_estimate=cost(2),
    )(meta, *pieces)


def pack_kernel(lane_ref, k_ref, v_ref, q_ref, router_ref, gains_ref, tok_ref, qkv_ref, small_ref, mine_ref):
    width = k_ref.shape[1]
    for i, ref in enumerate((k_ref, v_ref, q_ref)):
        qkv_ref[:, i * width : (i + 1) * width] = ref[...]
    experts, share = router_ref.shape
    small_ref[...] = jnp.concatenate(
        [router_ref[...].astype(F32), gains_ref[...].astype(F32),
         jnp.zeros((small_ref.shape[0] - experts - 2, share), F32)], axis=0).astype(BF16)
    mine_ref[...] = tok_ref[...]


def pack(at, parts, key_weight, value_weight, query_weight, router_t, gains, tokens):
    rows, width = tokens.shape
    share, cols = key_weight.shape
    part = (rows // parts, width)
    shapes = [(share, 3 * cols), (16, share), part]
    operands = (key_weight, value_weight, query_weight, router_t, gains)
    return pl.pallas_call(
        pack_kernel,
        grid_spec=pltpu.PrefetchScalarGridSpec(
            num_scalar_prefetch=1,
            grid=(1,),
            in_specs=[whole(o.shape) for o in operands]
            + [pl.BlockSpec(part, lambda i, at: (at[LANE], 0))],
            out_specs=[whole(shape) for shape in shapes],
        ),
        out_shape=[jax.ShapeDtypeStruct(shape, BF16) for shape in shapes],
        compiler_params=params(),
        cost_estimate=cost(2),
    )(at, *operands, tokens)


def mask_bias(kseg, qseg, keys, queries):
    key = lax.broadcasted_iota(jnp.int32, (keys, queries), 0)
    query = lax.broadcasted_iota(jnp.int32, (keys, queries), 1)
    allowed = (key > query) & (key <= query + WINDOW) & (kseg == qseg)
    return jnp.where(allowed, 0.0, -1e30).astype(F32)


def head_only(values, head):
    lane = lax.broadcasted_iota(jnp.int32, values.shape, 1)
    return jnp.where(lane // HD == head, values, jnp.zeros_like(values))


def loaded(ref, width):
    values = ref[...]
    if width % values.shape[1] == 0:
        return values
    lane = lax.broadcasted_iota(jnp.int32, values.shape, 1) + pl.program_id(0) * values.shape[1]
    return jnp.where(lane < width, values, jnp.zeros_like(values))


def attend_kernel(tile, width, q_ref, k_ref, v_ref, kseg_ref, qseg_ref, out_ref, lse_ref, bias_ref):
    rows = q_ref.shape[0]
    span = WINDOW + tile
    tiles = rows // tile

    @pl.when(pl.program_id(0) == 0)
    def _():
        for j in range(tiles):
            bias_ref[j] = mask_bias(
                kseg_ref[pl.ds(j * tile, span), :], qseg_ref[:, pl.ds(j * tile, tile)], span, tile
            )

    keys = loaded(k_ref, width)
    values_t = loaded(v_ref, width).T
    queries = loaded(q_ref, width)
    for j in range(tiles):
        start = j * tile
        query = queries[start : start + tile]
        parts = []
        for head in range(2):
            scores = dot_nt(keys[start : start + span], head_only(query, head)) + bias_ref[j]
            top = jnp.max(scores, axis=0, keepdims=True)
            expo = jnp.exp(scores - top)
            total = jnp.sum(expo, axis=0, keepdims=True)
            part = dot(
                values_t[head * HD : (head + 1) * HD, start : start + span], expo.astype(BF16)
            )
            parts.append(part / total)
            lse_ref[0, pl.ds(head, 1), pl.ds(start, tile)] = top + jnp.log(total)
        out_ref[pl.ds(start, tile), :] = jnp.concatenate(parts, axis=0).T.astype(BF16)


def attend(query, keys, values, kseg, qseg):
    rows, width = query.shape
    span = keys.shape[0]
    tile = min(256, rows)
    pairs = -(-width // (2 * HD))
    columns = lambda count: pl.BlockSpec((count, 2 * HD), lambda i: (0, i))
    return pl.pallas_call(
        functools.partial(attend_kernel, tile, width),
        grid=(pairs,),
        in_specs=[columns(rows), columns(span), columns(span), whole((span, 1)), whole((1, rows))],
        out_specs=[columns(rows), pl.BlockSpec((1, 2, rows), lambda i: (i, 0, 0))],
        out_shape=[
            jax.ShapeDtypeStruct((rows, width), BF16),
            jax.ShapeDtypeStruct((pairs, 2, rows), F32),
        ],
        scratch_shapes=[pltpu.VMEM((rows // tile, WINDOW + tile, tile), F32)],
        compiler_params=params(),
        cost_estimate=cost(13),
    )(query, keys, values, kseg, qseg)


def attend_back_kernel(
    tile, width, q_ref, k_ref, v_ref, g_ref, lse_ref, kseg_ref, qseg_ref, cos_ref, sin_ref,
    dq_ref, dk_ref, dv_ref, bias_ref, dk_acc, dv_acc,
):
    rows = q_ref.shape[0]
    span = WINDOW + tile
    tiles = rows // tile
    total_keys = k_ref.shape[0]

    @pl.when(pl.program_id(0) == 0)
    def _():
        for j in range(tiles):
            bias_ref[j] = mask_bias(
                kseg_ref[pl.ds(j * tile, span), :], qseg_ref[:, pl.ds(j * tile, tile)], span, tile
            )

    keys = loaded(k_ref, width)
    values = loaded(v_ref, width)
    queries = loaded(q_ref, width)
    grads = loaded(g_ref, width)
    keys_t = keys.T
    dk_acc[...] = jnp.zeros_like(dk_acc)
    dv_acc[...] = jnp.zeros_like(dv_acc)
    cosine = cos_ref[...]
    sine = sin_ref[...]
    lead = total_keys - rows
    for j in range(tiles):
        start = j * tile
        query = queries[start : start + tile]
        grad = grads[start : start + tile]
        parts = []
        for head in range(2):
            query_one = head_only(query, head)
            grad_one = head_only(grad, head)
            scores = dot_nt(keys[start : start + span], query_one) + bias_ref[j]
            probs = jnp.exp(scores - lse_ref[0, pl.ds(head, 1), pl.ds(start, tile)])
            grad_probs = dot_nt(values[start : start + span], grad_one)
            delta = jnp.sum(probs * grad_probs, axis=0, keepdims=True)
            grad_scores = (probs * (grad_probs - delta)).astype(BF16)
            dv_acc[pl.ds(start, span), :] += dot(probs.astype(BF16), grad_one)
            dk_acc[pl.ds(start, span), :] += dot(grad_scores, query_one)
            parts.append(
                dot(keys_t[head * HD : (head + 1) * HD, start : start + span], grad_scores)
            )
        dq = jnp.concatenate(parts, axis=0).T * HD**-0.5
        places = pl.ds(lead + start, tile)
        dq_ref[pl.ds(start, tile), :] = (
            dq * cos_ref[places, :] - swap_halves(dq) * sin_ref[places, :]
        ).astype(BF16)
    dk = dk_acc[...]
    dk_ref[...] = (dk * cosine - swap_halves(dk) * sine).astype(BF16)
    dv_ref[...] = dv_acc[...].astype(BF16)


def attend_back(query, keys, values, grad, lse, kseg, qseg, cosine, sine):
    rows, width = query.shape
    span = keys.shape[0]
    tile = min(256, rows)
    pairs = -(-width // (2 * HD))
    columns = lambda count: pl.BlockSpec((count, 2 * HD), lambda i: (0, i))
    return pl.pallas_call(
        functools.partial(attend_back_kernel, tile, width),
        grid=(pairs,),
        in_specs=[
            columns(rows), columns(span), columns(span), columns(rows),
            pl.BlockSpec((1, 2, rows), lambda i: (i, 0, 0)),
            whole((span, 1)), whole((1, rows)), whole((span, 2 * HD)), whole((span, 2 * HD)),
        ],
        out_specs=[columns(rows), columns(span), columns(span)],
        out_shape=[
            jax.ShapeDtypeStruct((rows, width), BF16),
            jax.ShapeDtypeStruct((span, width), BF16),
            jax.ShapeDtypeStruct((span, width), BF16),
        ],
        scratch_shapes=[
            pltpu.VMEM((rows // tile, WINDOW + tile, tile), F32),
            pltpu.VMEM((span, 2 * HD), F32),
            pltpu.VMEM((span, 2 * HD), F32),
        ],
        compiler_params=params(),
        cost_estimate=cost(18),
    )(query, keys, values, grad, lse, kseg, qseg, cosine, sine)


def expert_kernel(which, capacity, parts, experts, full, shared, pieces, added, steps, n_saved, meta_ref, *refs):
    w_all, w_sems = refs[-2:]
    owned = w_all.shape[1] // 3
    order = [kind * owned + j for j in range(owned) for kind in range(3)]
    order += list(range(3 * owned, w_all.shape[1]))
    if pieces:
        count = steps * parts
        x_refs, c_refs, refs = refs[:count], refs[count : 2 * count], refs[2 * count :]
        x_all, c_all, t_all = refs[-5:-2]
        tok, width = x_all.shape[1:]
        block = tok * parts
        for j in range(parts):
            spot = lax.rem(meta_ref[LANE] + parts - j, parts)
            for i in range(steps):

                @pl.when(pl.program_id(0) == i)
                def _():
                    x_all[spot] = x_refs[i * parts + j][...]
                    c_all[spot] = c_refs[i * parts + j][:tok]
                    if j == 0:
                        t_all[...] = c_refs[i * parts][tok:]

        inputs = x_all[...].reshape(block, width)
        cot = c_all[...].reshape(block, width)
        low_table = t_all[...]
    else:
        x_ref, c_ref = refs[:2]
        refs = refs[2:]
        block, width = x_ref.shape[1:]
        tok = block // parts
        inputs = x_ref[0]
        cot = c_ref[0, :block]
        low_table = c_ref[0, block:]
    w_ref, rt_ref = refs[:2]
    refs = refs[2:]

    def weight_copy(which):
        return pltpu.make_async_copy(w_ref.at[:, which], w_all.at[:, which], w_sems.at[which])

    @pl.when(pl.program_id(0) == 0)
    def _():
        for j in range(w_all.shape[1]):
            weight_copy(order[j]).start()

    if added:
        more_dx_ref, more_out_ref = refs[:2]
        refs = refs[2:]
    refs = refs[n_saved:]
    if full:
        dx_ref, out_ref = refs[:2]
        refs = refs[2:]
    sx_ref, sr_ref, sh_ref, sa_ref, sb_ref = refs[:5]
    if shared:
        ssh_ref, ssa_ref, ssb_ref = refs[5:8]
    if pieces:
        ssx_ref, ssc_ref = refs[5:7]
        ssx_ref[0] = inputs
        ssc_ref[0, :block] = cot
        ssc_ref[0, block:] = low_table
    hidden = w_ref.shape[3]
    table = low_table[:, :block].astype(F32)[:experts]

    def weights(which):
        @pl.when(pl.program_id(0) == 0)
        def _():
            weight_copy(which).wait()

        return w_all[:, which].reshape(width, hidden)

    logits = dot_nt(rt_ref[...], inputs)[:experts]
    named = table >= 0.0
    top = jnp.max(jnp.where(named, logits, -1e30), axis=0, keepdims=True)
    expo = jnp.where(named, jnp.exp(logits - top), 0.0)
    gates = expo / jnp.sum(expo, axis=0, keepdims=True)
    row = lax.broadcasted_iota(jnp.int32, (experts, block), 0)
    slot = lax.broadcasted_iota(jnp.int32, (capacity, block), 0).astype(F32)
    hits, spreads, gate_slots = [], [], []
    for j in range(owned):
        mine = row == meta_ref[which] + j
        gate = jnp.sum(jnp.where(mine, gates, 0.0), axis=0, keepdims=True)
        position = jnp.sum(jnp.where(mine, table, 0.0), axis=0, keepdims=True)
        hit = slot == position
        hits.append(hit)
        spreads.append(jnp.where(hit, 1.0, 0.0).astype(BF16))
        gate_slots.append(jnp.sum(jnp.where(hit, gate, 0.0), axis=1, keepdims=True))
    spread = jnp.concatenate(spreads, axis=0)
    routed = dot(spread, inputs).astype(BF16)
    cots = dot(spread, cot)
    gate_slots = jnp.concatenate(gate_slots, axis=0)
    grads = (gate_slots * cots).astype(BF16)

    def branch(left, right, gate_weights, up_weights, down_weights):
        gating = dot(left, gate_weights)
        linear = dot(left, up_weights)
        sigma = jax.nn.sigmoid(gating)
        silu = gating * sigma
        active = (silu * linear).astype(BF16)
        grad_active = dot(right, down_weights)
        slope = sigma * (1.0 + gating * (1.0 - sigma))
        grad_gating = (grad_active * linear * slope).astype(BF16)
        grad_linear = (grad_active * silu).astype(BF16)
        if not full:
            return active, grad_gating, grad_linear
        result = dot_nt(active, down_weights)
        grad_left = dot_nt(grad_gating, gate_weights) + dot_nt(grad_linear, up_weights)
        return active, grad_gating, grad_linear, result, grad_left

    weighted = []
    gate_lines = []
    for j in range(owned):
        rows = slice(j * capacity, (j + 1) * capacity)
        sx_ref[0, j] = routed[rows]
        sr_ref[0, j] = grads[rows]
        got = branch(
            routed[rows], grads[rows], weights(j), weights(owned + j), weights(2 * owned + j))
        sh_ref[0, j], sa_ref[0, j], sb_ref[0, j] = got[:3]
        if full:
            result, grad_left = got[3:]
            grad_gates = jnp.sum(result * cots[rows], axis=1, keepdims=True)
            gate_lines.append(jnp.sum(jnp.where(hits[j], grad_gates, 0.0), axis=0, keepdims=True))
            weighted.append(jnp.concatenate(
                [(gate_slots[rows] * result).astype(BF16), grad_left.astype(BF16)], axis=1))
    if shared:
        units = ssh_ref.shape[2]
        first, second = weights(3 * owned), weights(3 * owned + 1)
        got = branch(inputs, cot, first[:, :units], first[:, units : 2 * units], second[:, :units])
        ssh_ref[0], ssa_ref[0], ssb_ref[0] = got[:3]
    if not full:
        return
    back = dot_tn(spread, jnp.concatenate(weighted, axis=0))
    out, dx = back[:, :width], back[:, width:]
    if shared:
        out = out + got[3]
        dx = dx + got[4]
    line = lax.broadcasted_iota(jnp.int32, (16, width), 0)
    for j in range(parts):
        piece = slice(j * tok, (j + 1) * tok)
        spare = jnp.zeros((1, width - tok), F32)
        extra = jnp.zeros((16, width), F32)
        for i in range(owned):
            padded = jnp.concatenate([gate_lines[i][:, piece], spare], axis=1)
            extra = jnp.where(line == meta_ref[which] + i, padded, extra)
        out_piece, dx_piece = out[piece], dx[piece]
        if added:
            out_piece = out_piece + more_out_ref[0, j].astype(F32)
            dx_piece = dx_piece + more_dx_ref[0, j, :tok].astype(F32)
            extra = extra + more_dx_ref[0, j, tok:].astype(F32)
        out_ref[0, j] = out_piece.astype(BF16)
        dx_ref[0, j, :tok] = dx_piece.astype(BF16)
        dx_ref[0, j, tok:] = extra.astype(BF16)


def expert_shapes(owned, capacity, width, hidden):
    return [(owned, capacity, width)] * 2 + [(owned, capacity, hidden)] * 3


def placed(shape, where):
    return pl.BlockSpec((1,) + shape, lambda i, meta: (where(i, meta),) + (0,) * len(shape))


def expert_blocks(
    first, blocks, steps, capacity, parts, experts, units, full, at, which, sources, weights, router_t, more, saved,
):
    pieces = isinstance(sources[0], list)
    shared = units > 0
    if pieces:
        tok, width = sources[0][0][0].shape
    else:
        block, width = sources[0].shape[1:]
        tok = block // parts
    block = tok * parts
    hidden = weights.shape[3]
    owned = weights.shape[1] // 3
    here = lambda i, meta: first + i
    step = lambda i, meta: i
    shapes = expert_shapes(owned, capacity, width, hidden)
    if shared:
        shapes += [(block, units)] * 3
    if pieces:
        shapes += [(block, width), (block + 16, width)]
    tops = [(parts, tok + 16, width), (parts, tok, width)] if full else []
    outs = [jax.ShapeDtypeStruct((blocks // 2,) + shape, BF16) for shape in tops]
    outs += [jax.ShapeDtypeStruct((blocks,) + shape, BF16) for shape in shapes]
    specs = [placed(shape, here) for shape in tops + shapes]
    if pieces:
        operands = [piece for source in sources for block_pieces in source for piece in block_pieces]
        in_specs = [whole(one.shape) for one in operands]
        scratch = [pltpu.VMEM((parts, tok, width), BF16)] * 2 + [pltpu.VMEM((16, width), BF16)]
    else:
        operands = list(sources)
        in_specs = [placed(one.shape[1:], here) for one in operands]
        scratch = []
    scratch += [pltpu.VMEM(weights.shape, BF16), pltpu.SemaphoreType.DMA((weights.shape[1],))]
    operands += [weights, router_t] + list(more)
    in_specs += [pl.BlockSpec(memory_space=pl.ANY), whole(router_t.shape)] + [placed(one.shape[1:], step) for one in more]
    in_specs += [pl.BlockSpec(memory_space=pl.ANY)] * len(saved)
    return pl.pallas_call(
        functools.partial(
            expert_kernel, which, capacity, parts, experts, full, shared, pieces, len(more) > 0, steps, len(saved)),
        grid_spec=pltpu.PrefetchScalarGridSpec(
            num_scalar_prefetch=1,
            grid=(steps,),
            in_specs=in_specs,
            out_specs=specs,
            scratch_shapes=scratch,
        ),
        out_shape=outs,
        input_output_aliases={1 + len(operands) + i: i for i in range(len(saved))},
        compiler_params=params(),
        cost_estimate=cost((12 if full else 6) * steps),
    )(at, *operands, *saved)


def pair_sums_kernel(counts, index_ref, *refs):
    outs = refs[len(refs) - len(counts) :]
    for count, out_ref in zip(counts, outs):
        job, refs = refs[:count], refs[count:]
        total = job[0][0].astype(F32) + job[1][0].astype(F32)
        for ref in job[2:]:
            total = total + ref[...].astype(F32)
        out_ref[...] = total.astype(BF16)


def pair_sums(at, jobs):
    cut = all(kept.ndim == 4 for _, kept, _, _ in jobs)
    operands, in_specs, out_specs, out_shape = [], [], [], []
    for index, kept, got, far in jobs:
        shape = kept.shape[1:]
        part = ((1,) if cut else shape[:1]) + shape[1:]
        rest = (0,) * (len(shape) - 1)
        picked = pl.BlockSpec((1,) + part, lambda i, at, index=index, rest=rest: (at[index], i) + rest)
        plain = pl.BlockSpec(part, lambda i, at, rest=rest: (i,) + rest)
        operands += [kept, got, *far]
        in_specs += [picked, picked] + [plain] * len(far)
        out_specs.append(plain)
        out_shape.append(jax.ShapeDtypeStruct(shape, BF16))
    return pl.pallas_call(
        functools.partial(pair_sums_kernel, [2 + len(far) for _, _, _, far in jobs]),
        grid_spec=pltpu.PrefetchScalarGridSpec(
            num_scalar_prefetch=1,
            grid=(jobs[0][1].shape[1] if cut else 1,),
            in_specs=in_specs,
            out_specs=out_specs,
        ),
        out_shape=out_shape,
        compiler_params=params(),
        cost_estimate=cost(3),
    )(at, *operands)


def attn_pieces_kernel(meta_ref, kept_ref, got_ref, *refs):
    count = len(refs) - 1
    far_refs, out_refs, all_ref = refs[: count - 4], refs[count - 4 : count], refs[-1]
    total = kept_ref[0].astype(F32) + got_ref[0].astype(F32)
    for ref in far_refs:
        total = total + ref[...].astype(F32)
    share, columns = total.shape
    all_ref[:share] = total
    if share < all_ref.shape[0]:
        all_ref[share:] = jnp.zeros((all_ref.shape[0] - share, columns), F32)
    rows = out_refs[0].shape[0]
    for d, ref in enumerate(out_refs):
        first = lax.rem(meta_ref[PLANE] + d, 4) * rows
        ref[...] = all_ref[pl.ds(pl.multiple_of(first, 16), rows)].astype(BF16)


def attn_pieces(at, kept, got, far):
    share, columns = kept.shape[1:]
    rows = -(-share // 64) * 16
    picked = pl.BlockSpec((1, share, columns), lambda i, at: (at[PAIR], 0, 0))
    return pl.pallas_call(
        attn_pieces_kernel,
        grid_spec=pltpu.PrefetchScalarGridSpec(
            num_scalar_prefetch=1,
            grid=(1,),
            in_specs=[picked, picked] + [whole(one.shape) for one in far],
            out_specs=[whole((rows, columns))] * 4,
            scratch_shapes=[pltpu.VMEM((4 * rows, columns), F32)],
        ),
        out_shape=[jax.ShapeDtypeStruct((rows, columns), BF16)] * 4,
        compiler_params=params(),
        cost_estimate=cost(3),
    )(at, kept, got, *far)


def split_rows(value, core, sent_ref, kept_ref, *at):
    pairs = sent_ref.shape[0]
    share = value.shape[0] // (2 * pairs)
    for q in range(pairs):
        first = value[2 * q * share : (2 * q + 1) * share].astype(BF16)
        second = value[(2 * q + 1) * share : (2 * q + 2) * share].astype(BF16)
        index = (q,) + at
        kept_ref[index] = jnp.where(core == 0, first, second)
        sent_ref[index] = jnp.where(core == 0, second, first)


def weight_kernel(count, core_ref, left_ref, *refs):
    steps, _, slots, rows = left_ref.shape
    left = left_ref[...].reshape(steps * slots, rows)
    for n, right_ref in enumerate(refs[:count]):
        right = right_ref[...].reshape(steps * slots, right_ref.shape[3])
        split_rows(dot_tn(left, right), core_ref[CORE], *refs[count + 2 * n : count + 2 * n + 2], 0)


def weight_grads(core, left, rights, pairs):
    steps, owned, slots, width = left.shape
    columns = rights[0].shape[3]
    share = width // (2 * pairs)
    shape = jax.ShapeDtypeStruct((pairs, owned, share, columns), BF16)
    spec = pl.BlockSpec((pairs, 1, share, columns), lambda j, core: (0, j, 0, 0))
    given = pl.pallas_call(
        functools.partial(weight_kernel, len(rights)),
        grid_spec=pltpu.PrefetchScalarGridSpec(
            num_scalar_prefetch=1,
            grid=(owned,),
            in_specs=[
                pl.BlockSpec((steps, 1, slots, one.shape[3]), lambda j, core: (0, j, 0, 0))
                for one in [left, *rights]
            ],
            out_specs=[spec] * (2 * len(rights)),
        ),
        out_shape=[shape] * (2 * len(rights)),
        compiler_params=params(),
        cost_estimate=cost(5 * len(rights)),
    )(core, left, *rights)
    return [given[2 * n : 2 * n + 2] for n in range(len(rights))]


def shared_grad_kernel(core_ref, x_ref, c_ref, a_ref, b_ref, h_ref, sent_ref, kept_ref, total_ref):
    step = pl.program_id(0)
    block, units = a_ref.shape[1:]

    @pl.when(step == 0)
    def _():
        total_ref[...] = jnp.zeros_like(total_ref)

    total_ref[:, :units] += dot_tn(x_ref[0], a_ref[0])
    total_ref[:, units : 2 * units] += dot_tn(x_ref[0], b_ref[0])
    total_ref[:, 2 * units :] += dot_tn(c_ref[0, :block], h_ref[0])

    @pl.when(step == pl.num_programs(0) - 1)
    def _():
        split_rows(total_ref[...], core_ref[CORE], sent_ref, kept_ref)


def shared_grads(core, x, c, a, b, h, pairs):
    operands = (x, c, a, b, h)
    width, units = x.shape[2], a.shape[2]
    shape = jax.ShapeDtypeStruct((pairs, width // (2 * pairs), 3 * units), BF16)
    return pl.pallas_call(
        shared_grad_kernel,
        grid_spec=pltpu.PrefetchScalarGridSpec(
            num_scalar_prefetch=1,
            grid=(x.shape[0],),
            in_specs=[pl.BlockSpec((1,) + o.shape[1:], lambda i, core: (i, 0, 0)) for o in operands],
            out_specs=[whole(shape.shape), whole(shape.shape)],
            scratch_shapes=[pltpu.VMEM((width, 3 * units), F32)],
        ),
        out_shape=[shape, shape],
        compiler_params=params(),
        cost_estimate=cost(8),
    )(core, *operands)


def attn_grad_kernel(core_ref, hid_ref, dk_ref, dv_ref, dq_ref, gm_ref, at_ref, small_ref, sent_ref, kept_ref):
    lead = hid_ref.shape[0] - dq_ref.shape[0]
    value = jnp.concatenate(
        [
            dot_tn(hid_ref[...], dk_ref[...]),
            dot_tn(hid_ref[...], dv_ref[...]),
            dot_tn(hid_ref[lead:, :], dq_ref[...]),
            dot_tn(gm_ref[...], at_ref[...]),
            small_ref[...].T,
        ],
        axis=1,
    )
    split_rows(value, core_ref[CORE], sent_ref, kept_ref)


def attn_grads_of(core, hid, dk, dv, dq, grad_mixed_low, attended, small, pairs):
    width, cols = hid.shape[1], dk.shape[1]
    shape = jax.ShapeDtypeStruct((pairs, width // (2 * pairs), 4 * cols + small.shape[0]), BF16)
    operands = (hid, dk, dv, dq, grad_mixed_low, attended, small)
    return pl.pallas_call(
        attn_grad_kernel,
        grid_spec=pltpu.PrefetchScalarGridSpec(
            num_scalar_prefetch=1,
            grid=(1,),
            in_specs=[whole(o.shape) for o in operands],
            out_specs=[whole(shape.shape), whole(shape.shape)],
        ),
        out_shape=[shape, shape],
        compiler_params=params(),
        cost_estimate=cost(8),
    )(core, *operands)


def hidden_back_kernel(count, *refs):
    sources = refs[:count]
    dk_ref, dv_ref, dq_ref, w_ref = refs[count : count + 4]
    out_refs, gain_ref = refs[count + 4 : -1], refs[-1]
    cols = dk_ref.shape[1]
    step = pl.program_id(0)

    @pl.when(step == 0)
    def _():
        gain_ref[...] = jnp.zeros_like(gain_ref)

    for i, tok_ref in enumerate(sources):

        @pl.when(step == i)
        def _():
            grad = dot_nt(dk_ref[...], w_ref[:, :cols]) + dot_nt(dv_ref[...], w_ref[:, cols : 2 * cols])
            if i == count - 1:
                grad = grad + dot_nt(dq_ref[...], w_ref[:, 2 * cols : 3 * cols])
            out_refs[i][...] = grad.astype(BF16)
            inputs = tok_ref[...].astype(F32)
            scale = lax.rsqrt(jnp.mean(inputs * inputs, axis=-1, keepdims=True) + EPS)
            gain_ref[...] += jnp.sum(grad * (inputs * scale), axis=0, keepdims=True)


def hidden_back(sources, dk, dv, dq, weights):
    count = len(sources)
    rows, width = sources[0].shape
    cols = dk.shape[1]
    part = pl.BlockSpec((rows, cols), lambda i: (i, 0))
    return pl.pallas_call(
        functools.partial(hidden_back_kernel, count),
        grid=(count,),
        in_specs=[whole((rows, width))] * count
        + [part, part, whole((rows, cols)), whole(weights.shape)],
        out_specs=[whole((rows, width))] * count + [whole((1, width))],
        out_shape=[jax.ShapeDtypeStruct((rows, width), BF16)] * count + [jax.ShapeDtypeStruct((1, width), F32)],
        compiler_params=params(),
        cost_estimate=cost(7),
    )(*sources, dk, dv, dq, weights)


def collect_kernel(places_ref, first_ref, second_ref, out_ref):
    for half, ref in enumerate((first_ref, second_ref)):

        @pl.when(pl.program_id(0) // (pl.num_programs(0) // 2) == half)
        def _():
            out_ref[...] = ref[0].astype(F32)


def collect(at, first, second):
    _, owned, rows, columns = first.shape
    half = 2 * owned
    block = (1, rows, columns)

    def part(start):
        def index(step, places):
            local = jnp.clip(step - start, 0, half - 1)
            return (local // owned, local % owned, 0, 0)

        return pl.BlockSpec((1,) + block, index)

    return pl.pallas_call(
        collect_kernel,
        grid_spec=pltpu.PrefetchScalarGridSpec(
            num_scalar_prefetch=1,
            grid=(2 * half,),
            in_specs=[part(0), part(half)],
            out_specs=pl.BlockSpec(
                block, lambda step, at: (at[OWN_HALF + step // half] * half + step % half, 0, 0)),
        ),
        out_shape=jax.ShapeDtypeStruct((2 * half, rows, columns), F32),
        compiler_params=params(),
        cost_estimate=cost(5),
    )(at, first, second)


def norm_back(grad, values, scale, gain):
    grad_gain = jnp.sum(grad * values * scale, axis=0)
    scaled = grad * gain
    grad_values = scale * scaled - values * scale * scale * scale * jnp.mean(
        scaled * values, axis=-1, keepdims=True
    )
    return grad_values, grad_gain


def local(
    tokens,
    segments,
    routes,
    query_weight,
    key_weight,
    value_weight,
    out_weight,
    attn_gain,
    ffn_gain,
    router_weight,
    shared_gate,
    shared_up,
    shared_down,
    expert_gate,
    expert_up,
    expert_down,
    cotangent,
):
    fsdp, ctx, tp = (lax.axis_size(a) for a in ("fsdp", "ctx", "tp"))
    pairs = fsdp // 2
    me = lax.axis_index("fsdp")
    pair, core = me // 2, me % 2
    plane = lax.axis_index("ctx")
    lane = lax.axis_index("tp")
    tokens, cotangent, routes = tokens[0], cotangent[0], routes[0]
    block, width = tokens.shape
    share, cols = query_weight.shape
    experts = expert_gate.shape[0]
    hidden_units = expert_gate.shape[2]
    units = shared_gate.shape[1] // 2
    owned = experts // ctx
    top_count = routes.shape[1]
    capacity = 3 * top_count * block // (2 * experts)
    tok = block // tp
    entries = [
        lane, pair, core, plane, owned * plane, owned * (plane ^ 2), plane ^ 2, plane // 2, 1 - plane // 2, plane % 2
    ] + [(pair + j) % pairs for j in range(1, pairs)]
    at = lax.optimization_barrier(jnp.stack(entries).astype(jnp.int32))

    phases = Phases()

    def to_pairs(piece):
        return [pair_shift(piece, d) for d in range(1, pairs)]

    def to_tp(piece):
        return [tp_shift(piece, j) for j in range(1, tp)]

    def joined(*pieces):
        return place(pieces, lane).reshape(block, width)

    other_plane = plane ^ 2

    gains = jnp.concatenate([attn_gain[None], ffn_gain[None]], axis=0)
    qkv_mine, small_mine, tokens_mine = pack(
        at, tp, key_weight, value_weight, query_weight, router_weight.T, gains, tokens)
    small_core = core_swap(small_mine)
    qkv_mine, small_mine, tokens_mine, small_core = phases.run(
        lambda *given: given, qkv_mine, small_mine, tokens_mine, small_core)


    def send_first(qkv, small, small_core, tokens_mine, cotangent):
        prepared = prepare(at, tp, experts, routes.T, cotangent, segments)
        return (
            to_pairs(qkv), core_swap(qkv), to_pairs(jnp.concatenate([small, small_core], axis=0)),
            ctx_open(tokens_mine, 1),
            prepared)

    qkv_far, qkv_core, small_far, prev_one_mine, prepared = phases.run(
        send_first, qkv_mine, small_mine, small_core, tokens_mine, cotangent)
    cosine, sine, kseg, qseg, hits = prepared[:5]
    cot_own = prepared[5:]
    gathered = small_mine, small_core, small_far

    def all_small(small_mine, small_core, small_far):
        rows = place([jnp.concatenate([small_mine, small_core], axis=0)] + small_far, pair)
        rows = rows.reshape(pairs, 2, 16, share)
        rows = jnp.where(core == 0, rows, rows[:, ::-1])
        return rows.reshape(fsdp, 16, share).transpose(1, 0, 2).reshape(16, width)

    def send_second(qkv_far, prev_one_mine, out_weight, gathered, *stacks):
        return (
            [core_swap(one) for one in qkv_far], to_tp(prev_one_mine), ctx_open(prev_one_mine, 1),
            to_pairs(out_weight.T), all_small(*gathered), bundles(at, owned, units, stacks[:3], stacks[3:]))

    qkv_far_core, prev_one_other, prev_two_mine, out_far, small_all, (weights_mine, again_mine) = phases.run(
        send_second, qkv_far, prev_one_mine, out_weight, gathered, expert_gate, expert_up,
        jnp.swapaxes(expert_down, 1, 2), shared_gate, shared_up, shared_down.T)
    weights = lax.all_gather(weights_mine, "fsdp", axis=0)
    attn_scale = small_all[experts : experts + 1].astype(F32)
    ffn_scale = small_all[experts + 1 : experts + 2].astype(F32)
    router_t = jnp.concatenate([small_all[:experts], jnp.zeros((16 - experts, width), BF16)], axis=0)
    router_full = small_all[:experts].T
    here = [(plane + d) % ctx for d in range(ctx)]
    half = ctx // 2

    def near_projection(prev_one_mine, prev_one_other, prev_two_mine, cot, out_weight, out_far, same, cross, scale):
        sent = (
            to_tp(prev_two_mine), ctx_swap(cot), [core_swap(one) for one in [out_weight.T] + out_far])
        return sent, project_near(
            at, tokens, [prev_one_mine] + prev_one_other, same, cross, scale, cosine, sine)

    (prev_two_other, cot_one, out_cross), first = phases.run(
        near_projection, prev_one_mine, prev_one_other, prev_two_mine, cot_own[0], out_weight, out_far,
        [qkv_mine] + qkv_far, [qkv_core] + qkv_far_core, attn_scale)
    query, qkv_full, prev_one = first[3:]

    def attention(prev_two_mine, prev_two_other, cot, cot_one, out_weight, out_far, out_cross):
        sent = ctx_swap(cot, 2), to_tp(cot_one)
        hid, keys, values, prev_two = project_far(
            at, [prev_two_mine] + prev_two_other, qkv_full, attn_scale, cosine, sine, first[:3])
        attended, lse = attend(query, keys, values, kseg, qseg)
        same = place([out_weight.T] + out_far, pair)
        cross = place(out_cross, pair)
        out_full = place_rows([same, cross], core).reshape(width, cols)
        partial = dot_nt(attended, out_full).astype(BF16).reshape(tp, tok, width)
        return sent, hid, keys, values, prev_two, attended, lse, out_full, partial

    (cot_two, cot_one_other), hid, keys, values, prev_two, attended, lse, out_full, partial = phases.run(
        attention, prev_two_mine, prev_two_other, cot_own[0], cot_one, out_weight, out_far, out_cross)

    def sent_tp(total):
        return [tp_shift(pick(total, (lane + j) % tp), j) for j in range(1, tp)]

    def sum_tp(total, got):
        result = pick(total, lane).astype(F32)
        for one in got:
            result = result + one.astype(F32)
        return result

    partial_other, cot_three, again_mine = phases.run(
        lambda partial, cot_two, again_mine: (sent_tp(partial), ctx_swap(cot_two), again_mine),
        partial, cot_two, again_mine)
    other_weights = lax.all_gather(again_mine, "fsdp", axis=0)
    inputs_mine = tokens_mine.astype(F32)

    def normalize(partial, got):
        mixed = inputs_mine + sum_tp(partial, got)
        scale_ffn = lax.rsqrt(jnp.mean(mixed * mixed, axis=-1, keepdims=True) + EPS)
        return (mixed * scale_ffn * ffn_scale).astype(BF16), mixed, scale_ffn

    normed_low, mixed, scale_ffn = phases.run(normalize, partial, partial_other)

    x_zero, x_one = phases.run(lambda one: (to_tp(one), ctx_swap(one)), normed_low)
    half = ctx // 2

    def joint(mine, other):
        return [[one] + list(two) for one, two in zip(mine, other)]

    def blocks_of(first, steps, full, which, with_units, sources, weights, more, saved):
        return expert_blocks(
            first, ctx, steps, capacity, tp, experts, with_units, full, at, which, sources, weights, router_t, more, saved)

    def own_step(first, full, weights, x_pieces, cot_pieces, saved):
        return blocks_of(first, 1, full, OWN_EXPERTS, 0, ([x_pieces], [cot_pieces]), weights, [], saved)

    def block_zero(normed_low, x_zero, cot_own, x_one, cot_two, weights):
        sent = to_tp(x_one), ctx_swap(normed_low, 2), to_tp(cot_two)
        return sent, own_step(0, True, weights, [normed_low] + x_zero, cot_own, [])

    (other_one, x_two, cot_two_other), saved = phases.run(
        block_zero, normed_low, x_zero, cot_own, x_one, cot_two, weights)

    def block_one(x_one, other_one, cot_one, cot_one_other, x_two, cot_three, weights, saved):
        sent = to_tp(x_two), ctx_swap(x_two), to_tp(cot_three)
        return sent, own_step(1, True, weights, [x_one] + other_one, [cot_one] + cot_one_other, saved)

    (other_two, x_three, cot_three_other), saved = phases.run(
        block_one, x_one, other_one, cot_one, cot_one_other, x_two, cot_three, weights, saved)
    more = saved[:2]

    def block_two(x_two, other_two, cot_two, cot_two_other, x_three, weights, saved):
        sent = to_tp(x_three)
        return sent, own_step(2, False, weights, [x_two] + other_two, [cot_two] + cot_two_other, saved)

    other_three, saved = phases.run(
        block_two, x_two, other_two, cot_two, cot_two_other, x_three, weights, saved[2:])

    def weight_step(left, right):
        return weight_grads(at, left, [right], pairs)[0]

    def weight_pair(left, one, two):
        return weight_grads(at, left, [one, two], pairs)

    def own_rest(x_three, other_three, cot_three, cot_three_other, weights, saved):
        saved = own_step(3, False, weights, [x_three] + other_three, [cot_three] + cot_three_other, saved)
        sx, sr, sh, sa, sb = saved[:5]
        down = weight_step(sr, sh)
        return saved, down, core_swap(down[0]), *weight_pair(sx, sa, sb)

    saved, down, down_got, gate, up = phases.run(
        own_rest, x_three, other_three, cot_three, cot_three_other, weights, saved)
    sx, sr, sh, sa, sb, ssx, ssc = saved


    def sums(sent, *own):
        jobs = [(NEXT_PAIR + j - 1, *sent, []) for j in range(1, pairs)] if sent else []
        given = pair_sums(at, jobs + [(PAIR, *one) for one in own])
        return [given[: len(jobs)], *given[len(jobs) :]]

    def sent_pairs(rows):
        return [pair_shift(one, j + 1) for j, one in enumerate(rows)]

    def other_full(down, gate_sent, up_sent, ssx, other_weights, more):
        sent = sent_pairs(sums(down)[0]), core_swap(gate_sent), core_swap(up_sent)
        return sent, blocks_of(0, half, True, FAR_EXPERTS, units, (ssx, ssc), other_weights, more, [])

    (down_far, gate_got, up_got), got = phases.run(
        other_full, (down[1], down_got), gate[0], up[0], ssx, other_weights, more)
    dx, out = (one.reshape((half * tp,) + one.shape[2:]) for one in got[:2])

    def sent_tp_of(stack, block_index):
        return [tp_shift(pick(stack, block_index * tp + (lane + j) % tp), j) for j in range(1, tp)]

    def sum_tp_of(stack, block_index, far):
        result = pick(stack, block_index * tp + lane).astype(F32)
        for one in far:
            result = result + one.astype(F32)
        return result

    def back_through_norm(dx_sum):
        grad_normed = dx_sum[:tok]
        grad_gates = dx_sum[tok : tok + experts, :tok].T
        named = lax.dynamic_slice_in_dim(hits, lane * tok, tok, 1).T > 0.0
        logits = jnp.where(named, dot(normed_low, router_full), -1e30)
        expo = jnp.where(named, jnp.exp(logits - jnp.max(logits, axis=-1, keepdims=True)), 0.0)
        gates = expo / jnp.sum(expo, axis=-1, keepdims=True)
        grad_logits = (
            gates * (grad_gates - jnp.sum(gates * grad_gates, axis=-1, keepdims=True))
        ).astype(BF16)
        grad_normed = grad_normed + dot_nt(grad_logits, router_full)
        grad_mixed_norm, grad_ffn_gain = norm_back(grad_normed, mixed, scale_ffn, ffn_scale)
        grad_out = lax.dynamic_slice_in_dim(cotangent, lane * tok, tok, 0).astype(F32)
        grad_mixed = grad_out + grad_mixed_norm
        return grad_mixed.astype(BF16), grad_mixed, grad_ffn_gain, dot_tn(grad_logits, normed_low)

    def phase_one(gate, dx, down, ssx, saved):
        rows, own_down = sums(gate, down)
        sent = sent_pairs(rows), sent_tp_of(dx, 1), sent_tp_of(dx, 0)
        saved = blocks_of(half, half, False, FAR_EXPERTS, units, (ssx, ssc), other_weights, [], saved)
        return sent, saved, weight_step(saved[1], saved[2]), own_down

    (gate_far, dx_one, dx_zero), other_saved, other_down, own_down = phases.run(
        phase_one, (gate[1], gate_got), dx, (down[1], down_got, down_far), ssx, got[2:])
    ox, orr, oh, oa, ob, ssh, ssa, ssb = other_saved
    groups = [[2 * i, 2 * i + 1] for i in range(ctx // 2)]

    def neighbours(piece):
        return lax.all_gather(piece, "ctx", axis=0, axis_index_groups=groups)

    both_down = neighbours(own_down)

    def phase_two(up, down_sent, dx, dx_one, gate, ox, out):
        rows, own_gate = sums(up, gate)
        sent = (
            sent_pairs(rows), core_swap(down_sent),
            ctx_swap(sum_tp_of(dx, 1, dx_one).astype(BF16)), sent_tp_of(out, 1))
        other_gate, other_up = weight_pair(ox, oa, ob)
        return sent, own_gate, other_gate, other_up

    (up_far, down_got, home, out_one), own_gate, other_gate, other_up = phases.run(
        phase_two, (up[1], up_got), other_down[0], dx, dx_one, (gate[1], gate_got, gate_far), ox, out)

    both_gate = neighbours(own_gate)

    def phase_three(down, gate_sent, both, dx, dx_zero, home, up, ssx, out, out_one):
        back = back_through_norm(sum_tp_of(dx, 0, dx_zero) + home.astype(F32))
        rows, own_up = sums(down, up)
        sent = (
            sent_pairs(rows), core_swap(gate_sent), to_tp(back[0]), ctx_swap(sum_tp_of(out, 1, out_one).astype(BF16)))
        shared = shared_grads(at, ssx, ssc, ssa, ssb, ssh, pairs)
        return sent, back, own_up, shared, both

    sent, back, own_up, shared, both_down = phases.run(
        phase_three, (other_down[1], down_got), other_gate[0], both_down, dx, dx_zero, home, (up[1], up_got, up_far), ssx,
        out, out_one)
    down_far, gate_got, grad_mixed_other, out_home = sent
    both_up = neighbours(own_up)
    grad_mixed_low, grad_mixed, grad_ffn_gain, grad_router = back

    def phase_four(gate, up_sent, shared_sent, both, down, grad_mixed_low, grad_mixed_other, out):
        summed, own_other_down = sums(gate, down)
        sent = sent_pairs(summed), core_swap(up_sent), core_swap(shared_sent), sent_tp_of(out, 0)
        rows = joined(grad_mixed_low, *grad_mixed_other)
        grad_attended = dot(rows, out_full).astype(BF16)
        grads = attend_back(query, keys, values, grad_attended, lse, kseg, qseg, cosine, sine)
        return sent, rows, grads, own_other_down, both

    (gate_far, up_got, shared_got, out_zero), grad_mixed_rows, (dq, dk, dv), own_other_down, both_gate = phases.run(
        phase_four, (other_gate[1], gate_got), other_up[0], shared[0], both_gate,
        (other_down[1], down_got, down_far), grad_mixed_low, grad_mixed_other, out)

    both_other_down = neighbours(own_other_down)

    def phase_five(up, both, dq, dk, dv, hid, gate):
        back = hidden_back([prev_two, prev_one, tokens], dk, dv, dq, qkv_full)
        hidden_parts = [one.reshape(tp, tok, width) for one in back[:-1]]
        small_rows = jnp.concatenate(
            [grad_router, grad_ffn_gain[None], back[-1], jnp.zeros((128 - experts - 2, width), F32)], axis=0)
        rows, own_other_gate = sums(up, gate)
        sent = sent_pairs(rows), sent_tp(hidden_parts[0])
        attn = attn_grads_of(at, hid, dk, dv, dq, grad_mixed_rows, attended, small_rows, pairs)
        return sent, hidden_parts, attn, own_other_gate, both

    (up_far, far_two), hidden_parts, attn, own_other_gate, both_up = phases.run(
        phase_five, (other_up[1], up_got), both_up, dq, dk, dv, hid,
        (other_gate[1], gate_got, gate_far))

    both_other_gate = neighbours(own_other_gate)

    def phase_six(attn, both, hidden_parts, far_two, up, shared, out, out_zero, out_home):
        attn_got = core_swap(attn[0])
        _, own_other_up = sums(None, up)
        sent = (
            sent_pairs(sums((attn[1], attn_got))[0]), ctx_open(sum_tp(hidden_parts[0], far_two).astype(BF16), -1),
            sent_tp(hidden_parts[1]), sent_pairs(sums(shared)[0]))
        output_mine = (mixed + sum_tp_of(out, 0, out_zero) + out_home.astype(F32)).astype(BF16)
        return sent, attn_got, own_other_up, both, collect(at, both_down, both), output_mine, to_tp(output_mine)

    (attn_far, carried, far_one, shared_far), attn_got, own_other_up, both_other_down, grad_expert_down, output_mine, output_other = phases.run(
        phase_six, attn, both_other_down, hidden_parts, far_two, (other_up[1], up_got, up_far), (shared[1], shared_got),
        out, out_zero, out_home)
    both_other_up = neighbours(own_other_up)

    def phase_seven(attn, both, hidden_parts, far_one, carried, both_gate, shared):
        pieces = attn_pieces(at, *attn)
        carried = ctx_open(
            (sum_tp(hidden_parts[1], far_one) + carried.astype(F32)).astype(BF16), -1)
        sent = (
            [ctx_shift(pieces[d], d) for d in range(1, ctx)], carried, sent_tp(hidden_parts[2]))
        return sent, pieces[0], collect(at, both_gate, both), sums(None, shared)[1]

    (attn_got, carried, hidden_other), attn_piece, grad_expert_gate, own_shared = phases.run(
        phase_seven, (attn[1], attn_got, attn_far), both_other_gate, hidden_parts, far_one, carried, both_gate,
        (shared[1], shared_got, shared_far))

    def input_back(total, got, carried):
        grad_hidden = sum_tp(total, got) + carried.astype(F32)
        scale_attn = lax.rsqrt(jnp.mean(inputs_mine * inputs_mine, axis=-1, keepdims=True) + EPS)
        scaled = grad_hidden * attn_scale
        grad_norm = scale_attn * scaled - inputs_mine * scale_attn * scale_attn * scale_attn * jnp.mean(
            scaled * inputs_mine, axis=-1, keepdims=True)
        return (grad_mixed + grad_norm).astype(BF16)

    def phase_eight(
        attn_piece, attn_got, hidden_parts, hidden_other, carried, both_up, both_other_up, own_shared, output_mine, output_other
    ):
        total = attn_piece.astype(F32)
        for one in attn_got:
            total = total + one.astype(F32)
        total = total.astype(BF16)
        input_mine = input_back(hidden_parts[2], hidden_other, carried)
        return (
            total, [ctx_shift(total, d) for d in range(1, ctx)], ctx_swap(own_shared), to_tp(input_mine),
            joined(output_mine, *output_other), input_mine, collect(at, both_up, both_other_up))

    attn_piece, attn_got, far_shared, input_other, output, input_mine, grad_expert_up = phases.run(
        phase_eight, attn_piece, attn_got, hidden_parts, hidden_other, carried, both_up, both_other_up, own_shared,
        output_mine, output_other)
    halves = jnp.where(
        plane % 2 == 0, jnp.stack([own_shared, far_shared]), jnp.stack([far_shared, own_shared])).astype(F32)
    result = [jnp.concatenate([one[:, i * units : (i + 1) * units] for one in halves], axis=1) for i in range(3)]
    input_grad = joined(input_mine, *input_other)
    grad_key_weight, grad_value_weight, grad_query_weight, grad_out_rows, small_out = finish(
        at, tie([attn_piece] + attn_got, grad_expert_up), share, cols)
    small_out = all_sum(small_out, "tp")
    grad_out_rows = grad_out_rows.T
    grad_expert_down = jnp.swapaxes(grad_expert_down, 1, 2)
    grad_shared_gate, grad_shared_up, grad_shared_down = result[0], result[1], result[2].T
    return (
        output[None],
        input_grad[None],
        grad_query_weight,
        grad_key_weight,
        grad_value_weight,
        grad_out_rows,
        small_out[experts + 1],
        small_out[experts],
        small_out[:experts].T,
        grad_shared_gate,
        grad_shared_up,
        grad_shared_down,
        grad_expert_gate,
        grad_expert_up,
        grad_expert_down,
    )


def solution(mesh):
    in_specs = (
        P("fsdp", "ctx", None),
        P("fsdp", None),
        P("fsdp", "ctx", None),
        P("fsdp", "tp"),
        P("fsdp", "tp"),
        P("fsdp", "tp"),
        P("tp", "fsdp"),
        P("fsdp"),
        P("fsdp"),
        P("fsdp", None),
        P("fsdp", "tp"),
        P("fsdp", "tp"),
        P("tp", "fsdp"),
        P(None, "fsdp", "tp"),
        P(None, "fsdp", "tp"),
        P(None, "tp", "fsdp"),
        P("fsdp", "ctx", None),
    )
    out_specs = (
        P("fsdp", "ctx", None),
        P("fsdp", "ctx", None),
        P("fsdp", "tp"),
        P("fsdp", "tp"),
        P("fsdp", "tp"),
        P("tp", "fsdp"),
        P("fsdp"),
        P("fsdp"),
        P("fsdp", None),
        P("fsdp", "tp"),
        P("fsdp", "tp"),
        P("tp", "fsdp"),
        P(None, "fsdp", "tp"),
        P(None, "fsdp", "tp"),
        P(None, "tp", "fsdp"),
    )
    return jax.shard_map(local, mesh=mesh, in_specs=in_specs, out_specs=out_specs, check_vma=False)
```

```python
import functools

import jax
import jax.numpy as jnp
from jax import lax
from jax.experimental import pallas as pl
from jax.experimental.pallas import tpu as pltpu
from jax.sharding import PartitionSpec as P

HD = 64
WINDOW = 1024
EPS = 1e-06
F32 = jnp.float32
BF16 = jnp.bfloat16
VMEM_BYTES = 56 * 1024 * 1024
COST_SCALE = 0.3


def dot(left, right):
    return lax.dot_general(left, right, (((1,), (0,)), ((), ())), preferred_element_type=F32)


def dot_nt(left, right):
    return lax.dot_general(left, right, (((1,), (1,)), ((), ())), preferred_element_type=F32)


def dot_tn(left, right):
    return lax.dot_general(left, right, (((0,), (0,)), ((), ())), preferred_element_type=F32)


def core_swap(block):
    size = lax.axis_size("fsdp")
    return lax.ppermute(block, "fsdp", [(i, i ^ 1) for i in range(size)])


def pair_shift(block, distance):
    size = lax.axis_size("fsdp")
    pairs = size // 2
    route = [(i, ((i // 2 + distance) % pairs) * 2 + i % 2) for i in range(size)]
    return lax.ppermute(block, "fsdp", route)


def pair_swap(block, reach):
    size = lax.axis_size("fsdp")
    return lax.ppermute(block, "fsdp", [(i, i ^ (2 * reach)) for i in range(size)])


def tp_shift(block, distance):
    size = lax.axis_size("tp")
    return lax.ppermute(block, "tp", [(i, (i + distance) % size) for i in range(size)])


def ctx_shift(block, distance):
    size = lax.axis_size("ctx")
    return lax.ppermute(block, "ctx", [(i, (i + distance) % size) for i in range(size)])


def ctx_swap(block, reach=1):
    size = lax.axis_size("ctx")
    return lax.ppermute(block, "ctx", [(i, i ^ reach) for i in range(size)])


def ctx_open(block, distance):
    size = lax.axis_size("ctx")
    route = [(i, i + distance) for i in range(size) if 0 <= i + distance < size]
    return lax.ppermute(block, "ctx", route)


def pick(stack, index):
    return lax.dynamic_index_in_dim(stack, index, 0, keepdims=False)


def place_rows(pieces, me):
    first, second = pieces
    return jnp.where(
        me == 0, jnp.stack([first, second], axis=1), jnp.stack([second, first], axis=1))


def place(pieces, me):
    count = len(pieces)
    if count == 1:
        return pieces[0][None]
    if count == 2:
        first, second = pieces
        return jnp.where(me == 0, jnp.stack([first, second]), jnp.stack([second, first]))
    result = jnp.zeros((count,) + pieces[0].shape, pieces[0].dtype)
    for d, piece in enumerate(pieces):
        result = lax.dynamic_update_index_in_dim(result, piece, (me - d) % count, 0)
    return result


def tie(values, *others):
    return lax.optimization_barrier((values, others))[0]


class Phases:
    def __init__(self):
        self.last = []

    def run(self, function, *values):
        given = function(*(tie(values, self.last) if self.last else values))
        self.last = jax.tree.leaves(given)
        return given


def all_sum(block, axis):
    size = lax.axis_size(axis)
    reach = 1
    while reach < size:
        other = lax.ppermute(block, axis, [(i, i ^ reach) for i in range(size)])
        block = block + other
        reach *= 2
    return block


LANE, PAIR, CORE, PLANE, OWN_EXPERTS, FAR_EXPERTS, FAR_PLANE, OWN_HALF, OTHER_HALF, PARITY, NEXT_PAIR = range(11)


def whole(shape):
    return pl.BlockSpec(shape, lambda *_: (0,) * len(shape))


def params():
    return pltpu.CompilerParams(vmem_limit_bytes=VMEM_BYTES)


def cost(microseconds):
    return pl.CostEstimate(flops=0, bytes_accessed=int(microseconds * COST_SCALE * 3.4e6), transcendentals=0)


def swap_halves(values):
    width = values.shape[-1]
    lane = lax.broadcasted_iota(jnp.int32, values.shape, 1)
    up = pltpu.roll(values, width - HD // 2, 1)
    down = pltpu.roll(values, HD // 2, 1)
    return jnp.where(lane % HD < HD // 2, up, down)


def widen(table, width):
    copies = -(-width // table.shape[1])
    return jnp.concatenate([table] * copies, axis=1)[:, :width]


def rotated(values, cosine, sine):
    return (values * cosine + swap_halves(values) * sine).astype(BF16)


def project_rows(inputs, gain, weights, cos_ref, sin_ref, hid_ref, k_ref, v_ref):
    scale = lax.rsqrt(jnp.mean(inputs * inputs, axis=-1, keepdims=True) + EPS)
    hidden = (inputs * scale * gain).astype(BF16)
    hid_ref[...] = hidden
    width = k_ref.shape[1]
    k_ref[...] = rotated(
        dot(hidden, weights[:, :width]), widen(cos_ref[...], width), widen(sin_ref[...], width))
    v_ref[...] = dot(hidden, weights[:, width : 2 * width]).astype(BF16)
    return hidden


def project_near_kernel(parts, pairs, meta_ref, tok_ref, *refs):
    prev_refs, refs = refs[:parts], refs[parts:]
    same_refs, cross_refs, refs = refs[:pairs], refs[pairs : 2 * pairs], refs[2 * pairs :]
    gain_ref, cos_ref, sin_ref, hid_ref, k_ref, v_ref, q_ref, w_ref, prev_ref, w_all, x_all = refs
    tok, features = x_all.shape[1:]
    share, columns = w_all.shape[1:]

    @pl.when(pl.program_id(0) == 0)
    def _():
        for d in range(pairs):
            row = 2 * lax.rem(meta_ref[PAIR] + pairs - d, pairs)
            w_all[row + meta_ref[CORE]] = same_refs[d][...]
            w_all[row + 1 - meta_ref[CORE]] = cross_refs[d][...]
        for j in range(parts):
            x_all[lax.rem(meta_ref[LANE] + parts - j, parts)] = prev_refs[j][...]
        weights = w_all[...].reshape(2 * pairs * share, columns)
        w_ref[...] = weights
        inputs = x_all[...].reshape(parts * tok, features)
        prev_ref[...] = inputs
        project_rows(inputs.astype(F32), gain_ref[...], weights, cos_ref, sin_ref, hid_ref, k_ref, v_ref)

    @pl.when(pl.program_id(0) == 1)
    def _():
        weights = w_all[...].reshape(2 * pairs * share, columns)
        hidden = project_rows(
            tok_ref[...].astype(F32), gain_ref[...], weights, cos_ref, sin_ref, hid_ref, k_ref, v_ref)
        width = k_ref.shape[1]
        query = dot(hidden, weights[:, 2 * width :])
        q_ref[...] = rotated(
            query, widen(cos_ref[...], width), widen(sin_ref[...], width)) * jnp.asarray(HD**-0.5, BF16)


def project_near(meta, tokens, prev_pieces, same, cross, gain, cosine, sine):
    rows, features = tokens.shape
    share, columns = same[0].shape
    width = columns // 3
    tok = prev_pieces[0].shape[0]
    count = 2 * len(same) * share
    shapes = [(3 * rows, features), (3 * rows, width), (3 * rows, width)]
    block = lambda i, meta: (i + 1, 0)
    others = [(rows, width), (count, columns), (rows, features)]
    operands = [tokens, *prev_pieces, *same, *cross, gain]
    table = pl.BlockSpec((rows, cosine.shape[1]), block)
    return pl.pallas_call(
        functools.partial(project_near_kernel, len(prev_pieces), len(same)),
        grid_spec=pltpu.PrefetchScalarGridSpec(
            num_scalar_prefetch=1,
            grid=(2,),
            in_specs=[whole(o.shape) for o in operands] + [table, table],
            out_specs=[pl.BlockSpec((rows, shape[1]), block) for shape in shapes]
            + [whole(shape) for shape in others],
            scratch_shapes=[
                pltpu.VMEM((2 * len(same), share, columns), BF16),
                pltpu.VMEM((len(prev_pieces), tok, features), BF16),
            ],
        ),
        out_shape=[jax.ShapeDtypeStruct(shape, BF16) for shape in shapes + others],
        compiler_params=params(),
        cost_estimate=cost(7),
    )(meta, *operands, cosine, sine)


def project_far_kernel(parts, meta_ref, *refs):
    prev_refs, refs = refs[:parts], refs[parts:]
    w_ref, gain_ref, cos_ref, sin_ref, _, _, _, hid_ref, k_ref, v_ref, prev_ref, x_all = refs
    tok, features = x_all.shape[1:]
    for j in range(parts):
        x_all[lax.rem(meta_ref[LANE] + parts - j, parts)] = prev_refs[j][...]
    inputs = x_all[...].reshape(parts * tok, features)
    prev_ref[...] = inputs
    project_rows(inputs.astype(F32), gain_ref[...], w_ref[...], cos_ref, sin_ref, hid_ref, k_ref, v_ref)


def project_far(meta, prev_pieces, weights, gain, cosine, sine, saved):
    tok, features = prev_pieces[0].shape
    rows = tok * len(prev_pieces)
    width = weights.shape[1] // 3
    first = lambda i, meta: (0, 0)
    operands = [*prev_pieces, weights, gain]
    table = pl.BlockSpec((rows, cosine.shape[1]), first)
    return pl.pallas_call(
        functools.partial(project_far_kernel, len(prev_pieces)),
        grid_spec=pltpu.PrefetchScalarGridSpec(
            num_scalar_prefetch=1,
            grid=(1,),
            in_specs=[whole(o.shape) for o in operands] + [table, table]
            + [pl.BlockSpec(memory_space=pl.ANY)] * 3,
            out_specs=[pl.BlockSpec((rows, one.shape[1]), first) for one in saved]
            + [whole((rows, features))],
            scratch_shapes=[pltpu.VMEM((len(prev_pieces), tok, features), BF16)],
        ),
        out_shape=[jax.ShapeDtypeStruct(one.shape, BF16) for one in saved]
        + [jax.ShapeDtypeStruct((rows, features), BF16)],
        input_output_aliases={1 + len(operands) + 2 + i: i for i in range(3)},
        compiler_params=params(),
        cost_estimate=cost(4),
    )(meta, *operands, cosine, sine, *saved)


def prepare_kernel(parts, meta_ref, routes_ref, cot_ref, rates_ref, seg_ref, *refs):
    cos_ref, sin_ref, kseg_ref, qseg_ref, hits_ref = refs[:5]
    mine_ref, other_refs, seg_all = refs[5], refs[6:-1], refs[-1]
    block, width = cot_ref.shape
    tok = block // parts
    experts = hits_ref.shape[0]
    rows, lanes = cos_ref.shape
    short = 64
    origin = (meta_ref[PLANE] - 2) * block
    far = (lax.broadcasted_iota(jnp.int32, (rows // short, lanes), 0) * short + origin).astype(F32) * rates_ref[...]
    near = lax.broadcasted_iota(jnp.int32, (short, lanes), 0).astype(F32) * rates_ref[...]
    far_cos, far_sin, near_cos, near_sin = jnp.cos(far), jnp.sin(far), jnp.cos(near), jnp.sin(near)
    sign = jnp.where(lax.broadcasted_iota(jnp.int32, (short, lanes), 1) % HD < HD // 2, -1.0, 1.0)
    signed_sin, signed_cos = sign * near_sin, sign * near_cos
    for h in range(rows // short):
        part = slice(h * short, (h + 1) * short)
        one_cos, one_sin = far_cos[h : h + 1], far_sin[h : h + 1]
        cos_ref[part] = one_cos * near_cos - one_sin * near_sin
        sin_ref[part] = one_sin * signed_cos + one_cos * signed_sin
    seg_all[:, : 2 * block] = jnp.full((1, 2 * block), -1, jnp.int32)
    seg_all[:, 2 * block :] = seg_ref[...]
    kseg = seg_all[:, pl.ds(pl.multiple_of(meta_ref[PLANE] * block, block), rows)]
    qseg_ref[...] = kseg[:, rows - block :]
    kseg_ref[...] = jnp.broadcast_to(kseg, (8, rows)).T[:, :1]
    row = lax.broadcasted_iota(jnp.int32, (experts, block), 0)
    named = row == routes_ref[0:1, :]
    for j in range(1, routes_ref.shape[0]):
        named = named | (row == routes_ref[j : j + 1, :])
    hits = jnp.where(named, 1.0, 0.0).astype(F32)
    before = lax.broadcasted_iota(jnp.int32, (block, block), 0) < lax.broadcasted_iota(jnp.int32, (block, block), 1)
    rank = dot(hits.astype(BF16), jnp.where(before, 1.0, 0.0).astype(BF16))
    hits_ref[...] = hits
    table = jnp.concatenate([jnp.where(named, rank, -1.0), jnp.zeros((16 - experts, block), F32)], axis=0)
    mine_ref[tok:, :] = jnp.concatenate([table, jnp.zeros((16, width - block), F32)], axis=1).astype(BF16)
    for j, ref in enumerate((mine_ref,) + other_refs):
        start = lax.rem(meta_ref[LANE] + parts - j, parts) * tok
        ref[:tok, :] = cot_ref[pl.ds(pl.multiple_of(start, tok), tok), :]


def prepare(meta, parts, experts, routes_t, cotangent, segments):
    block, width = cotangent.shape
    tok = block // parts
    index = jnp.arange(2 * HD, dtype=jnp.int32)
    rates = (10000.0 ** (-2.0 * (index % (HD // 2)).astype(F32) / HD))[None, :]
    shapes = [
        ((3 * block, 2 * HD), F32), ((3 * block, 2 * HD), F32), ((3 * block, 1), jnp.int32), ((1, block), jnp.int32),
        ((experts, block), F32), ((tok + 16, width), BF16),
    ] + [((tok, width), BF16)] * (parts - 1)
    operands = (routes_t, cotangent, rates, segments)
    return pl.pallas_call(
        functools.partial(prepare_kernel, parts),
        grid_spec=pltpu.PrefetchScalarGridSpec(
            num_scalar_prefetch=1,
            grid=(1,),
            in_specs=[whole(o.shape) for o in operands],
            out_specs=[whole(shape) for shape, _ in shapes],
            scratch_shapes=[pltpu.VMEM((1, segments.shape[1] + 2 * block), jnp.int32)],
        ),
        out_shape=[jax.ShapeDtypeStruct(shape, kind) for shape, kind in shapes],
        compiler_params=params(),
        cost_estimate=cost(3),
    )(meta, *operands)


def bundle_kernel(at_ref, *refs):
    own, far, shared, (own_ref, far_ref) = refs[:3], refs[3:6], refs[6:9], refs[9:]
    owned = own[0].shape[0]
    for i in range(3):
        own_ref[i * owned : (i + 1) * owned] = own[i][...]
        far_ref[i * owned : (i + 1) * owned] = far[i][...]
    units = shared[0].shape[1]
    gate_ref, up_ref, down_ref = shared
    far_ref[3 * owned, :, :units] = gate_ref[...]
    far_ref[3 * owned, :, units:] = up_ref[...]
    far_ref[3 * owned + 1, :, :units] = down_ref[...]
    far_ref[3 * owned + 1, :, units:] = jnp.zeros_like(down_ref)


def bundles(at, owned, units, stacks, shared):
    _, share, hidden = stacks[0].shape

    def rows_of(which):
        return [pl.BlockSpec((owned, share, hidden), lambda i, at: (at[which], 0, 0))] * 3

    shapes = [(3 * owned, share, hidden), (3 * owned + 2, share, hidden)]
    return pl.pallas_call(
        bundle_kernel,
        grid_spec=pltpu.PrefetchScalarGridSpec(
            num_scalar_prefetch=1,
            grid=(1,),
            in_specs=rows_of(PLANE) + rows_of(FAR_PLANE)
            + [pl.BlockSpec((share, units), lambda i, at: (0, at[PARITY]))] * 3,
            out_specs=[whole(shape) for shape in shapes],
        ),
        out_shape=[jax.ShapeDtypeStruct(shape, BF16) for shape in shapes],
        compiler_params=params(),
        cost_estimate=cost(5),
    )(at, *stacks, *stacks, *shared)


def finish_kernel(meta_ref, mine_ref, *refs):
    count = len(refs) - 6
    pieces = (mine_ref,) + refs[:count]
    k_ref, v_ref, q_ref, o_ref, small_ref, all_ref = refs[count:]
    total = len(pieces)
    rows = mine_ref.shape[0]
    for d, ref in enumerate(pieces):
        all_ref[lax.rem(meta_ref[PLANE] + total - d, total)] = ref[...].astype(F32)
    whole_rows = all_ref[...].reshape(total * rows, mine_ref.shape[1])
    share, cols = k_ref.shape
    for i, ref in enumerate((k_ref, v_ref, q_ref, o_ref)):
        ref[...] = whole_rows[:share, i * cols : (i + 1) * cols]
    small_ref[...] = whole_rows[:share, 4 * cols :].T[:16]


def finish(meta, pieces, share, cols):
    rows, columns = pieces[0].shape
    shapes = [(share, cols)] * 4 + [(16, share)]
    return pl.pallas_call(
        finish_kernel,
        grid_spec=pltpu.PrefetchScalarGridSpec(
            num_scalar_prefetch=1,
            grid=(1,),
            in_specs=[whole(piece.shape) for piece in pieces],
            out_specs=[whole(shape) for shape in shapes],
            scratch_shapes=[pltpu.VMEM((len(pieces), rows, columns), F32)],
        ),
        out_shape=[jax.ShapeDtypeStruct(shape, F32) for shape in shapes],
        compiler_params=params(),
        cost_estimate=cost(2),
    )(meta, *pieces)


def pack_kernel(lane_ref, k_ref, v_ref, q_ref, router_ref, gains_ref, tok_ref, qkv_ref, small_ref, mine_ref):
    width = k_ref.shape[1]
    for i, ref in enumerate((k_ref, v_ref, q_ref)):
        qkv_ref[:, i * width : (i + 1) * width] = ref[...]
    experts, share = router_ref.shape
    small_ref[...] = jnp.concatenate(
        [router_ref[...].astype(F32), gains_ref[...].astype(F32),
         jnp.zeros((small_ref.shape[0] - experts - 2, share), F32)], axis=0).astype(BF16)
    mine_ref[...] = tok_ref[...]


def pack(at, parts, key_weight, value_weight, query_weight, router_t, gains, tokens):
    rows, width = tokens.shape
    share, cols = key_weight.shape
    part = (rows // parts, width)
    shapes = [(share, 3 * cols), (16, share), part]
    operands = (key_weight, value_weight, query_weight, router_t, gains)
    return pl.pallas_call(
        pack_kernel,
        grid_spec=pltpu.PrefetchScalarGridSpec(
            num_scalar_prefetch=1,
            grid=(1,),
            in_specs=[whole(o.shape) for o in operands]
            + [pl.BlockSpec(part, lambda i, at: (at[LANE], 0))],
            out_specs=[whole(shape) for shape in shapes],
        ),
        out_shape=[jax.ShapeDtypeStruct(shape, BF16) for shape in shapes],
        compiler_params=params(),
        cost_estimate=cost(2),
    )(at, *operands, tokens)


def mask_bias(kseg, qseg, keys, queries):
    key = lax.broadcasted_iota(jnp.int32, (keys, queries), 0)
    query = lax.broadcasted_iota(jnp.int32, (keys, queries), 1)
    allowed = (key > query) & (key <= query + WINDOW) & (kseg == qseg)
    return jnp.where(allowed, 0.0, -1e30).astype(F32)


def head_only(values, head):
    lane = lax.broadcasted_iota(jnp.int32, values.shape, 1)
    return jnp.where(lane // HD == head, values, jnp.zeros_like(values))


def loaded(ref, width):
    values = ref[...]
    if width % values.shape[1] == 0:
        return values
    lane = lax.broadcasted_iota(jnp.int32, values.shape, 1) + pl.program_id(0) * values.shape[1]
    return jnp.where(lane < width, values, jnp.zeros_like(values))


def attend_kernel(tile, width, q_ref, k_ref, v_ref, kseg_ref, qseg_ref, out_ref, lse_ref, bias_ref):
    rows = q_ref.shape[0]
    span = WINDOW + tile
    tiles = rows // tile

    @pl.when(pl.program_id(0) == 0)
    def _():
        for j in range(tiles):
            bias_ref[j] = mask_bias(
                kseg_ref[pl.ds(j * tile, span), :], qseg_ref[:, pl.ds(j * tile, tile)], span, tile
            )

    keys = loaded(k_ref, width)
    values_t = loaded(v_ref, width).T
    queries = loaded(q_ref, width)
    for j in range(tiles):
        start = j * tile
        query = queries[start : start + tile]
        parts = []
        for head in range(2):
            scores = dot_nt(keys[start : start + span], head_only(query, head)) + bias_ref[j]
            top = jnp.max(scores, axis=0, keepdims=True)
            expo = jnp.exp(scores - top)
            total = jnp.sum(expo, axis=0, keepdims=True)
            part = dot(
                values_t[head * HD : (head + 1) * HD, start : start + span], expo.astype(BF16)
            )
            parts.append(part / total)
            lse_ref[0, pl.ds(head, 1), pl.ds(start, tile)] = top + jnp.log(total)
        out_ref[pl.ds(start, tile), :] = jnp.concatenate(parts, axis=0).T.astype(BF16)


def attend(query, keys, values, kseg, qseg):
    rows, width = query.shape
    span = keys.shape[0]
    tile = min(256, rows)
    pairs = -(-width // (2 * HD))
    columns = lambda count: pl.BlockSpec((count, 2 * HD), lambda i: (0, i))
    return pl.pallas_call(
        functools.partial(attend_kernel, tile, width),
        grid=(pairs,),
        in_specs=[columns(rows), columns(span), columns(span), whole((span, 1)), whole((1, rows))],
        out_specs=[columns(rows), pl.BlockSpec((1, 2, rows), lambda i: (i, 0, 0))],
        out_shape=[
            jax.ShapeDtypeStruct((rows, width), BF16),
            jax.ShapeDtypeStruct((pairs, 2, rows), F32),
        ],
        scratch_shapes=[pltpu.VMEM((rows // tile, WINDOW + tile, tile), F32)],
        compiler_params=params(),
        cost_estimate=cost(13),
    )(query, keys, values, kseg, qseg)


def attend_back_kernel(
    tile, width, q_ref, k_ref, v_ref, g_ref, lse_ref, kseg_ref, qseg_ref, cos_ref, sin_ref,
    dq_ref, dk_ref, dv_ref, bias_ref, dk_acc, dv_acc,
):
    rows = q_ref.shape[0]
    span = WINDOW + tile
    tiles = rows // tile
    total_keys = k_ref.shape[0]

    @pl.when(pl.program_id(0) == 0)
    def _():
        for j in range(tiles):
            bias_ref[j] = mask_bias(
                kseg_ref[pl.ds(j * tile, span), :], qseg_ref[:, pl.ds(j * tile, tile)], span, tile
            )

    keys = loaded(k_ref, width)
    values = loaded(v_ref, width)
    queries = loaded(q_ref, width)
    grads = loaded(g_ref, width)
    keys_t = keys.T
    dk_acc[...] = jnp.zeros_like(dk_acc)
    dv_acc[...] = jnp.zeros_like(dv_acc)
    cosine = cos_ref[...]
    sine = sin_ref[...]
    lead = total_keys - rows
    for j in range(tiles):
        start = j * tile
        query = queries[start : start + tile]
        grad = grads[start : start + tile]
        parts = []
        for head in range(2):
            query_one = head_only(query, head)
            grad_one = head_only(grad, head)
            scores = dot_nt(keys[start : start + span], query_one) + bias_ref[j]
            probs = jnp.exp(scores - lse_ref[0, pl.ds(head, 1), pl.ds(start, tile)])
            grad_probs = dot_nt(values[start : start + span], grad_one)
            delta = jnp.sum(probs * grad_probs, axis=0, keepdims=True)
            grad_scores = (probs * (grad_probs - delta)).astype(BF16)
            dv_acc[pl.ds(start, span), :] += dot(probs.astype(BF16), grad_one)
            dk_acc[pl.ds(start, span), :] += dot(grad_scores, query_one)
            parts.append(
                dot(keys_t[head * HD : (head + 1) * HD, start : start + span], grad_scores)
            )
        dq = jnp.concatenate(parts, axis=0).T * HD**-0.5
        places = pl.ds(lead + start, tile)
        dq_ref[pl.ds(start, tile), :] = (
            dq * cos_ref[places, :] - swap_halves(dq) * sin_ref[places, :]
        ).astype(BF16)
    dk = dk_acc[...]
    dk_ref[...] = (dk * cosine - swap_halves(dk) * sine).astype(BF16)
    dv_ref[...] = dv_acc[...].astype(BF16)


def attend_back(query, keys, values, grad, lse, kseg, qseg, cosine, sine):
    rows, width = query.shape
    span = keys.shape[0]
    tile = min(256, rows)
    pairs = -(-width // (2 * HD))
    columns = lambda count: pl.BlockSpec((count, 2 * HD), lambda i: (0, i))
    return pl.pallas_call(
        functools.partial(attend_back_kernel, tile, width),
        grid=(pairs,),
        in_specs=[
            columns(rows), columns(span), columns(span), columns(rows),
            pl.BlockSpec((1, 2, rows), lambda i: (i, 0, 0)),
            whole((span, 1)), whole((1, rows)), whole((span, 2 * HD)), whole((span, 2 * HD)),
        ],
        out_specs=[columns(rows), columns(span), columns(span)],
        out_shape=[
            jax.ShapeDtypeStruct((rows, width), BF16),
            jax.ShapeDtypeStruct((span, width), BF16),
            jax.ShapeDtypeStruct((span, width), BF16),
        ],
        scratch_shapes=[
            pltpu.VMEM((rows // tile, WINDOW + tile, tile), F32),
            pltpu.VMEM((span, 2 * HD), F32),
            pltpu.VMEM((span, 2 * HD), F32),
        ],
        compiler_params=params(),
        cost_estimate=cost(18),
    )(query, keys, values, grad, lse, kseg, qseg, cosine, sine)


def expert_kernel(which, capacity, parts, experts, full, shared, pieces, added, steps, n_saved, meta_ref, *refs):
    w_all, w_sems = refs[-2:]
    owned = w_all.shape[1] // 3
    order = [kind * owned + j for j in range(owned) for kind in range(3)]
    order += list(range(3 * owned, w_all.shape[1]))
    if pieces:
        count = steps * parts
        x_refs, c_refs, refs = refs[:count], refs[count : 2 * count], refs[2 * count :]
        x_all, c_all, t_all = refs[-5:-2]
        tok, width = x_all.shape[1:]
        block = tok * parts
        for j in range(parts):
            spot = lax.rem(meta_ref[LANE] + parts - j, parts)
            for i in range(steps):

                @pl.when(pl.program_id(0) == i)
                def _():
                    x_all[spot] = x_refs[i * parts + j][...]
                    c_all[spot] = c_refs[i * parts + j][:tok]
                    if j == 0:
                        t_all[...] = c_refs[i * parts][tok:]

        inputs = x_all[...].reshape(block, width)
        cot = c_all[...].reshape(block, width)
        low_table = t_all[...]
    else:
        x_ref, c_ref = refs[:2]
        refs = refs[2:]
        block, width = x_ref.shape[1:]
        tok = block // parts
        inputs = x_ref[0]
        cot = c_ref[0, :block]
        low_table = c_ref[0, block:]
    w_ref, rt_ref = refs[:2]
    refs = refs[2:]

    def weight_copy(which):
        return pltpu.make_async_copy(w_ref.at[:, which], w_all.at[:, which], w_sems.at[which])

    @pl.when(pl.program_id(0) == 0)
    def _():
        for j in range(w_all.shape[1]):
            weight_copy(order[j]).start()

    if added:
        more_dx_ref, more_out_ref = refs[:2]
        refs = refs[2:]
    refs = refs[n_saved:]
    if full:
        dx_ref, out_ref = refs[:2]
        refs = refs[2:]
    sx_ref, sr_ref, sh_ref, sa_ref, sb_ref = refs[:5]
    if shared:
        ssh_ref, ssa_ref, ssb_ref = refs[5:8]
    if pieces:
        ssx_ref, ssc_ref = refs[5:7]
        ssx_ref[0] = inputs
        ssc_ref[0, :block] = cot
        ssc_ref[0, block:] = low_table
    hidden = w_ref.shape[3]
    table = low_table[:, :block].astype(F32)[:experts]

    def weights(which):
        @pl.when(pl.program_id(0) == 0)
        def _():
            weight_copy(which).wait()

        return w_all[:, which].reshape(width, hidden)

    logits = dot_nt(rt_ref[...], inputs)[:experts]
    named = table >= 0.0
    top = jnp.max(jnp.where(named, logits, -1e30), axis=0, keepdims=True)
    expo = jnp.where(named, jnp.exp(logits - top), 0.0)
    gates = expo / jnp.sum(expo, axis=0, keepdims=True)
    row = lax.broadcasted_iota(jnp.int32, (experts, block), 0)
    slot = lax.broadcasted_iota(jnp.int32, (capacity, block), 0).astype(F32)
    hits, spreads, gate_slots = [], [], []
    for j in range(owned):
        mine = row == meta_ref[which] + j
        gate = jnp.sum(jnp.where(mine, gates, 0.0), axis=0, keepdims=True)
        position = jnp.sum(jnp.where(mine, table, 0.0), axis=0, keepdims=True)
        hit = slot == position
        hits.append(hit)
        spreads.append(jnp.where(hit, 1.0, 0.0).astype(BF16))
        gate_slots.append(jnp.sum(jnp.where(hit, gate, 0.0), axis=1, keepdims=True))
    spread = jnp.concatenate(spreads, axis=0)
    routed = dot(spread, inputs).astype(BF16)
    cots = dot(spread, cot)
    gate_slots = jnp.concatenate(gate_slots, axis=0)
    grads = (gate_slots * cots).astype(BF16)

    def branch(left, right, gate_weights, up_weights, down_weights):
        gating = dot(left, gate_weights)
        linear = dot(left, up_weights)
        sigma = jax.nn.sigmoid(gating)
        silu = gating * sigma
        active = (silu * linear).astype(BF16)
        grad_active = dot(right, down_weights)
        slope = sigma * (1.0 + gating * (1.0 - sigma))
        grad_gating = (grad_active * linear * slope).astype(BF16)
        grad_linear = (grad_active * silu).astype(BF16)
        if not full:
            return active, grad_gating, grad_linear
        result = dot_nt(active, down_weights)
        grad_left = dot_nt(grad_gating, gate_weights) + dot_nt(grad_linear, up_weights)
        return active, grad_gating, grad_linear, result, grad_left

    weighted = []
    gate_lines = []
    for j in range(owned):
        rows = slice(j * capacity, (j + 1) * capacity)
        sx_ref[0, j] = routed[rows]
        sr_ref[0, j] = grads[rows]
        got = branch(
            routed[rows], grads[rows], weights(j), weights(owned + j), weights(2 * owned + j))
        sh_ref[0, j], sa_ref[0, j], sb_ref[0, j] = got[:3]
        if full:
            result, grad_left = got[3:]
            grad_gates = jnp.sum(result * cots[rows], axis=1, keepdims=True)
            gate_lines.append(jnp.sum(jnp.where(hits[j], grad_gates, 0.0), axis=0, keepdims=True))
            weighted.append(jnp.concatenate(
                [(gate_slots[rows] * result).astype(BF16), grad_left.astype(BF16)], axis=1))
    if shared:
        units = ssh_ref.shape[2]
        first, second = weights(3 * owned), weights(3 * owned + 1)
        got = branch(inputs, cot, first[:, :units], first[:, units : 2 * units], second[:, :units])
        ssh_ref[0], ssa_ref[0], ssb_ref[0] = got[:3]
    if not full:
        return
    back = dot_tn(spread, jnp.concatenate(weighted, axis=0))
    out, dx = back[:, :width], back[:, width:]
    if shared:
        out = out + got[3]
        dx = dx + got[4]
    line = lax.broadcasted_iota(jnp.int32, (16, width), 0)
    for j in range(parts):
        piece = slice(j * tok, (j + 1) * tok)
        spare = jnp.zeros((1, width - tok), F32)
        extra = jnp.zeros((16, width), F32)
        for i in range(owned):
            padded = jnp.concatenate([gate_lines[i][:, piece], spare], axis=1)
            extra = jnp.where(line == meta_ref[which] + i, padded, extra)
        out_piece, dx_piece = out[piece], dx[piece]
        if added:
            out_piece = out_piece + more_out_ref[0, j].astype(F32)
            dx_piece = dx_piece + more_dx_ref[0, j, :tok].astype(F32)
            extra = extra + more_dx_ref[0, j, tok:].astype(F32)
        out_ref[0, j] = out_piece.astype(BF16)
        dx_ref[0, j, :tok] = dx_piece.astype(BF16)
        dx_ref[0, j, tok:] = extra.astype(BF16)


def expert_shapes(owned, capacity, width, hidden):
    return [(owned, capacity, width)] * 2 + [(owned, capacity, hidden)] * 3


def placed(shape, where):
    return pl.BlockSpec((1,) + shape, lambda i, meta: (where(i, meta),) + (0,) * len(shape))


def expert_blocks(
    first, blocks, steps, capacity, parts, experts, units, full, at, which, sources, weights, router_t, more, saved,
):
    pieces = isinstance(sources[0], list)
    shared = units > 0
    if pieces:
        tok, width = sources[0][0][0].shape
    else:
        block, width = sources[0].shape[1:]
        tok = block // parts
    block = tok * parts
    hidden = weights.shape[3]
    owned = weights.shape[1] // 3
    here = lambda i, meta: first + i
    step = lambda i, meta: i
    shapes = expert_shapes(owned, capacity, width, hidden)
    if shared:
        shapes += [(block, units)] * 3
    if pieces:
        shapes += [(block, width), (block + 16, width)]
    tops = [(parts, tok + 16, width), (parts, tok, width)] if full else []
    outs = [jax.ShapeDtypeStruct((blocks // 2,) + shape, BF16) for shape in tops]
    outs += [jax.ShapeDtypeStruct((blocks,) + shape, BF16) for shape in shapes]
    specs = [placed(shape, here) for shape in tops + shapes]
    if pieces:
        operands = [piece for source in sources for block_pieces in source for piece in block_pieces]
        in_specs = [whole(one.shape) for one in operands]
        scratch = [pltpu.VMEM((parts, tok, width), BF16)] * 2 + [pltpu.VMEM((16, width), BF16)]
    else:
        operands = list(sources)
        in_specs = [placed(one.shape[1:], here) for one in operands]
        scratch = []
    scratch += [pltpu.VMEM(weights.shape, BF16), pltpu.SemaphoreType.DMA((weights.shape[1],))]
    operands += [weights, router_t] + list(more)
    in_specs += [pl.BlockSpec(memory_space=pl.ANY), whole(router_t.shape)] + [placed(one.shape[1:], step) for one in more]
    in_specs += [pl.BlockSpec(memory_space=pl.ANY)] * len(saved)
    return pl.pallas_call(
        functools.partial(
            expert_kernel, which, capacity, parts, experts, full, shared, pieces, len(more) > 0, steps, len(saved)),
        grid_spec=pltpu.PrefetchScalarGridSpec(
            num_scalar_prefetch=1,
            grid=(steps,),
            in_specs=in_specs,
            out_specs=specs,
            scratch_shapes=scratch,
        ),
        out_shape=outs,
        input_output_aliases={1 + len(operands) + i: i for i in range(len(saved))},
        compiler_params=params(),
        cost_estimate=cost((12 if full else 6) * steps),
    )(at, *operands, *saved)


def pair_sums_kernel(counts, index_ref, *refs):
    outs = refs[len(refs) - len(counts) :]
    for count, out_ref in zip(counts, outs):
        job, refs = refs[:count], refs[count:]
        total = job[0][0].astype(F32) + job[1][0].astype(F32)
        for ref in job[2:]:
            total = total + ref[...].astype(F32)
        out_ref[...] = total.astype(BF16)


def pair_sums(at, jobs):
    cut = all(kept.ndim == 4 for _, kept, _, _ in jobs)
    operands, in_specs, out_specs, out_shape = [], [], [], []
    for index, kept, got, far in jobs:
        shape = kept.shape[1:]
        part = ((1,) if cut else shape[:1]) + shape[1:]
        rest = (0,) * (len(shape) - 1)
        picked = pl.BlockSpec((1,) + part, lambda i, at, index=index, rest=rest: (at[index], i) + rest)
        plain = pl.BlockSpec(part, lambda i, at, rest=rest: (i,) + rest)
        operands += [kept, got, *far]
        in_specs += [picked, picked] + [plain] * len(far)
        out_specs.append(plain)
        out_shape.append(jax.ShapeDtypeStruct(shape, BF16))
    return pl.pallas_call(
        functools.partial(pair_sums_kernel, [2 + len(far) for _, _, _, far in jobs]),
        grid_spec=pltpu.PrefetchScalarGridSpec(
            num_scalar_prefetch=1,
            grid=(jobs[0][1].shape[1] if cut else 1,),
            in_specs=in_specs,
            out_specs=out_specs,
        ),
        out_shape=out_shape,
        compiler_params=params(),
        cost_estimate=cost(3),
    )(at, *operands)


def attn_pieces_kernel(meta_ref, kept_ref, got_ref, *refs):
    count = len(refs) - 1
    far_refs, out_refs, all_ref = refs[: count - 4], refs[count - 4 : count], refs[-1]
    total = kept_ref[0].astype(F32) + got_ref[0].astype(F32)
    for ref in far_refs:
        total = total + ref[...].astype(F32)
    share, columns = total.shape
    all_ref[:share] = total
    if share < all_ref.shape[0]:
        all_ref[share:] = jnp.zeros((all_ref.shape[0] - share, columns), F32)
    rows = out_refs[0].shape[0]
    for d, ref in enumerate(out_refs):
        first = lax.rem(meta_ref[PLANE] + d, 4) * rows
        ref[...] = all_ref[pl.ds(pl.multiple_of(first, 16), rows)].astype(BF16)


def attn_pieces(at, kept, got, far):
    share, columns = kept.shape[1:]
    rows = -(-share // 64) * 16
    picked = pl.BlockSpec((1, share, columns), lambda i, at: (at[PAIR], 0, 0))
    return pl.pallas_call(
        attn_pieces_kernel,
        grid_spec=pltpu.PrefetchScalarGridSpec(
            num_scalar_prefetch=1,
            grid=(1,),
            in_specs=[picked, picked] + [whole(one.shape) for one in far],
            out_specs=[whole((rows, columns))] * 4,
            scratch_shapes=[pltpu.VMEM((4 * rows, columns), F32)],
        ),
        out_shape=[jax.ShapeDtypeStruct((rows, columns), BF16)] * 4,
        compiler_params=params(),
        cost_estimate=cost(3),
    )(at, kept, got, *far)


def split_rows(value, core, sent_ref, kept_ref, *at):
    pairs = sent_ref.shape[0]
    share = value.shape[0] // (2 * pairs)
    for q in range(pairs):
        first = value[2 * q * share : (2 * q + 1) * share].astype(BF16)
        second = value[(2 * q + 1) * share : (2 * q + 2) * share].astype(BF16)
        index = (q,) + at
        kept_ref[index] = jnp.where(core == 0, first, second)
        sent_ref[index] = jnp.where(core == 0, second, first)


def weight_kernel(count, core_ref, left_ref, *refs):
    steps, _, slots, rows = left_ref.shape
    left = left_ref[...].reshape(steps * slots, rows)
    for n, right_ref in enumerate(refs[:count]):
        right = right_ref[...].reshape(steps * slots, right_ref.shape[3])
        split_rows(dot_tn(left, right), core_ref[CORE], *refs[count + 2 * n : count + 2 * n + 2], 0)


def weight_grads(core, left, rights, pairs):
    steps, owned, slots, width = left.shape
    columns = rights[0].shape[3]
    share = width // (2 * pairs)
    shape = jax.ShapeDtypeStruct((pairs, owned, share, columns), BF16)
    spec = pl.BlockSpec((pairs, 1, share, columns), lambda j, core: (0, j, 0, 0))
    given = pl.pallas_call(
        functools.partial(weight_kernel, len(rights)),
        grid_spec=pltpu.PrefetchScalarGridSpec(
            num_scalar_prefetch=1,
            grid=(owned,),
            in_specs=[
                pl.BlockSpec((steps, 1, slots, one.shape[3]), lambda j, core: (0, j, 0, 0))
                for one in [left, *rights]
            ],
            out_specs=[spec] * (2 * len(rights)),
        ),
        out_shape=[shape] * (2 * len(rights)),
        compiler_params=params(),
        cost_estimate=cost(5 * len(rights)),
    )(core, left, *rights)
    return [given[2 * n : 2 * n + 2] for n in range(len(rights))]


def shared_grad_kernel(core_ref, x_ref, c_ref, a_ref, b_ref, h_ref, sent_ref, kept_ref, total_ref):
    step = pl.program_id(0)
    block, units = a_ref.shape[1:]

    @pl.when(step == 0)
    def _():
        total_ref[...] = jnp.zeros_like(total_ref)

    total_ref[:, :units] += dot_tn(x_ref[0], a_ref[0])
    total_ref[:, units : 2 * units] += dot_tn(x_ref[0], b_ref[0])
    total_ref[:, 2 * units :] += dot_tn(c_ref[0, :block], h_ref[0])

    @pl.when(step == pl.num_programs(0) - 1)
    def _():
        split_rows(total_ref[...], core_ref[CORE], sent_ref, kept_ref)


def shared_grads(core, x, c, a, b, h, pairs):
    operands = (x, c, a, b, h)
    width, units = x.shape[2], a.shape[2]
    shape = jax.ShapeDtypeStruct((pairs, width // (2 * pairs), 3 * units), BF16)
    return pl.pallas_call(
        shared_grad_kernel,
        grid_spec=pltpu.PrefetchScalarGridSpec(
            num_scalar_prefetch=1,
            grid=(x.shape[0],),
            in_specs=[pl.BlockSpec((1,) + o.shape[1:], lambda i, core: (i, 0, 0)) for o in operands],
            out_specs=[whole(shape.shape), whole(shape.shape)],
            scratch_shapes=[pltpu.VMEM((width, 3 * units), F32)],
        ),
        out_shape=[shape, shape],
        compiler_params=params(),
        cost_estimate=cost(8),
    )(core, *operands)


def attn_grad_kernel(core_ref, hid_ref, dk_ref, dv_ref, dq_ref, gm_ref, at_ref, small_ref, sent_ref, kept_ref):
    lead = hid_ref.shape[0] - dq_ref.shape[0]
    value = jnp.concatenate(
        [
            dot_tn(hid_ref[...], dk_ref[...]),
            dot_tn(hid_ref[...], dv_ref[...]),
            dot_tn(hid_ref[lead:, :], dq_ref[...]),
            dot_tn(gm_ref[...], at_ref[...]),
            small_ref[...].T,
        ],
        axis=1,
    )
    split_rows(value, core_ref[CORE], sent_ref, kept_ref)


def attn_grads_of(core, hid, dk, dv, dq, grad_mixed_low, attended, small, pairs):
    width, cols = hid.shape[1], dk.shape[1]
    shape = jax.ShapeDtypeStruct((pairs, width // (2 * pairs), 4 * cols + small.shape[0]), BF16)
    operands = (hid, dk, dv, dq, grad_mixed_low, attended, small)
    return pl.pallas_call(
        attn_grad_kernel,
        grid_spec=pltpu.PrefetchScalarGridSpec(
            num_scalar_prefetch=1,
            grid=(1,),
            in_specs=[whole(o.shape) for o in operands],
            out_specs=[whole(shape.shape), whole(shape.shape)],
        ),
        out_shape=[shape, shape],
        compiler_params=params(),
        cost_estimate=cost(8),
    )(core, *operands)


def hidden_back_kernel(count, *refs):
    sources = refs[:count]
    dk_ref, dv_ref, dq_ref, w_ref = refs[count : count + 4]
    out_refs, gain_ref = refs[count + 4 : -1], refs[-1]
    cols = dk_ref.shape[1]
    step = pl.program_id(0)

    @pl.when(step == 0)
    def _():
        gain_ref[...] = jnp.zeros_like(gain_ref)

    for i, tok_ref in enumerate(sources):

        @pl.when(step == i)
        def _():
            grad = dot_nt(dk_ref[...], w_ref[:, :cols]) + dot_nt(dv_ref[...], w_ref[:, cols : 2 * cols])
            if i == count - 1:
                grad = grad + dot_nt(dq_ref[...], w_ref[:, 2 * cols : 3 * cols])
            out_refs[i][...] = grad.astype(BF16)
            inputs = tok_ref[...].astype(F32)
            scale = lax.rsqrt(jnp.mean(inputs * inputs, axis=-1, keepdims=True) + EPS)
            gain_ref[...] += jnp.sum(grad * (inputs * scale), axis=0, keepdims=True)


def hidden_back(sources, dk, dv, dq, weights):
    count = len(sources)
    rows, width = sources[0].shape
    cols = dk.shape[1]
    part = pl.BlockSpec((rows, cols), lambda i: (i, 0))
    return pl.pallas_call(
        functools.partial(hidden_back_kernel, count),
        grid=(count,),
        in_specs=[whole((rows, width))] * count
        + [part, part, whole((rows, cols)), whole(weights.shape)],
        out_specs=[whole((rows, width))] * count + [whole((1, width))],
        out_shape=[jax.ShapeDtypeStruct((rows, width), BF16)] * count + [jax.ShapeDtypeStruct((1, width), F32)],
        compiler_params=params(),
        cost_estimate=cost(7),
    )(*sources, dk, dv, dq, weights)


def collect_kernel(places_ref, first_ref, second_ref, out_ref):
    for half, ref in enumerate((first_ref, second_ref)):

        @pl.when(pl.program_id(0) // (pl.num_programs(0) // 2) == half)
        def _():
            out_ref[...] = ref[0].astype(F32)


def collect(at, first, second):
    _, owned, rows, columns = first.shape
    half = 2
    block = (owned, rows, columns)

    def part(start):
        def index(step, at):
            return (jnp.clip(step - start, 0, half - 1), 0, 0, 0)

        return pl.BlockSpec((1,) + block, index)

    return pl.pallas_call(
        collect_kernel,
        grid_spec=pltpu.PrefetchScalarGridSpec(
            num_scalar_prefetch=1,
            grid=(2 * half,),
            in_specs=[part(0), part(half)],
            out_specs=pl.BlockSpec(
                block, lambda step, at: (at[OWN_HALF + step // half] * half + step % half, 0, 0)),
        ),
        out_shape=jax.ShapeDtypeStruct((2 * half * owned, rows, columns), F32),
        compiler_params=params(),
        cost_estimate=cost(5),
    )(at, first, second)


def norm_back(grad, values, scale, gain):
    grad_gain = jnp.sum(grad * values * scale, axis=0)
    scaled = grad * gain
    grad_values = scale * scaled - values * scale * scale * scale * jnp.mean(
        scaled * values, axis=-1, keepdims=True
    )
    return grad_values, grad_gain


def local(
    tokens,
    segments,
    routes,
    query_weight,
    key_weight,
    value_weight,
    out_weight,
    attn_gain,
    ffn_gain,
    router_weight,
    shared_gate,
    shared_up,
    shared_down,
    expert_gate,
    expert_up,
    expert_down,
    cotangent,
):
    fsdp, ctx, tp = (lax.axis_size(a) for a in ("fsdp", "ctx", "tp"))
    pairs = fsdp // 2
    me = lax.axis_index("fsdp")
    pair, core = me // 2, me % 2
    plane = lax.axis_index("ctx")
    lane = lax.axis_index("tp")
    tokens, cotangent, routes = tokens[0], cotangent[0], routes[0]
    block, width = tokens.shape
    share, cols = query_weight.shape
    experts = expert_gate.shape[0]
    hidden_units = expert_gate.shape[2]
    units = shared_gate.shape[1] // 2
    owned = experts // ctx
    top_count = routes.shape[1]
    capacity = 3 * top_count * block // (2 * experts)
    tok = block // tp
    entries = [
        lane, pair, core, plane, owned * plane, owned * (plane ^ 2), plane ^ 2, plane // 2, 1 - plane // 2, plane % 2
    ] + [(pair + j) % pairs for j in range(1, pairs)]
    at = lax.optimization_barrier(jnp.stack(entries).astype(jnp.int32))

    phases = Phases()

    def to_pairs(piece):
        return [pair_shift(piece, d) for d in range(1, pairs)]

    def to_tp(piece):
        return [tp_shift(piece, j) for j in range(1, tp)]

    def joined(*pieces):
        return place(pieces, lane).reshape(block, width)

    other_plane = plane ^ 2

    gains = jnp.concatenate([attn_gain[None], ffn_gain[None]], axis=0)
    qkv_mine, small_mine, tokens_mine = pack(
        at, tp, key_weight, value_weight, query_weight, router_weight.T, gains, tokens)
    small_core = core_swap(small_mine)
    qkv_mine, small_mine, tokens_mine, small_core = phases.run(
        lambda *given: given, qkv_mine, small_mine, tokens_mine, small_core)


    def send_first(qkv, small, small_core, tokens_mine, cotangent):
        prepared = prepare(at, tp, experts, routes.T, cotangent, segments)
        return (
            to_pairs(qkv), core_swap(qkv), to_pairs(jnp.concatenate([small, small_core], axis=0)),
            ctx_open(tokens_mine, 1),
            prepared)

    qkv_far, qkv_core, small_far, prev_one_mine, prepared = phases.run(
        send_first, qkv_mine, small_mine, small_core, tokens_mine, cotangent)
    cosine, sine, kseg, qseg, hits = prepared[:5]
    cot_own = prepared[5:]
    gathered = small_mine, small_core, small_far

    def all_small(small_mine, small_core, small_far):
        rows = place([jnp.concatenate([small_mine, small_core], axis=0)] + small_far, pair)
        rows = rows.reshape(pairs, 2, 16, share)
        rows = jnp.where(core == 0, rows, rows[:, ::-1])
        return rows.reshape(fsdp, 16, share).transpose(1, 0, 2).reshape(16, width)

    def send_second(qkv_far, prev_one_mine, out_weight, gathered, *stacks):
        return (
            [core_swap(one) for one in qkv_far], to_tp(prev_one_mine), ctx_open(prev_one_mine, 1),
            to_pairs(out_weight.T), all_small(*gathered), bundles(at, owned, units, stacks[:3], stacks[3:]))

    qkv_far_core, prev_one_other, prev_two_mine, out_far, small_all, (weights_mine, again_mine) = phases.run(
        send_second, qkv_far, prev_one_mine, out_weight, gathered, expert_gate, expert_up,
        jnp.swapaxes(expert_down, 1, 2), shared_gate, shared_up, shared_down.T)
    weights = lax.all_gather(weights_mine, "fsdp", axis=0)
    attn_scale = small_all[experts : experts + 1].astype(F32)
    ffn_scale = small_all[experts + 1 : experts + 2].astype(F32)
    router_t = jnp.concatenate([small_all[:experts], jnp.zeros((16 - experts, width), BF16)], axis=0)
    router_full = small_all[:experts].T
    here = [(plane + d) % ctx for d in range(ctx)]
    half = ctx // 2

    def near_projection(prev_one_mine, prev_one_other, prev_two_mine, cot, out_weight, out_far, same, cross, scale):
        sent = (
            to_tp(prev_two_mine), ctx_swap(cot), [core_swap(one) for one in [out_weight.T] + out_far])
        return sent, project_near(
            at, tokens, [prev_one_mine] + prev_one_other, same, cross, scale, cosine, sine)

    (prev_two_other, cot_one, out_cross), first = phases.run(
        near_projection, prev_one_mine, prev_one_other, prev_two_mine, cot_own[0], out_weight, out_far,
        [qkv_mine] + qkv_far, [qkv_core] + qkv_far_core, attn_scale)
    query, qkv_full, prev_one = first[3:]

    def attention(prev_two_mine, prev_two_other, cot, cot_one, out_weight, out_far, out_cross):
        sent = ctx_swap(cot, 2), to_tp(cot_one)
        hid, keys, values, prev_two = project_far(
            at, [prev_two_mine] + prev_two_other, qkv_full, attn_scale, cosine, sine, first[:3])
        attended, lse = attend(query, keys, values, kseg, qseg)
        same = place([out_weight.T] + out_far, pair)
        cross = place(out_cross, pair)
        out_full = place_rows([same, cross], core).reshape(width, cols)
        partial = dot_nt(attended, out_full).astype(BF16).reshape(tp, tok, width)
        return sent, hid, keys, values, prev_two, attended, lse, out_full, partial

    (cot_two, cot_one_other), hid, keys, values, prev_two, attended, lse, out_full, partial = phases.run(
        attention, prev_two_mine, prev_two_other, cot_own[0], cot_one, out_weight, out_far, out_cross)

    def sent_tp(total):
        return [tp_shift(pick(total, (lane + j) % tp), j) for j in range(1, tp)]

    def sum_tp(total, got):
        result = pick(total, lane).astype(F32)
        for one in got:
            result = result + one.astype(F32)
        return result

    partial_other, cot_three, again_mine = phases.run(
        lambda partial, cot_two, again_mine: (sent_tp(partial), ctx_swap(cot_two), again_mine),
        partial, cot_two, again_mine)
    other_weights = lax.all_gather(again_mine, "fsdp", axis=0)
    inputs_mine = tokens_mine.astype(F32)

    def normalize(partial, got):
        mixed = inputs_mine + sum_tp(partial, got)
        scale_ffn = lax.rsqrt(jnp.mean(mixed * mixed, axis=-1, keepdims=True) + EPS)
        return (mixed * scale_ffn * ffn_scale).astype(BF16), mixed, scale_ffn

    normed_low, mixed, scale_ffn = phases.run(normalize, partial, partial_other)

    x_zero, x_one = phases.run(lambda one: (to_tp(one), ctx_swap(one)), normed_low)
    half = ctx // 2

    def joint(mine, other):
        return [[one] + list(two) for one, two in zip(mine, other)]

    def blocks_of(first, steps, full, which, with_units, sources, weights, more, saved):
        return expert_blocks(
            first, ctx, steps, capacity, tp, experts, with_units, full, at, which, sources, weights, router_t, more, saved)

    def own_step(first, full, weights, x_pieces, cot_pieces, saved):
        return blocks_of(first, 1, full, OWN_EXPERTS, 0, ([x_pieces], [cot_pieces]), weights, [], saved)

    def block_zero(normed_low, x_zero, cot_own, x_one, cot_two, weights):
        sent = to_tp(x_one), ctx_swap(normed_low, 2), to_tp(cot_two)
        return sent, own_step(0, True, weights, [normed_low] + x_zero, cot_own, [])

    (other_one, x_two, cot_two_other), saved = phases.run(
        block_zero, normed_low, x_zero, cot_own, x_one, cot_two, weights)

    def block_one(x_one, other_one, cot_one, cot_one_other, x_two, cot_three, weights, saved):
        sent = to_tp(x_two), ctx_swap(x_two), to_tp(cot_three)
        return sent, own_step(1, True, weights, [x_one] + other_one, [cot_one] + cot_one_other, saved)

    (other_two, x_three, cot_three_other), saved = phases.run(
        block_one, x_one, other_one, cot_one, cot_one_other, x_two, cot_three, weights, saved)
    more = saved[:2]

    def block_two(x_two, other_two, cot_two, cot_two_other, x_three, weights, saved):
        sent = to_tp(x_three)
        return sent, own_step(2, False, weights, [x_two] + other_two, [cot_two] + cot_two_other, saved)

    other_three, saved = phases.run(
        block_two, x_two, other_two, cot_two, cot_two_other, x_three, weights, saved[2:])

    def weight_step(left, right):
        return weight_grads(at, left, [right], pairs)[0]

    def weight_pair(left, one, two):
        return weight_grads(at, left, [one, two], pairs)

    def own_rest(x_three, other_three, cot_three, cot_three_other, weights, saved):
        saved = own_step(3, False, weights, [x_three] + other_three, [cot_three] + cot_three_other, saved)
        sx, sr, sh, sa, sb = saved[:5]
        down = weight_step(sr, sh)
        return saved, down, core_swap(down[0]), *weight_pair(sx, sa, sb)

    saved, down, down_got, gate, up = phases.run(
        own_rest, x_three, other_three, cot_three, cot_three_other, weights, saved)
    sx, sr, sh, sa, sb, ssx, ssc = saved


    def sums(sent, *own):
        jobs = [(NEXT_PAIR + j - 1, *sent, []) for j in range(1, pairs)] if sent else []
        given = pair_sums(at, jobs + [(PAIR, *one) for one in own])
        return [given[: len(jobs)], *given[len(jobs) :]]

    def sent_pairs(rows):
        return [pair_shift(one, j + 1) for j, one in enumerate(rows)]

    def other_full(down, gate_sent, up_sent, ssx, other_weights, more):
        sent = sent_pairs(sums(down)[0]), core_swap(gate_sent), core_swap(up_sent)
        return sent, blocks_of(0, half, True, FAR_EXPERTS, units, (ssx, ssc), other_weights, more, [])

    (down_far, gate_got, up_got), got = phases.run(
        other_full, (down[1], down_got), gate[0], up[0], ssx, other_weights, more)
    dx, out = (one.reshape((half * tp,) + one.shape[2:]) for one in got[:2])

    def sent_tp_of(stack, block_index):
        return [tp_shift(pick(stack, block_index * tp + (lane + j) % tp), j) for j in range(1, tp)]

    def sum_tp_of(stack, block_index, far):
        result = pick(stack, block_index * tp + lane).astype(F32)
        for one in far:
            result = result + one.astype(F32)
        return result

    def back_through_norm(dx_sum):
        grad_normed = dx_sum[:tok]
        grad_gates = dx_sum[tok : tok + experts, :tok].T
        named = lax.dynamic_slice_in_dim(hits, lane * tok, tok, 1).T > 0.0
        logits = jnp.where(named, dot(normed_low, router_full), -1e30)
        expo = jnp.where(named, jnp.exp(logits - jnp.max(logits, axis=-1, keepdims=True)), 0.0)
        gates = expo / jnp.sum(expo, axis=-1, keepdims=True)
        grad_logits = (
            gates * (grad_gates - jnp.sum(gates * grad_gates, axis=-1, keepdims=True))
        ).astype(BF16)
        grad_normed = grad_normed + dot_nt(grad_logits, router_full)
        grad_mixed_norm, grad_ffn_gain = norm_back(grad_normed, mixed, scale_ffn, ffn_scale)
        grad_out = lax.dynamic_slice_in_dim(cotangent, lane * tok, tok, 0).astype(F32)
        grad_mixed = grad_out + grad_mixed_norm
        return grad_mixed.astype(BF16), grad_mixed, grad_ffn_gain, dot_tn(grad_logits, normed_low)

    def phase_one(gate, dx, down, ssx, saved):
        rows, own_down = sums(gate, down)
        sent = sent_pairs(rows), sent_tp_of(dx, 1), sent_tp_of(dx, 0)
        saved = blocks_of(half, half, False, FAR_EXPERTS, units, (ssx, ssc), other_weights, [], saved)
        return sent, saved, weight_step(saved[1], saved[2]), own_down

    (gate_far, dx_one, dx_zero), other_saved, other_down, own_down = phases.run(
        phase_one, (gate[1], gate_got), dx, (down[1], down_got, down_far), ssx, got[2:])
    ox, orr, oh, oa, ob, ssh, ssa, ssb = other_saved
    groups = [[2 * i, 2 * i + 1] for i in range(ctx // 2)]

    def neighbours(piece):
        return lax.all_gather(piece, "ctx", axis=0, axis_index_groups=groups)

    both_down = neighbours(own_down)

    def phase_two(up, down_sent, dx, dx_one, gate, ox, out):
        rows, own_gate = sums(up, gate)
        sent = (
            sent_pairs(rows), core_swap(down_sent),
            ctx_swap(sum_tp_of(dx, 1, dx_one).astype(BF16)), sent_tp_of(out, 1))
        other_gate, other_up = weight_pair(ox, oa, ob)
        return sent, own_gate, other_gate, other_up

    (up_far, down_got, home, out_one), own_gate, other_gate, other_up = phases.run(
        phase_two, (up[1], up_got), other_down[0], dx, dx_one, (gate[1], gate_got, gate_far), ox, out)

    both_gate = neighbours(own_gate)

    def phase_three(down, gate_sent, both, dx, dx_zero, home, up, ssx, out, out_one):
        back = back_through_norm(sum_tp_of(dx, 0, dx_zero) + home.astype(F32))
        rows, own_up = sums(down, up)
        sent = (
            sent_pairs(rows), core_swap(gate_sent), to_tp(back[0]), ctx_swap(sum_tp_of(out, 1, out_one).astype(BF16)))
        shared = shared_grads(at, ssx, ssc, ssa, ssb, ssh, pairs)
        return sent, back, own_up, shared, both

    sent, back, own_up, shared, both_down = phases.run(
        phase_three, (other_down[1], down_got), other_gate[0], both_down, dx, dx_zero, home, (up[1], up_got, up_far), ssx,
        out, out_one)
    down_far, gate_got, grad_mixed_other, out_home = sent
    both_up = neighbours(own_up)
    grad_mixed_low, grad_mixed, grad_ffn_gain, grad_router = back

    def phase_four(gate, up_sent, shared_sent, both, down, grad_mixed_low, grad_mixed_other, out):
        summed, own_other_down = sums(gate, down)
        sent = sent_pairs(summed), core_swap(up_sent), core_swap(shared_sent), sent_tp_of(out, 0)
        rows = joined(grad_mixed_low, *grad_mixed_other)
        grad_attended = dot(rows, out_full).astype(BF16)
        grads = attend_back(query, keys, values, grad_attended, lse, kseg, qseg, cosine, sine)
        return sent, rows, grads, own_other_down, both

    (gate_far, up_got, shared_got, out_zero), grad_mixed_rows, (dq, dk, dv), own_other_down, both_gate = phases.run(
        phase_four, (other_gate[1], gate_got), other_up[0], shared[0], both_gate,
        (other_down[1], down_got, down_far), grad_mixed_low, grad_mixed_other, out)

    both_other_down = neighbours(own_other_down)

    def phase_five(up, both, dq, dk, dv, hid, gate):
        back = hidden_back([prev_two, prev_one, tokens], dk, dv, dq, qkv_full)
        hidden_parts = [one.reshape(tp, tok, width) for one in back[:-1]]
        small_rows = jnp.concatenate(
            [grad_router, grad_ffn_gain[None], back[-1], jnp.zeros((128 - experts - 2, width), F32)], axis=0)
        rows, own_other_gate = sums(up, gate)
        sent = sent_pairs(rows), sent_tp(hidden_parts[0])
        attn = attn_grads_of(at, hid, dk, dv, dq, grad_mixed_rows, attended, small_rows, pairs)
        return sent, hidden_parts, attn, own_other_gate, both

    (up_far, far_two), hidden_parts, attn, own_other_gate, both_up = phases.run(
        phase_five, (other_up[1], up_got), both_up, dq, dk, dv, hid,
        (other_gate[1], gate_got, gate_far))

    both_other_gate = neighbours(own_other_gate)

    def phase_six(attn, both, hidden_parts, far_two, up, shared, out, out_zero, out_home):
        attn_got = core_swap(attn[0])
        _, own_other_up = sums(None, up)
        sent = (
            sent_pairs(sums((attn[1], attn_got))[0]), ctx_open(sum_tp(hidden_parts[0], far_two).astype(BF16), -1),
            sent_tp(hidden_parts[1]), sent_pairs(sums(shared)[0]))
        output_mine = (mixed + sum_tp_of(out, 0, out_zero) + out_home.astype(F32)).astype(BF16)
        return sent, attn_got, own_other_up, both, collect(at, both_down, both), output_mine, to_tp(output_mine)

    (attn_far, carried, far_one, shared_far), attn_got, own_other_up, both_other_down, grad_expert_down, output_mine, output_other = phases.run(
        phase_six, attn, both_other_down, hidden_parts, far_two, (other_up[1], up_got, up_far), (shared[1], shared_got),
        out, out_zero, out_home)
    both_other_up = neighbours(own_other_up)

    def phase_seven(attn, both, hidden_parts, far_one, carried, both_gate, shared):
        pieces = attn_pieces(at, *attn)
        carried = ctx_open(
            (sum_tp(hidden_parts[1], far_one) + carried.astype(F32)).astype(BF16), -1)
        sent = (
            [ctx_shift(pieces[d], d) for d in range(1, ctx)], carried, sent_tp(hidden_parts[2]))
        return sent, pieces[0], collect(at, both_gate, both), sums(None, shared)[1]

    (attn_got, carried, hidden_other), attn_piece, grad_expert_gate, own_shared = phases.run(
        phase_seven, (attn[1], attn_got, attn_far), both_other_gate, hidden_parts, far_one, carried, both_gate,
        (shared[1], shared_got, shared_far))

    def input_back(total, got, carried):
        grad_hidden = sum_tp(total, got) + carried.astype(F32)
        scale_attn = lax.rsqrt(jnp.mean(inputs_mine * inputs_mine, axis=-1, keepdims=True) + EPS)
        scaled = grad_hidden * attn_scale
        grad_norm = scale_attn * scaled - inputs_mine * scale_attn * scale_attn * scale_attn * jnp.mean(
            scaled * inputs_mine, axis=-1, keepdims=True)
        return (grad_mixed + grad_norm).astype(BF16)

    def phase_eight(
        attn_piece, attn_got, hidden_parts, hidden_other, carried, both_up, both_other_up, own_shared, output_mine, output_other
    ):
        total = attn_piece.astype(F32)
        for one in attn_got:
            total = total + one.astype(F32)
        total = total.astype(BF16)
        input_mine = input_back(hidden_parts[2], hidden_other, carried)
        return (
            total, [ctx_shift(total, d) for d in range(1, ctx)], ctx_swap(own_shared), to_tp(input_mine),
            joined(output_mine, *output_other), input_mine, collect(at, both_up, both_other_up))

    attn_piece, attn_got, far_shared, input_other, output, input_mine, grad_expert_up = phases.run(
        phase_eight, attn_piece, attn_got, hidden_parts, hidden_other, carried, both_up, both_other_up, own_shared,
        output_mine, output_other)
    halves = jnp.where(
        plane % 2 == 0, jnp.stack([own_shared, far_shared]), jnp.stack([far_shared, own_shared])).astype(F32)
    result = [jnp.concatenate([one[:, i * units : (i + 1) * units] for one in halves], axis=1) for i in range(3)]
    input_grad = joined(input_mine, *input_other)
    grad_key_weight, grad_value_weight, grad_query_weight, grad_out_rows, small_out = finish(
        at, tie([attn_piece] + attn_got, grad_expert_up), share, cols)
    small_out = all_sum(small_out, "tp")
    grad_out_rows = grad_out_rows.T
    grad_expert_down = jnp.swapaxes(grad_expert_down, 1, 2)
    grad_shared_gate, grad_shared_up, grad_shared_down = result[0], result[1], result[2].T
    return (
        output[None],
        input_grad[None],
        grad_query_weight,
        grad_key_weight,
        grad_value_weight,
        grad_out_rows,
        small_out[experts + 1],
        small_out[experts],
        small_out[:experts].T,
        grad_shared_gate,
        grad_shared_up,
        grad_shared_down,
        grad_expert_gate,
        grad_expert_up,
        grad_expert_down,
    )


def solution(mesh):
    in_specs = (
        P("fsdp", "ctx", None),
        P("fsdp", None),
        P("fsdp", "ctx", None),
        P("fsdp", "tp"),
        P("fsdp", "tp"),
        P("fsdp", "tp"),
        P("tp", "fsdp"),
        P("fsdp"),
        P("fsdp"),
        P("fsdp", None),
        P("fsdp", "tp"),
        P("fsdp", "tp"),
        P("tp", "fsdp"),
        P(None, "fsdp", "tp"),
        P(None, "fsdp", "tp"),
        P(None, "tp", "fsdp"),
        P("fsdp", "ctx", None),
    )
    out_specs = (
        P("fsdp", "ctx", None),
        P("fsdp", "ctx", None),
        P("fsdp", "tp"),
        P("fsdp", "tp"),
        P("fsdp", "tp"),
        P("tp", "fsdp"),
        P("fsdp"),
        P("fsdp"),
        P("fsdp", None),
        P("fsdp", "tp"),
        P("fsdp", "tp"),
        P("tp", "fsdp"),
        P(None, "fsdp", "tp"),
        P(None, "fsdp", "tp"),
        P(None, "tp", "fsdp"),
    )
    return jax.shard_map(local, mesh=mesh, in_specs=in_specs, out_specs=out_specs, check_vma=False)
```
